32 devices in a mesh: rx: 2 (over core), space: 16 (over z, y, x).
Axes of the slice: x: 2, y: 2, z: 4, core: 2. Of those that a mesh axis runs over, the one named last changes fastest.
Arguments:
- conductivity: float32 [48, 32, 128], P('space'), may hold values from 0.1 to 1
- background: float32 [4, 2, 3, 48, 32, 128], P(None, None, None, 'space'), may hold values from -6 to 6
- warm_start: float32 [4, 2, 3, 48, 32, 128], P('rx', None, None, 'space'), may hold values from -8 to 8
- data_weight: float32 [4, 2, 3], P('rx'), may hold values from -640 to 640
- recv_cell: int32 [4], P('rx'), may hold values from 0 to 196607
- src_group: int32 [4], P('rx'), may hold values from 0 to 3
- group_freq: int32 [4], replicated, may hold values from 0 to 7
Outputs:
- block: float32 [8, 8], P('rx')
- smoothed: bfloat16 [4, 2, 48, 32, 128], P('rx', None, 'space')
The draws below stay inside these ranges and needn't reach their ends.
All inputs are finite; a program needn't handle non-finite values.
Results may differ from the reference program's by a relative error of at most 0.01.
Values may be sent and summed in bfloat16 or wider, within the bound.
No kernel may reach another device: no remote copies, remote signals or barrier semaphores. Data moves between devices by JAX's collectives and lax.ppermute only.
A program may use at most 64 MiB of HBM per device.

```python
import math
import jax
import jax.numpy as jnp
from jax import lax

NY = 32
NZ = 128
G = 4
NFREQ = 8
ITERS = 3
SOURCES = 4
NX = 48


def draw_warm_start(key, part):
    key_common, key_own = jax.random.split(jax.random.fold_in(key, 11))
    common_shape = (1, 2, 3, NX, NY, NZ)
    own_shape = (SOURCES, 2, 3, NX, NY, NZ)
    common = jax.random.normal(key_common, common_shape, jnp.float32)
    own = jax.random.normal(key_own, own_shape, jnp.float32)
    return jnp.clip(common + 0.7 * own, -8.0, 8.0)


def with_ends(values, rng, smallest, largest):
    extent = values.shape
    place = [jax.random.randint(jax.random.fold_in(rng, axis), (), 0, extent[axis]) for axis in range(len(extent))]
    values = values.at[tuple(place)].set(smallest)
    longest = extent.index(max(extent))
    place[longest] = (place[longest] + 1) % extent[longest]
    return values.at[tuple(place)].set(largest)


def block_scale(key, shape, cuts, smallest, high):
    gain, own = 1.0, jax.random.fold_in(key, 6)
    for position, shards_of in cuts:
        draws = jnp.exp(jax.random.uniform(jax.random.fold_in(own, position), (shards_of,), jnp.float32, smallest / len(cuts), high / len(cuts)))
        gain = gain * jnp.repeat(draws, shape[position] // shards_of).reshape([-1 if axis == position else 1 for axis in range(len(shape))])
    return gain


def noise(rng, dims, width, bound, cuts=(), held_as=jnp.bfloat16):
    drawn = jax.random.normal(rng, dims, jnp.float32) * width
    if len(cuts) > 0:
        drawn = block_scale(rng, dims, cuts, -0.22, 0.18) * drawn
    return jnp.clip(drawn, min=-bound, max=bound).astype(held_as)


def setup_inputs(seed: int = 0) -> dict:
    seeds = jax.random.split(jax.random.key(seed), 8)
    return {
        "conductivity": jnp.clip(jnp.exp(math.log(1.0) - 2.3025851 * jax.random.uniform(seeds[0], (NX, NY, NZ), jnp.float32) ** block_scale(seeds[0], (NX, NY, NZ), ((0, 16),), -0.2, 0.2)), 0.1, 1.0),
        "background": noise(seeds[1], (G, 2, 3, NX, NY, NZ), 1.0, 6.0, ((3, 16),), jnp.float32),
        "warm_start": draw_warm_start(jax.random.fold_in(seeds[7], 71), 0),
        "data_weight": noise(seeds[3], (SOURCES, 2, 3), ((NX * NY * NZ) ** 0.5 / 4), 640.0, ((0, 2),), jnp.float32),
        "recv_cell": with_ends(jax.random.randint(seeds[4], (SOURCES,), 0, NX * NY * NZ), jax.random.fold_in(seeds[4], 1), 0, (NX * NY * NZ) - 1).astype(jnp.int32),
        "src_group": with_ends(jax.random.randint(seeds[5], (SOURCES,), 0, G), jax.random.fold_in(seeds[5], 1), 0, G - 1).astype(jnp.int32),
        "group_freq": with_ends(jax.random.randint(seeds[6], (G,), 0, NFREQ), jax.random.fold_in(seeds[6], 1), 0, NFREQ - 1).astype(jnp.int32),
    }


RELAX = 0.2
KAPPA = 0.1


def forward_y(f):
    return jnp.concatenate([f[..., 1:, :] - f[..., :-1, :], -f[..., -1:, :]], axis=-2)


def forward_z(f):
    return jnp.concatenate([f[..., 1:] - f[..., :-1], -f[..., -1:]], axis=-1)


def backward_y(f):
    return jnp.concatenate([f[..., :1, :], f[..., 1:, :] - f[..., :-1, :]], axis=-2)


def backward_z(f):
    return jnp.concatenate([f[..., :1], f[..., 1:] - f[..., :-1]], axis=-1)


def curl_curl(padded):
    comp_x = padded[..., 0, :, :, :]
    comp_y = padded[..., 1, :, :, :]
    comp_z = padded[..., 2, :, :, :]
    low_x = comp_x[..., :-1, :, :]
    low_y = comp_y[..., :-1, :, :]
    low_z = comp_z[..., :-1, :, :]
    mag_x = forward_y(low_z) - forward_z(low_y)
    mag_y = forward_z(low_x) - (comp_z[..., 1:, :, :] - comp_z[..., :-1, :, :])
    mag_z = (comp_y[..., 1:, :, :] - comp_y[..., :-1, :, :]) - forward_y(low_x)
    curl_x = backward_y(mag_z[..., 1:, :, :]) - backward_z(mag_y[..., 1:, :, :])
    curl_y = backward_z(mag_x[..., 1:, :, :]) - (mag_z[..., 1:, :, :] - mag_z[..., :-1, :, :])
    curl_z = (mag_y[..., 1:, :, :] - mag_y[..., :-1, :, :]) - backward_y(mag_x[..., 1:, :, :])
    return jnp.stack([curl_x, curl_y, curl_z], axis=-4)


def operate(adjoint, padded, coef):
    curl = curl_curl(padded)
    real_part = curl[..., 0, :, :, :, :] - coef * adjoint[..., 1, :, :, :, :]
    imag_part = curl[..., 1, :, :, :, :] + coef * adjoint[..., 0, :, :, :, :]
    return jnp.stack([real_part, imag_part], axis=-5)


def sensitivity(adjoint, field, coef):
    field_re = field[..., 0, :, :, :, :]
    field_im = field[..., 1, :, :, :, :]
    adj_re = adjoint[..., 0, :, :, :, :]
    adj_im = adjoint[..., 1, :, :, :, :]
    prod_re = jnp.sum(field_re * adj_re - field_im * adj_im, axis=-4)
    prod_im = jnp.sum(field_re * adj_im + field_im * adj_re, axis=-4)
    return (coef * jnp.stack([prod_re, prod_im], axis=-4)).astype(jnp.bfloat16)


def neighbours_y(f):
    zeros = jnp.zeros_like(f[..., :1, :])
    return jnp.concatenate([f[..., 1:, :], zeros], axis=-2) + jnp.concatenate([zeros, f[..., :-1, :]], axis=-2)


def neighbours_z(f):
    zeros = jnp.zeros_like(f[..., :1])
    return jnp.concatenate([f[..., 1:], zeros], axis=-1) + jnp.concatenate([zeros, f[..., :-1]], axis=-1)


def smooth_step(padded):
    centre = padded[..., 1:-1, :, :]
    near = padded[..., 2:, :, :] + padded[..., :-2, :, :] + neighbours_y(centre) + neighbours_z(centre)
    return centre + KAPPA * (near - 6.0 * centre)


def reference(conductivity, background, warm_start, data_weight, recv_cell, src_group, group_freq):
    cells = NX * NY * NZ
    flat = jnp.arange(cells, dtype=jnp.int32).reshape(NX, NY, NZ)

    def one_source(items):
        start, weight, cell, group = items
        field = background[group]
        angular = 0.25 * jnp.power(jnp.float32(1.25), group_freq[group].astype(jnp.float32))
        coef = angular * conductivity
        point = (flat == cell).astype(jnp.float32)
        source_term = weight[:, :, None, None, None] * point
        adjoint = start
        for sweep in range(ITERS):
            padded = jnp.pad(adjoint, ((0, 0), (0, 0), (1, 1), (0, 0), (0, 0)))
            adjoint = adjoint + RELAX * (source_term - operate(adjoint, padded, coef))
        return sensitivity(adjoint, field, coef)

    rows = lax.map(one_source, (warm_start, data_weight, recv_cell, src_group))

    def smooth_one(row):
        value = row.astype(jnp.float32)
        for sweep in range(2):
            value = smooth_step(jnp.pad(value, ((0, 0), (1, 1), (0, 0), (0, 0))))
        return value.astype(jnp.bfloat16)

    smoothed = lax.map(smooth_one, rows)
    flat_rows = rows.reshape(2 * SOURCES, cells)
    flat_smooth = smoothed.reshape(2 * SOURCES, cells)
    block = jnp.dot(flat_rows, flat_smooth.T, preferred_element_type=jnp.float32) / cells
    return block, smoothed
```

```python
import functools

import jax
import jax.numpy as jnp
from jax import lax
from jax.experimental import pallas as pl
from jax.experimental.pallas import tpu as pltpu
from jax.sharding import PartitionSpec as P

RELAX = 0.2
KAPPA = 0.1
UP = 7
DOWN = 6
REACH = 2
FULL = pl.BlockSpec(memory_space=pltpu.VMEM)
HBM = pl.BlockSpec(memory_space=pltpu.HBM)
SCALARS = pl.BlockSpec(memory_space=pltpu.SMEM)
KERNEL = pltpu.CompilerParams(vmem_limit_bytes=8 * 2**20)
F32 = jnp.float32


class Steps:
    def __init__(self, breadth):
        sub = lax.broadcasted_iota(jnp.int32, (8, breadth), 0)
        lane = lax.broadcasted_iota(jnp.int32, (8, breadth), 1)
        self.breadth = breadth
        self.sub, self.lane = sub, lane
        self.not_last_row, self.not_first_row = sub < 7, sub > 0
        self.not_last, self.not_first = lane < breadth - 1, lane > 0

    def after_y(self, f):
        return f[1:] + [jnp.where(self.not_last_row, pltpu.roll(f[0], 7, 0), 0.0)]

    def before_y(self, f):
        return [jnp.where(self.not_first_row, pltpu.roll(f[-1], 1, 0), 0.0)] + f[:-1]

    def after_z(self, f):
        return [jnp.where(self.not_last, pltpu.roll(v, self.breadth - 1, 1), 0.0) for v in f]

    def before_z(self, f):
        return [jnp.where(self.not_first, pltpu.roll(v, 1, 1), 0.0) for v in f]

    def up_y(self, f):
        return sub_(self.after_y(f), f)

    def up_z(self, f):
        return sub_(self.after_z(f), f)

    def down_y(self, f):
        return sub_(f, self.before_y(f))

    def down_z(self, f):
        return sub_(f, self.before_z(f))


def sub_(a, b):
    return [x - y for x, y in zip(a, b)]


def add_(a, b):
    return [x + y for x, y in zip(a, b)]


def mul_(a, b):
    return [x * y for x, y in zip(a, b)]


def turned(ref, at, turns):
    return [ref[at + (pl.ds(r, 8, stride=turns), slice(None))] for r in range(turns)]


def joined(f, dtype):
    return jnp.concatenate(f, axis=0).astype(dtype)


def parted(value, turns):
    value = value.astype(F32)
    return [value[8 * r : 8 * r + 8] for r in range(turns)]


def angular_of(freq):
    angular = F32(0.25)
    for bit, factor in ((1, 1.25), (2, 1.25**2), (4, 1.25**4)):
        angular = angular * jnp.where((freq & bit) != 0, F32(factor), F32(1.0))
    return angular


def signed(part):
    return jnp.where(part == 0, F32(1.0), F32(-1.0))


class Point:
    def __init__(self, cell, first, turns, steps):
        height, breadth = 8 * turns, steps.breadth
        row = (cell // breadth) % height
        self.plane = cell // (height * breadth) - first
        self.turn = row % turns
        self.here = (steps.sub == row // turns) & (steps.lane == cell % breadth)

    def amount(self, low, high):
        reached = (self.plane >= low) & (self.plane < high)
        return jnp.where(reached, F32(RELAX), F32(0.0)), jnp.clip(self.plane, low, high - 1)


def magnetic_yz(steps, e, e_next):
    ex, ey, ez = e
    if e_next is None:
        hy = add_(steps.up_z(ex), ez)
        hz = [-v - w for v, w in zip(ey, steps.up_y(ex))]
    else:
        hy = sub_(steps.up_z(ex), sub_(e_next[2], ez))
        hz = sub_(sub_(e_next[1], ey), steps.up_y(ex))
    return hy, hz


def curl_back(steps, hx, hy, hz, before):
    hy_before, hz_before = before
    cx = sub_(steps.down_y(hz), steps.down_z(hy))
    cy = sub_(steps.down_z(hx), sub_(hz, hz_before))
    cz = sub_(sub_(hy, hy_before), steps.down_y(hx))
    return cx, cy, cz


def first_kernel(
    start_ref, cond_ref, weight_ref, cell_ref, group_ref, freq_ref, up_ref, down_ref, own_ref, edge_ref, held_ref,
    raw, raw_cond, weight, cell, group, freq, sems,
):
    count, _, _, depth, height, breadth = start_ref.shape
    turns = height // 8
    steps = Steps(breadth)
    pairs = ((start_ref, raw), (cond_ref, raw_cond), (weight_ref, weight), (cell_ref, cell), (group_ref, group), (freq_ref, freq))
    copies = [pltpu.make_async_copy(a, b, sems.at[k]) for k, (a, b) in enumerate(pairs)]
    for copy in copies:
        copy.start()
    for copy in copies:
        copy.wait()
    half = up_ref.dtype
    first = lax.axis_index("space") * depth
    for p in range(depth):
        plane = turned(raw_cond, (p,), turns)
        for r in range(turns):
            held_ref[p, r] = plane[r]
    up_ref[2 * count * UP] = joined([held_ref[depth - 1, r] for r in range(turns)], half)
    down_ref[2 * count * DOWN] = joined([held_ref[0, r] for r in range(turns)], half)

    def one(i, _):
        s, part = i // 2, i % 2
        scale = RELAX * signed(part) * angular_of(freq[group[s]])

        def electric(p):
            return [turned(raw, (s, part, comp, p), turns) for comp in range(3)]

        e = electric(0)
        for k, f in enumerate(e[1:]):
            down_ref[i * DOWN + k] = joined(f, half)
            for r in range(turns):
                edge_ref[i, k, r] = f[r]
        before = [-v for v in e[2]], e[1]
        for p in range(depth):
            e_next = electric(p + 1) if p < depth - 1 else None
            hy, hz = magnetic_yz(steps, e, e_next)
            if e_next is None:
                for k, f in enumerate((hy, hz)):
                    up_ref[i * UP + k] = joined(f, half)
                    for r in range(turns):
                        edge_ref[i, 2 + k, r] = f[r]
            hx = sub_(steps.up_y(e[2]), steps.up_z(e[1]))
            curl = curl_back(steps, hx, hy, hz, before)
            before = hy, hz
            coef = [scale * held_ref[p, r] for r in range(turns)]
            for comp in range(3):
                other = turned(raw, (s, 1 - part, comp, p), turns)
                for r in range(turns):
                    own_ref[i, comp, p, r] = e[comp][r] - RELAX * curl[comp][r] + coef[r] * other[r]
            e = e_next
        point = Point(cell[s], first, turns, steps)
        amount, at = point.amount(0, depth)
        for comp in range(3):
            add = jnp.where(point.here, amount * weight[s, part, comp], 0.0)
            own_ref[i, comp, at, point.turn] = own_ref[i, comp, at, point.turn] + add

        def swept(comp, p):
            return [own_ref[i, comp, p, r] for r in range(turns)]

        for comp in range(3):
            up_ref[i * UP + 2 + comp] = joined(swept(comp, depth - 1), half)
        ex, ey, ez = [swept(comp, depth - 2) for comp in range(3)]
        up_ref[i * UP + 5] = joined(add_(steps.up_z(ex), ez), half)
        up_ref[i * UP + 6] = joined([-v - w for v, w in zip(ey, steps.up_y(ex))], half)
        ex, ey, ez = [swept(comp, 0) for comp in range(3)]
        down_ref[i * DOWN + 2] = joined(ey, half)
        down_ref[i * DOWN + 3] = joined(ez, half)
        down_ref[i * DOWN + 4] = joined(sub_(steps.up_z(ex), swept(2, 1)), half)
        down_ref[i * DOWN + 5] = joined(sub_(swept(1, 1), steps.up_y(ex)), half)
        return 0

    lax.fori_loop(0, 2 * count, one, 0)


def stage_kernel(count, groups_at, scalar_ref, field_ref, out_ref, raw, sems):
    _, _, _, depth, height, _ = field_ref.shape
    turns = height // 8
    copies = []
    for s in range(count):
        group = scalar_ref[groups_at + s].astype(jnp.int32)
        copies.append(pltpu.make_async_copy(field_ref.at[group], raw.at[s], sems.at[s]))
        copies[-1].start()
    for copy in copies:
        copy.wait()

    def one(i, _):
        s, part = i // 2, i % 2
        for comp in range(3):
            for p in range(depth):
                plane = turned(raw, (s, part, comp, p), turns)
                for r in range(turns):
                    out_ref[i, comp, p, r] = plane[r]
        return 0

    lax.fori_loop(0, 2 * count, one, 0)


def sweep_kernel(
    scalar_ref, own_ref, edge_ref, held_ref, field_ref, low_ref, high_ref, rows_ref, up_ref, down_ref, one_, two_,
):
    parts, _, depth, turns, _, breadth = own_ref.shape
    count = parts // 2
    height = 8 * turns
    steps = Steps(breadth)
    first = scalar_ref[0].astype(jnp.int32)
    planes = scalar_ref[1].astype(jnp.int32)
    relax_low = jnp.where(first > 0, F32(RELAX), F32(0.0))
    relax_high = jnp.where(first + depth < planes, F32(RELAX), F32(0.0))
    weights_at = scalar_ref.shape[0] - 6 * count

    def angular_at(s):
        group = scalar_ref[2 + count + s].astype(jnp.int32)
        return angular_of(scalar_ref[2 + 2 * count + group].astype(jnp.int32))

    def load(ref, i, comp, p):
        return [ref[i, comp, p + 1, r] for r in range(turns)]

    def store(ref, i, comp, p, f):
        for r in range(turns):
            ref[i, comp, p + 1, r] = f[r]

    def scaled(a, f, factor):
        return [x + factor * y for x, y in zip(a, f)]

    def conductivity(p):
        if p < 0:
            return parted(low_ref[parts * UP], turns)
        if p >= depth:
            return parted(high_ref[parts * DOWN], turns)
        return [held_ref[p, r] for r in range(turns)]

    def add_point(ref, i, low, high):
        s, part = i // 2, i % 2
        point = Point(scalar_ref[2 + s].astype(jnp.int32), first, turns, steps)
        amount, at = point.amount(low, high)
        for comp in range(3):
            add = jnp.where(point.here, amount * scalar_ref[weights_at + i * 3 + comp], 0.0)
            ref[i, comp, at + 1, point.turn] = ref[i, comp, at + 1, point.turn] + add

    def received(ref, at):
        return parted(ref[at], turns)

    def join_slabs(i, _):
        ey, ez, ly, lz = [[edge_ref[i, k, r] for r in range(turns)] for k in range(4)]
        cross = add_(steps.down_y(ey), steps.down_z(ez))
        below = [received(low_ref, i * UP + 2 + comp) for comp in range(3)]
        store(one_, i, 0, -1, scaled(below[0], cross, -relax_low))
        store(one_, i, 1, -1, scaled(below[1], ey, relax_low))
        store(one_, i, 2, -1, scaled(below[2], ez, relax_low))
        low_y, low_z = received(low_ref, i * UP), received(low_ref, i * UP + 1)
        high_y, high_z = received(high_ref, i * DOWN), received(high_ref, i * DOWN + 1)
        cross = add_(steps.down_y(high_y), steps.down_z(high_z))
        for p in range(depth):
            e = [[own_ref[i, comp, p, r] for r in range(turns)] for comp in range(3)]
            if p == 0:
                e[1] = scaled(e[1], low_z, -RELAX)
                e[2] = scaled(e[2], low_y, RELAX)
            if p == depth - 1:
                e = [scaled(e[0], cross, -RELAX), scaled(e[1], high_y, RELAX), scaled(e[2], high_z, RELAX)]
            for comp in range(3):
                store(one_, i, comp, p, e[comp])
        store(one_, i, 1, depth, scaled(received(high_ref, i * DOWN + 2), lz, -relax_high))
        store(one_, i, 2, depth, scaled(received(high_ref, i * DOWN + 3), ly, relax_high))
        return 0

    def second_sweep(i, _):
        s, part = i // 2, i % 2
        other = i + 1 - 2 * part
        scale = RELAX * signed(part) * angular_at(s)
        e = [load(one_, i, comp, -1) for comp in range(3)]
        before = sub_(received(low_ref, i * UP + 5), e[2]), add_(received(low_ref, i * UP + 6), e[1])
        for p in range(-1, depth + 1):
            relax = relax_low if p < 0 else relax_high if p == depth else F32(RELAX)
            if p < depth:
                e_next = [load(one_, i, comp, p + 1) if comp or p < depth - 1 else None for comp in range(3)]
                hy, hz = magnetic_yz(steps, e, e_next)
            else:
                hy = add_(received(high_ref, i * DOWN + 4), e[2])
                hz = sub_(received(high_ref, i * DOWN + 5), e[1])
            hx = sub_(steps.up_y(e[2]), steps.up_z(e[1]))
            if p < depth:
                curl = curl_back(steps, hx, hy, hz, before)
            else:
                curl = None, sub_(steps.down_z(hx), sub_(hz, before[1])), sub_(sub_(hy, before[0]), steps.down_y(hx))
            before = hy, hz
            coef = [scale * v for v in conductivity(p)]
            for comp in range(1 if p == depth else 0, 3):
                beside = load(one_, other, comp, p)
                store(
                    two_, i, comp, p,
                    [e[comp][r] - relax * curl[comp][r] + coef[r] * beside[r] for r in range(turns)],
                )
            e = e_next
        add_point(two_, i, -1, depth + 1)
        return 0

    def third_sweep(i, _):
        s, part = i // 2, i % 2
        other = i + 1 - 2 * part
        scale = RELAX * signed(part) * angular_at(s)
        e = [load(two_, i, comp, 0) for comp in range(3)]
        before = magnetic_yz(steps, [load(two_, i, comp, -1) for comp in range(3)], e)
        for p in range(depth):
            e_next = [load(two_, i, comp, p + 1) if comp or p < depth - 1 else None for comp in range(3)]
            hy, hz = magnetic_yz(steps, e, e_next)
            hx = sub_(steps.up_y(e[2]), steps.up_z(e[1]))
            curl = curl_back(steps, hx, hy, hz, before)
            before = hy, hz
            coef = [scale * v for v in conductivity(p)]
            for comp in range(3):
                beside = load(two_, other, comp, p)
                store(
                    one_, i, comp, p,
                    [e[comp][r] - RELAX * curl[comp][r] + coef[r] * beside[r] for r in range(turns)],
                )
            e = e_next
        add_point(one_, i, 0, depth)
        return 0

    def sensitivity(s, _):
        angular = angular_at(s)
        for p in range(depth):
            total = [[None] * turns, [None] * turns]
            for r in range(turns):
                row_re = row_im = jnp.zeros((8, breadth), F32)
                for comp in range(3):
                    re, im = one_[2 * s, comp, p + 1, r], one_[2 * s + 1, comp, p + 1, r]
                    field_re, field_im = field_ref[2 * s, comp, p, r], field_ref[2 * s + 1, comp, p, r]
                    row_re += field_re * re - field_im * im
                    row_im += field_re * im + field_im * re
                coef = angular * held_ref[p, r]
                total[0][r] = coef * row_re
                total[1][r] = coef * row_im
            for part in range(2):
                value = joined(total[part], rows_ref.dtype)
                rows_ref[s, part, p] = value
                if p >= depth - REACH:
                    up_ref[s, part, p - depth + REACH] = value
                if p < REACH:
                    down_ref[s, part, p] = value
        return 0

    lax.fori_loop(0, parts, join_slabs, 0)
    lax.fori_loop(0, parts, second_sweep, 0)
    lax.fori_loop(0, parts, third_sweep, 0)
    lax.fori_loop(0, count, sensitivity, 0)


def smooth_kernel(scale, scalar_ref, rows_ref, low_ref, high_ref, all_ref, smooth_ref, block_ref, lines):
    count, _, depth, height, breadth = rows_ref.shape
    ranks = all_ref.shape[0]
    turns = height // 8
    steps = Steps(breadth)
    first = scalar_ref[0].astype(jnp.int32)
    planes = scalar_ref[1].astype(jnp.int32)
    below = jnp.where(first > 0, F32(1.0), F32(0.0))
    above = jnp.where(first + depth < planes, F32(1.0), F32(0.0))
    many = ranks * count * 2

    def near(before, centre, after):
        total = add_(add_(before, after), add_(steps.after_y(centre), steps.before_y(centre)))
        total = add_(total, add_(steps.after_z(centre), steps.before_z(centre)))
        return [c + KAPPA * (t - 6.0 * c) for c, t in zip(centre, total)]

    sums = []
    for s in range(count):
        for part in range(2):
            value = [parted(low_ref[s, part, p], turns) for p in range(REACH)]
            value += [parted(rows_ref[s, part, p], turns) for p in range(depth)]
            value += [parted(high_ref[s, part, p], turns) for p in range(REACH)]
            once = [near(*value[i - 1 : i + 2]) for i in range(1, depth + 3)]
            once[0] = [v * below for v in once[0]]
            once[-1] = [v * above for v in once[-1]]
            twice = [near(*once[i - 1 : i + 2]) for i in range(1, depth + 1)]
            slot = 2 * s + part
            for p in range(depth):
                for r in range(turns):
                    lines[slot, p, pl.ds(r, 8, stride=turns), :] = twice[p][r]
                smooth_ref[s, part, p] = lines[slot, p].astype(smooth_ref.dtype)
            twice = [[v.astype(smooth_ref.dtype).astype(F32) for v in f] for f in twice]
            for r in range(ranks):
                for t in range(count):
                    for q in range(2):
                        total = None
                        for p in range(depth):
                            for prod in mul_(twice[p], parted(all_ref[r, t, q, p], turns)):
                                total = prod if total is None else total + prod
                        sums.append(total)
    ones = jnp.ones((breadth, breadth), F32)
    table = jnp.concatenate(sums, axis=0)
    table = jnp.dot(table, ones, precision=lax.Precision.HIGHEST, preferred_element_type=F32)
    for a in range(2 * count):
        line = jnp.zeros((8, breadth), F32)
        for b in range(many):
            at = (a * many + b) * 8
            line = line + jnp.where(steps.lane == b, table[at : at + 8], 0.0)
        line = jnp.sum(line, axis=0, keepdims=True) * scale
        for peer in range(block_ref.shape[0]):
            block_ref[peer, a : a + 1, :] = line[:, :many]


def shards(conductivity, background, warm_start, data_weight, recv_cell, src_group, group_freq):
    count = warm_start.shape[0]
    depth, height, breadth = conductivity.shape
    turns = height // 8
    peers = lax.axis_size("space")
    ranks = lax.axis_size("rx")
    cells = depth * height * breadth * peers
    half = jnp.bfloat16
    first = lax.axis_index("space") * depth
    place = jnp.stack([first, jnp.int32(peers * depth)])
    integers = jnp.concatenate([place, recv_cell, src_group, group_freq]).astype(F32)
    scalars = jnp.concatenate([integers, data_weight.reshape(-1)])
    rising = [(i, i + 1) for i in range(peers - 1)]
    falling = [(i + 1, i) for i in range(peers - 1)]
    shape = jax.ShapeDtypeStruct

    plane = (turns, 8, breadth)
    up, down, own, edge, held = pl.pallas_call(
        first_kernel,
        out_shape=(
            shape((2 * count * UP + 1, height, breadth), half),
            shape((2 * count * DOWN + 1, height, breadth), half),
            shape((2 * count, 3, depth) + plane, F32),
            shape((2 * count, 4) + plane, F32),
            shape((depth,) + plane, F32),
        ),
        in_specs=[HBM] * 6,
        out_specs=(FULL,) * 5,
        scratch_shapes=[
            pltpu.VMEM(warm_start.shape, F32),
            pltpu.VMEM(conductivity.shape, F32),
            pltpu.SMEM(data_weight.shape, F32),
            pltpu.SMEM(recv_cell.shape, jnp.int32),
            pltpu.SMEM(src_group.shape, jnp.int32),
            pltpu.SMEM(group_freq.shape, jnp.int32),
            pltpu.SemaphoreType.DMA((6,)),
        ],
        compiler_params=KERNEL,
        name="first_sweep",
    )(warm_start, conductivity, data_weight, recv_cell, src_group, group_freq)
    low = lax.ppermute(up, "space", rising)
    high = lax.ppermute(down, "space", falling)

    field = pl.pallas_call(
        functools.partial(stage_kernel, count, 2 + count),
        out_shape=shape((2 * count, 3, depth) + plane, F32),
        in_specs=[SCALARS, HBM],
        out_specs=FULL,
        scratch_shapes=[
            pltpu.VMEM((count,) + background.shape[1:], F32),
            pltpu.SemaphoreType.DMA((count,)),
        ],
        compiler_params=KERNEL,
        name="stage_field",
    )(scalars, background)

    rows_of = shape((count, 2, depth, height, breadth), half)
    ends_of = shape((count, 2, REACH, height, breadth), half)
    adjoint_scratch = pltpu.VMEM((2 * count, 3, depth + 2) + plane, F32)
    rows, up, down = pl.pallas_call(
        sweep_kernel,
        out_shape=(rows_of, ends_of, ends_of),
        in_specs=[SCALARS] + [FULL] * 6,
        out_specs=(FULL,) * 3,
        scratch_shapes=[adjoint_scratch, adjoint_scratch],
        compiler_params=KERNEL,
        name="sweeps",
    )(scalars, own, edge, held, field, low, high)
    low = lax.ppermute(up, "space", rising)
    high = lax.ppermute(down, "space", falling)
    every = lax.all_gather(rows, "rx", axis=0)

    many = 2 * count * ranks
    smoothed, partial_block = pl.pallas_call(
        functools.partial(smooth_kernel, 1.0 / cells),
        out_shape=(rows_of, shape((peers, 2 * count, many), F32)),
        in_specs=[SCALARS] + [FULL] * 4,
        out_specs=(FULL, FULL),
        scratch_shapes=[pltpu.VMEM((2 * count, depth, height, breadth), F32)],
        compiler_params=KERNEL,
        name="smooth",
    )(scalars, rows, low, high, every)
    pieces = lax.all_to_all(partial_block, "space", 0, 0)
    return (jnp.sum(pieces, axis=0), smoothed)


def solution(mesh):
    in_specs = (
        P("space", None, None),
        P(None, None, None, "space", None, None),
        P("rx", None, None, "space", None, None),
        P("rx", None, None),
        P("rx"),
        P("rx"),
        P(),
    )
    out_specs = (P("rx", None), P("rx", None, "space", None, None))
    return jax.shard_map(shards, mesh=mesh, in_specs=in_specs, out_specs=out_specs, check_vma=False)
```

```python
import functools

import jax
import jax.numpy as jnp
from jax import lax
from jax.experimental import pallas as pl
from jax.experimental.pallas import tpu as pltpu
from jax.sharding import PartitionSpec as P

SENT = 6
RELAX = 0.2
KAPPA = 0.1
REACH = 2
FULL = pl.BlockSpec(memory_space=pltpu.VMEM)
HBM = pl.BlockSpec(memory_space=pltpu.HBM)
SCALARS = pl.BlockSpec(memory_space=pltpu.SMEM)
KERNEL = pltpu.CompilerParams(vmem_limit_bytes=8 * 2**20)
F32 = jnp.float32


class Steps:
    def __init__(self, height, breadth):
        self.height, self.breadth = height, breadth
        self.sub = lax.broadcasted_iota(jnp.int32, (8, breadth), 0)
        self.lane = lax.broadcasted_iota(jnp.int32, (height, breadth), 1)

    def after_y(self, f):
        f = pltpu.roll(f, self.height - 1, 0)
        return jnp.concatenate([f[:-8], jnp.where(self.sub < 7, f[-8:], 0.0)], axis=0)

    def before_y(self, f):
        f = pltpu.roll(f, 1, 0)
        return jnp.concatenate([jnp.where(self.sub > 0, f[:8], 0.0), f[8:]], axis=0)

    def after_z(self, f):
        return jnp.where(self.lane < self.breadth - 1, pltpu.roll(f, self.breadth - 1, 1), 0.0)

    def before_z(self, f):
        return jnp.where(self.lane > 0, pltpu.roll(f, 1, 1), 0.0)

    def up_y(self, f):
        return self.after_y(f) - f

    def up_z(self, f):
        return self.after_z(f) - f

    def down_y(self, f):
        return f - self.before_y(f)

    def down_z(self, f):
        return f - self.before_z(f)

    def magnetic_yz(self, e, e_next):
        ex, ey, ez = e
        if e_next is None:
            return self.up_z(ex) + ez, -ey - self.up_y(ex)
        return self.up_z(ex) - (e_next[2] - ez), (e_next[1] - ey) - self.up_y(ex)

    def magnetic_x(self, e):
        return self.up_y(e[2]) - self.up_z(e[1])

    def curl_back(self, comp, hx, hy, hz, before):
        if comp == 0:
            return self.down_y(hz) - self.down_z(hy)
        if comp == 1:
            return self.down_z(hx) - (hz - before[1])
        return (hy - before[0]) - self.down_y(hx)


def angular_of(freq):
    angular = F32(0.25)
    for bit, factor in ((1, 1.25), (2, 1.25**2), (4, 1.25**4)):
        angular = angular * jnp.where((freq & bit) != 0, F32(factor), F32(1.0))
    return angular


def split(number, size):
    if size & (size - 1):
        return number // size, number % size
    return number >> (size.bit_length() - 1), number & (size - 1)


class Point:
    def __init__(self, cell, first, steps):
        plane, inner = split(cell, steps.height * steps.breadth)
        row, lane = split(inner, steps.breadth)
        block, sub = split(row, 8)
        self.plane = plane - first
        self.rows = pl.ds(pl.multiple_of(block * 8, 8), 8)
        self.row, self.sub, self.lane, self.steps = row, sub, lane, steps

    def spread(self, value):
        here = (self.steps.sub == self.sub) & (self.steps.lane[:8] == self.lane)
        return jnp.where(here, RELAX * value, 0.0)

    def add_to(self, ref, low, high, shift, weight):
        @pl.when((self.plane >= low) & (self.plane < high))
        def _():
            for part in range(2):
                for comp in range(3):
                    at = (part, comp, self.plane + shift, self.rows)
                    ref[at] = ref[at] + self.spread(weight(part, comp))


def first_kernel(s, *refs):
    if s == 0:
        start_ref, cond_ref, weight_ref, cell_ref, group_ref, freq_ref = refs[:6]
        far_ref, near_ref, own_ref, edge_ref, held_ref, later_ref = refs[6:12]
        raw, weight, cell, group, freq, sent, sems = refs[12:]
        pairs = [
            (cell_ref, cell), (group_ref, group), (freq_ref, freq), (weight_ref, weight),
            (start_ref.at[0], raw), (cond_ref, held_ref), (start_ref.at[pl.ds(1, later_ref.shape[0])], later_ref),
        ]
    else:
        later_ref, held_ref, weight_ref, cell_ref, group_ref, freq_ref = refs[:6]
        far_ref, near_ref, own_ref, edge_ref = refs[6:10]
        weight, cell, group, freq, sent, sems = refs[10:]
        raw = later_ref.at[s - 1]
        pairs = [(cell_ref, cell), (group_ref, group), (freq_ref, freq), (weight_ref, weight)]
    depth, height, breadth = held_ref.shape
    copies = [pltpu.make_async_copy(a, b, sems.at[k]) for k, (a, b) in enumerate(pairs)]
    for copy in copies:
        copy.start()
    for copy in copies[:6]:
        copy.wait()
    steps = Steps(height, breadth)
    half = far_ref.dtype
    index = lax.axis_index("space")
    first = index * depth
    down = index & 1
    up = 1 - down
    scale = RELAX * angular_of(freq[group[s]])
    scales = scale, -scale
    point = Point(cell[s], first, steps)
    if s == 0:
        sent[up, 2 * SENT] = held_ref[depth - 1].astype(half)
        sent[down, 2 * SENT] = held_ref[0].astype(half)

    before = []
    for part in range(2):
        ey, ez = raw[part, 1, 0], raw[part, 2, 0]
        for k, f in enumerate((ey, ez)):
            sent[down, part * SENT + k] = f.astype(half)
            edge_ref[part, k] = f
        before.append((-ez, ey))
    for p in range(depth):
        for part in range(2):
            e = [raw[part, comp, p] for comp in range(3)]
            e_next = [None if comp == 0 else raw[part, comp, p + 1] for comp in range(3)] if p < depth - 1 else None
            hy, hz = steps.magnetic_yz(e, e_next)
            if e_next is None:
                for k, f in enumerate((hy, hz)):
                    sent[up, part * SENT + k] = f.astype(half)
                    edge_ref[part, 2 + k] = f
            hx = steps.magnetic_x(e)
            coef = scales[part] * held_ref[p]
            for comp in range(3):
                curl = steps.curl_back(comp, hx, hy, hz, before[part])
                own_ref[part, comp, p] = e[comp] - RELAX * curl + coef * raw[1 - part, comp, p]
            before[part] = hy, hz
    point.add_to(own_ref, 0, depth, 0, lambda part, comp: weight[s, part, comp])

    last = depth - 1
    at_last = jnp.where(point.plane == last, F32(1.0), F32(0.0))
    row = lax.broadcasted_iota(jnp.int32, (height, breadth), 0)
    here = jnp.where((row == point.row) & (steps.lane == point.lane), RELAX * at_last, 0.0)
    for part in range(2):
        ex, ey, ez = [own_ref[part, comp, 0] for comp in range(3)]
        hy, hz = steps.up_z(ex) - own_ref[part, 2, 1], own_ref[part, 1, 1] - steps.up_y(ex)
        for k, f in enumerate((ey, ez, hy, hz)):
            sent[down, part * SENT + 2 + k] = f.astype(half)
        e = [own_ref[part, comp, last] for comp in range(3)]
        behind = steps.magnetic_yz([own_ref[part, comp, last - 1] for comp in range(3)], e)
        hy, hz = steps.magnetic_yz(e, None)
        hx = steps.magnetic_x(e)
        coef = scales[part] * held_ref[last]
        after = []
        for comp in range(3):
            curl = steps.curl_back(comp, hx, hy, hz, behind)
            value = e[comp] - RELAX * curl + coef * own_ref[1 - part, comp, last]
            after.append(value + here * weight[s, part, comp])
        for k, f in enumerate((hy, hz) + steps.magnetic_yz(after, None)):
            sent[up, part * SENT + 2 + k] = f.astype(half)
    far_ref[...] = sent[0]
    near_ref[...] = sent[1]
    for copy in copies[6:]:
        copy.wait()


def stage_kernel(count, groups_at, scalar_ref, field_ref, out_ref, sems):
    copies = []
    for s in range(count):
        group = scalar_ref[groups_at + s].astype(jnp.int32)
        copies.append(pltpu.make_async_copy(field_ref.at[group], out_ref.at[s], sems.at[s]))
        copies[-1].start()
    for copy in copies:
        copy.wait()


def sweep_kernel(s, count, *refs):
    last = s == count - 1
    if last:
        scalar_ref, own_ref, edge_ref, held_ref, field_ref, far_in, near_in, far_cond, near_cond = refs[:9]
        earlier = refs[9 : 9 + s]
        rows_ref, far_ref, near_ref, one_, two_, got, conds, sent = refs[9 + s :]
    else:
        scalar_ref, own_ref, edge_ref, held_ref, field_ref, far_in, near_in, far_cond, near_cond = refs[:9]
        rows_ref, one_, two_, got, conds = refs[9:]
    depth, height, breadth = held_ref.shape
    steps = Steps(height, breadth)
    first = scalar_ref[0].astype(jnp.int32)
    planes = scalar_ref[1].astype(jnp.int32)
    relax_low = jnp.where(first > 0, F32(RELAX), F32(0.0))
    relax_high = jnp.where(first + depth < planes, F32(RELAX), F32(0.0))
    group = scalar_ref[2 + count + s].astype(jnp.int32)
    angular = angular_of(scalar_ref[2 + 2 * count + group].astype(jnp.int32))
    scales = RELAX * angular, -RELAX * angular
    point = Point(scalar_ref[2 + s].astype(jnp.int32), first, steps)
    weights_at = scalar_ref.shape[0] - 6 * count + 6 * s
    odd = lax.axis_index("space") & 1
    low, high = odd, 1 - odd
    got[0] = far_in[...]
    got[1] = near_in[...]
    conds[0] = far_cond[2 * SENT]
    conds[1] = near_cond[2 * SENT]

    def received(side, part, k):
        return got[side, part * SENT + k].astype(F32)

    def conductivity(p):
        if p < 0:
            return conds[low].astype(F32)
        if p >= depth:
            return conds[high].astype(F32)
        return held_ref[p]

    def weight(part, comp):
        return scalar_ref[weights_at + part * 3 + comp]

    for part in range(2):
        ey, ez, ly, lz = [edge_ref[part, k] for k in range(4)]
        one_[part, 0, 0] = -relax_low * (steps.down_y(ey) + steps.down_z(ez))
        one_[part, 1, 0] = relax_low * ey
        one_[part, 2, 0] = relax_low * ez
        e = [own_ref[part, comp, 0] for comp in range(3)]
        one_[part, 0, 1] = e[0]
        one_[part, 1, 1] = e[1] - RELAX * received(low, part, 1)
        one_[part, 2, 1] = e[2] + RELAX * received(low, part, 0)
        for p in range(1, depth - 1):
            for comp in range(3):
                one_[part, comp, p + 1] = own_ref[part, comp, p]
        e = [own_ref[part, comp, depth - 1] for comp in range(3)]
        high_y, high_z = received(high, part, 0), received(high, part, 1)
        one_[part, 0, depth] = e[0] - RELAX * (steps.down_y(high_y) + steps.down_z(high_z))
        one_[part, 1, depth] = e[1] + RELAX * high_y
        one_[part, 2, depth] = e[2] + RELAX * high_z
        one_[part, 1, depth + 1] = received(high, part, 2) - relax_high * lz
        one_[part, 2, depth + 1] = received(high, part, 3) + relax_high * ly

    before = [(-one_[part, 2, 0], one_[part, 1, 0]) for part in range(2)]
    for p in range(-1, depth + 1):
        relax = relax_low if p < 0 else relax_high if p == depth else F32(RELAX)
        for part in range(2):
            e = [one_[part, comp, p + 1] if comp or p < depth else None for comp in range(3)]
            if p < depth:
                e_next = [None if comp == 0 else one_[part, comp, p + 2] for comp in range(3)]
                hy, hz = steps.magnetic_yz(e, e_next)
            else:
                hy, hz = received(high, part, 4) + e[2], received(high, part, 5) - e[1]
            hx = steps.magnetic_x(e)
            coef = scales[part] * conductivity(p)
            for comp in range(1 if p == depth else 0, 3):
                curl = steps.curl_back(comp, hx, hy, hz, before[part])
                two_[part, comp, p + 1] = e[comp] - relax * curl + coef * one_[1 - part, comp, p + 1]
            if p < 0:
                hy, hz = hy + received(low, part, 2), hz + received(low, part, 3)
            before[part] = hy, hz
    point.add_to(two_, 0, depth + 1, 1, weight)

    before = []
    for part in range(2):
        e = [two_[part, comp, 0] for comp in range(3)]
        hy, hz = steps.magnetic_yz(e, [None, two_[part, 1, 1], two_[part, 2, 1]])
        before.append((hy + received(low, part, 4), hz + received(low, part, 5)))
    for p in range(depth):
        for part in range(2):
            e = [two_[part, comp, p + 1] for comp in range(3)]
            hy, hz = steps.magnetic_yz(e, [None, two_[part, 1, p + 2], two_[part, 2, p + 2]])
            hx = steps.magnetic_x(e)
            coef = scales[part] * conductivity(p)
            for comp in range(3):
                curl = steps.curl_back(comp, hx, hy, hz, before[part])
                one_[part, comp, p + 1] = e[comp] - RELAX * curl + coef * two_[1 - part, comp, p + 1]
            before[part] = hy, hz
    point.add_to(one_, 0, depth, 1, weight)

    for p in range(depth):
        row_re = row_im = None
        for comp in range(3):
            re, im = one_[0, comp, p + 1], one_[1, comp, p + 1]
            field_re, field_im = field_ref[s, 0, comp, p], field_ref[s, 1, comp, p]
            add_re, add_im = field_re * re - field_im * im, field_re * im + field_im * re
            row_re, row_im = (add_re, add_im) if comp == 0 else (row_re + add_re, row_im + add_im)
        coef = angular * held_ref[p]
        for part, value in enumerate((row_re, row_im)):
            value = (coef * value).astype(rows_ref.dtype)
            if not last:
                rows_ref[part, p] = value
                continue
            rows_ref[s, part, p] = value
            if p >= depth - REACH:
                sent[high, s, part, p - depth + REACH] = value
            if p < REACH:
                sent[low, s, part, p] = value
    if last:
        for t, ref in enumerate(earlier):
            rows_ref[t] = ref[...]
            sent[high, t] = ref[:, depth - REACH :]
            sent[low, t] = ref[:, :REACH]
        far_ref[...] = sent[0]
        near_ref[...] = sent[1]


def smooth_kernel(scale, scalar_ref, rows_ref, far_in, near_in, all_ref, smooth_ref, block_ref, got):
    count, _, depth, height, breadth = rows_ref.shape
    ranks = all_ref.shape[0]
    steps = Steps(height, breadth)
    first = scalar_ref[0].astype(jnp.int32)
    planes = scalar_ref[1].astype(jnp.int32)
    below = jnp.where(first > 0, F32(1.0), F32(0.0))
    above = jnp.where(first + depth < planes, F32(1.0), F32(0.0))
    many = ranks * count * 2
    got[0] = far_in[...]
    got[1] = near_in[...]
    odd = lax.axis_index("space") & 1
    low, high = odd, 1 - odd

    def near(before, centre, after):
        total = (before + after) + (steps.after_y(centre) + steps.before_y(centre))
        total = total + (steps.after_z(centre) + steps.before_z(centre))
        return (1.0 - 6.0 * KAPPA) * centre + KAPPA * total

    for s in range(count):
        for part in range(2):
            value = [got[low, s, part, p].astype(F32) for p in range(REACH)]
            value += [rows_ref[s, part, p].astype(F32) for p in range(depth)]
            value += [got[high, s, part, p].astype(F32) for p in range(REACH)]
            once = [near(*value[i - 1 : i + 2]) for i in range(1, depth + 3)]
            once[0] = once[0] * below
            once[-1] = once[-1] * above
            for p in range(depth):
                smooth_ref[s, part, p] = near(*once[p : p + 3]).astype(smooth_ref.dtype)

    sums = [[None] * many for _ in range(2 * count)]
    for p in range(depth):
        for k in range(0, height, 16):
            mine = [smooth_ref[a // 2, a % 2, p, k : k + 16].astype(F32) for a in range(2 * count)]
            for b in range(many):
                r, t = divmod(b // 2, count)
                other = all_ref[r, t, b % 2, p, k : k + 16].astype(F32)
                for a in range(2 * count):
                    prod = mine[a] * other
                    prod = prod[:8] + prod[8:]
                    sums[a][b] = prod if sums[a][b] is None else sums[a][b] + prod
    ones = jnp.ones((breadth, breadth), F32)
    table = jnp.concatenate([v for line in sums for v in line], axis=0)
    table = jnp.dot(table, ones, precision=lax.Precision.HIGHEST, preferred_element_type=F32)
    for a in range(2 * count):
        line = None
        for b in range(many):
            at = (a * many + b) * 8
            add = jnp.where(steps.lane[:8] == b, table[at : at + 8], 0.0)
            line = add if line is None else line + add
        line = jnp.sum(line, axis=0, keepdims=True) * scale
        for peer in range(block_ref.shape[0]):
            block_ref[peer, a : a + 1, :] = line[:, :many]


def in_hbm(x):
    return pltpu.with_memory_space_constraint(x, pltpu.HBM)


def shards(conductivity, background, warm_start, data_weight, recv_cell, src_group, group_freq):
    count = warm_start.shape[0]
    depth, height, breadth = conductivity.shape
    plane = (height, breadth)
    peers = lax.axis_size("space")
    ranks = lax.axis_size("rx")
    cells = depth * height * breadth * peers
    half = jnp.bfloat16
    first = lax.axis_index("space") * depth
    place = jnp.stack([first, jnp.int32(peers * depth)])
    integers = jnp.concatenate([place, recv_cell, src_group, group_freq]).astype(F32)
    scalars = jnp.concatenate([integers, data_weight.reshape(-1)])
    far = [(i, i + 1) for i in range(1, peers - 1, 2)]
    near = [(i, i + 1) for i in range(0, peers - 1, 2)]
    far, near = [pairs + [(j, i) for i, j in pairs] for pairs in (far, near)]
    shape = jax.ShapeDtypeStruct
    small = [in_hbm(x) for x in (data_weight, recv_cell, src_group, group_freq)]
    small_scratch = [
        pltpu.SMEM(data_weight.shape, F32),
        pltpu.SMEM(recv_cell.shape, jnp.int32),
        pltpu.SMEM(src_group.shape, jnp.int32),
        pltpu.SMEM(group_freq.shape, jnp.int32),
    ]

    own, edges, fars, nears = [], [], [], []
    for s in range(count):
        message = shape((2 * SENT + (s == 0),) + plane, half)
        outs = [message, message, shape((2, 3, depth) + plane, F32), shape((2, 4) + plane, F32)]
        scratch = small_scratch + [pltpu.VMEM((2,) + message.shape, half), pltpu.SemaphoreType.DMA((7,))]
        if s == 0:
            operands = [in_hbm(warm_start), in_hbm(conductivity)] + small
            specs = [HBM] * 6
            outs += [shape(conductivity.shape, F32), shape((count - 1,) + warm_start.shape[1:], F32)]
            scratch = [pltpu.VMEM(warm_start.shape[1:], F32)] + scratch
        else:
            operands = [later, held] + small
            specs = [FULL] * 2 + [HBM] * 4
        result = pl.pallas_call(
            functools.partial(first_kernel, s),
            out_shape=tuple(outs),
            in_specs=specs,
            out_specs=(FULL,) * len(outs),
            scratch_shapes=scratch,
            compiler_params=KERNEL,
            name="first_sweep",
        )(*operands)
        if s == 0:
            held, later = result[4:]
        own.append(result[2])
        edges.append(result[3])
        fars.append(lax.ppermute(result[0], "space", far))
        nears.append(lax.ppermute(result[1], "space", near))

    field = pl.pallas_call(
        functools.partial(stage_kernel, count, 2 + count),
        out_shape=shape((count,) + background.shape[1:], F32),
        in_specs=[SCALARS, HBM],
        out_specs=FULL,
        scratch_shapes=[pltpu.SemaphoreType.DMA((count,))],
        compiler_params=KERNEL,
        name="stage_field",
    )(scalars, in_hbm(background))

    rows_of = shape((count, 2, depth) + plane, half)
    ends_of = shape((count, 2, REACH) + plane, half)
    adjoint_scratch = pltpu.VMEM((2, 3, depth + 2) + plane, F32)
    earlier = []
    for s in range(count):
        last = s == count - 1
        operands = [scalars, own[s], edges[s], held, field, fars[s], nears[s], fars[0], nears[0]]
        scratch = [
            adjoint_scratch,
            adjoint_scratch,
            pltpu.VMEM((2,) + fars[s].shape, half),
            pltpu.VMEM((2,) + plane, half),
        ]
        if last:
            operands += earlier
            outs = (rows_of, ends_of, ends_of)
            scratch.append(pltpu.VMEM((2,) + ends_of.shape, half))
        else:
            outs = (shape((2, depth) + plane, half),)
        result = pl.pallas_call(
            functools.partial(sweep_kernel, s, count),
            out_shape=outs,
            in_specs=[SCALARS] + [FULL] * (len(operands) - 1),
            out_specs=(FULL,) * len(outs),
            scratch_shapes=scratch,
            compiler_params=KERNEL,
            name="sweeps",
        )(*operands)
        earlier.append(result[0])
    rows, to_far, to_near = result
    from_far = lax.ppermute(to_far, "space", far)
    from_near = lax.ppermute(to_near, "space", near)
    every = lax.all_gather(rows, "rx", axis=0)

    many = 2 * count * ranks
    smoothed, partial_block = pl.pallas_call(
        functools.partial(smooth_kernel, 1.0 / cells),
        out_shape=(rows_of, shape((peers, 2 * count, many), F32)),
        in_specs=[SCALARS] + [FULL] * 4,
        out_specs=(FULL, FULL),
        scratch_shapes=[pltpu.VMEM((2,) + ends_of.shape, half)],
        compiler_params=KERNEL,
        name="smooth",
    )(scalars, rows, from_far, from_near, every)
    pieces = lax.all_to_all(partial_block, "space", 0, 0)
    return (jnp.sum(pieces, axis=0), smoothed)


def solution(mesh):
    in_specs = (
        P("space", None, None),
        P(None, None, None, "space", None, None),
        P("rx", None, None, "space", None, None),
        P("rx", None, None),
        P("rx"),
        P("rx"),
        P(),
    )
    out_specs = (P("rx", None), P("rx", None, "space", None, None))
    return jax.shard_map(shards, mesh=mesh, in_specs=in_specs, out_specs=out_specs, check_vma=False)
```

```python
import functools

import jax
import jax.numpy as jnp
from jax import lax
from jax.experimental import pallas as pl
from jax.experimental.pallas import tpu as pltpu
from jax.sharding import PartitionSpec as P

SENT = 6
RELAX = 0.2
KAPPA = 0.1
REACH = 2
FULL = pl.BlockSpec(memory_space=pltpu.VMEM)
HBM = pl.BlockSpec(memory_space=pltpu.HBM)
SCALARS = pl.BlockSpec(memory_space=pltpu.SMEM)
KERNEL = pltpu.CompilerParams(vmem_limit_bytes=8 * 2**20)
F32 = jnp.float32


class Steps:
    def __init__(self, height, breadth):
        self.height, self.breadth = height, breadth
        self.sub = lax.broadcasted_iota(jnp.int32, (8, breadth), 0)
        self.lane = lax.broadcasted_iota(jnp.int32, (height, breadth), 1)

    def after_y(self, f):
        f = pltpu.roll(f, self.height - 1, 0)
        return jnp.concatenate([f[:-8], jnp.where(self.sub < 7, f[-8:], 0.0)], axis=0)

    def before_y(self, f):
        f = pltpu.roll(f, 1, 0)
        return jnp.concatenate([jnp.where(self.sub > 0, f[:8], 0.0), f[8:]], axis=0)

    def after_z(self, f):
        return jnp.where(self.lane < self.breadth - 1, pltpu.roll(f, self.breadth - 1, 1), 0.0)

    def before_z(self, f):
        return jnp.where(self.lane > 0, pltpu.roll(f, 1, 1), 0.0)

    def up_y(self, f):
        return self.after_y(f) - f

    def up_z(self, f):
        return self.after_z(f) - f

    def down_y(self, f):
        return f - self.before_y(f)

    def down_z(self, f):
        return f - self.before_z(f)

    def magnetic_yz(self, e, e_next):
        ex, ey, ez = e
        if e_next is None:
            return self.up_z(ex) + ez, -ey - self.up_y(ex)
        return self.up_z(ex) - (e_next[2] - ez), (e_next[1] - ey) - self.up_y(ex)

    def magnetic_x(self, e):
        return self.up_y(e[2]) - self.up_z(e[1])

    def curl_back(self, comp, hx, hy, hz, before):
        if comp == 0:
            return self.down_y(hz) - self.down_z(hy)
        if comp == 1:
            return self.down_z(hx) - (hz - before[1])
        return (hy - before[0]) - self.down_y(hx)


def angular_of(freq):
    angular = F32(0.25)
    for bit, factor in ((1, 1.25), (2, 1.25**2), (4, 1.25**4)):
        angular = angular * jnp.where((freq & bit) != 0, F32(factor), F32(1.0))
    return angular


def split(number, size):
    if size & (size - 1):
        return number // size, number % size
    return number >> (size.bit_length() - 1), number & (size - 1)


class Point:
    def __init__(self, cell, first, steps):
        plane, inner = split(cell, steps.height * steps.breadth)
        row, lane = split(inner, steps.breadth)
        block, sub = split(row, 8)
        self.plane = plane - first
        self.rows = pl.ds(pl.multiple_of(block * 8, 8), 8)
        self.row, self.sub, self.lane, self.steps = row, sub, lane, steps

    def spread(self, value):
        here = (self.steps.sub == self.sub) & (self.steps.lane[:8] == self.lane)
        return jnp.where(here, RELAX * value, 0.0)

    def add_to(self, ref, low, high, shift, weight):
        @pl.when((self.plane >= low) & (self.plane < high))
        def _():
            for part in range(2):
                for comp in range(3):
                    at = (part, comp, self.plane + shift, self.rows)
                    ref[at] = ref[at] + self.spread(weight(part, comp))


def first_kernel(
    start_ref, cond_ref, back_ref, weight_ref, cell_ref, group_ref, freq_ref,
    far_ref, near_ref, own_ref, edge_ref, held_ref, field_ref,
    raw, weight, cell, group, freq, sent, sems,
):
    count, _, _, depth, height, breadth = start_ref.shape
    pairs = ((group_ref, group), (freq_ref, freq), (cell_ref, cell), (weight_ref, weight), (cond_ref, held_ref))
    copies = [pltpu.make_async_copy(a, b, sems.at[k]) for k, (a, b) in enumerate(pairs)]

    def start_of(s):
        return pltpu.make_async_copy(start_ref.at[s], raw.at[s], sems.at[len(pairs) + s])

    for copy in copies + [start_of(s) for s in range(count)]:
        copy.start()
    copies[0].wait()
    fields = [
        pltpu.make_async_copy(back_ref.at[group[s]], field_ref.at[s], sems.at[len(pairs) + count + s])
        for s in range(count)
    ]
    for copy in fields:
        copy.start()
    for copy in copies[1:]:
        copy.wait()
    steps = Steps(height, breadth)
    half = far_ref.dtype
    index = lax.axis_index("space")
    first = index * depth
    down = index & 1
    up = 1 - down
    row = lax.broadcasted_iota(jnp.int32, (height, breadth), 0)
    last = depth - 1
    sent[up, 2 * count * SENT] = held_ref[last].astype(half)
    sent[down, 2 * count * SENT] = held_ref[0].astype(half)

    def one_source(s, _):
        start_of(s).wait()
        scale = RELAX * angular_of(freq[group[s]])
        scales = scale, -scale
        point = Point(cell[s], first, steps)
        base = 2 * s * SENT
        before = []
        for part in range(2):
            ey, ez = raw[s, part, 1, 0], raw[s, part, 2, 0]
            for k, f in enumerate((ey, ez)):
                sent[down, base + part * SENT + k] = f.astype(half)
                edge_ref[s, part, k] = f
            before.append((-ez, ey))
        for p in range(depth):
            for part in range(2):
                e = [raw[s, part, comp, p] for comp in range(3)]
                e_next = None
                if p < last:
                    e_next = [None if comp == 0 else raw[s, part, comp, p + 1] for comp in range(3)]
                hy, hz = steps.magnetic_yz(e, e_next)
                if p == last:
                    for k, f in enumerate((hy, hz)):
                        sent[up, base + part * SENT + k] = f.astype(half)
                        edge_ref[s, part, 2 + k] = f
                hx = steps.magnetic_x(e)
                coef = scales[part] * held_ref[p]
                for comp in range(3):
                    curl = steps.curl_back(comp, hx, hy, hz, before[part])
                    own_ref[s, part, comp, p] = e[comp] - RELAX * curl + coef * raw[s, 1 - part, comp, p]
                before[part] = hy, hz
        point.add_to(own_ref.at[s], 0, depth, 0, lambda part, comp: weight[s, part, comp])

        at_last = jnp.where(point.plane == last, F32(1.0), F32(0.0))
        here = jnp.where((row == point.row) & (steps.lane == point.lane), RELAX * at_last, 0.0)
        for part in range(2):
            ex, ey, ez = [own_ref[s, part, comp, 0] for comp in range(3)]
            hy, hz = steps.up_z(ex) - own_ref[s, part, 2, 1], own_ref[s, part, 1, 1] - steps.up_y(ex)
            for k, f in enumerate((ey, ez, hy, hz)):
                sent[down, base + part * SENT + 2 + k] = f.astype(half)
            e = [own_ref[s, part, comp, last] for comp in range(3)]
            behind = steps.magnetic_yz([own_ref[s, part, comp, last - 1] for comp in range(3)], e)
            hy, hz = steps.magnetic_yz(e, None)
            hx = steps.magnetic_x(e)
            coef = scales[part] * held_ref[last]
            after = []
            for comp in range(3):
                curl = steps.curl_back(comp, hx, hy, hz, behind)
                value = e[comp] - RELAX * curl + coef * own_ref[s, 1 - part, comp, last]
                after.append(value + here * weight[s, part, comp])
            for k, f in enumerate((hy, hz) + steps.magnetic_yz(after, None)):
                sent[up, base + part * SENT + 2 + k] = f.astype(half)
        return 0

    lax.fori_loop(0, count, one_source, 0)
    far_ref[...] = sent[0]
    near_ref[...] = sent[1]
    for copy in fields:
        copy.wait()


def sweep_kernel(
    planes, scalar_ref, own_ref, edge_ref, held_ref, field_ref, far_in, near_in, rows_ref, far_ref, near_ref, one_, two_, got, sent,
):
    count, _, _, depth, height, breadth = own_ref.shape
    steps = Steps(height, breadth)
    index = lax.axis_index("space")
    first = index * depth
    relax_low = jnp.where(first > 0, F32(RELAX), F32(0.0))
    relax_high = jnp.where(first + depth < planes, F32(RELAX), F32(0.0))
    odd = index & 1
    low, high = odd, 1 - odd
    got[0] = far_in[...]
    got[1] = near_in[...]

    def conductivity(p):
        if p < 0:
            return got[low, 2 * count * SENT].astype(F32)
        if p >= depth:
            return got[high, 2 * count * SENT].astype(F32)
        return held_ref[p]

    def one_source(s, _):
        group = scalar_ref[count + s].astype(jnp.int32)
        angular = angular_of(scalar_ref[2 * count + group].astype(jnp.int32))
        scales = RELAX * angular, -RELAX * angular
        point = Point(scalar_ref[s].astype(jnp.int32), first, steps)
        weights_at = scalar_ref.shape[0] - 6 * count + 6 * s

        def received(side, part, k):
            return got[side, (2 * s + part) * SENT + k].astype(F32)

        for part in range(2):
            ey, ez, ly, lz = [edge_ref[s, part, k] for k in range(4)]
            one_[part, 0, 0] = -relax_low * (steps.down_y(ey) + steps.down_z(ez))
            one_[part, 1, 0] = relax_low * ey
            one_[part, 2, 0] = relax_low * ez
            e = [own_ref[s, part, comp, 0] for comp in range(3)]
            one_[part, 0, 1] = e[0]
            one_[part, 1, 1] = e[1] - RELAX * received(low, part, 1)
            one_[part, 2, 1] = e[2] + RELAX * received(low, part, 0)
            for p in range(1, depth - 1):
                for comp in range(3):
                    one_[part, comp, p + 1] = own_ref[s, part, comp, p]
            e = [own_ref[s, part, comp, depth - 1] for comp in range(3)]
            high_y, high_z = received(high, part, 0), received(high, part, 1)
            one_[part, 0, depth] = e[0] - RELAX * (steps.down_y(high_y) + steps.down_z(high_z))
            one_[part, 1, depth] = e[1] + RELAX * high_y
            one_[part, 2, depth] = e[2] + RELAX * high_z
            one_[part, 1, depth + 1] = received(high, part, 2) - relax_high * lz
            one_[part, 2, depth + 1] = received(high, part, 3) + relax_high * ly

        def sweep(ref, into, low_plane, planes_swept, k):
            if low_plane < 0:
                before = [(-ref[part, 2, 0], ref[part, 1, 0]) for part in range(2)]
            else:
                before = []
                for part in range(2):
                    e = [ref[part, comp, 0] for comp in range(3)]
                    hy, hz = steps.magnetic_yz(e, [None, ref[part, 1, 1], ref[part, 2, 1]])
                    before.append((hy + received(low, part, k), hz + received(low, part, k + 1)))
            for p in range(low_plane, planes_swept):
                relax = relax_low if p < 0 else relax_high if p == depth else F32(RELAX)
                for part in range(2):
                    e = [ref[part, comp, p + 1] if comp or p < depth else None for comp in range(3)]
                    if p < depth:
                        e_next = [None if comp == 0 else ref[part, comp, p + 2] for comp in range(3)]
                        hy, hz = steps.magnetic_yz(e, e_next)
                    else:
                        hy, hz = received(high, part, 4) + e[2], received(high, part, 5) - e[1]
                    hx = steps.magnetic_x(e)
                    coef = scales[part] * conductivity(p)
                    for comp in range(1 if p == depth else 0, 3):
                        curl = steps.curl_back(comp, hx, hy, hz, before[part])
                        into[part, comp, p + 1] = e[comp] - relax * curl + coef * ref[1 - part, comp, p + 1]
                    if p < 0:
                        hy, hz = hy + received(low, part, k), hz + received(low, part, k + 1)
                    before[part] = hy, hz
            point.add_to(into, 0, planes_swept, 1, lambda part, comp: scalar_ref[weights_at + part * 3 + comp])

        sweep(one_, two_, -1, depth + 1, 2)
        sweep(two_, one_, 0, depth, 4)

        for p in range(depth):
            row_re = row_im = None
            for comp in range(3):
                re, im = one_[0, comp, p + 1], one_[1, comp, p + 1]
                field_re, field_im = field_ref[s, 0, comp, p], field_ref[s, 1, comp, p]
                add_re, add_im = field_re * re - field_im * im, field_re * im + field_im * re
                row_re, row_im = (add_re, add_im) if comp == 0 else (row_re + add_re, row_im + add_im)
            coef = angular * held_ref[p]
            for part, value in enumerate((row_re, row_im)):
                value = (coef * value).astype(rows_ref.dtype)
                rows_ref[s, part, p] = value
                if p >= depth - REACH:
                    sent[high, s, part, p - depth + REACH] = value
                if p < REACH:
                    sent[low, s, part, p] = value
        return 0

    lax.fori_loop(0, count, one_source, 0)
    far_ref[...] = sent[0]
    near_ref[...] = sent[1]


def in_plane(steps, f):
    total = (steps.after_y(f) + steps.before_y(f)) + (steps.after_z(f) + steps.before_z(f))
    return (1.0 - 6.0 * KAPPA) * f + KAPPA * total


def smooth_kernel(planes, rows_ref, alone_ref):
    count, _, depth, height, breadth = rows_ref.shape
    steps = Steps(height, breadth)
    first = lax.axis_index("space") * depth
    below = jnp.where(first > 0, F32(KAPPA), F32(0.0))
    above = jnp.where(first + depth < planes, F32(KAPPA), F32(0.0))

    def one_row(i, _):
        s, part = i >> 1, i & 1
        value = [rows_ref[s, part, p].astype(F32) for p in range(depth)]
        once = []
        for p in range(depth):
            beside = [value[q] for q in (p - 1, p + 1) if 0 <= q < depth]
            once.append(in_plane(steps, value[p]) + KAPPA * functools.reduce(jnp.add, beside))
        once = [below * value[0]] + once + [above * value[-1]]
        for p in range(depth):
            alone_ref[s, part, p] = in_plane(steps, once[p + 1]) + KAPPA * (once[p] + once[p + 2])
        return 0

    lax.fori_loop(0, 2 * count, one_row, 0)


def block_kernel(cells, rows_ref, alone_ref, far_in, near_in, all_ref, smooth_ref, block_ref, got, rounded, sums, sem):
    count, _, depth, height, breadth = rows_ref.shape
    ranks = all_ref.shape[0]
    steps = Steps(height, breadth)
    many = ranks * count * 2
    got[0] = far_in[...]
    got[1] = near_in[...]
    odd = lax.axis_index("space") & 1
    low, high = odd, 1 - odd

    def one_row(i, _):
        s, part = i >> 1, i & 1
        value = [alone_ref[s, part, p] for p in range(depth)]
        for side, nearest, order in ((low, REACH - 1, 1), (high, 0, -1)):
            close = got[side, s, part, nearest].astype(F32)
            beyond = got[side, s, part, REACH - 1 - nearest].astype(F32)
            end = 0 if order > 0 else depth - 1
            value[end] = value[end] + (2.0 * KAPPA * in_plane(steps, close) + KAPPA * KAPPA * beyond)
            value[end + order] = value[end + order] + KAPPA * KAPPA * close
        for p in range(depth):
            rounded[s, part, p] = value[p].astype(rounded.dtype)
        return 0

    lax.fori_loop(0, 2 * count, one_row, 0)
    out = pltpu.make_async_copy(rounded, smooth_ref, sem)
    out.start()

    sums[...] = jnp.zeros_like(sums)

    def one_plane(p, _):
        mine = [rounded[a // 2, a % 2, p].astype(F32) for a in range(2 * count)]
        for b in range(many):
            r, t = divmod(b // 2, count)
            other = all_ref[r, t, b % 2, p].astype(F32)
            for a in range(2 * count):
                prod = mine[a] * other
                total = prod[:8]
                for k in range(8, height, 8):
                    total = total + prod[k : k + 8]
                sums[a * many + b] = sums[a * many + b] + total
        return 0

    lax.fori_loop(0, depth, one_plane, 0)
    half = jnp.bfloat16
    ones = jnp.ones((breadth, breadth), half)
    for a in range(2 * count):
        table = sums[a * many : (a + 1) * many].reshape(many * 8, breadth)
        coarse = table.astype(half)
        fine = (table - coarse.astype(F32)).astype(half)
        table = jnp.dot(coarse, ones, preferred_element_type=F32) + jnp.dot(fine, ones, preferred_element_type=F32)
        line = None
        for b in range(many):
            add = jnp.where(steps.lane[:8] == b, table[b * 8 : b * 8 + 8], 0.0)
            line = add if line is None else line + add
        line = jnp.sum(line, axis=0, keepdims=True) * (1.0 / cells)
        for peer in range(block_ref.shape[0]):
            block_ref[peer, a : a + 1, :] = line[:, :many]
    out.wait()


def in_hbm(x):
    return pltpu.with_memory_space_constraint(x, pltpu.HBM)


def shards(conductivity, background, warm_start, data_weight, recv_cell, src_group, group_freq):
    count = warm_start.shape[0]
    depth, height, breadth = conductivity.shape
    plane = (height, breadth)
    peers = lax.axis_size("space")
    ranks = lax.axis_size("rx")
    cells = depth * height * breadth * peers
    half = jnp.bfloat16
    integers = jnp.concatenate([recv_cell, src_group, group_freq]).astype(F32)
    scalars = jnp.concatenate([integers, data_weight.reshape(-1)])
    far = [(i, i + 1) for i in range(1, peers - 1, 2)]
    near = [(i, i + 1) for i in range(0, peers - 1, 2)]
    far, near = [pairs + [(j, i) for i, j in pairs] for pairs in (far, near)]
    shape = jax.ShapeDtypeStruct

    message = shape((2 * count * SENT + 1,) + plane, half)
    to_far, to_near, own, edge, held, field = pl.pallas_call(
        first_kernel,
        out_shape=(
            message,
            message,
            shape(warm_start.shape, F32),
            shape((count, 2, 4) + plane, F32),
            shape(conductivity.shape, F32),
            shape((count,) + background.shape[1:], F32),
        ),
        in_specs=[HBM] * 7,
        out_specs=(FULL,) * 6,
        scratch_shapes=[
            pltpu.VMEM(warm_start.shape, F32),
            pltpu.SMEM(data_weight.shape, F32),
            pltpu.SMEM(recv_cell.shape, jnp.int32),
            pltpu.SMEM(src_group.shape, jnp.int32),
            pltpu.SMEM(group_freq.shape, jnp.int32),
            pltpu.VMEM((2,) + message.shape, half),
            pltpu.SemaphoreType.DMA((5 + 2 * count,)),
        ],
        compiler_params=KERNEL,
        name="first_sweep",
    )(*[in_hbm(x) for x in (warm_start, conductivity, background, data_weight, recv_cell, src_group, group_freq)])
    from_far = lax.ppermute(to_far, "space", far)
    from_near = lax.ppermute(to_near, "space", near)

    rows_of = shape((count, 2, depth) + plane, half)
    ends_of = shape((count, 2, REACH) + plane, half)
    rows, to_far, to_near = pl.pallas_call(
        functools.partial(sweep_kernel, peers * depth),
        out_shape=(rows_of, ends_of, ends_of),
        in_specs=[SCALARS] + [FULL] * 6,
        out_specs=(FULL,) * 3,
        scratch_shapes=[
            pltpu.VMEM((2, 3, depth + 2) + plane, F32),
            pltpu.VMEM((2, 3, depth + 2) + plane, F32),
            pltpu.VMEM((2,) + message.shape, half),
            pltpu.VMEM((2,) + ends_of.shape, half),
        ],
        compiler_params=KERNEL,
        name="sweeps",
    )(scalars, own, edge, held, field, from_far, from_near)
    from_far = lax.ppermute(to_far, "space", far)
    from_near = lax.ppermute(to_near, "space", near)
    every = lax.all_gather(rows, "rx", axis=0)

    many = 2 * count * ranks
    alone = pl.pallas_call(
        functools.partial(smooth_kernel, peers * depth),
        out_shape=shape(rows_of.shape, F32),
        in_specs=[FULL],
        out_specs=FULL,
        compiler_params=KERNEL,
        name="smooth",
    )(rows)
    smoothed, partial_block = pl.pallas_call(
        functools.partial(block_kernel, cells),
        out_shape=(rows_of, shape((peers, 2 * count, many), F32)),
        in_specs=[FULL] * 5,
        out_specs=(HBM, FULL),
        scratch_shapes=[
            pltpu.VMEM((2,) + ends_of.shape, half),
            pltpu.VMEM(rows_of.shape, half),
            pltpu.VMEM((2 * count * many, 8, breadth), F32),
            pltpu.SemaphoreType.DMA,
        ],
        compiler_params=KERNEL,
        name="block",
    )(rows, alone, from_far, from_near, every)
    backwards = [list(range(peers - 1, -1, -1))]
    pieces = lax.all_to_all(partial_block, "space", 0, 0, axis_index_groups=backwards)
    return (jnp.sum(pieces, axis=0), smoothed)


def solution(mesh):
    in_specs = (
        P("space", None, None),
        P(None, None, None, "space", None, None),
        P("rx", None, None, "space", None, None),
        P("rx", None, None),
        P("rx"),
        P("rx"),
        P(),
    )
    out_specs = (P("rx", None), P("rx", None, "space", None, None))
    return jax.shard_map(shards, mesh=mesh, in_specs=in_specs, out_specs=out_specs, check_vma=False)
```

```python
import functools

import jax
import jax.numpy as jnp
from jax import lax
from jax.experimental import pallas as pl
from jax.experimental.pallas import tpu as pltpu
from jax.sharding import PartitionSpec as P

EARLY, LATE = 4, 2
RELAX = 0.2
KAPPA = 0.1
REACH = 2
FULL = pl.BlockSpec(memory_space=pltpu.VMEM)
HBM = pl.BlockSpec(memory_space=pltpu.HBM)
SCALARS = pl.BlockSpec(memory_space=pltpu.SMEM)
KERNEL = pltpu.CompilerParams(vmem_limit_bytes=8 * 2**20)
F32 = jnp.float32


class Steps:
    def __init__(self, height, breadth):
        self.height, self.breadth = height, breadth
        self.sub = lax.broadcasted_iota(jnp.int32, (8, breadth), 0)
        self.lane = lax.broadcasted_iota(jnp.int32, (height, breadth), 1)

    def after_y(self, f):
        f = pltpu.roll(f, self.height - 1, 0)
        return jnp.concatenate([f[:-8], jnp.where(self.sub < 7, f[-8:], 0.0)], axis=0)

    def before_y(self, f):
        f = pltpu.roll(f, 1, 0)
        return jnp.concatenate([jnp.where(self.sub > 0, f[:8], 0.0), f[8:]], axis=0)

    def after_z(self, f):
        return jnp.where(self.lane < self.breadth - 1, pltpu.roll(f, self.breadth - 1, 1), 0.0)

    def before_z(self, f):
        return jnp.where(self.lane > 0, pltpu.roll(f, 1, 1), 0.0)

    def up_y(self, f):
        return self.after_y(f) - f

    def up_z(self, f):
        return self.after_z(f) - f

    def down_y(self, f):
        return f - self.before_y(f)

    def down_z(self, f):
        return f - self.before_z(f)

    def magnetic_yz(self, e, e_next):
        ex, ey, ez = e
        if e_next is None:
            return self.up_z(ex) + ez, -ey - self.up_y(ex)
        return self.up_z(ex) - (e_next[2] - ez), (e_next[1] - ey) - self.up_y(ex)

    def magnetic_x(self, e):
        return self.up_y(e[2]) - self.up_z(e[1])

    def curl_back(self, comp, hx, hy, hz, before):
        if comp == 0:
            return self.down_y(hz) - self.down_z(hy)
        if comp == 1:
            return self.down_z(hx) - (hz - before[1])
        return (hy - before[0]) - self.down_y(hx)


def angular_of(freq):
    angular = F32(0.25)
    for bit, factor in ((1, 1.25), (2, 1.25**2), (4, 1.25**4)):
        angular = angular * jnp.where((freq & bit) != 0, F32(factor), F32(1.0))
    return angular


def split(number, size):
    if size & (size - 1):
        return number // size, number % size
    return number >> (size.bit_length() - 1), number & (size - 1)


class Point:
    def __init__(self, cell, first, steps):
        plane, inner = split(cell, steps.height * steps.breadth)
        row, lane = split(inner, steps.breadth)
        block, sub = split(row, 8)
        self.plane = plane - first
        self.rows = pl.ds(pl.multiple_of(block * 8, 8), 8)
        self.row, self.sub, self.lane, self.steps = row, sub, lane, steps

    def spread(self, value):
        here = (self.steps.sub == self.sub) & (self.steps.lane[:8] == self.lane)
        return jnp.where(here, RELAX * value, 0.0)

    def add_to(self, ref, low, high, shift, weight):
        @pl.when((self.plane >= low) & (self.plane < high))
        def _():
            for part in range(2):
                for comp in range(3):
                    at = (part, comp, self.plane + shift, self.rows)
                    ref[at] = ref[at] + self.spread(weight(part, comp))


def first_kernel(
    start_ref, cond_ref, back_ref, weight_ref, cell_ref, group_ref, freq_ref,
    far_ref, near_ref, own_ref, edge_ref, held_ref, field_ref,
    raw, weight, cell, group, freq, sent, sems,
):
    count, _, _, depth, height, breadth = start_ref.shape
    pairs = ((group_ref, group), (freq_ref, freq), (cell_ref, cell), (weight_ref, weight), (cond_ref, held_ref))
    copies = [pltpu.make_async_copy(a, b, sems.at[k]) for k, (a, b) in enumerate(pairs)]

    def start_of(s):
        return pltpu.make_async_copy(start_ref.at[s], raw.at[s], sems.at[len(pairs) + s])

    for copy in copies + [start_of(s) for s in range(count)]:
        copy.start()
    copies[0].wait()
    fields = [
        pltpu.make_async_copy(back_ref.at[group[s]], field_ref.at[s], sems.at[len(pairs) + count + s])
        for s in range(count)
    ]
    for copy in fields:
        copy.start()
    for copy in copies[1:]:
        copy.wait()
    steps = Steps(height, breadth)
    half = far_ref.dtype
    index = lax.axis_index("space")
    first = index * depth
    down = index & 1
    up = 1 - down
    last = depth - 1
    sent[up, 2 * count * EARLY] = held_ref[last].astype(half)
    sent[down, 2 * count * EARLY] = held_ref[0].astype(half)

    def one_source(s, _):
        start_of(s).wait()
        scale = RELAX * angular_of(freq[group[s]])
        scales = scale, -scale
        point = Point(cell[s], first, steps)
        before = []
        for part in range(2):
            ey, ez = raw[s, part, 1, 0], raw[s, part, 2, 0]
            for k, f in enumerate((ey, ez)):
                sent[down, (2 * s + part) * EARLY + k] = f.astype(half)
                edge_ref[s, part, k] = f
            before.append((-ez, ey))
        for p in range(depth):
            for part in range(2):
                e = [raw[s, part, comp, p] for comp in range(3)]
                e_next = None
                if p < last:
                    e_next = [None if comp == 0 else raw[s, part, comp, p + 1] for comp in range(3)]
                hy, hz = steps.magnetic_yz(e, e_next)
                if p == last:
                    for k, f in enumerate((hy, hz)):
                        sent[up, (2 * s + part) * EARLY + k] = f.astype(half)
                        edge_ref[s, part, 2 + k] = f
                hx = steps.magnetic_x(e)
                coef = scales[part] * held_ref[p]
                for comp in range(3):
                    curl = steps.curl_back(comp, hx, hy, hz, before[part])
                    own_ref[s, part, comp, p] = e[comp] - RELAX * curl + coef * raw[s, 1 - part, comp, p]
                before[part] = hy, hz
        point.add_to(own_ref.at[s], 0, depth, 0, lambda part, comp: weight[s, part, comp])
        for part in range(2):
            for k, f in enumerate((own_ref[s, part, 1, 0], own_ref[s, part, 2, 0])):
                sent[down, (2 * s + part) * EARLY + 2 + k] = f.astype(half)
            share = steps.magnetic_yz([own_ref[s, part, comp, last] for comp in range(3)], None)
            for k, f in enumerate(share):
                sent[up, (2 * s + part) * EARLY + 2 + k] = f.astype(half)
        return 0

    lax.fori_loop(0, count, one_source, 0)
    far_ref[...] = sent[0]
    near_ref[...] = sent[1]
    for copy in fields:
        copy.wait()


class Sources:
    def __init__(self, ref, count, steps, first):
        self.ref, self.count, self.steps, self.first = ref, count, steps, first

    def angular(self, s):
        group = self.ref[self.count + s].astype(jnp.int32)
        return angular_of(self.ref[2 * self.count + group].astype(jnp.int32))

    def point(self, s):
        return Point(self.ref[s].astype(jnp.int32), self.first, self.steps)

    def weight(self, s, part, comp):
        return self.ref[self.ref.shape[0] - 6 * self.count + 6 * s + part * 3 + comp]


def second_kernel(scalar_ref, own_ref, held_ref, far_ref, near_ref, sent):
    count, _, _, depth, height, breadth = own_ref.shape
    steps = Steps(height, breadth)
    half = far_ref.dtype
    index = lax.axis_index("space")
    down = index & 1
    up = 1 - down
    last = depth - 1
    sources = Sources(scalar_ref, count, steps, index * depth)
    row = lax.broadcasted_iota(jnp.int32, (height, breadth), 0)

    def one_source(s, _):
        scale = RELAX * sources.angular(s)
        scales = scale, -scale
        point = sources.point(s)
        at_last = jnp.where(point.plane == last, F32(1.0), F32(0.0))
        here = jnp.where((row == point.row) & (steps.lane == point.lane), RELAX * at_last, 0.0)
        for part in range(2):
            base = (2 * s + part) * LATE
            ex = own_ref[s, part, 0, 0]
            sent[down, base] = (steps.up_z(ex) - own_ref[s, part, 2, 1]).astype(half)
            sent[down, base + 1] = (own_ref[s, part, 1, 1] - steps.up_y(ex)).astype(half)
            e = [own_ref[s, part, comp, last] for comp in range(3)]
            behind = steps.magnetic_yz([own_ref[s, part, comp, last - 1] for comp in range(3)], e)
            hy, hz = steps.magnetic_yz(e, None)
            hx = steps.magnetic_x(e)
            coef = scales[part] * held_ref[last]
            after = []
            for comp in range(3):
                curl = steps.curl_back(comp, hx, hy, hz, behind)
                value = e[comp] - RELAX * curl + coef * own_ref[s, 1 - part, comp, last]
                after.append(value + here * sources.weight(s, part, comp))
            for k, f in enumerate(steps.magnetic_yz(after, None)):
                sent[up, base + k] = f.astype(half)
        return 0

    lax.fori_loop(0, count, one_source, 0)
    far_ref[...] = sent[0]
    near_ref[...] = sent[1]


def sweep_two_kernel(planes, scalar_ref, own_ref, edge_ref, held_ref, far_in, near_in, two_ref, top_ref, one_, got):
    count, _, _, depth, height, breadth = own_ref.shape
    steps = Steps(height, breadth)
    index = lax.axis_index("space")
    first = index * depth
    relax_low = jnp.where(first > 0, F32(RELAX), F32(0.0))
    relax_high = jnp.where(first + depth < planes, F32(RELAX), F32(0.0))
    low = index & 1
    high = 1 - low
    got[0] = far_in[...]
    got[1] = near_in[...]
    sources = Sources(scalar_ref, count, steps, first)

    def one_source(s, _):
        scale = RELAX * sources.angular(s)
        scales = scale, -scale

        def received(side, part, k):
            return got[side, (2 * s + part) * EARLY + k].astype(F32)

        for part in range(2):
            ey, ez, ly, lz = [edge_ref[s, part, k] for k in range(4)]
            one_[part, 0, 0] = -relax_low * (steps.down_y(ey) + steps.down_z(ez))
            one_[part, 1, 0] = relax_low * ey
            one_[part, 2, 0] = relax_low * ez
            e = [own_ref[s, part, comp, 0] for comp in range(3)]
            one_[part, 0, 1] = e[0]
            one_[part, 1, 1] = e[1] - RELAX * received(low, part, 1)
            one_[part, 2, 1] = e[2] + RELAX * received(low, part, 0)
            for p in range(1, depth - 1):
                for comp in range(3):
                    one_[part, comp, p + 1] = own_ref[s, part, comp, p]
            e = [own_ref[s, part, comp, depth - 1] for comp in range(3)]
            high_y, high_z = received(high, part, 0), received(high, part, 1)
            one_[part, 0, depth] = e[0] - RELAX * (steps.down_y(high_y) + steps.down_z(high_z))
            one_[part, 1, depth] = e[1] + RELAX * high_y
            one_[part, 2, depth] = e[2] + RELAX * high_z
            top_y = received(high, part, 2) - relax_high * lz
            top_z = received(high, part, 3) + relax_high * ly
            one_[part, 1, depth + 1] = top_y
            one_[part, 2, depth + 1] = top_z
            top_ref[s, part, 0] = top_y
            top_ref[s, part, 1] = top_z

        before = [(-one_[part, 2, 0], one_[part, 1, 0]) for part in range(2)]
        for p in range(-1, depth):
            relax = relax_low if p < 0 else F32(RELAX)
            for part in range(2):
                e = [one_[part, comp, p + 1] for comp in range(3)]
                hy, hz = steps.magnetic_yz(e, [None, one_[part, 1, p + 2], one_[part, 2, p + 2]])
                hx = steps.magnetic_x(e)
                held = got[low, 2 * count * EARLY].astype(F32) if p < 0 else held_ref[p]
                coef = scales[part] * held
                for comp in range(3):
                    curl = steps.curl_back(comp, hx, hy, hz, before[part])
                    two_ref[s, part, comp, p + 1] = e[comp] - relax * curl + coef * one_[1 - part, comp, p + 1]
                if p < 0:
                    hy, hz = hy + received(low, part, 2), hz + received(low, part, 3)
                before[part] = hy, hz
        for part in range(2):
            for k, f in enumerate(before[part]):
                top_ref[s, part, 2 + k] = f
        sources.point(s).add_to(two_ref.at[s], 0, depth, 1, functools.partial(sources.weight, s))
        return 0

    lax.fori_loop(0, count, one_source, 0)


def sweep_three_kernel(
    planes, scalar_ref, two_ref, top_ref, held_ref, field_ref, far_cond, near_cond, far_in, near_in,
    rows_ref, far_ref, near_ref, above, last_, got, conds, sent,
):
    count, _, _, _, height, breadth = two_ref.shape
    depth = held_ref.shape[0]
    steps = Steps(height, breadth)
    index = lax.axis_index("space")
    first = index * depth
    relax_high = jnp.where(first + depth < planes, F32(RELAX), F32(0.0))
    low = index & 1
    high = 1 - low
    got[0] = far_in[...]
    got[1] = near_in[...]
    conds[0] = far_cond[2 * count * EARLY]
    conds[1] = near_cond[2 * count * EARLY]
    sources = Sources(scalar_ref, count, steps, first)

    def one_source(s, _):
        angular = sources.angular(s)
        scales = RELAX * angular, -RELAX * angular
        point = sources.point(s)
        weight = functools.partial(sources.weight, s)

        def received(side, part, k):
            return got[side, (2 * s + part) * LATE + k].astype(F32)

        held_above = conds[high].astype(F32)
        for part in range(2):
            ey, ez, hy_before, hz_before = [top_ref[s, part, k] for k in range(4)]
            hy, hz = received(high, part, 0) + ez, received(high, part, 1) - ey
            hx = steps.magnetic_x((None, ey, ez))
            coef = scales[part] * held_above
            for k, e in enumerate((ey, ez)):
                curl = steps.curl_back(1 + k, hx, hy, hz, (hy_before, hz_before))
                above[part, 1 + k, 0] = e - relax_high * curl + coef * top_ref[s, 1 - part, k]
        point.add_to(above, depth, depth + 1, -depth, weight)

        before = []
        for part in range(2):
            e = [two_ref[s, part, comp, 0] for comp in range(3)]
            hy, hz = steps.magnetic_yz(e, [None, two_ref[s, part, 1, 1], two_ref[s, part, 2, 1]])
            before.append((hy + received(low, part, 0), hz + received(low, part, 1)))
        for p in range(depth):
            for part in range(2):
                e = [two_ref[s, part, comp, p + 1] for comp in range(3)]
                if p < depth - 1:
                    e_next = [None, two_ref[s, part, 1, p + 2], two_ref[s, part, 2, p + 2]]
                else:
                    e_next = [None, above[part, 1, 0], above[part, 2, 0]]
                hy, hz = steps.magnetic_yz(e, e_next)
                hx = steps.magnetic_x(e)
                coef = scales[part] * held_ref[p]
                for comp in range(3):
                    curl = steps.curl_back(comp, hx, hy, hz, before[part])
                    last_[part, comp, p] = e[comp] - RELAX * curl + coef * two_ref[s, 1 - part, comp, p + 1]
                before[part] = hy, hz
        point.add_to(last_, 0, depth, 0, weight)

        for p in range(depth):
            row_re = row_im = None
            for comp in range(3):
                re, im = last_[0, comp, p], last_[1, comp, p]
                field_re, field_im = field_ref[s, 0, comp, p], field_ref[s, 1, comp, p]
                add_re, add_im = field_re * re - field_im * im, field_re * im + field_im * re
                row_re, row_im = (add_re, add_im) if comp == 0 else (row_re + add_re, row_im + add_im)
            coef = angular * held_ref[p]
            for part, value in enumerate((row_re, row_im)):
                value = (coef * value).astype(rows_ref.dtype)
                rows_ref[s, part, p] = value
                if p >= depth - REACH:
                    sent[high, s, part, p - depth + REACH] = value
                if p < REACH:
                    sent[low, s, part, p] = value
        return 0

    lax.fori_loop(0, count, one_source, 0)
    far_ref[...] = sent[0]
    near_ref[...] = sent[1]


def in_plane(steps, f):
    total = (steps.after_y(f) + steps.before_y(f)) + (steps.after_z(f) + steps.before_z(f))
    return (1.0 - 6.0 * KAPPA) * f + KAPPA * total


def smooth_kernel(planes, rows_ref, alone_ref):
    count, _, depth, height, breadth = rows_ref.shape
    steps = Steps(height, breadth)
    first = lax.axis_index("space") * depth
    below = jnp.where(first > 0, F32(KAPPA), F32(0.0))
    above = jnp.where(first + depth < planes, F32(KAPPA), F32(0.0))

    def one_row(i, _):
        s, part = i >> 1, i & 1
        value = [rows_ref[s, part, p].astype(F32) for p in range(depth)]
        once = []
        for p in range(depth):
            beside = [value[q] for q in (p - 1, p + 1) if 0 <= q < depth]
            once.append(in_plane(steps, value[p]) + KAPPA * functools.reduce(jnp.add, beside))
        once = [below * value[0]] + once + [above * value[-1]]
        for p in range(depth):
            alone_ref[s, part, p] = in_plane(steps, once[p + 1]) + KAPPA * (once[p] + once[p + 2])
        return 0

    lax.fori_loop(0, 2 * count, one_row, 0)


def block_kernel(cells, rows_ref, alone_ref, far_in, near_in, all_ref, smooth_ref, block_ref, got, rounded, sums, sem):
    count, _, depth, height, breadth = rows_ref.shape
    ranks = all_ref.shape[0]
    steps = Steps(height, breadth)
    many = ranks * count * 2
    got[0] = far_in[...]
    got[1] = near_in[...]
    odd = lax.axis_index("space") & 1
    low, high = odd, 1 - odd

    def one_row(i, _):
        s, part = i >> 1, i & 1
        value = [alone_ref[s, part, p] for p in range(depth)]
        for side, nearest, order in ((low, REACH - 1, 1), (high, 0, -1)):
            close = got[side, s, part, nearest].astype(F32)
            beyond = got[side, s, part, REACH - 1 - nearest].astype(F32)
            end = 0 if order > 0 else depth - 1
            value[end] = value[end] + (2.0 * KAPPA * in_plane(steps, close) + KAPPA * KAPPA * beyond)
            value[end + order] = value[end + order] + KAPPA * KAPPA * close
        for p in range(depth):
            rounded[s, part, p] = value[p].astype(rounded.dtype)
        return 0

    lax.fori_loop(0, 2 * count, one_row, 0)
    out = pltpu.make_async_copy(rounded, smooth_ref, sem)
    out.start()

    sums[...] = jnp.zeros_like(sums)

    def one_plane(p, _):
        mine = [rounded[a // 2, a % 2, p].astype(F32) for a in range(2 * count)]
        for b in range(many):
            r, t = divmod(b // 2, count)
            other = all_ref[r, t, b % 2, p].astype(F32)
            for a in range(2 * count):
                prod = mine[a] * other
                total = prod[:8]
                for k in range(8, height, 8):
                    total = total + prod[k : k + 8]
                sums[a * many + b] = sums[a * many + b] + total
        return 0

    lax.fori_loop(0, depth, one_plane, 0)
    half = jnp.bfloat16
    ones = jnp.ones((breadth, breadth), half)
    for a in range(2 * count):
        table = sums[a * many : (a + 1) * many].reshape(many * 8, breadth)
        coarse = table.astype(half)
        fine = (table - coarse.astype(F32)).astype(half)
        table = jnp.dot(coarse, ones, preferred_element_type=F32) + jnp.dot(fine, ones, preferred_element_type=F32)
        line = None
        for b in range(many):
            add = jnp.where(steps.lane[:8] == b, table[b * 8 : b * 8 + 8], 0.0)
            line = add if line is None else line + add
        line = jnp.sum(line, axis=0, keepdims=True) * (1.0 / cells)
        for peer in range(block_ref.shape[0]):
            block_ref[peer, a : a + 1, :] = line[:, :many]
    out.wait()


def in_hbm(x):
    return pltpu.with_memory_space_constraint(x, pltpu.HBM)


def shards(conductivity, background, warm_start, data_weight, recv_cell, src_group, group_freq):
    count = warm_start.shape[0]
    depth, height, breadth = conductivity.shape
    plane = (height, breadth)
    peers = lax.axis_size("space")
    ranks = lax.axis_size("rx")
    cells = depth * height * breadth * peers
    half = jnp.bfloat16
    integers = jnp.concatenate([recv_cell, src_group, group_freq]).astype(F32)
    scalars = jnp.concatenate([integers, data_weight.reshape(-1)])
    far = [(i, i + 1) for i in range(1, peers - 1, 2)]
    near = [(i, i + 1) for i in range(0, peers - 1, 2)]
    far, near = [pairs + [(j, i) for i, j in pairs] for pairs in (far, near)]
    shape = jax.ShapeDtypeStruct

    early = shape((2 * count * EARLY + 1,) + plane, half)
    late = shape((2 * count * LATE,) + plane, half)
    to_far, to_near, own, edge, held, field = pl.pallas_call(
        first_kernel,
        out_shape=(
            early,
            early,
            shape(warm_start.shape, F32),
            shape((count, 2, 4) + plane, F32),
            shape(conductivity.shape, F32),
            shape((count,) + background.shape[1:], F32),
        ),
        in_specs=[HBM] * 7,
        out_specs=(FULL,) * 6,
        scratch_shapes=[
            pltpu.VMEM(warm_start.shape, F32),
            pltpu.SMEM(data_weight.shape, F32),
            pltpu.SMEM(recv_cell.shape, jnp.int32),
            pltpu.SMEM(src_group.shape, jnp.int32),
            pltpu.SMEM(group_freq.shape, jnp.int32),
            pltpu.VMEM((2,) + early.shape, half),
            pltpu.SemaphoreType.DMA((5 + 2 * count,)),
        ],
        compiler_params=KERNEL,
        name="first_sweep",
    )(*[in_hbm(x) for x in (warm_start, conductivity, background, data_weight, recv_cell, src_group, group_freq)])
    far_early = lax.ppermute(to_far, "space", far)
    near_early = lax.ppermute(to_near, "space", near)

    to_far, to_near = pl.pallas_call(
        second_kernel,
        out_shape=(late, late),
        in_specs=[SCALARS] + [FULL] * 2,
        out_specs=(FULL,) * 2,
        scratch_shapes=[pltpu.VMEM((2,) + late.shape, half)],
        compiler_params=KERNEL,
        name="late_message",
    )(scalars, own, held)
    far_late = lax.ppermute(to_far, "space", far)
    near_late = lax.ppermute(to_near, "space", near)

    two, top = pl.pallas_call(
        functools.partial(sweep_two_kernel, peers * depth),
        out_shape=(shape((count, 2, 3, depth + 1) + plane, F32), shape((count, 2, 4) + plane, F32)),
        in_specs=[SCALARS] + [FULL] * 5,
        out_specs=(FULL,) * 2,
        scratch_shapes=[
            pltpu.VMEM((2, 3, depth + 2) + plane, F32),
            pltpu.VMEM((2,) + early.shape, half),
        ],
        compiler_params=KERNEL,
        name="sweep_two",
    )(scalars, own, edge, held, far_early, near_early)

    rows_of = shape((count, 2, depth) + plane, half)
    ends_of = shape((count, 2, REACH) + plane, half)
    rows, to_far, to_near = pl.pallas_call(
        functools.partial(sweep_three_kernel, peers * depth),
        out_shape=(rows_of, ends_of, ends_of),
        in_specs=[SCALARS] + [FULL] * 8,
        out_specs=(FULL,) * 3,
        scratch_shapes=[
            pltpu.VMEM((2, 3, 1) + plane, F32),
            pltpu.VMEM((2, 3, depth) + plane, F32),
            pltpu.VMEM((2,) + late.shape, half),
            pltpu.VMEM((2,) + plane, half),
            pltpu.VMEM((2,) + ends_of.shape, half),
        ],
        compiler_params=KERNEL,
        name="sweep_three",
    )(scalars, two, top, held, field, far_early, near_early, far_late, near_late)
    from_far = lax.ppermute(to_far, "space", far)
    from_near = lax.ppermute(to_near, "space", near)
    every = lax.all_gather(rows, "rx", axis=0)

    many = 2 * count * ranks
    alone = pl.pallas_call(
        functools.partial(smooth_kernel, peers * depth),
        out_shape=shape(rows_of.shape, F32),
        in_specs=[FULL],
        out_specs=FULL,
        compiler_params=KERNEL,
        name="smooth",
    )(rows)
    smoothed, partial_block = pl.pallas_call(
        functools.partial(block_kernel, cells),
        out_shape=(rows_of, shape((peers, 2 * count, many), F32)),
        in_specs=[FULL] * 5,
        out_specs=(HBM, FULL),
        scratch_shapes=[
            pltpu.VMEM((2,) + ends_of.shape, half),
            pltpu.VMEM(rows_of.shape, half),
            pltpu.VMEM((2 * count * many, 8, breadth), F32),
            pltpu.SemaphoreType.DMA,
        ],
        compiler_params=KERNEL,
        name="block",
    )(rows, alone, from_far, from_near, every)
    backwards = [list(range(peers - 1, -1, -1))]
    pieces = lax.all_to_all(partial_block, "space", 0, 0, axis_index_groups=backwards)
    return (jnp.sum(pieces, axis=0), smoothed)


def solution(mesh):
    in_specs = (
        P("space", None, None),
        P(None, None, None, "space", None, None),
        P("rx", None, None, "space", None, None),
        P("rx", None, None),
        P("rx"),
        P("rx"),
        P(),
    )
    out_specs = (P("rx", None), P("rx", None, "space", None, None))
    return jax.shard_map(shards, mesh=mesh, in_specs=in_specs, out_specs=out_specs, check_vma=False)
```

```python
import functools

import jax
import jax.numpy as jnp
from jax import lax
from jax.experimental import pallas as pl
from jax.experimental.pallas import tpu as pltpu
from jax.sharding import PartitionSpec as P

SENT = 6
RELAX = 0.2
KAPPA = 0.1
REACH = 2
FULL = pl.BlockSpec(memory_space=pltpu.VMEM)
HBM = pl.BlockSpec(memory_space=pltpu.HBM)
SCALARS = pl.BlockSpec(memory_space=pltpu.SMEM)
KERNEL = pltpu.CompilerParams(vmem_limit_bytes=8 * 2**20)
F32 = jnp.float32


class Steps:
    def __init__(self, height, breadth):
        self.height, self.breadth = height, breadth
        self.sub = lax.broadcasted_iota(jnp.int32, (8, breadth), 0)
        self.lane = lax.broadcasted_iota(jnp.int32, (height, breadth), 1)

    def after_y(self, f):
        f = pltpu.roll(f, self.height - 1, 0)
        return jnp.concatenate([f[:-8], jnp.where(self.sub < 7, f[-8:], 0.0)], axis=0)

    def before_y(self, f):
        f = pltpu.roll(f, 1, 0)
        return jnp.concatenate([jnp.where(self.sub > 0, f[:8], 0.0), f[8:]], axis=0)

    def after_z(self, f):
        return jnp.where(self.lane < self.breadth - 1, pltpu.roll(f, self.breadth - 1, 1), 0.0)

    def before_z(self, f):
        return jnp.where(self.lane > 0, pltpu.roll(f, 1, 1), 0.0)

    def up_y(self, f):
        return self.after_y(f) - f

    def up_z(self, f):
        return self.after_z(f) - f

    def down_y(self, f):
        return f - self.before_y(f)

    def down_z(self, f):
        return f - self.before_z(f)

    def magnetic_yz(self, e, e_next):
        ex, ey, ez = e
        if e_next is None:
            return self.up_z(ex) + ez, -ey - self.up_y(ex)
        return self.up_z(ex) - (e_next[2] - ez), (e_next[1] - ey) - self.up_y(ex)

    def magnetic_x(self, e):
        return self.up_y(e[2]) - self.up_z(e[1])

    def curl_back(self, comp, hx, hy, hz, before):
        if comp == 0:
            return self.down_y(hz) - self.down_z(hy)
        if comp == 1:
            return self.down_z(hx) - (hz - before[1])
        return (hy - before[0]) - self.down_y(hx)


def angular_of(freq):
    angular = F32(0.25)
    for bit, factor in ((1, 1.25), (2, 1.25**2), (4, 1.25**4)):
        angular = angular * jnp.where((freq & bit) != 0, F32(factor), F32(1.0))
    return angular


def split(number, size):
    if size & (size - 1):
        return number // size, number % size
    return number >> (size.bit_length() - 1), number & (size - 1)


class Point:
    def __init__(self, cell, first, steps):
        plane, inner = split(cell, steps.height * steps.breadth)
        row, lane = split(inner, steps.breadth)
        block, sub = split(row, 8)
        self.plane = plane - first
        self.rows = pl.ds(pl.multiple_of(block * 8, 8), 8)
        self.row, self.sub, self.lane, self.steps = row, sub, lane, steps

    def add_to(self, ref, low, high, shift, weight):
        reached = (self.plane >= low) & (self.plane < high)
        here = (self.steps.sub == self.sub) & (self.steps.lane[:8] == self.lane)
        amount = jnp.where(here, jnp.where(reached, F32(RELAX), F32(0.0)), 0.0)
        plane = jnp.clip(self.plane, low, high - 1) + shift
        for part in range(2):
            for comp in range(3):
                at = (part, comp, plane, self.rows)
                ref[at] = ref[at] + amount * weight(part, comp)


def first_kernel(
    start_ref, cond_ref, back_ref, weight_ref, cell_ref, group_ref, freq_ref,
    far_ref, near_ref, own_ref, edge_ref, held_ref, field_ref,
    raw, weight, cell, group, freq, sent, sems,
):
    count, _, _, depth, height, breadth = start_ref.shape
    pairs = ((group_ref, group), (freq_ref, freq), (cell_ref, cell), (weight_ref, weight), (cond_ref, held_ref))
    copies = [pltpu.make_async_copy(a, b, sems.at[k]) for k, (a, b) in enumerate(pairs)]

    def start_of(s):
        return pltpu.make_async_copy(start_ref.at[s], raw.at[s], sems.at[len(pairs) + s])

    for copy in copies + [start_of(s) for s in range(count)]:
        copy.start()
    copies[0].wait()
    fields = [
        pltpu.make_async_copy(back_ref.at[group[s]], field_ref.at[s], sems.at[len(pairs) + count + s])
        for s in range(count)
    ]
    for copy in fields:
        copy.start()
    for copy in copies[1:]:
        copy.wait()
    steps = Steps(height, breadth)
    half = far_ref.dtype
    index = lax.axis_index("space")
    first = index * depth
    down = index & 1
    up = 1 - down
    row = lax.broadcasted_iota(jnp.int32, (height, breadth), 0)
    last = depth - 1
    sent[up, 2 * count * SENT] = held_ref[last].astype(half)
    sent[down, 2 * count * SENT] = held_ref[0].astype(half)

    def one_source(s, _):
        start_of(s).wait()
        scale = RELAX * angular_of(freq[group[s]])
        scales = scale, -scale
        point = Point(cell[s], first, steps)
        base = 2 * s * SENT
        before = []
        for part in range(2):
            ey, ez = raw[s, part, 1, 0], raw[s, part, 2, 0]
            for k, f in enumerate((ey, ez)):
                sent[down, base + part * SENT + k] = f.astype(half)
                edge_ref[s, part, k] = f
            before.append((-ez, ey))
        for p in range(depth):
            for part in range(2):
                e = [raw[s, part, comp, p] for comp in range(3)]
                e_next = None
                if p < last:
                    e_next = [None if comp == 0 else raw[s, part, comp, p + 1] for comp in range(3)]
                hy, hz = steps.magnetic_yz(e, e_next)
                if p == last:
                    for k, f in enumerate((hy, hz)):
                        sent[up, base + part * SENT + k] = f.astype(half)
                        edge_ref[s, part, 2 + k] = f
                hx = steps.magnetic_x(e)
                coef = scales[part] * held_ref[p]
                for comp in range(3):
                    curl = steps.curl_back(comp, hx, hy, hz, before[part])
                    own_ref[s, part, comp, p] = e[comp] - RELAX * curl + coef * raw[s, 1 - part, comp, p]
                before[part] = hy, hz
        point.add_to(own_ref.at[s], 0, depth, 0, lambda part, comp: weight[s, part, comp])

        at_last = jnp.where(point.plane == last, F32(1.0), F32(0.0))
        here = jnp.where((row == point.row) & (steps.lane == point.lane), RELAX * at_last, 0.0)
        for part in range(2):
            ex, ey, ez = [own_ref[s, part, comp, 0] for comp in range(3)]
            hy, hz = steps.up_z(ex) - own_ref[s, part, 2, 1], own_ref[s, part, 1, 1] - steps.up_y(ex)
            for k, f in enumerate((ey, ez, hy, hz)):
                sent[down, base + part * SENT + 2 + k] = f.astype(half)
            e = [own_ref[s, part, comp, last] for comp in range(3)]
            behind = steps.magnetic_yz([own_ref[s, part, comp, last - 1] for comp in range(3)], e)
            hy, hz = steps.magnetic_yz(e, None)
            hx = steps.magnetic_x(e)
            coef = scales[part] * held_ref[last]
            after = []
            for comp in range(3):
                curl = steps.curl_back(comp, hx, hy, hz, behind)
                value = e[comp] - RELAX * curl + coef * own_ref[s, 1 - part, comp, last]
                after.append(value + here * weight[s, part, comp])
            for k, f in enumerate((hy, hz) + steps.magnetic_yz(after, None)):
                sent[up, base + part * SENT + 2 + k] = f.astype(half)
        return 0

    lax.fori_loop(0, count, one_source, 0)
    far_ref[...] = sent[0]
    near_ref[...] = sent[1]
    for copy in fields:
        copy.wait()


def sweep_kernel(
    planes, scalar_ref, own_ref, edge_ref, held_ref, field_ref, far_in, near_in, rows_ref, far_ref, near_ref, one_, two_, got, sent,
):
    count, _, _, depth, height, breadth = own_ref.shape
    steps = Steps(height, breadth)
    index = lax.axis_index("space")
    first = index * depth
    relax_low = jnp.where(first > 0, F32(RELAX), F32(0.0))
    relax_high = jnp.where(first + depth < planes, F32(RELAX), F32(0.0))
    odd = index & 1
    low, high = odd, 1 - odd
    got[0] = far_in[...]
    got[1] = near_in[...]

    def conductivity(p):
        if p < 0:
            return got[low, 2 * count * SENT].astype(F32)
        if p >= depth:
            return got[high, 2 * count * SENT].astype(F32)
        return held_ref[p]

    def one_source(s, _):
        group = scalar_ref[count + s].astype(jnp.int32)
        angular = angular_of(scalar_ref[2 * count + group].astype(jnp.int32))
        scales = RELAX * angular, -RELAX * angular
        point = Point(scalar_ref[s].astype(jnp.int32), first, steps)
        weights_at = scalar_ref.shape[0] - 6 * count + 6 * s

        def received(side, part, k):
            return got[side, (2 * s + part) * SENT + k].astype(F32)

        for part in range(2):
            ey, ez, ly, lz = [edge_ref[s, part, k] for k in range(4)]
            one_[part, 0, 0] = -relax_low * (steps.down_y(ey) + steps.down_z(ez))
            one_[part, 1, 0] = relax_low * ey
            one_[part, 2, 0] = relax_low * ez
            e = [own_ref[s, part, comp, 0] for comp in range(3)]
            one_[part, 0, 1] = e[0]
            one_[part, 1, 1] = e[1] - RELAX * received(low, part, 1)
            one_[part, 2, 1] = e[2] + RELAX * received(low, part, 0)
            for p in range(1, depth - 1):
                for comp in range(3):
                    one_[part, comp, p + 1] = own_ref[s, part, comp, p]
            e = [own_ref[s, part, comp, depth - 1] for comp in range(3)]
            high_y, high_z = received(high, part, 0), received(high, part, 1)
            one_[part, 0, depth] = e[0] - RELAX * (steps.down_y(high_y) + steps.down_z(high_z))
            one_[part, 1, depth] = e[1] + RELAX * high_y
            one_[part, 2, depth] = e[2] + RELAX * high_z
            two_[part, 0, depth + 1] = jnp.zeros((height, breadth), F32)
            one_[part, 1, depth + 1] = received(high, part, 2) - relax_high * lz
            one_[part, 2, depth + 1] = received(high, part, 3) + relax_high * ly

        def sweep(ref, into, low_plane, planes_swept, k):
            if low_plane < 0:
                before = [(-ref[part, 2, 0], ref[part, 1, 0]) for part in range(2)]
            else:
                before = []
                for part in range(2):
                    e = [ref[part, comp, 0] for comp in range(3)]
                    hy, hz = steps.magnetic_yz(e, [None, ref[part, 1, 1], ref[part, 2, 1]])
                    before.append((hy + received(low, part, k), hz + received(low, part, k + 1)))
            for p in range(low_plane, planes_swept):
                relax = relax_low if p < 0 else relax_high if p == depth else F32(RELAX)
                for part in range(2):
                    e = [ref[part, comp, p + 1] if comp or p < depth else None for comp in range(3)]
                    if p < depth:
                        e_next = [None if comp == 0 else ref[part, comp, p + 2] for comp in range(3)]
                        hy, hz = steps.magnetic_yz(e, e_next)
                    else:
                        hy, hz = received(high, part, 4) + e[2], received(high, part, 5) - e[1]
                    hx = steps.magnetic_x(e)
                    coef = scales[part] * conductivity(p)
                    for comp in range(1 if p == depth else 0, 3):
                        curl = steps.curl_back(comp, hx, hy, hz, before[part])
                        into[part, comp, p + 1] = e[comp] - relax * curl + coef * ref[1 - part, comp, p + 1]
                    if p < 0:
                        hy, hz = hy + received(low, part, k), hz + received(low, part, k + 1)
                    before[part] = hy, hz
            point.add_to(into, 0, planes_swept, 1, lambda part, comp: scalar_ref[weights_at + part * 3 + comp])

        sweep(one_, two_, -1, depth + 1, 2)
        sweep(two_, one_, 0, depth, 4)

        for p in range(depth):
            row_re = row_im = None
            for comp in range(3):
                re, im = one_[0, comp, p + 1], one_[1, comp, p + 1]
                field_re, field_im = field_ref[s, 0, comp, p], field_ref[s, 1, comp, p]
                add_re, add_im = field_re * re - field_im * im, field_re * im + field_im * re
                row_re, row_im = (add_re, add_im) if comp == 0 else (row_re + add_re, row_im + add_im)
            coef = angular * held_ref[p]
            for part, value in enumerate((row_re, row_im)):
                value = (coef * value).astype(rows_ref.dtype)
                rows_ref[s, part, p] = value
                if p >= depth - REACH:
                    sent[high, s, part, p - depth + REACH] = value
                if p < REACH:
                    sent[low, s, part, p] = value
        return 0

    lax.fori_loop(0, count, one_source, 0)
    far_ref[...] = sent[0]
    near_ref[...] = sent[1]


def in_plane(steps, f):
    total = (steps.after_y(f) + steps.before_y(f)) + (steps.after_z(f) + steps.before_z(f))
    return (1.0 - 6.0 * KAPPA) * f + KAPPA * total


def smooth_kernel(planes, rows_ref, alone_ref):
    count, _, depth, height, breadth = rows_ref.shape
    steps = Steps(height, breadth)
    first = lax.axis_index("space") * depth
    below = jnp.where(first > 0, F32(KAPPA), F32(0.0))
    above = jnp.where(first + depth < planes, F32(KAPPA), F32(0.0))

    def one_row(s, part):
        value = [rows_ref[s, part, p].astype(F32) for p in range(depth)]
        once = []
        for p in range(depth):
            beside = [value[q] for q in (p - 1, p + 1) if 0 <= q < depth]
            once.append(in_plane(steps, value[p]) + KAPPA * functools.reduce(jnp.add, beside))
        once = [below * value[0]] + once + [above * value[-1]]
        for p in range(depth):
            alone_ref[s, part, p] = in_plane(steps, once[p + 1]) + KAPPA * (once[p] + once[p + 2])

    def one_source(s, _):
        for part in range(2):
            one_row(s, part)
        return 0

    lax.fori_loop(0, count, one_source, 0)


def block_kernel(cells, rows_ref, alone_ref, far_in, near_in, all_ref, smooth_ref, block_ref, got, rounded, sums, sem):
    count, _, depth, height, breadth = rows_ref.shape
    ranks = all_ref.shape[0]
    steps = Steps(height, breadth)
    many = ranks * count * 2
    got[0] = far_in[...]
    got[1] = near_in[...]
    odd = lax.axis_index("space") & 1
    low, high = odd, 1 - odd

    def one_row(s, part):
        value = [alone_ref[s, part, p] for p in range(depth)]
        for side, nearest, order in ((low, REACH - 1, 1), (high, 0, -1)):
            close = got[side, s, part, nearest].astype(F32)
            beyond = got[side, s, part, REACH - 1 - nearest].astype(F32)
            end = 0 if order > 0 else depth - 1
            value[end] = value[end] + (2.0 * KAPPA * in_plane(steps, close) + KAPPA * KAPPA * beyond)
            value[end + order] = value[end + order] + KAPPA * KAPPA * close
        for p in range(depth):
            rounded[s, part, p] = value[p].astype(rounded.dtype)

    def one_source(s, _):
        for part in range(2):
            one_row(s, part)
        return 0

    lax.fori_loop(0, count, one_source, 0)
    out = pltpu.make_async_copy(rounded, smooth_ref, sem)
    out.start()

    sums[...] = jnp.zeros_like(sums)

    def one_plane(p, _):
        mine = [rounded[a // 2, a % 2, p].astype(F32) for a in range(2 * count)]
        for b in range(many):
            r, t = divmod(b // 2, count)
            other = all_ref[r, t, b % 2, p].astype(F32)
            for a in range(2 * count):
                prod = mine[a] * other
                total = prod[:8]
                for k in range(8, height, 8):
                    total = total + prod[k : k + 8]
                sums[a * many + b] = sums[a * many + b] + total
        return 0

    lax.fori_loop(0, depth, one_plane, 0)
    half = jnp.bfloat16
    ones = jnp.ones((breadth, breadth), half)
    for a in range(2 * count):
        table = sums[a * many : (a + 1) * many].reshape(many * 8, breadth)
        coarse = table.astype(half)
        fine = (table - coarse.astype(F32)).astype(half)
        table = jnp.dot(coarse, ones, preferred_element_type=F32) + jnp.dot(fine, ones, preferred_element_type=F32)
        line = None
        for b in range(many):
            add = jnp.where(steps.lane[:8] == b, table[b * 8 : b * 8 + 8], 0.0)
            line = add if line is None else line + add
        line = jnp.sum(line, axis=0, keepdims=True) * (1.0 / cells)
        for peer in range(block_ref.shape[0]):
            block_ref[peer, a : a + 1, :] = line[:, :many]
    out.wait()


def in_hbm(x):
    return pltpu.with_memory_space_constraint(x, pltpu.HBM)


def shards(conductivity, background, warm_start, data_weight, recv_cell, src_group, group_freq):
    count = warm_start.shape[0]
    depth, height, breadth = conductivity.shape
    plane = (height, breadth)
    peers = lax.axis_size("space")
    ranks = lax.axis_size("rx")
    cells = depth * height * breadth * peers
    half = jnp.bfloat16
    integers = jnp.concatenate([recv_cell, src_group, group_freq]).astype(F32)
    scalars = jnp.concatenate([integers, data_weight.reshape(-1)])
    far = [(i, i + 1) for i in range(1, peers - 1, 2)]
    near = [(i, i + 1) for i in range(0, peers - 1, 2)]
    far, near = [pairs + [(j, i) for i, j in pairs] for pairs in (far, near)]
    shape = jax.ShapeDtypeStruct

    message = shape((2 * count * SENT + 1,) + plane, half)
    to_far, to_near, own, edge, held, field = pl.pallas_call(
        first_kernel,
        out_shape=(
            message,
            message,
            shape(warm_start.shape, F32),
            shape((count, 2, 4) + plane, F32),
            shape(conductivity.shape, F32),
            shape((count,) + background.shape[1:], F32),
        ),
        in_specs=[HBM] * 7,
        out_specs=(FULL,) * 6,
        scratch_shapes=[
            pltpu.VMEM(warm_start.shape, F32),
            pltpu.SMEM(data_weight.shape, F32),
            pltpu.SMEM(recv_cell.shape, jnp.int32),
            pltpu.SMEM(src_group.shape, jnp.int32),
            pltpu.SMEM(group_freq.shape, jnp.int32),
            pltpu.VMEM((2,) + message.shape, half),
            pltpu.SemaphoreType.DMA((5 + 2 * count,)),
        ],
        compiler_params=KERNEL,
        name="first_sweep",
    )(*[in_hbm(x) for x in (warm_start, conductivity, background, data_weight, recv_cell, src_group, group_freq)])
    from_far = lax.ppermute(to_far, "space", far)
    from_near = lax.ppermute(to_near, "space", near)

    rows_of = shape((count, 2, depth) + plane, half)
    ends_of = shape((count, 2, REACH) + plane, half)
    rows, to_far, to_near = pl.pallas_call(
        functools.partial(sweep_kernel, peers * depth),
        out_shape=(rows_of, ends_of, ends_of),
        in_specs=[SCALARS] + [FULL] * 6,
        out_specs=(FULL,) * 3,
        scratch_shapes=[
            pltpu.VMEM((2, 3, depth + 2) + plane, F32),
            pltpu.VMEM((2, 3, depth + 2) + plane, F32),
            pltpu.VMEM((2,) + message.shape, half),
            pltpu.VMEM((2,) + ends_of.shape, half),
        ],
        compiler_params=KERNEL,
        name="sweeps",
    )(scalars, own, edge, held, field, from_far, from_near)
    from_far = lax.ppermute(to_far, "space", far)
    from_near = lax.ppermute(to_near, "space", near)
    every = lax.all_gather(rows, "rx", axis=0)

    many = 2 * count * ranks
    alone = pl.pallas_call(
        functools.partial(smooth_kernel, peers * depth),
        out_shape=shape(rows_of.shape, F32),
        in_specs=[FULL],
        out_specs=FULL,
        compiler_params=KERNEL,
        name="smooth",
    )(rows)
    smoothed, partial_block = pl.pallas_call(
        functools.partial(block_kernel, cells),
        out_shape=(rows_of, shape((peers, 2 * count, many), F32)),
        in_specs=[FULL] * 5,
        out_specs=(HBM, FULL),
        scratch_shapes=[
            pltpu.VMEM((2,) + ends_of.shape, half),
            pltpu.VMEM(rows_of.shape, half),
            pltpu.VMEM((2 * count * many, 8, breadth), F32),
            pltpu.SemaphoreType.DMA,
        ],
        compiler_params=KERNEL,
        name="block",
    )(rows, alone, from_far, from_near, every)
    backwards = [list(range(peers - 1, -1, -1))]
    pieces = lax.all_to_all(partial_block, "space", 0, 0, axis_index_groups=backwards)
    return (jnp.sum(pieces, axis=0), smoothed)


def solution(mesh):
    in_specs = (
        P("space", None, None),
        P(None, None, None, "space", None, None),
        P("rx", None, None, "space", None, None),
        P("rx", None, None),
        P("rx"),
        P("rx"),
        P(),
    )
    out_specs = (P("rx", None), P("rx", None, "space", None, None))
    return jax.shard_map(shards, mesh=mesh, in_specs=in_specs, out_specs=out_specs, check_vma=False)
```

```python
import functools

import jax
import jax.numpy as jnp
from jax import lax
from jax.experimental import pallas as pl
from jax.experimental.pallas import tpu as pltpu
from jax.sharding import PartitionSpec as P

SENT = 6
RELAX = 0.2
KAPPA = 0.1
REACH = 2
FULL = pl.BlockSpec(memory_space=pltpu.VMEM)
HBM = pl.BlockSpec(memory_space=pltpu.HBM)
SCALARS = pl.BlockSpec(memory_space=pltpu.SMEM)
KERNEL = pltpu.CompilerParams(vmem_limit_bytes=8 * 2**20)
F32 = jnp.float32


class Steps:
    def __init__(self, height, breadth):
        self.height, self.breadth = height, breadth
        self.sub = lax.broadcasted_iota(jnp.int32, (8, breadth), 0)
        self.lane = lax.broadcasted_iota(jnp.int32, (height, breadth), 1)

    def after_y(self, f):
        f = pltpu.roll(f, self.height - 1, 0)
        return jnp.concatenate([f[:-8], jnp.where(self.sub < 7, f[-8:], 0.0)], axis=0)

    def before_y(self, f):
        f = pltpu.roll(f, 1, 0)
        return jnp.concatenate([jnp.where(self.sub > 0, f[:8], 0.0), f[8:]], axis=0)

    def after_z(self, f):
        return jnp.where(self.lane < self.breadth - 1, pltpu.roll(f, self.breadth - 1, 1), 0.0)

    def before_z(self, f):
        return jnp.where(self.lane > 0, pltpu.roll(f, 1, 1), 0.0)

    def up_y(self, f):
        return self.after_y(f) - f

    def up_z(self, f):
        return self.after_z(f) - f

    def down_y(self, f):
        return f - self.before_y(f)

    def down_z(self, f):
        return f - self.before_z(f)

    def magnetic_yz(self, e, e_next):
        ex, ey, ez = e
        if e_next is None:
            return self.up_z(ex) + ez, -ey - self.up_y(ex)
        return self.up_z(ex) - (e_next[2] - ez), (e_next[1] - ey) - self.up_y(ex)

    def magnetic_x(self, e):
        return self.up_y(e[2]) - self.up_z(e[1])

    def curl_back(self, comp, hx, hy, hz, before):
        if comp == 0:
            return self.down_y(hz) - self.down_z(hy)
        if comp == 1:
            return self.down_z(hx) - (hz - before[1])
        return (hy - before[0]) - self.down_y(hx)


def angular_of(freq):
    angular = F32(0.25)
    for bit, factor in ((1, 1.25), (2, 1.25**2), (4, 1.25**4)):
        angular = angular * jnp.where((freq & bit) != 0, F32(factor), F32(1.0))
    return angular


def split(number, size):
    if size & (size - 1):
        return number // size, number % size
    return number >> (size.bit_length() - 1), number & (size - 1)


class Point:
    def __init__(self, cell, first, steps):
        plane, inner = split(cell, steps.height * steps.breadth)
        row, lane = split(inner, steps.breadth)
        block, sub = split(row, 8)
        self.plane = plane - first
        self.rows = pl.ds(pl.multiple_of(block * 8, 8), 8)
        self.row, self.sub, self.lane, self.steps = row, sub, lane, steps

    def add_to(self, ref, low, high, shift, weight):
        reached = (self.plane >= low) & (self.plane < high)
        here = (self.steps.sub == self.sub) & (self.steps.lane[:8] == self.lane)
        amount = jnp.where(here, jnp.where(reached, F32(RELAX), F32(0.0)), 0.0)
        plane = jnp.clip(self.plane, low, high - 1) + shift
        for part in range(2):
            for comp in range(3):
                at = (part, comp, plane, self.rows)
                ref[at] = ref[at] + amount * weight(part, comp)


def first_kernel(
    start_ref, cond_ref, back_ref, weight_ref, cell_ref, group_ref, freq_ref,
    *refs,
):
    count, _, _, depth, height, breadth = start_ref.shape
    fars, nears = refs[:count], refs[count : 2 * count]
    own_ref, edge_ref, held_ref, field_ref, raw, weight, cell, group, freq, sent, sems = refs[2 * count :]
    pairs = ((group_ref, group), (freq_ref, freq), (cell_ref, cell), (weight_ref, weight), (cond_ref, held_ref))
    copies = [pltpu.make_async_copy(a, b, sems.at[k]) for k, (a, b) in enumerate(pairs)]

    def start_of(s):
        return pltpu.make_async_copy(start_ref.at[s], raw.at[s], sems.at[len(pairs) + s])

    for copy in [start_of(0)] + copies + [start_of(s) for s in range(1, count)]:
        copy.start()
    copies[0].wait()
    fields = [
        pltpu.make_async_copy(back_ref.at[group[s]], field_ref.at[s], sems.at[len(pairs) + count + s])
        for s in range(count)
    ]
    for copy in fields:
        copy.start()
    for copy in copies[1:]:
        copy.wait()
    steps = Steps(height, breadth)
    half = sent.dtype
    index = lax.axis_index("space")
    first = index * depth
    down = index & 1
    up = 1 - down
    row = lax.broadcasted_iota(jnp.int32, (height, breadth), 0)
    last = depth - 1
    sent[up, 0, 2 * SENT] = held_ref[last].astype(half)
    sent[down, 0, 2 * SENT] = held_ref[0].astype(half)

    def one_source(s, _):
        start_of(s).wait()
        scale = RELAX * angular_of(freq[group[s]])
        scales = scale, -scale
        point = Point(cell[s], first, steps)
        before = []
        for part in range(2):
            ey, ez = raw[s, part, 1, 0], raw[s, part, 2, 0]
            for k, f in enumerate((ey, ez)):
                sent[down, s, part * SENT + k] = f.astype(half)
                edge_ref[s, part, k] = f
            before.append((-ez, ey))
        for p in range(depth):
            for part in range(2):
                e = [raw[s, part, comp, p] for comp in range(3)]
                e_next = None
                if p < last:
                    e_next = [None if comp == 0 else raw[s, part, comp, p + 1] for comp in range(3)]
                hy, hz = steps.magnetic_yz(e, e_next)
                if p == last:
                    for k, f in enumerate((hy, hz)):
                        sent[up, s, part * SENT + k] = f.astype(half)
                        edge_ref[s, part, 2 + k] = f
                hx = steps.magnetic_x(e)
                coef = scales[part] * held_ref[p]
                for comp in range(3):
                    curl = steps.curl_back(comp, hx, hy, hz, before[part])
                    own_ref[s, part, comp, p] = e[comp] - RELAX * curl + coef * raw[s, 1 - part, comp, p]
                before[part] = hy, hz
        point.add_to(own_ref.at[s], 0, depth, 0, lambda part, comp: weight[s, part, comp])

        at_last = jnp.where(point.plane == last, F32(1.0), F32(0.0))
        here = jnp.where((row == point.row) & (steps.lane == point.lane), RELAX * at_last, 0.0)
        for part in range(2):
            ex, ey, ez = [own_ref[s, part, comp, 0] for comp in range(3)]
            hy, hz = steps.up_z(ex) - own_ref[s, part, 2, 1], own_ref[s, part, 1, 1] - steps.up_y(ex)
            for k, f in enumerate((ey, ez, hy, hz)):
                sent[down, s, part * SENT + 2 + k] = f.astype(half)
            e = [own_ref[s, part, comp, last] for comp in range(3)]
            behind = steps.magnetic_yz([own_ref[s, part, comp, last - 1] for comp in range(3)], e)
            hy, hz = steps.magnetic_yz(e, None)
            hx = steps.magnetic_x(e)
            coef = scales[part] * held_ref[last]
            after = []
            for comp in range(3):
                curl = steps.curl_back(comp, hx, hy, hz, behind)
                value = e[comp] - RELAX * curl + coef * own_ref[s, 1 - part, comp, last]
                after.append(value + here * weight[s, part, comp])
            for k, f in enumerate((hy, hz) + steps.magnetic_yz(after, None)):
                sent[up, s, part * SENT + 2 + k] = f.astype(half)
        return 0

    lax.fori_loop(0, count, one_source, 0)
    for s in range(count):
        fars[s][...] = sent[0, s, : fars[s].shape[0]]
        nears[s][...] = sent[1, s, : nears[s].shape[0]]
    for copy in fields:
        copy.wait()


def sweep_kernel(s, planes, scalar_ref, own_ref, edge_ref, held_ref, field_ref, far_in, near_in, far_cond, near_cond, *refs):
    count, _, _, depth, height, breadth = own_ref.shape
    final = s == count - 1
    if final:
        earlier = refs[:s]
        rows_ref, far_ref, near_ref, one_, two_, got, conds, sent = refs[s:]
    else:
        rows_ref, one_, two_, got, conds = refs
    steps = Steps(height, breadth)
    index = lax.axis_index("space")
    first = index * depth
    relax_low = jnp.where(first > 0, F32(RELAX), F32(0.0))
    relax_high = jnp.where(first + depth < planes, F32(RELAX), F32(0.0))
    low = index & 1
    high = 1 - low
    got[0] = far_in[: 2 * SENT]
    got[1] = near_in[: 2 * SENT]
    conds[0] = far_cond[2 * SENT]
    conds[1] = near_cond[2 * SENT]
    group = scalar_ref[count + s].astype(jnp.int32)
    angular = angular_of(scalar_ref[2 * count + group].astype(jnp.int32))
    scales = RELAX * angular, -RELAX * angular
    point = Point(scalar_ref[s].astype(jnp.int32), first, steps)
    weights_at = scalar_ref.shape[0] - 6 * count + 6 * s

    def conductivity(p):
        if p < 0:
            return conds[low].astype(F32)
        if p >= depth:
            return conds[high].astype(F32)
        return held_ref[p]

    def received(side, part, k):
        return got[side, part * SENT + k].astype(F32)

    def weight(part, comp):
        return scalar_ref[weights_at + part * 3 + comp]

    for part in range(2):
        ey, ez, ly, lz = [edge_ref[s, part, k] for k in range(4)]
        one_[part, 0, 0] = -relax_low * (steps.down_y(ey) + steps.down_z(ez))
        one_[part, 1, 0] = relax_low * ey
        one_[part, 2, 0] = relax_low * ez
        e = [own_ref[s, part, comp, 0] for comp in range(3)]
        one_[part, 0, 1] = e[0]
        one_[part, 1, 1] = e[1] - RELAX * received(low, part, 1)
        one_[part, 2, 1] = e[2] + RELAX * received(low, part, 0)
        for p in range(1, depth - 1):
            for comp in range(3):
                one_[part, comp, p + 1] = own_ref[s, part, comp, p]
        e = [own_ref[s, part, comp, depth - 1] for comp in range(3)]
        high_y, high_z = received(high, part, 0), received(high, part, 1)
        one_[part, 0, depth] = e[0] - RELAX * (steps.down_y(high_y) + steps.down_z(high_z))
        one_[part, 1, depth] = e[1] + RELAX * high_y
        one_[part, 2, depth] = e[2] + RELAX * high_z
        one_[part, 1, depth + 1] = received(high, part, 2) - relax_high * lz
        one_[part, 2, depth + 1] = received(high, part, 3) + relax_high * ly

    before = [(-one_[part, 2, 0], one_[part, 1, 0]) for part in range(2)]
    for p in range(-1, depth + 1):
        relax = relax_low if p < 0 else relax_high if p == depth else F32(RELAX)
        for part in range(2):
            e = [one_[part, comp, p + 1] if comp or p < depth else None for comp in range(3)]
            if p < depth:
                hy, hz = steps.magnetic_yz(e, [None, one_[part, 1, p + 2], one_[part, 2, p + 2]])
            else:
                hy, hz = received(high, part, 4) + e[2], received(high, part, 5) - e[1]
            hx = steps.magnetic_x(e)
            coef = scales[part] * conductivity(p)
            for comp in range(1 if p == depth else 0, 3):
                curl = steps.curl_back(comp, hx, hy, hz, before[part])
                two_[part, comp, p + 1] = e[comp] - relax * curl + coef * one_[1 - part, comp, p + 1]
            if p < 0:
                hy, hz = hy + received(low, part, 2), hz + received(low, part, 3)
            before[part] = hy, hz
    for part in range(2):
        two_[part, 0, depth + 1] = jnp.zeros((height, breadth), F32)
    point.add_to(two_, 0, depth + 1, 1, weight)

    row = lax.broadcasted_iota(jnp.int32, (height, breadth), 0)
    here = (row == point.row) & (steps.lane == point.lane)
    before = []
    for part in range(2):
        e = [two_[part, comp, 0] for comp in range(3)]
        hy, hz = steps.magnetic_yz(e, [None, two_[part, 1, 1], two_[part, 2, 1]])
        before.append((hy + received(low, part, 4), hz + received(low, part, 5)))
    for p in range(depth):
        spot = jnp.where(here, jnp.where(point.plane == p, F32(RELAX), F32(0.0)), 0.0)
        after = []
        for part in range(2):
            e = [two_[part, comp, p + 1] for comp in range(3)]
            hy, hz = steps.magnetic_yz(e, [None, two_[part, 1, p + 2], two_[part, 2, p + 2]])
            hx = steps.magnetic_x(e)
            coef = scales[part] * held_ref[p]
            for comp in range(3):
                curl = steps.curl_back(comp, hx, hy, hz, before[part])
                value = e[comp] - RELAX * curl + coef * two_[1 - part, comp, p + 1]
                after.append(value + spot * weight(part, comp))
            before[part] = hy, hz
        row_re = row_im = None
        for comp in range(3):
            re, im = after[comp], after[3 + comp]
            field_re, field_im = field_ref[s, 0, comp, p], field_ref[s, 1, comp, p]
            add_re, add_im = field_re * re - field_im * im, field_re * im + field_im * re
            row_re, row_im = (add_re, add_im) if comp == 0 else (row_re + add_re, row_im + add_im)
        coef = angular * held_ref[p]
        for part, value in enumerate((row_re, row_im)):
            value = (coef * value).astype(rows_ref.dtype)
            if not final:
                rows_ref[part, p] = value
                continue
            rows_ref[s, part, p] = value
            if p >= depth - REACH:
                sent[high, s, part, p - depth + REACH] = value
            if p < REACH:
                sent[low, s, part, p] = value
    if final:
        for t, ref in enumerate(earlier):
            rows_ref[t] = ref[...]
            sent[high, t] = ref[:, depth - REACH :]
            sent[low, t] = ref[:, :REACH]
        far_ref[...] = sent[0]
        near_ref[...] = sent[1]


def in_plane(steps, f):
    total = (steps.after_y(f) + steps.before_y(f)) + (steps.after_z(f) + steps.before_z(f))
    return (1.0 - 6.0 * KAPPA) * f + KAPPA * total


def smooth_kernel(planes, rows_ref, alone_ref):
    count, _, depth, height, breadth = rows_ref.shape
    steps = Steps(height, breadth)
    first = lax.axis_index("space") * depth
    below = jnp.where(first > 0, F32(KAPPA), F32(0.0))
    above = jnp.where(first + depth < planes, F32(KAPPA), F32(0.0))

    def one_row(s, part):
        value = [rows_ref[s, part, p].astype(F32) for p in range(depth)]
        once = []
        for p in range(depth):
            beside = [value[q] for q in (p - 1, p + 1) if 0 <= q < depth]
            once.append(in_plane(steps, value[p]) + KAPPA * functools.reduce(jnp.add, beside))
        once = [below * value[0]] + once + [above * value[-1]]
        for p in range(depth):
            alone_ref[s, part, p] = in_plane(steps, once[p + 1]) + KAPPA * (once[p] + once[p + 2])

    def one_source(s, _):
        for part in range(2):
            one_row(s, part)
        return 0

    lax.fori_loop(0, count, one_source, 0)


def block_kernel(cells, rows_ref, alone_ref, far_in, near_in, all_ref, smooth_ref, block_ref, got, rounded, sums, sem):
    count, _, depth, height, breadth = rows_ref.shape
    ranks = all_ref.shape[0]
    steps = Steps(height, breadth)
    many = ranks * count * 2
    got[0] = far_in[...]
    got[1] = near_in[...]
    odd = lax.axis_index("space") & 1
    low, high = odd, 1 - odd

    def one_row(s, part):
        value = [alone_ref[s, part, p] for p in range(depth)]
        for side, nearest, order in ((low, REACH - 1, 1), (high, 0, -1)):
            close = got[side, s, part, nearest].astype(F32)
            beyond = got[side, s, part, REACH - 1 - nearest].astype(F32)
            end = 0 if order > 0 else depth - 1
            value[end] = value[end] + (2.0 * KAPPA * in_plane(steps, close) + KAPPA * KAPPA * beyond)
            value[end + order] = value[end + order] + KAPPA * KAPPA * close
        for p in range(depth):
            rounded[s, part, p] = value[p].astype(rounded.dtype)

    def one_source(s, _):
        for part in range(2):
            one_row(s, part)
        return 0

    lax.fori_loop(0, count, one_source, 0)
    out = pltpu.make_async_copy(rounded, smooth_ref, sem)
    out.start()

    sums[...] = jnp.zeros_like(sums)

    def one_plane(p, _):
        mine = [rounded[a // 2, a % 2, p].astype(F32) for a in range(2 * count)]
        for b in range(many):
            r, t = divmod(b // 2, count)
            other = all_ref[r, t, b % 2, p].astype(F32)
            for a in range(2 * count):
                prod = mine[a] * other
                total = prod[:8]
                for k in range(8, height, 8):
                    total = total + prod[k : k + 8]
                sums[a * many + b] = sums[a * many + b] + total
        return 0

    lax.fori_loop(0, depth, one_plane, 0)
    half = jnp.bfloat16
    ones = jnp.ones((breadth, breadth), half)
    for a in range(2 * count):
        table = sums[a * many : (a + 1) * many].reshape(many * 8, breadth)
        coarse = table.astype(half)
        fine = (table - coarse.astype(F32)).astype(half)
        table = jnp.dot(coarse, ones, preferred_element_type=F32) + jnp.dot(fine, ones, preferred_element_type=F32)
        line = None
        for b in range(many):
            add = jnp.where(steps.lane[:8] == b, table[b * 8 : b * 8 + 8], 0.0)
            line = add if line is None else line + add
        line = jnp.sum(line, axis=0, keepdims=True) * (1.0 / cells)
        for peer in range(block_ref.shape[0]):
            block_ref[peer, a : a + 1, :] = line[:, :many]
    out.wait()


def in_hbm(x):
    return pltpu.with_memory_space_constraint(x, pltpu.HBM)


def shards(conductivity, background, warm_start, data_weight, recv_cell, src_group, group_freq):
    count = warm_start.shape[0]
    depth, height, breadth = conductivity.shape
    plane = (height, breadth)
    peers = lax.axis_size("space")
    ranks = lax.axis_size("rx")
    cells = depth * height * breadth * peers
    half = jnp.bfloat16
    integers = jnp.concatenate([recv_cell, src_group, group_freq]).astype(F32)
    scalars = jnp.concatenate([integers, data_weight.reshape(-1)])
    far = [(i, i + 1) for i in range(1, peers - 1, 2)]
    near = [(i, i + 1) for i in range(0, peers - 1, 2)]
    far, near = [pairs + [(j, i) for i, j in pairs] for pairs in (far, near)]
    shape = jax.ShapeDtypeStruct

    messages = [shape((2 * SENT + (s == 0),) + plane, half) for s in range(count)]
    outs = pl.pallas_call(
        first_kernel,
        out_shape=tuple(messages)
        + tuple(messages)
        + (
            shape(warm_start.shape, F32),
            shape((count, 2, 4) + plane, F32),
            shape(conductivity.shape, F32),
            shape((count,) + background.shape[1:], F32),
        ),
        in_specs=[HBM] * 7,
        out_specs=(FULL,) * (2 * count + 4),
        scratch_shapes=[
            pltpu.VMEM(warm_start.shape, F32),
            pltpu.SMEM(data_weight.shape, F32),
            pltpu.SMEM(recv_cell.shape, jnp.int32),
            pltpu.SMEM(src_group.shape, jnp.int32),
            pltpu.SMEM(group_freq.shape, jnp.int32),
            pltpu.VMEM((2, count) + messages[0].shape, half),
            pltpu.SemaphoreType.DMA((5 + 2 * count,)),
        ],
        compiler_params=KERNEL,
        name="first_sweep",
    )(*[in_hbm(x) for x in (warm_start, conductivity, background, data_weight, recv_cell, src_group, group_freq)])
    own, edge, held, field = outs[2 * count :]
    fars, nears = [], []
    for s in range(count):
        fars.append(lax.ppermute(outs[s], "space", far))
        nears.append(lax.ppermute(outs[count + s], "space", near))

    rows_of = shape((count, 2, depth) + plane, half)
    ends_of = shape((count, 2, REACH) + plane, half)
    earlier = []
    for s in range(count):
        operands = [scalars, own, edge, held, field, fars[s], nears[s], fars[0], nears[0]]
        scratch = [
            pltpu.VMEM((2, 3, depth + 2) + plane, F32),
            pltpu.VMEM((2, 3, depth + 2) + plane, F32),
            pltpu.VMEM((2, 2 * SENT) + plane, half),
            pltpu.VMEM((2,) + plane, half),
        ]
        results = (shape((2, depth) + plane, half),)
        if s == count - 1:
            operands += earlier
            results = (rows_of, ends_of, ends_of)
            scratch.append(pltpu.VMEM((2,) + ends_of.shape, half))
        results = pl.pallas_call(
            functools.partial(sweep_kernel, s, peers * depth),
            out_shape=results,
            in_specs=[SCALARS] + [FULL] * (len(operands) - 1),
            out_specs=(FULL,) * len(results),
            scratch_shapes=scratch,
            compiler_params=KERNEL,
            name="sweeps",
        )(*operands)
        earlier.append(results[0])
    rows, to_far, to_near = results
    from_far = lax.ppermute(to_far, "space", far)
    from_near = lax.ppermute(to_near, "space", near)
    every = lax.all_gather(rows, "rx", axis=0)

    many = 2 * count * ranks
    alone = pl.pallas_call(
        functools.partial(smooth_kernel, peers * depth),
        out_shape=shape(rows_of.shape, F32),
        in_specs=[FULL],
        out_specs=FULL,
        compiler_params=KERNEL,
        name="smooth",
    )(rows)
    smoothed, partial_block = pl.pallas_call(
        functools.partial(block_kernel, cells),
        out_shape=(rows_of, shape((peers, 2 * count, many), F32)),
        in_specs=[FULL] * 5,
        out_specs=(HBM, FULL),
        scratch_shapes=[
            pltpu.VMEM((2,) + ends_of.shape, half),
            pltpu.VMEM(rows_of.shape, half),
            pltpu.VMEM((2 * count * many, 8, breadth), F32),
            pltpu.SemaphoreType.DMA,
        ],
        compiler_params=KERNEL,
        name="block",
    )(rows, alone, from_far, from_near, every)
    backwards = [list(range(peers - 1, -1, -1))]
    pieces = lax.all_to_all(partial_block, "space", 0, 0, axis_index_groups=backwards)
    return (jnp.sum(pieces, axis=0), smoothed)


def solution(mesh):
    in_specs = (
        P("space", None, None),
        P(None, None, None, "space", None, None),
        P("rx", None, None, "space", None, None),
        P("rx", None, None),
        P("rx"),
        P("rx"),
        P(),
    )
    out_specs = (P("rx", None), P("rx", None, "space", None, None))
    return jax.shard_map(shards, mesh=mesh, in_specs=in_specs, out_specs=out_specs, check_vma=False)
```

```python
import functools

import jax
import jax.numpy as jnp
from jax import lax
from jax.experimental import pallas as pl
from jax.experimental.pallas import tpu as pltpu
from jax.sharding import PartitionSpec as P

SENT = 6
RELAX = 0.2
KAPPA = 0.1
REACH = 2
FULL = pl.BlockSpec(memory_space=pltpu.VMEM)
HBM = pl.BlockSpec(memory_space=pltpu.HBM)
SCALARS = pl.BlockSpec(memory_space=pltpu.SMEM)
KERNEL = pltpu.CompilerParams(vmem_limit_bytes=8 * 2**20)
F32 = jnp.float32


class Steps:
    def __init__(self, height, breadth):
        self.height, self.breadth = height, breadth
        self.sub = lax.broadcasted_iota(jnp.int32, (8, breadth), 0)
        self.lane = lax.broadcasted_iota(jnp.int32, (height, breadth), 1)

    def after_y(self, f):
        f = pltpu.roll(f, self.height - 1, 0)
        return jnp.concatenate([f[:-8], jnp.where(self.sub < 7, f[-8:], 0.0)], axis=0)

    def before_y(self, f):
        f = pltpu.roll(f, 1, 0)
        return jnp.concatenate([jnp.where(self.sub > 0, f[:8], 0.0), f[8:]], axis=0)

    def after_z(self, f):
        return jnp.where(self.lane < self.breadth - 1, pltpu.roll(f, self.breadth - 1, 1), 0.0)

    def before_z(self, f):
        return jnp.where(self.lane > 0, pltpu.roll(f, 1, 1), 0.0)

    def up_y(self, f):
        return self.after_y(f) - f

    def up_z(self, f):
        return self.after_z(f) - f

    def down_y(self, f):
        return f - self.before_y(f)

    def down_z(self, f):
        return f - self.before_z(f)

    def magnetic_yz(self, e, e_next):
        ex, ey, ez = e
        if e_next is None:
            return self.up_z(ex) + ez, -ey - self.up_y(ex)
        return self.up_z(ex) - (e_next[2] - ez), (e_next[1] - ey) - self.up_y(ex)

    def magnetic_x(self, e):
        return self.up_y(e[2]) - self.up_z(e[1])

    def curl_back(self, comp, hx, hy, hz, before):
        if comp == 0:
            return self.down_y(hz) - self.down_z(hy)
        if comp == 1:
            return self.down_z(hx) - (hz - before[1])
        return (hy - before[0]) - self.down_y(hx)


def angular_of(freq):
    angular = F32(0.25)
    for bit, factor in ((1, 1.25), (2, 1.25**2), (4, 1.25**4)):
        angular = angular * jnp.where((freq & bit) != 0, F32(factor), F32(1.0))
    return angular


def split(number, size):
    if size & (size - 1):
        return number // size, number % size
    return number >> (size.bit_length() - 1), number & (size - 1)


class Point:
    def __init__(self, cell, first, steps):
        plane, inner = split(cell, steps.height * steps.breadth)
        row, lane = split(inner, steps.breadth)
        block, sub = split(row, 8)
        self.plane = plane - first
        self.rows = pl.ds(pl.multiple_of(block * 8, 8), 8)
        self.row, self.sub, self.lane, self.steps = row, sub, lane, steps

    def add_to(self, ref, low, high, shift, weight):
        reached = (self.plane >= low) & (self.plane < high)
        here = (self.steps.sub == self.sub) & (self.steps.lane[:8] == self.lane)
        amount = jnp.where(here, jnp.where(reached, F32(RELAX), F32(0.0)), 0.0)
        plane = jnp.clip(self.plane, low, high - 1) + shift
        for part in range(2):
            for comp in range(3):
                at = (part, comp, plane, self.rows)
                ref[at] = ref[at] + amount * weight(part, comp)


def receive(got, far_in, near_in, at_end):
    got[1] = near_in[...]

    @pl.when(at_end)
    def _():
        got[0] = jnp.zeros(far_in.shape, far_in.dtype)

    @pl.when(jnp.logical_not(at_end))
    def _():
        got[0] = far_in[...]


def first_kernel(
    start_ref, cond_ref, back_ref, weight_ref, cell_ref, group_ref, freq_ref,
    far_ref, near_ref, own_ref, edge_ref, held_ref, field_ref,
    raw, weight, cell, group, freq, sent, sems,
):
    count, _, _, depth, height, breadth = start_ref.shape
    pairs = ((group_ref, group), (freq_ref, freq), (cell_ref, cell), (weight_ref, weight), (cond_ref, held_ref))
    copies = [pltpu.make_async_copy(a, b, sems.at[k]) for k, (a, b) in enumerate(pairs)]

    def start_of(s):
        return pltpu.make_async_copy(start_ref.at[s], raw.at[s], sems.at[len(pairs) + s])

    for copy in copies + [start_of(s) for s in range(count)]:
        copy.start()
    copies[0].wait()
    fields = [
        pltpu.make_async_copy(back_ref.at[group[s]], field_ref.at[s], sems.at[len(pairs) + count + s])
        for s in range(count)
    ]
    for copy in fields:
        copy.start()
    for copy in copies[1:]:
        copy.wait()
    steps = Steps(height, breadth)
    half = far_ref.dtype
    index = lax.axis_index("space")
    first = index * depth
    down = index & 1
    up = 1 - down
    row = lax.broadcasted_iota(jnp.int32, (height, breadth), 0)
    last = depth - 1
    sent[up, 2 * count * SENT] = held_ref[last].astype(half)
    sent[down, 2 * count * SENT] = held_ref[0].astype(half)

    def one_source(s, _):
        start_of(s).wait()
        scale = RELAX * angular_of(freq[group[s]])
        scales = scale, -scale
        point = Point(cell[s], first, steps)
        base = 2 * s * SENT
        before = []
        for part in range(2):
            ey, ez = raw[s, part, 1, 0], raw[s, part, 2, 0]
            for k, f in enumerate((ey, ez)):
                sent[down, base + part * SENT + k] = f.astype(half)
                edge_ref[s, part, k] = f
            before.append((-ez, ey))
        for p in range(depth):
            for part in range(2):
                e = [raw[s, part, comp, p] for comp in range(3)]
                e_next = None
                if p < last:
                    e_next = [None if comp == 0 else raw[s, part, comp, p + 1] for comp in range(3)]
                hy, hz = steps.magnetic_yz(e, e_next)
                if p == last:
                    for k, f in enumerate((hy, hz)):
                        sent[up, base + part * SENT + k] = f.astype(half)
                        edge_ref[s, part, 2 + k] = f
                hx = steps.magnetic_x(e)
                coef = scales[part] * held_ref[p]
                for comp in range(3):
                    curl = steps.curl_back(comp, hx, hy, hz, before[part])
                    own_ref[s, part, comp, p] = e[comp] - RELAX * curl + coef * raw[s, 1 - part, comp, p]
                before[part] = hy, hz
        point.add_to(own_ref.at[s], 0, depth, 0, lambda part, comp: weight[s, part, comp])

        at_last = jnp.where(point.plane == last, F32(1.0), F32(0.0))
        here = jnp.where((row == point.row) & (steps.lane == point.lane), RELAX * at_last, 0.0)
        for part in range(2):
            ex, ey, ez = [own_ref[s, part, comp, 0] for comp in range(3)]
            hy, hz = steps.up_z(ex) - own_ref[s, part, 2, 1], own_ref[s, part, 1, 1] - steps.up_y(ex)
            for k, f in enumerate((ey, ez, hy, hz)):
                sent[down, base + part * SENT + 2 + k] = f.astype(half)
            e = [own_ref[s, part, comp, last] for comp in range(3)]
            behind = steps.magnetic_yz([own_ref[s, part, comp, last - 1] for comp in range(3)], e)
            hy, hz = steps.magnetic_yz(e, None)
            hx = steps.magnetic_x(e)
            coef = scales[part] * held_ref[last]
            after = []
            for comp in range(3):
                curl = steps.curl_back(comp, hx, hy, hz, behind)
                value = e[comp] - RELAX * curl + coef * own_ref[s, 1 - part, comp, last]
                after.append(value + here * weight[s, part, comp])
            for k, f in enumerate((hy, hz) + steps.magnetic_yz(after, None)):
                sent[up, base + part * SENT + 2 + k] = f.astype(half)
        return 0

    lax.fori_loop(0, count, one_source, 0)
    far_ref[...] = sent[0]
    near_ref[...] = sent[1]
    for copy in fields:
        copy.wait()


def sweep_kernel(
    planes, scalar_ref, own_ref, edge_ref, held_ref, field_ref, far_in, near_in, rows_ref, far_ref, near_ref, one_, two_, got, sent,
):
    count, _, _, depth, height, breadth = own_ref.shape
    steps = Steps(height, breadth)
    index = lax.axis_index("space")
    first = index * depth
    relax_low = jnp.where(first > 0, F32(RELAX), F32(0.0))
    relax_high = jnp.where(first + depth < planes, F32(RELAX), F32(0.0))
    odd = index & 1
    low, high = odd, 1 - odd
    receive(got, far_in, near_in, (first == 0) | (first + depth == planes))

    def conductivity(p):
        if p < 0:
            return got[low, 2 * count * SENT].astype(F32)
        if p >= depth:
            return got[high, 2 * count * SENT].astype(F32)
        return held_ref[p]

    def one_source(s, _):
        group = scalar_ref[count + s].astype(jnp.int32)
        angular = angular_of(scalar_ref[2 * count + group].astype(jnp.int32))
        scales = RELAX * angular, -RELAX * angular
        point = Point(scalar_ref[s].astype(jnp.int32), first, steps)
        weights_at = scalar_ref.shape[0] - 6 * count + 6 * s

        def received(side, part, k):
            return got[side, (2 * s + part) * SENT + k].astype(F32)

        for part in range(2):
            ey, ez, ly, lz = [edge_ref[s, part, k] for k in range(4)]
            one_[part, 0, 0] = -relax_low * (steps.down_y(ey) + steps.down_z(ez))
            one_[part, 1, 0] = relax_low * ey
            one_[part, 2, 0] = relax_low * ez
            e = [own_ref[s, part, comp, 0] for comp in range(3)]
            one_[part, 0, 1] = e[0]
            one_[part, 1, 1] = e[1] - RELAX * received(low, part, 1)
            one_[part, 2, 1] = e[2] + RELAX * received(low, part, 0)
            for p in range(1, depth - 1):
                for comp in range(3):
                    one_[part, comp, p + 1] = own_ref[s, part, comp, p]
            e = [own_ref[s, part, comp, depth - 1] for comp in range(3)]
            high_y, high_z = received(high, part, 0), received(high, part, 1)
            one_[part, 0, depth] = e[0] - RELAX * (steps.down_y(high_y) + steps.down_z(high_z))
            one_[part, 1, depth] = e[1] + RELAX * high_y
            one_[part, 2, depth] = e[2] + RELAX * high_z
            two_[part, 0, depth + 1] = jnp.zeros((height, breadth), F32)
            one_[part, 1, depth + 1] = received(high, part, 2) - relax_high * lz
            one_[part, 2, depth + 1] = received(high, part, 3) + relax_high * ly

        def sweep(ref, into, low_plane, planes_swept, k):
            if low_plane < 0:
                before = [(-ref[part, 2, 0], ref[part, 1, 0]) for part in range(2)]
            else:
                before = []
                for part in range(2):
                    e = [ref[part, comp, 0] for comp in range(3)]
                    hy, hz = steps.magnetic_yz(e, [None, ref[part, 1, 1], ref[part, 2, 1]])
                    before.append((hy + received(low, part, k), hz + received(low, part, k + 1)))
            for p in range(low_plane, planes_swept):
                relax = relax_low if p < 0 else relax_high if p == depth else F32(RELAX)
                for part in range(2):
                    e = [ref[part, comp, p + 1] if comp or p < depth else None for comp in range(3)]
                    if p < depth:
                        e_next = [None if comp == 0 else ref[part, comp, p + 2] for comp in range(3)]
                        hy, hz = steps.magnetic_yz(e, e_next)
                    else:
                        hy, hz = received(high, part, 4) + e[2], received(high, part, 5) - e[1]
                    hx = steps.magnetic_x(e)
                    coef = scales[part] * conductivity(p)
                    for comp in range(1 if p == depth else 0, 3):
                        curl = steps.curl_back(comp, hx, hy, hz, before[part])
                        into[part, comp, p + 1] = e[comp] - relax * curl + coef * ref[1 - part, comp, p + 1]
                    if p < 0:
                        hy, hz = hy + received(low, part, k), hz + received(low, part, k + 1)
                    before[part] = hy, hz
            point.add_to(into, 0, planes_swept, 1, lambda part, comp: scalar_ref[weights_at + part * 3 + comp])

        sweep(one_, two_, -1, depth + 1, 2)
        sweep(two_, one_, 0, depth, 4)

        for p in range(depth):
            row_re = row_im = None
            for comp in range(3):
                re, im = one_[0, comp, p + 1], one_[1, comp, p + 1]
                field_re, field_im = field_ref[s, 0, comp, p], field_ref[s, 1, comp, p]
                add_re, add_im = field_re * re - field_im * im, field_re * im + field_im * re
                row_re, row_im = (add_re, add_im) if comp == 0 else (row_re + add_re, row_im + add_im)
            coef = angular * held_ref[p]
            for part, value in enumerate((row_re, row_im)):
                value = (coef * value).astype(rows_ref.dtype)
                rows_ref[s, part, p] = value
                if p >= depth - REACH:
                    sent[high, s, part, p - depth + REACH] = value
                if p < REACH:
                    sent[low, s, part, p] = value
        return 0

    lax.fori_loop(0, count, one_source, 0)
    far_ref[...] = sent[0]
    near_ref[...] = sent[1]


def in_plane(steps, f):
    total = (steps.after_y(f) + steps.before_y(f)) + (steps.after_z(f) + steps.before_z(f))
    return (1.0 - 6.0 * KAPPA) * f + KAPPA * total


def smooth_kernel(planes, rows_ref, alone_ref):
    count, _, depth, height, breadth = rows_ref.shape
    steps = Steps(height, breadth)
    first = lax.axis_index("space") * depth
    below = jnp.where(first > 0, F32(KAPPA), F32(0.0))
    above = jnp.where(first + depth < planes, F32(KAPPA), F32(0.0))

    def one_row(s, part):
        value = [rows_ref[s, part, p].astype(F32) for p in range(depth)]
        once = []
        for p in range(depth):
            beside = [value[q] for q in (p - 1, p + 1) if 0 <= q < depth]
            once.append(in_plane(steps, value[p]) + KAPPA * functools.reduce(jnp.add, beside))
        once = [below * value[0]] + once + [above * value[-1]]
        for p in range(depth):
            alone_ref[s, part, p] = in_plane(steps, once[p + 1]) + KAPPA * (once[p] + once[p + 2])

    def one_source(s, _):
        for part in range(2):
            one_row(s, part)
        return 0

    lax.fori_loop(0, count, one_source, 0)


def block_kernel(cells, rows_ref, alone_ref, far_in, near_in, all_ref, smooth_ref, block_ref, got, rounded, sums, sem):
    count, _, depth, height, breadth = rows_ref.shape
    ranks = all_ref.shape[0]
    steps = Steps(height, breadth)
    many = ranks * count * 2
    index = lax.axis_index("space")
    receive(got, far_in, near_in, (index == 0) | (index == lax.axis_size("space") - 1))
    odd = index & 1
    low, high = odd, 1 - odd

    def one_row(s, part):
        value = [alone_ref[s, part, p] for p in range(depth)]
        for side, nearest, order in ((low, REACH - 1, 1), (high, 0, -1)):
            close = got[side, s, part, nearest].astype(F32)
            beyond = got[side, s, part, REACH - 1 - nearest].astype(F32)
            end = 0 if order > 0 else depth - 1
            value[end] = value[end] + (2.0 * KAPPA * in_plane(steps, close) + KAPPA * KAPPA * beyond)
            value[end + order] = value[end + order] + KAPPA * KAPPA * close
        for p in range(depth):
            rounded[s, part, p] = value[p].astype(rounded.dtype)

    def one_source(s, _):
        for part in range(2):
            one_row(s, part)
        return 0

    lax.fori_loop(0, count, one_source, 0)
    out = pltpu.make_async_copy(rounded, smooth_ref, sem)
    out.start()

    sums[...] = jnp.zeros_like(sums)

    def one_plane(p, _):
        mine = [rounded[a // 2, a % 2, p].astype(F32) for a in range(2 * count)]
        for b in range(many):
            r, t = divmod(b // 2, count)
            other = all_ref[r, t, b % 2, p].astype(F32)
            for a in range(2 * count):
                prod = mine[a] * other
                total = prod[:8]
                for k in range(8, height, 8):
                    total = total + prod[k : k + 8]
                sums[a * many + b] = sums[a * many + b] + total
        return 0

    lax.fori_loop(0, depth, one_plane, 0)
    half = jnp.bfloat16
    ones = jnp.ones((breadth, breadth), half)
    for a in range(2 * count):
        table = sums[a * many : (a + 1) * many].reshape(many * 8, breadth)
        coarse = table.astype(half)
        fine = (table - coarse.astype(F32)).astype(half)
        table = jnp.dot(coarse, ones, preferred_element_type=F32) + jnp.dot(fine, ones, preferred_element_type=F32)
        line = None
        for b in range(many):
            add = jnp.where(steps.lane[:8] == b, table[b * 8 : b * 8 + 8], 0.0)
            line = add if line is None else line + add
        line = jnp.sum(line, axis=0, keepdims=True) * (1.0 / cells)
        for peer in range(block_ref.shape[0]):
            block_ref[peer, a : a + 1, :] = line[:, :many]
    out.wait()


def in_hbm(x):
    return pltpu.with_memory_space_constraint(x, pltpu.HBM)


def shards(conductivity, background, warm_start, data_weight, recv_cell, src_group, group_freq):
    count = warm_start.shape[0]
    depth, height, breadth = conductivity.shape
    plane = (height, breadth)
    peers = lax.axis_size("space")
    ranks = lax.axis_size("rx")
    cells = depth * height * breadth * peers
    half = jnp.bfloat16
    integers = jnp.concatenate([recv_cell, src_group, group_freq]).astype(F32)
    scalars = jnp.concatenate([integers, data_weight.reshape(-1)])
    assert peers % 2 == 0
    far = [(i, (i + 1) % peers) for i in range(1, peers, 2)]
    near = [(i, i + 1) for i in range(0, peers, 2)]
    far, near = [pairs + [(j, i) for i, j in pairs] for pairs in (far, near)]
    shape = jax.ShapeDtypeStruct

    message = shape((2 * count * SENT + 1,) + plane, half)
    to_far, to_near, own, edge, held, field = pl.pallas_call(
        first_kernel,
        out_shape=(
            message,
            message,
            shape(warm_start.shape, F32),
            shape((count, 2, 4) + plane, F32),
            shape(conductivity.shape, F32),
            shape((count,) + background.shape[1:], F32),
        ),
        in_specs=[HBM] * 7,
        out_specs=(FULL,) * 6,
        scratch_shapes=[
            pltpu.VMEM(warm_start.shape, F32),
            pltpu.SMEM(data_weight.shape, F32),
            pltpu.SMEM(recv_cell.shape, jnp.int32),
            pltpu.SMEM(src_group.shape, jnp.int32),
            pltpu.SMEM(group_freq.shape, jnp.int32),
            pltpu.VMEM((2,) + message.shape, half),
            pltpu.SemaphoreType.DMA((5 + 2 * count,)),
        ],
        compiler_params=KERNEL,
        name="first_sweep",
    )(*[in_hbm(x) for x in (warm_start, conductivity, background, data_weight, recv_cell, src_group, group_freq)])
    from_far = lax.ppermute(to_far, "space", far)
    from_near = lax.ppermute(to_near, "space", near)

    rows_of = shape((count, 2, depth) + plane, half)
    ends_of = shape((count, 2, REACH) + plane, half)
    rows, to_far, to_near = pl.pallas_call(
        functools.partial(sweep_kernel, peers * depth),
        out_shape=(rows_of, ends_of, ends_of),
        in_specs=[SCALARS] + [FULL] * 6,
        out_specs=(FULL,) * 3,
        scratch_shapes=[
            pltpu.VMEM((2, 3, depth + 2) + plane, F32),
            pltpu.VMEM((2, 3, depth + 2) + plane, F32),
            pltpu.VMEM((2,) + message.shape, half),
            pltpu.VMEM((2,) + ends_of.shape, half),
        ],
        compiler_params=KERNEL,
        name="sweeps",
    )(scalars, own, edge, held, field, from_far, from_near)
    from_far = lax.ppermute(to_far, "space", far)
    from_near = lax.ppermute(to_near, "space", near)
    every = lax.all_gather(rows, "rx", axis=0)

    many = 2 * count * ranks
    alone = pl.pallas_call(
        functools.partial(smooth_kernel, peers * depth),
        out_shape=shape(rows_of.shape, F32),
        in_specs=[FULL],
        out_specs=FULL,
        compiler_params=KERNEL,
        name="smooth",
    )(rows)
    smoothed, partial_block = pl.pallas_call(
        functools.partial(block_kernel, cells),
        out_shape=(rows_of, shape((peers, 2 * count, many), F32)),
        in_specs=[FULL] * 5,
        out_specs=(HBM, FULL),
        scratch_shapes=[
            pltpu.VMEM((2,) + ends_of.shape, half),
            pltpu.VMEM(rows_of.shape, half),
            pltpu.VMEM((2 * count * many, 8, breadth), F32),
            pltpu.SemaphoreType.DMA,
        ],
        compiler_params=KERNEL,
        name="block",
    )(rows, alone, from_far, from_near, every)
    backwards = [list(range(peers - 1, -1, -1))]
    pieces = lax.all_to_all(partial_block, "space", 0, 0, axis_index_groups=backwards)
    return (jnp.sum(pieces, axis=0), smoothed)


def solution(mesh):
    in_specs = (
        P("space", None, None),
        P(None, None, None, "space", None, None),
        P("rx", None, None, "space", None, None),
        P("rx", None, None),
        P("rx"),
        P("rx"),
        P(),
    )
    out_specs = (P("rx", None), P("rx", None, "space", None, None))
    return jax.shard_map(shards, mesh=mesh, in_specs=in_specs, out_specs=out_specs, check_vma=False)
```

```python
import functools

import jax
import jax.numpy as jnp
from jax import lax
from jax.experimental import pallas as pl
from jax.experimental.pallas import tpu as pltpu
from jax.sharding import PartitionSpec as P

SENT = 6
RELAX = 0.2
KAPPA = 0.1
REACH = 2
FULL = pl.BlockSpec(memory_space=pltpu.VMEM)
HBM = pl.BlockSpec(memory_space=pltpu.HBM)
SCALARS = pl.BlockSpec(memory_space=pltpu.SMEM)
KERNEL = pltpu.CompilerParams(vmem_limit_bytes=8 * 2**20)
F32 = jnp.float32


class Steps:
    def __init__(self, height, breadth):
        self.height, self.breadth = height, breadth
        self.sub = lax.broadcasted_iota(jnp.int32, (8, breadth), 0)
        self.lane = lax.broadcasted_iota(jnp.int32, (height, breadth), 1)

    def after_y(self, f):
        f = pltpu.roll(f, self.height - 1, 0)
        return jnp.concatenate([f[:-8], jnp.where(self.sub < 7, f[-8:], 0.0)], axis=0)

    def before_y(self, f):
        f = pltpu.roll(f, 1, 0)
        return jnp.concatenate([jnp.where(self.sub > 0, f[:8], 0.0), f[8:]], axis=0)

    def after_z(self, f):
        return jnp.where(self.lane < self.breadth - 1, pltpu.roll(f, self.breadth - 1, 1), 0.0)

    def before_z(self, f):
        return jnp.where(self.lane > 0, pltpu.roll(f, 1, 1), 0.0)

    def up_y(self, f):
        return self.after_y(f) - f

    def up_z(self, f):
        return self.after_z(f) - f

    def down_y(self, f):
        return f - self.before_y(f)

    def down_z(self, f):
        return f - self.before_z(f)

    def magnetic_yz(self, e, e_next):
        ex, ey, ez = e
        if e_next is None:
            return self.up_z(ex) + ez, -ey - self.up_y(ex)
        return self.up_z(ex) - (e_next[2] - ez), (e_next[1] - ey) - self.up_y(ex)

    def magnetic_x(self, e):
        return self.up_y(e[2]) - self.up_z(e[1])

    def curl_back(self, comp, hx, hy, hz, before):
        if comp == 0:
            return self.down_y(hz) - self.down_z(hy)
        if comp == 1:
            return self.down_z(hx) - (hz - before[1])
        return (hy - before[0]) - self.down_y(hx)


def angular_of(freq):
    angular = F32(0.25)
    for bit, factor in ((1, 1.25), (2, 1.25**2), (4, 1.25**4)):
        angular = angular * jnp.where((freq & bit) != 0, F32(factor), F32(1.0))
    return angular


def split(number, size):
    if size & (size - 1):
        return number // size, number % size
    return number >> (size.bit_length() - 1), number & (size - 1)


class Point:
    def __init__(self, cell, first, steps):
        plane, inner = split(cell, steps.height * steps.breadth)
        row, lane = split(inner, steps.breadth)
        block, sub = split(row, 8)
        self.plane = plane - first
        self.rows = pl.ds(pl.multiple_of(block * 8, 8), 8)
        self.row, self.sub, self.lane, self.steps = row, sub, lane, steps

    def add_to(self, ref, low, high, shift, weight):
        reached = (self.plane >= low) & (self.plane < high)
        here = (self.steps.sub == self.sub) & (self.steps.lane[:8] == self.lane)
        amount = jnp.where(here, jnp.where(reached, F32(RELAX), F32(0.0)), 0.0)
        plane = jnp.clip(self.plane, low, high - 1) + shift
        for part in range(2):
            for comp in range(3):
                at = (part, comp, plane, self.rows)
                ref[at] = ref[at] + amount * weight(part, comp)


def receive(got, far_in, near_in, at_end):
    got[1] = near_in[...]

    @pl.when(at_end)
    def _():
        got[0] = jnp.zeros(far_in.shape, far_in.dtype)

    @pl.when(jnp.logical_not(at_end))
    def _():
        got[0] = far_in[...]


def first_kernel(
    start_ref, cond_ref, back_ref, weight_ref, cell_ref, group_ref, freq_ref,
    far_ref, near_ref, own_ref, edge_ref, held_ref, field_ref,
    raw, weight, cell, group, freq, sent, sems,
):
    count, _, _, depth, height, breadth = start_ref.shape
    pairs = ((group_ref, group), (freq_ref, freq), (cell_ref, cell), (weight_ref, weight), (cond_ref, held_ref))
    copies = [pltpu.make_async_copy(a, b, sems.at[k]) for k, (a, b) in enumerate(pairs)]

    def start_of(s):
        return pltpu.make_async_copy(start_ref.at[s], raw.at[s], sems.at[len(pairs) + s])

    for copy in copies + [start_of(s) for s in range(count)]:
        copy.start()
    copies[0].wait()
    fields = [
        pltpu.make_async_copy(back_ref.at[group[s]], field_ref.at[s], sems.at[len(pairs) + count + s])
        for s in range(count)
    ]
    for copy in fields:
        copy.start()
    for copy in copies[1:]:
        copy.wait()
    steps = Steps(height, breadth)
    half = far_ref.dtype
    index = lax.axis_index("space")
    first = index * depth
    down = index & 1
    up = 1 - down
    row = lax.broadcasted_iota(jnp.int32, (height, breadth), 0)
    last = depth - 1
    sent[up, 2 * count * SENT] = held_ref[last].astype(half)
    sent[down, 2 * count * SENT] = held_ref[0].astype(half)

    def one_source(s, _):
        start_of(s).wait()
        scale = RELAX * angular_of(freq[group[s]])
        scales = scale, -scale
        point = Point(cell[s], first, steps)
        base = 2 * s * SENT
        before = []
        for part in range(2):
            ey, ez = raw[s, part, 1, 0], raw[s, part, 2, 0]
            for k, f in enumerate((ey, ez)):
                sent[down, base + part * SENT + k] = f.astype(half)
                edge_ref[s, part, k] = f
            before.append((-ez, ey))
        for p in range(depth):
            for part in range(2):
                e = [raw[s, part, comp, p] for comp in range(3)]
                e_next = None
                if p < last:
                    e_next = [None if comp == 0 else raw[s, part, comp, p + 1] for comp in range(3)]
                hy, hz = steps.magnetic_yz(e, e_next)
                if p == last:
                    for k, f in enumerate((hy, hz)):
                        sent[up, base + part * SENT + k] = f.astype(half)
                        edge_ref[s, part, 2 + k] = f
                hx = steps.magnetic_x(e)
                coef = scales[part] * held_ref[p]
                for comp in range(3):
                    curl = steps.curl_back(comp, hx, hy, hz, before[part])
                    own_ref[s, part, comp, p] = e[comp] - RELAX * curl + coef * raw[s, 1 - part, comp, p]
                before[part] = hy, hz
        point.add_to(own_ref.at[s], 0, depth, 0, lambda part, comp: weight[s, part, comp])

        at_last = jnp.where(point.plane == last, F32(1.0), F32(0.0))
        here = jnp.where((row == point.row) & (steps.lane == point.lane), RELAX * at_last, 0.0)
        for part in range(2):
            ex, ey, ez = [own_ref[s, part, comp, 0] for comp in range(3)]
            hy, hz = steps.up_z(ex) - own_ref[s, part, 2, 1], own_ref[s, part, 1, 1] - steps.up_y(ex)
            for k, f in enumerate((ey, ez, hy, hz)):
                sent[down, base + part * SENT + 2 + k] = f.astype(half)
            e = [own_ref[s, part, comp, last] for comp in range(3)]
            behind = steps.magnetic_yz([own_ref[s, part, comp, last - 1] for comp in range(3)], e)
            hy, hz = steps.magnetic_yz(e, None)
            hx = steps.magnetic_x(e)
            coef = scales[part] * held_ref[last]
            after = []
            for comp in range(3):
                curl = steps.curl_back(comp, hx, hy, hz, behind)
                value = e[comp] - RELAX * curl + coef * own_ref[s, 1 - part, comp, last]
                after.append(value + here * weight[s, part, comp])
            for k, f in enumerate((hy, hz) + steps.magnetic_yz(after, None)):
                sent[up, base + part * SENT + 2 + k] = f.astype(half)
        return 0

    lax.fori_loop(0, count, one_source, 0)
    far_ref[...] = sent[0]
    near_ref[...] = sent[1]
    for copy in fields:
        copy.wait()


def sweep_kernel(
    planes, scalar_ref, own_ref, edge_ref, held_ref, field_ref, far_in, near_in, rows_ref, far_ref, near_ref, one_, two_, got, sent,
):
    count, _, _, depth, height, breadth = own_ref.shape
    steps = Steps(height, breadth)
    index = lax.axis_index("space")
    first = index * depth
    relax_low = jnp.where(first > 0, F32(RELAX), F32(0.0))
    relax_high = jnp.where(first + depth < planes, F32(RELAX), F32(0.0))
    odd = index & 1
    low, high = odd, 1 - odd
    receive(got, far_in, near_in, (first == 0) | (first + depth == planes))

    def conductivity(p):
        if p < 0:
            return got[low, 2 * count * SENT].astype(F32)
        if p >= depth:
            return got[high, 2 * count * SENT].astype(F32)
        return held_ref[p]

    def one_source(s, _):
        group = scalar_ref[count + s].astype(jnp.int32)
        angular = angular_of(scalar_ref[2 * count + group].astype(jnp.int32))
        scales = RELAX * angular, -RELAX * angular
        point = Point(scalar_ref[s].astype(jnp.int32), first, steps)
        weights_at = scalar_ref.shape[0] - 6 * count + 6 * s

        def received(side, part, k):
            return got[side, (2 * s + part) * SENT + k].astype(F32)

        for part in range(2):
            ey, ez, ly, lz = [edge_ref[s, part, k] for k in range(4)]
            one_[part, 0, 0] = -relax_low * (steps.down_y(ey) + steps.down_z(ez))
            one_[part, 1, 0] = relax_low * ey
            one_[part, 2, 0] = relax_low * ez
            e = [own_ref[s, part, comp, 0] for comp in range(3)]
            one_[part, 0, 1] = e[0]
            one_[part, 1, 1] = e[1] - RELAX * received(low, part, 1)
            one_[part, 2, 1] = e[2] + RELAX * received(low, part, 0)
            for p in range(1, depth - 1):
                for comp in range(3):
                    one_[part, comp, p + 1] = own_ref[s, part, comp, p]
            e = [own_ref[s, part, comp, depth - 1] for comp in range(3)]
            high_y, high_z = received(high, part, 0), received(high, part, 1)
            one_[part, 0, depth] = e[0] - RELAX * (steps.down_y(high_y) + steps.down_z(high_z))
            one_[part, 1, depth] = e[1] + RELAX * high_y
            one_[part, 2, depth] = e[2] + RELAX * high_z
            two_[part, 0, depth + 1] = jnp.zeros((height, breadth), F32)
            one_[part, 1, depth + 1] = received(high, part, 2) - relax_high * lz
            one_[part, 2, depth + 1] = received(high, part, 3) + relax_high * ly

        def sweep(ref, into, low_plane, planes_swept, k):
            if low_plane < 0:
                before = [(-ref[part, 2, 0], ref[part, 1, 0]) for part in range(2)]
            else:
                before = []
                for part in range(2):
                    e = [ref[part, comp, 0] for comp in range(3)]
                    hy, hz = steps.magnetic_yz(e, [None, ref[part, 1, 1], ref[part, 2, 1]])
                    before.append((hy + received(low, part, k), hz + received(low, part, k + 1)))
            for p in range(low_plane, planes_swept):
                relax = relax_low if p < 0 else relax_high if p == depth else F32(RELAX)
                for part in range(2):
                    e = [ref[part, comp, p + 1] if comp or p < depth else None for comp in range(3)]
                    if p < depth:
                        e_next = [None if comp == 0 else ref[part, comp, p + 2] for comp in range(3)]
                        hy, hz = steps.magnetic_yz(e, e_next)
                    else:
                        hy, hz = received(high, part, 4) + e[2], received(high, part, 5) - e[1]
                    hx = steps.magnetic_x(e)
                    coef = scales[part] * conductivity(p)
                    for comp in range(1 if p == depth else 0, 3):
                        curl = steps.curl_back(comp, hx, hy, hz, before[part])
                        into[part, comp, p + 1] = e[comp] - relax * curl + coef * ref[1 - part, comp, p + 1]
                    if p < 0:
                        hy, hz = hy + received(low, part, k), hz + received(low, part, k + 1)
                    before[part] = hy, hz
            point.add_to(into, 0, planes_swept, 1, lambda part, comp: scalar_ref[weights_at + part * 3 + comp])

        sweep(one_, two_, -1, depth + 1, 2)
        sweep(two_, one_, 0, depth, 4)

        for p in range(depth):
            row_re = row_im = None
            for comp in range(3):
                re, im = one_[0, comp, p + 1], one_[1, comp, p + 1]
                field_re, field_im = field_ref[s, 0, comp, p], field_ref[s, 1, comp, p]
                add_re, add_im = field_re * re - field_im * im, field_re * im + field_im * re
                row_re, row_im = (add_re, add_im) if comp == 0 else (row_re + add_re, row_im + add_im)
            coef = angular * held_ref[p]
            for part, value in enumerate((row_re, row_im)):
                value = (coef * value).astype(rows_ref.dtype)
                rows_ref[s, part, p] = value
                if p >= depth - REACH:
                    sent[high, s, part, p - depth + REACH] = value
                if p < REACH:
                    sent[low, s, part, p] = value
        return 0

    lax.fori_loop(0, count, one_source, 0)
    far_ref[...] = sent[0]
    near_ref[...] = sent[1]


def in_plane(steps, f):
    total = (steps.after_y(f) + steps.before_y(f)) + (steps.after_z(f) + steps.before_z(f))
    return (1.0 - 6.0 * KAPPA) * f + KAPPA * total


def smooth_kernel(planes, rows_ref, alone_ref):
    count, _, depth, height, breadth = rows_ref.shape
    steps = Steps(height, breadth)
    first = lax.axis_index("space") * depth
    below = jnp.where(first > 0, F32(KAPPA), F32(0.0))
    above = jnp.where(first + depth < planes, F32(KAPPA), F32(0.0))

    def one_row(s, part):
        value = [rows_ref[s, part, p].astype(F32) for p in range(depth)]
        once = []
        for p in range(depth):
            beside = [value[q] for q in (p - 1, p + 1) if 0 <= q < depth]
            once.append(in_plane(steps, value[p]) + KAPPA * functools.reduce(jnp.add, beside))
        once = [below * value[0]] + once + [above * value[-1]]
        for p in range(depth):
            alone_ref[s, part, p] = in_plane(steps, once[p + 1]) + KAPPA * (once[p] + once[p + 2])

    def one_source(s, _):
        for part in range(2):
            one_row(s, part)
        return 0

    lax.fori_loop(0, count, one_source, 0)


def block_kernel(cells, rows_ref, alone_ref, far_in, near_in, all_ref, smooth_ref, block_ref, got, rounded, sums, sem):
    count, _, depth, height, breadth = rows_ref.shape
    ranks = all_ref.shape[0]
    steps = Steps(height, breadth)
    many = ranks * count * 2
    index = lax.axis_index("space")
    receive(got, far_in, near_in, (index == 0) | (index == lax.axis_size("space") - 1))
    odd = index & 1
    low, high = odd, 1 - odd

    def one_row(s, part):
        value = [alone_ref[s, part, p] for p in range(depth)]
        for side, nearest, order in ((low, REACH - 1, 1), (high, 0, -1)):
            close = got[side, s, part, nearest].astype(F32)
            beyond = got[side, s, part, REACH - 1 - nearest].astype(F32)
            end = 0 if order > 0 else depth - 1
            value[end] = value[end] + (2.0 * KAPPA * in_plane(steps, close) + KAPPA * KAPPA * beyond)
            value[end + order] = value[end + order] + KAPPA * KAPPA * close
        for p in range(depth):
            rounded[s, part, p] = value[p].astype(rounded.dtype)

    def one_source(s, _):
        for part in range(2):
            one_row(s, part)
        return 0

    lax.fori_loop(0, count, one_source, 0)
    out = pltpu.make_async_copy(rounded, smooth_ref, sem)
    out.start()

    sums[...] = jnp.zeros_like(sums)

    def one_plane(p, _):
        mine = [rounded[a // 2, a % 2, p].astype(F32) for a in range(2 * count)]
        for b in range(many):
            r, t = divmod(b // 2, count)
            other = all_ref[r, t, b % 2, p].astype(F32)
            for a in range(2 * count):
                prod = mine[a] * other
                total = prod[:8]
                for k in range(8, height, 8):
                    total = total + prod[k : k + 8]
                sums[a * many + b] = sums[a * many + b] + total
        return 0

    lax.fori_loop(0, depth, one_plane, 0)
    half = jnp.bfloat16
    ones = jnp.ones((breadth, breadth), half)
    for a in range(2 * count):
        table = sums[a * many : (a + 1) * many].reshape(many * 8, breadth)
        coarse = table.astype(half)
        fine = (table - coarse.astype(F32)).astype(half)
        table = jnp.dot(coarse, ones, preferred_element_type=F32) + jnp.dot(fine, ones, preferred_element_type=F32)
        line = None
        for b in range(many):
            add = jnp.where(steps.lane[:8] == b, table[b * 8 : b * 8 + 8], 0.0)
            line = add if line is None else line + add
        line = jnp.sum(line, axis=0, keepdims=True) * (1.0 / cells)
        for peer in range(block_ref.shape[0]):
            block_ref[peer, a : a + 1, :] = line[:, :many]
    out.wait()


def in_hbm(x):
    return pltpu.with_memory_space_constraint(x, pltpu.HBM)


def shards(conductivity, background, warm_start, data_weight, recv_cell, src_group, group_freq):
    count = warm_start.shape[0]
    depth, height, breadth = conductivity.shape
    plane = (height, breadth)
    peers = lax.axis_size("space")
    ranks = lax.axis_size("rx")
    cells = depth * height * breadth * peers
    half = jnp.bfloat16
    integers = jnp.concatenate([recv_cell, src_group, group_freq]).astype(F32)
    scalars = jnp.concatenate([integers, data_weight.reshape(-1)])
    assert peers % 2 == 0 and ranks % 2 == 0
    both = ("rx", "space")
    far = [(r * peers + i, r * peers + i + 1) for r in range(ranks) for i in range(1, peers - 1, 2)]
    far += [(r * peers + i, (r + 1) * peers + i) for r in range(0, ranks, 2) for i in (0, peers - 1)]
    near = [(i, i + 1) for i in range(0, peers, 2)]
    far, near = [pairs + [(j, i) for i, j in pairs] for pairs in (far, near)]
    shape = jax.ShapeDtypeStruct

    message = shape((2 * count * SENT + 1,) + plane, half)
    to_far, to_near, own, edge, held, field = pl.pallas_call(
        first_kernel,
        out_shape=(
            message,
            message,
            shape(warm_start.shape, F32),
            shape((count, 2, 4) + plane, F32),
            shape(conductivity.shape, F32),
            shape((count,) + background.shape[1:], F32),
        ),
        in_specs=[HBM] * 7,
        out_specs=(FULL,) * 6,
        scratch_shapes=[
            pltpu.VMEM(warm_start.shape, F32),
            pltpu.SMEM(data_weight.shape, F32),
            pltpu.SMEM(recv_cell.shape, jnp.int32),
            pltpu.SMEM(src_group.shape, jnp.int32),
            pltpu.SMEM(group_freq.shape, jnp.int32),
            pltpu.VMEM((2,) + message.shape, half),
            pltpu.SemaphoreType.DMA((5 + 2 * count,)),
        ],
        compiler_params=KERNEL,
        name="first_sweep",
    )(*[in_hbm(x) for x in (warm_start, conductivity, background, data_weight, recv_cell, src_group, group_freq)])
    from_far = lax.ppermute(to_far, both, far)
    from_near = lax.ppermute(to_near, "space", near)

    rows_of = shape((count, 2, depth) + plane, half)
    ends_of = shape((count, 2, REACH) + plane, half)
    rows, to_far, to_near = pl.pallas_call(
        functools.partial(sweep_kernel, peers * depth),
        out_shape=(rows_of, ends_of, ends_of),
        in_specs=[SCALARS] + [FULL] * 6,
        out_specs=(FULL,) * 3,
        scratch_shapes=[
            pltpu.VMEM((2, 3, depth + 2) + plane, F32),
            pltpu.VMEM((2, 3, depth + 2) + plane, F32),
            pltpu.VMEM((2,) + message.shape, half),
            pltpu.VMEM((2,) + ends_of.shape, half),
        ],
        compiler_params=KERNEL,
        name="sweeps",
    )(scalars, own, edge, held, field, from_far, from_near)
    from_far = lax.ppermute(to_far, both, far)
    from_near = lax.ppermute(to_near, "space", near)
    every = lax.all_gather(rows, "rx", axis=0)

    many = 2 * count * ranks
    alone = pl.pallas_call(
        functools.partial(smooth_kernel, peers * depth),
        out_shape=shape(rows_of.shape, F32),
        in_specs=[FULL],
        out_specs=FULL,
        compiler_params=KERNEL,
        name="smooth",
    )(rows)
    smoothed, partial_block = pl.pallas_call(
        functools.partial(block_kernel, cells),
        out_shape=(rows_of, shape((peers, 2 * count, many), F32)),
        in_specs=[FULL] * 5,
        out_specs=(HBM, FULL),
        scratch_shapes=[
            pltpu.VMEM((2,) + ends_of.shape, half),
            pltpu.VMEM(rows_of.shape, half),
            pltpu.VMEM((2 * count * many, 8, breadth), F32),
            pltpu.SemaphoreType.DMA,
        ],
        compiler_params=KERNEL,
        name="block",
    )(rows, alone, from_far, from_near, every)
    backwards = [list(range(peers - 1, -1, -1))]
    pieces = lax.all_to_all(partial_block, "space", 0, 0, axis_index_groups=backwards)
    return (jnp.sum(pieces, axis=0), smoothed)


def solution(mesh):
    in_specs = (
        P("space", None, None),
        P(None, None, None, "space", None, None),
        P("rx", None, None, "space", None, None),
        P("rx", None, None),
        P("rx"),
        P("rx"),
        P(),
    )
    out_specs = (P("rx", None), P("rx", None, "space", None, None))
    return jax.shard_map(shards, mesh=mesh, in_specs=in_specs, out_specs=out_specs, check_vma=False)
```

```python
import functools

import jax
import jax.numpy as jnp
from jax import lax
from jax.experimental import pallas as pl
from jax.experimental.pallas import tpu as pltpu
from jax.sharding import PartitionSpec as P

SENT = 6
RELAX = 0.2
KAPPA = 0.1
REACH = 2
FULL = pl.BlockSpec(memory_space=pltpu.VMEM)
HBM = pl.BlockSpec(memory_space=pltpu.HBM)
SCALARS = pl.BlockSpec(memory_space=pltpu.SMEM)
KERNEL = pltpu.CompilerParams(vmem_limit_bytes=8 * 2**20)
F32 = jnp.float32


class Steps:
    def __init__(self, height, breadth):
        self.height, self.breadth = height, breadth
        self.sub = lax.broadcasted_iota(jnp.int32, (8, breadth), 0)
        self.lane = lax.broadcasted_iota(jnp.int32, (height, breadth), 1)

    def after_y(self, f):
        f = pltpu.roll(f, self.height - 1, 0)
        return jnp.concatenate([f[:-8], jnp.where(self.sub < 7, f[-8:], 0.0)], axis=0)

    def before_y(self, f):
        f = pltpu.roll(f, 1, 0)
        return jnp.concatenate([jnp.where(self.sub > 0, f[:8], 0.0), f[8:]], axis=0)

    def after_z(self, f):
        return jnp.where(self.lane < self.breadth - 1, pltpu.roll(f, self.breadth - 1, 1), 0.0)

    def before_z(self, f):
        return jnp.where(self.lane > 0, pltpu.roll(f, 1, 1), 0.0)

    def up_y(self, f):
        return self.after_y(f) - f

    def up_z(self, f):
        return self.after_z(f) - f

    def down_y(self, f):
        return f - self.before_y(f)

    def down_z(self, f):
        return f - self.before_z(f)

    def magnetic_yz(self, e, e_next):
        ex, ey, ez = e
        if e_next is None:
            return self.up_z(ex) + ez, -ey - self.up_y(ex)
        return self.up_z(ex) - (e_next[2] - ez), (e_next[1] - ey) - self.up_y(ex)

    def magnetic_x(self, e):
        return self.up_y(e[2]) - self.up_z(e[1])

    def curl_back(self, comp, hx, hy, hz, before):
        if comp == 0:
            return self.down_y(hz) - self.down_z(hy)
        if comp == 1:
            return self.down_z(hx) - (hz - before[1])
        return (hy - before[0]) - self.down_y(hx)


def angular_of(freq):
    angular = F32(0.25)
    for bit, factor in ((1, 1.25), (2, 1.25**2), (4, 1.25**4)):
        angular = angular * jnp.where((freq & bit) != 0, F32(factor), F32(1.0))
    return angular


def split(number, size):
    if size & (size - 1):
        return number // size, number % size
    return number >> (size.bit_length() - 1), number & (size - 1)


class Point:
    def __init__(self, cell, first, steps):
        plane, inner = split(cell, steps.height * steps.breadth)
        row, lane = split(inner, steps.breadth)
        block, sub = split(row, 8)
        self.plane = plane - first
        self.rows = pl.ds(pl.multiple_of(block * 8, 8), 8)
        self.row, self.sub, self.lane, self.steps = row, sub, lane, steps

    def add_to(self, ref, low, high, shift, weight):
        reached = (self.plane >= low) & (self.plane < high)
        here = (self.steps.sub == self.sub) & (self.steps.lane[:8] == self.lane)
        amount = jnp.where(here, jnp.where(reached, F32(RELAX), F32(0.0)), 0.0)
        plane = jnp.clip(self.plane, low, high - 1) + shift
        for part in range(2):
            for comp in range(3):
                at = (part, comp, plane, self.rows)
                ref[at] = ref[at] + amount * weight(part, comp)


def receive(got, far_in, near_in, at_end):
    got[1] = near_in[: got.shape[1]]

    @pl.when(at_end)
    def _():
        got[0] = jnp.zeros(got.shape[1:], got.dtype)

    @pl.when(jnp.logical_not(at_end))
    def _():
        got[0] = far_in[: got.shape[1]]


def first_kernel(s, planes_ref, *refs):
    if s == 0:
        cond_ref, back_ref, weight_ref, cell_ref, group_ref, freq_ref = refs[:6]
        far_ref, near_ref, own_ref, edge_ref, held_ref, later_ref, field_ref = refs[6:13]
        raw, weight_of, cell, group, freq, sent, sems = refs[13:]
        count = planes_ref.shape[0]
        small = ((group_ref, group), (freq_ref, freq), (cell_ref, cell), (weight_ref, weight_of), (cond_ref, held_ref))
        copies = [pltpu.make_async_copy(planes_ref.at[0], raw, sems.at[0])]
        copies += [pltpu.make_async_copy(a, b, sems.at[k + 1]) for k, (a, b) in enumerate(small)]
        others = [pltpu.make_async_copy(planes_ref.at[pl.ds(1, count - 1)], later_ref, sems.at[len(copies)])]
        for copy in copies + others:
            copy.start()
        copies[1].wait()
        for t in range(count):
            field = pltpu.make_async_copy(back_ref.at[group[t]], field_ref.at[t], sems.at[len(copies) + 1 + t])
            field.start()
            others.append(field)
        for copy in copies[:1] + copies[2:]:
            copy.wait()
        angular = angular_of(freq[group[s]])
        cell_at = cell[s]

        def weight(part, comp):
            return weight_of[s, part, comp]
    else:
        scalar_ref, held_ref, far_ref, near_ref, own_ref, edge_ref, sent = refs
        raw = planes_ref.at[s - 1]
        count = planes_ref.shape[0] + 1
        others = []
        group = scalar_ref[count + s].astype(jnp.int32)
        angular = angular_of(scalar_ref[2 * count + group].astype(jnp.int32))
        cell_at = scalar_ref[s].astype(jnp.int32)
        weights_at = scalar_ref.shape[0] - 6 * count + 6 * s

        def weight(part, comp):
            return scalar_ref[weights_at + part * 3 + comp]

    depth, height, breadth = held_ref.shape
    steps = Steps(height, breadth)
    half = sent.dtype
    index = lax.axis_index("space")
    first = index * depth
    down = index & 1
    up = 1 - down
    last = depth - 1
    scales = RELAX * angular, -RELAX * angular
    point = Point(cell_at, first, steps)
    if s == 0:
        sent[up, 2 * SENT] = held_ref[last].astype(half)
        sent[down, 2 * SENT] = held_ref[0].astype(half)

    before = []
    for part in range(2):
        ey, ez = raw[part, 1, 0], raw[part, 2, 0]
        for k, f in enumerate((ey, ez)):
            sent[down, part * SENT + k] = f.astype(half)
            edge_ref[part, k] = f
        before.append((-ez, ey))
    for p in range(depth):
        for part in range(2):
            e = [raw[part, comp, p] for comp in range(3)]
            e_next = [None if comp == 0 else raw[part, comp, p + 1] for comp in range(3)] if p < last else None
            hy, hz = steps.magnetic_yz(e, e_next)
            if p == last:
                for k, f in enumerate((hy, hz)):
                    sent[up, part * SENT + k] = f.astype(half)
                    edge_ref[part, 2 + k] = f
            hx = steps.magnetic_x(e)
            coef = scales[part] * held_ref[p]
            for comp in range(3):
                curl = steps.curl_back(comp, hx, hy, hz, before[part])
                own_ref[part, comp, p] = e[comp] - RELAX * curl + coef * raw[1 - part, comp, p]
            before[part] = hy, hz
    point.add_to(own_ref, 0, depth, 0, weight)

    row = lax.broadcasted_iota(jnp.int32, (height, breadth), 0)
    at_last = jnp.where(point.plane == last, F32(1.0), F32(0.0))
    here = jnp.where((row == point.row) & (steps.lane == point.lane), RELAX * at_last, 0.0)
    for part in range(2):
        ex, ey, ez = [own_ref[part, comp, 0] for comp in range(3)]
        hy, hz = steps.up_z(ex) - own_ref[part, 2, 1], own_ref[part, 1, 1] - steps.up_y(ex)
        for k, f in enumerate((ey, ez, hy, hz)):
            sent[down, part * SENT + 2 + k] = f.astype(half)
        e = [own_ref[part, comp, last] for comp in range(3)]
        behind = steps.magnetic_yz([own_ref[part, comp, last - 1] for comp in range(3)], e)
        hy, hz = steps.magnetic_yz(e, None)
        hx = steps.magnetic_x(e)
        coef = scales[part] * held_ref[last]
        after = []
        for comp in range(3):
            curl = steps.curl_back(comp, hx, hy, hz, behind)
            value = e[comp] - RELAX * curl + coef * own_ref[1 - part, comp, last]
            after.append(value + here * weight(part, comp))
        for k, f in enumerate((hy, hz) + steps.magnetic_yz(after, None)):
            sent[up, part * SENT + 2 + k] = f.astype(half)
    far_ref[...] = sent[0]
    near_ref[...] = sent[1]
    for copy in others:
        copy.wait()


def sweep_kernel(s, planes, scalar_ref, own_ref, edge_ref, held_ref, field_ref, far_in, near_in, far_cond, near_cond, *refs):
    depth, height, breadth = held_ref.shape
    count = field_ref.shape[0]
    final = s == count - 1
    if final:
        earlier = refs[:s]
        rows_ref, far_ref, near_ref, one_, two_, got, conds, sent = refs[s:]
    else:
        rows_ref, one_, two_, got, conds = refs
    steps = Steps(height, breadth)
    index = lax.axis_index("space")
    first = index * depth
    relax_low = jnp.where(first > 0, F32(RELAX), F32(0.0))
    relax_high = jnp.where(first + depth < planes, F32(RELAX), F32(0.0))
    low = index & 1
    high = 1 - low
    receive(got, far_in, near_in, (first == 0) | (first + depth == planes))
    conds[0] = far_cond[2 * SENT]
    conds[1] = near_cond[2 * SENT]
    group = scalar_ref[count + s].astype(jnp.int32)
    angular = angular_of(scalar_ref[2 * count + group].astype(jnp.int32))
    scales = RELAX * angular, -RELAX * angular
    point = Point(scalar_ref[s].astype(jnp.int32), first, steps)
    weights_at = scalar_ref.shape[0] - 6 * count + 6 * s

    def conductivity(p):
        if p < 0:
            return conds[low].astype(F32)
        if p >= depth:
            return conds[high].astype(F32)
        return held_ref[p]

    def received(side, part, k):
        return got[side, part * SENT + k].astype(F32)

    def weight(part, comp):
        return scalar_ref[weights_at + part * 3 + comp]

    for part in range(2):
        ey, ez, ly, lz = [edge_ref[part, k] for k in range(4)]
        one_[part, 0, 0] = -relax_low * (steps.down_y(ey) + steps.down_z(ez))
        one_[part, 1, 0] = relax_low * ey
        one_[part, 2, 0] = relax_low * ez
        e = [own_ref[part, comp, 0] for comp in range(3)]
        one_[part, 0, 1] = e[0]
        one_[part, 1, 1] = e[1] - RELAX * received(low, part, 1)
        one_[part, 2, 1] = e[2] + RELAX * received(low, part, 0)
        for p in range(1, depth - 1):
            for comp in range(3):
                one_[part, comp, p + 1] = own_ref[part, comp, p]
        e = [own_ref[part, comp, depth - 1] for comp in range(3)]
        high_y, high_z = received(high, part, 0), received(high, part, 1)
        one_[part, 0, depth] = e[0] - RELAX * (steps.down_y(high_y) + steps.down_z(high_z))
        one_[part, 1, depth] = e[1] + RELAX * high_y
        one_[part, 2, depth] = e[2] + RELAX * high_z
        one_[part, 1, depth + 1] = received(high, part, 2) - relax_high * lz
        one_[part, 2, depth + 1] = received(high, part, 3) + relax_high * ly

    before = [(-one_[part, 2, 0], one_[part, 1, 0]) for part in range(2)]
    for p in range(-1, depth + 1):
        relax = relax_low if p < 0 else relax_high if p == depth else F32(RELAX)
        for part in range(2):
            e = [one_[part, comp, p + 1] if comp or p < depth else None for comp in range(3)]
            if p < depth:
                hy, hz = steps.magnetic_yz(e, [None, one_[part, 1, p + 2], one_[part, 2, p + 2]])
            else:
                hy, hz = received(high, part, 4) + e[2], received(high, part, 5) - e[1]
            hx = steps.magnetic_x(e)
            coef = scales[part] * conductivity(p)
            for comp in range(1 if p == depth else 0, 3):
                curl = steps.curl_back(comp, hx, hy, hz, before[part])
                two_[part, comp, p + 1] = e[comp] - relax * curl + coef * one_[1 - part, comp, p + 1]
            if p < 0:
                hy, hz = hy + received(low, part, 2), hz + received(low, part, 3)
            before[part] = hy, hz
    for part in range(2):
        two_[part, 0, depth + 1] = jnp.zeros((height, breadth), F32)
    point.add_to(two_, 0, depth + 1, 1, weight)

    row = lax.broadcasted_iota(jnp.int32, (height, breadth), 0)
    here = (row == point.row) & (steps.lane == point.lane)
    before = []
    for part in range(2):
        e = [two_[part, comp, 0] for comp in range(3)]
        hy, hz = steps.magnetic_yz(e, [None, two_[part, 1, 1], two_[part, 2, 1]])
        before.append((hy + received(low, part, 4), hz + received(low, part, 5)))
    for p in range(depth):
        spot = jnp.where(here, jnp.where(point.plane == p, F32(RELAX), F32(0.0)), 0.0)
        after = []
        for part in range(2):
            e = [two_[part, comp, p + 1] for comp in range(3)]
            hy, hz = steps.magnetic_yz(e, [None, two_[part, 1, p + 2], two_[part, 2, p + 2]])
            hx = steps.magnetic_x(e)
            coef = scales[part] * held_ref[p]
            for comp in range(3):
                curl = steps.curl_back(comp, hx, hy, hz, before[part])
                value = e[comp] - RELAX * curl + coef * two_[1 - part, comp, p + 1]
                after.append(value + spot * weight(part, comp))
            before[part] = hy, hz
        row_re = row_im = None
        for comp in range(3):
            re, im = after[comp], after[3 + comp]
            field_re, field_im = field_ref[s, 0, comp, p], field_ref[s, 1, comp, p]
            add_re, add_im = field_re * re - field_im * im, field_re * im + field_im * re
            row_re, row_im = (add_re, add_im) if comp == 0 else (row_re + add_re, row_im + add_im)
        coef = angular * held_ref[p]
        for part, value in enumerate((row_re, row_im)):
            value = (coef * value).astype(rows_ref.dtype)
            if not final:
                rows_ref[part, p] = value
                continue
            rows_ref[s, part, p] = value
            if p >= depth - REACH:
                sent[high, s, part, p - depth + REACH] = value
            if p < REACH:
                sent[low, s, part, p] = value
    if final:
        for t, ref in enumerate(earlier):
            rows_ref[t] = ref[...]
            sent[high, t] = ref[:, depth - REACH :]
            sent[low, t] = ref[:, :REACH]
        far_ref[...] = sent[0]
        near_ref[...] = sent[1]


def in_plane(steps, f):
    total = (steps.after_y(f) + steps.before_y(f)) + (steps.after_z(f) + steps.before_z(f))
    return (1.0 - 6.0 * KAPPA) * f + KAPPA * total


def smooth_kernel(planes, rows_ref, alone_ref):
    count, _, depth, height, breadth = rows_ref.shape
    steps = Steps(height, breadth)
    first = lax.axis_index("space") * depth
    below = jnp.where(first > 0, F32(KAPPA), F32(0.0))
    above = jnp.where(first + depth < planes, F32(KAPPA), F32(0.0))

    def one_row(s, part):
        value = [rows_ref[s, part, p].astype(F32) for p in range(depth)]
        once = []
        for p in range(depth):
            beside = [value[q] for q in (p - 1, p + 1) if 0 <= q < depth]
            once.append(in_plane(steps, value[p]) + KAPPA * functools.reduce(jnp.add, beside))
        once = [below * value[0]] + once + [above * value[-1]]
        for p in range(depth):
            alone_ref[s, part, p] = in_plane(steps, once[p + 1]) + KAPPA * (once[p] + once[p + 2])

    def one_source(s, _):
        for part in range(2):
            one_row(s, part)
        return 0

    lax.fori_loop(0, count, one_source, 0)


def block_kernel(cells, rows_ref, alone_ref, far_in, near_in, all_ref, smooth_ref, block_ref, got, rounded, sums, sem):
    count, _, depth, height, breadth = rows_ref.shape
    ranks = all_ref.shape[0]
    steps = Steps(height, breadth)
    many = ranks * count * 2
    index = lax.axis_index("space")
    receive(got, far_in, near_in, (index == 0) | (index == lax.axis_size("space") - 1))
    odd = index & 1
    low, high = odd, 1 - odd

    def one_row(s, part):
        value = [alone_ref[s, part, p] for p in range(depth)]
        for side, nearest, order in ((low, REACH - 1, 1), (high, 0, -1)):
            close = got[side, s, part, nearest].astype(F32)
            beyond = got[side, s, part, REACH - 1 - nearest].astype(F32)
            end = 0 if order > 0 else depth - 1
            value[end] = value[end] + (2.0 * KAPPA * in_plane(steps, close) + KAPPA * KAPPA * beyond)
            value[end + order] = value[end + order] + KAPPA * KAPPA * close
        for p in range(depth):
            rounded[s, part, p] = value[p].astype(rounded.dtype)

    def one_source(s, _):
        for part in range(2):
            one_row(s, part)
        return 0

    lax.fori_loop(0, count, one_source, 0)
    out = pltpu.make_async_copy(rounded, smooth_ref, sem)
    out.start()

    sums[...] = jnp.zeros_like(sums)

    def one_plane(p, _):
        mine = [rounded[a // 2, a % 2, p].astype(F32) for a in range(2 * count)]
        for b in range(many):
            r, t = divmod(b // 2, count)
            other = all_ref[r, t, b % 2, p].astype(F32)
            for a in range(2 * count):
                prod = mine[a] * other
                total = prod[:8]
                for k in range(8, height, 8):
                    total = total + prod[k : k + 8]
                sums[a * many + b] = sums[a * many + b] + total
        return 0

    lax.fori_loop(0, depth, one_plane, 0)
    half = jnp.bfloat16
    ones = jnp.ones((breadth, breadth), half)
    for a in range(2 * count):
        table = sums[a * many : (a + 1) * many].reshape(many * 8, breadth)
        coarse = table.astype(half)
        fine = (table - coarse.astype(F32)).astype(half)
        table = jnp.dot(coarse, ones, preferred_element_type=F32) + jnp.dot(fine, ones, preferred_element_type=F32)
        line = None
        for b in range(many):
            add = jnp.where(steps.lane[:8] == b, table[b * 8 : b * 8 + 8], 0.0)
            line = add if line is None else line + add
        line = jnp.sum(line, axis=0, keepdims=True) * (1.0 / cells)
        for peer in range(block_ref.shape[0]):
            block_ref[peer, a : a + 1, :] = line[:, :many]
    out.wait()


def in_hbm(x):
    return pltpu.with_memory_space_constraint(x, pltpu.HBM)


def shards(conductivity, background, warm_start, data_weight, recv_cell, src_group, group_freq):
    count = warm_start.shape[0]
    depth, height, breadth = conductivity.shape
    plane = (height, breadth)
    peers = lax.axis_size("space")
    ranks = lax.axis_size("rx")
    cells = depth * height * breadth * peers
    half = jnp.bfloat16
    integers = jnp.concatenate([recv_cell, src_group, group_freq]).astype(F32)
    scalars = jnp.concatenate([integers, data_weight.reshape(-1)])
    assert peers % 2 == 0 and ranks % 2 == 0
    both = ("rx", "space")
    far = [(r * peers + i, r * peers + i + 1) for r in range(ranks) for i in range(1, peers - 1, 2)]
    far += [(r * peers + i, (r + 1) * peers + i) for r in range(0, ranks, 2) for i in (0, peers - 1)]
    near = [(i, i + 1) for i in range(0, peers, 2)]
    far, near = [pairs + [(j, i) for i, j in pairs] for pairs in (far, near)]
    shape = jax.ShapeDtypeStruct

    own, edges, fars, nears = [], [], [], []
    for s in range(count):
        message = shape((2 * SENT + (s == 0),) + plane, half)
        outs = [message, message, shape(warm_start.shape[1:], F32), shape((2, 4) + plane, F32)]
        scratch = [pltpu.VMEM((2,) + message.shape, half)]
        if s == 0:
            operands = [warm_start, conductivity, background, data_weight, recv_cell, src_group, group_freq]
            operands = [in_hbm(x) for x in operands]
            specs = [HBM] * 7
            outs += [
                shape(conductivity.shape, F32),
                shape((count - 1,) + warm_start.shape[1:], F32),
                shape((count,) + background.shape[1:], F32),
            ]
            scratch = [
                pltpu.VMEM(warm_start.shape[1:], F32),
                pltpu.SMEM(data_weight.shape, F32),
                pltpu.SMEM(recv_cell.shape, jnp.int32),
                pltpu.SMEM(src_group.shape, jnp.int32),
                pltpu.SMEM(group_freq.shape, jnp.int32),
            ] + scratch + [pltpu.SemaphoreType.DMA((7 + count,))]
        else:
            operands = [later, scalars, held]
            specs = [FULL, SCALARS, FULL]
        result = pl.pallas_call(
            functools.partial(first_kernel, s),
            out_shape=tuple(outs),
            in_specs=specs,
            out_specs=(FULL,) * len(outs),
            scratch_shapes=scratch,
            compiler_params=KERNEL,
            name="first_sweep",
        )(*operands)
        if s == 0:
            held, later, field = result[4:]
        own.append(result[2])
        edges.append(result[3])
        fars.append(lax.ppermute(result[0], both, far))
        nears.append(lax.ppermute(result[1], "space", near))

    rows_of = shape((count, 2, depth) + plane, half)
    ends_of = shape((count, 2, REACH) + plane, half)
    earlier = []
    for s in range(count):
        operands = [scalars, own[s], edges[s], held, field, fars[s], nears[s], fars[0], nears[0]]
        scratch = [
            pltpu.VMEM((2, 3, depth + 2) + plane, F32),
            pltpu.VMEM((2, 3, depth + 2) + plane, F32),
            pltpu.VMEM((2, 2 * SENT) + plane, half),
            pltpu.VMEM((2,) + plane, half),
        ]
        results = (shape((2, depth) + plane, half),)
        if s == count - 1:
            operands += earlier
            results = (rows_of, ends_of, ends_of)
            scratch.append(pltpu.VMEM((2,) + ends_of.shape, half))
        results = pl.pallas_call(
            functools.partial(sweep_kernel, s, peers * depth),
            out_shape=results,
            in_specs=[SCALARS] + [FULL] * (len(operands) - 1),
            out_specs=(FULL,) * len(results),
            scratch_shapes=scratch,
            compiler_params=KERNEL,
            name="sweeps",
        )(*operands)
        earlier.append(results[0])
    rows, to_far, to_near = results
    from_far = lax.ppermute(to_far, both, far)
    from_near = lax.ppermute(to_near, "space", near)
    every = lax.all_gather(rows, "rx", axis=0)

    many = 2 * count * ranks
    alone = pl.pallas_call(
        functools.partial(smooth_kernel, peers * depth),
        out_shape=shape(rows_of.shape, F32),
        in_specs=[FULL],
        out_specs=FULL,
        compiler_params=KERNEL,
        name="smooth",
    )(rows)
    smoothed, partial_block = pl.pallas_call(
        functools.partial(block_kernel, cells),
        out_shape=(rows_of, shape((peers, 2 * count, many), F32)),
        in_specs=[FULL] * 5,
        out_specs=(HBM, FULL),
        scratch_shapes=[
            pltpu.VMEM((2,) + ends_of.shape, half),
            pltpu.VMEM(rows_of.shape, half),
            pltpu.VMEM((2 * count * many, 8, breadth), F32),
            pltpu.SemaphoreType.DMA,
        ],
        compiler_params=KERNEL,
        name="block",
    )(rows, alone, from_far, from_near, every)
    backwards = [list(range(peers - 1, -1, -1))]
    pieces = lax.all_to_all(partial_block, "space", 0, 0, axis_index_groups=backwards)
    return (jnp.sum(pieces, axis=0), smoothed)


def solution(mesh):
    in_specs = (
        P("space", None, None),
        P(None, None, None, "space", None, None),
        P("rx", None, None, "space", None, None),
        P("rx", None, None),
        P("rx"),
        P("rx"),
        P(),
    )
    out_specs = (P("rx", None), P("rx", None, "space", None, None))
    return jax.shard_map(shards, mesh=mesh, in_specs=in_specs, out_specs=out_specs, check_vma=False)
```

```python
import functools

import jax
import jax.numpy as jnp
from jax import lax
from jax.experimental import pallas as pl
from jax.experimental.pallas import tpu as pltpu
from jax.sharding import PartitionSpec as P

SENT = 6
RELAX = 0.2
KAPPA = 0.1
REACH = 2
FULL = pl.BlockSpec(memory_space=pltpu.VMEM)
HBM = pl.BlockSpec(memory_space=pltpu.HBM)
SCALARS = pl.BlockSpec(memory_space=pltpu.SMEM)
KERNEL = pltpu.CompilerParams(vmem_limit_bytes=8 * 2**20)
F32 = jnp.float32


class Steps:
    def __init__(self, height, breadth):
        self.height, self.breadth = height, breadth
        self.sub = lax.broadcasted_iota(jnp.int32, (8, breadth), 0)
        self.lane = lax.broadcasted_iota(jnp.int32, (height, breadth), 1)

    def after_y(self, f):
        f = pltpu.roll(f, self.height - 1, 0)
        return jnp.concatenate([f[:-8], jnp.where(self.sub < 7, f[-8:], 0.0)], axis=0)

    def before_y(self, f):
        f = pltpu.roll(f, 1, 0)
        return jnp.concatenate([jnp.where(self.sub > 0, f[:8], 0.0), f[8:]], axis=0)

    def after_z(self, f):
        return jnp.where(self.lane < self.breadth - 1, pltpu.roll(f, self.breadth - 1, 1), 0.0)

    def before_z(self, f):
        return jnp.where(self.lane > 0, pltpu.roll(f, 1, 1), 0.0)

    def up_y(self, f):
        return self.after_y(f) - f

    def up_z(self, f):
        return self.after_z(f) - f

    def down_y(self, f):
        return f - self.before_y(f)

    def down_z(self, f):
        return f - self.before_z(f)

    def magnetic_yz(self, e, e_next):
        ex, ey, ez = e
        if e_next is None:
            return self.up_z(ex) + ez, -ey - self.up_y(ex)
        return self.up_z(ex) - (e_next[2] - ez), (e_next[1] - ey) - self.up_y(ex)

    def magnetic_x(self, e):
        return self.up_y(e[2]) - self.up_z(e[1])

    def curl_back(self, comp, hx, hy, hz, before):
        if comp == 0:
            return self.down_y(hz) - self.down_z(hy)
        if comp == 1:
            return self.down_z(hx) - (hz - before[1])
        return (hy - before[0]) - self.down_y(hx)


def angular_of(freq):
    angular = F32(0.25)
    for bit, factor in ((1, 1.25), (2, 1.25**2), (4, 1.25**4)):
        angular = angular * jnp.where((freq & bit) != 0, F32(factor), F32(1.0))
    return angular


def split(number, size):
    if size & (size - 1):
        return number // size, number % size
    return number >> (size.bit_length() - 1), number & (size - 1)


class Point:
    def __init__(self, cell, first, steps):
        plane, inner = split(cell, steps.height * steps.breadth)
        row, lane = split(inner, steps.breadth)
        block, sub = split(row, 8)
        self.plane = plane - first
        self.rows = pl.ds(pl.multiple_of(block * 8, 8), 8)
        self.row, self.sub, self.lane, self.steps = row, sub, lane, steps

    def add_to(self, ref, low, high, shift, weight):
        reached = (self.plane >= low) & (self.plane < high)
        here = (self.steps.sub == self.sub) & (self.steps.lane[:8] == self.lane)
        amount = jnp.where(here, jnp.where(reached, F32(RELAX), F32(0.0)), 0.0)
        plane = jnp.clip(self.plane, low, high - 1) + shift
        for part in range(2):
            for comp in range(3):
                at = (part, comp, plane, self.rows)
                ref[at] = ref[at] + amount * weight(part, comp)


def receive(got, far_in, near_in, at_end):
    got[1] = near_in[: got.shape[1]]

    @pl.when(at_end)
    def _():
        got[0] = jnp.zeros(got.shape[1:], got.dtype)

    @pl.when(jnp.logical_not(at_end))
    def _():
        got[0] = far_in[: got.shape[1]]


def first_kernel(s, planes_ref, *refs):
    if s == 0:
        cond_ref, weight_ref, cell_ref, group_ref, freq_ref = refs[:5]
        far_ref, near_ref, own_ref, edge_ref, held_ref, later_ref = refs[5:11]
        raw, weight_of, cell, group, freq, sent, sems = refs[11:]
        count = planes_ref.shape[0]
        small = ((group_ref, group), (freq_ref, freq), (cell_ref, cell), (weight_ref, weight_of), (cond_ref, held_ref))
        copies = [pltpu.make_async_copy(planes_ref.at[0], raw, sems.at[0])]
        copies += [pltpu.make_async_copy(a, b, sems.at[k + 1]) for k, (a, b) in enumerate(small)]
        others = [pltpu.make_async_copy(planes_ref.at[pl.ds(1, count - 1)], later_ref, sems.at[len(copies)])]
        for copy in copies + others:
            copy.start()
        for copy in copies:
            copy.wait()
        angular = angular_of(freq[group[s]])
        cell_at = cell[s]

        def weight(part, comp):
            return weight_of[s, part, comp]
    else:
        scalar_ref, held_ref, back_ref, far_ref, near_ref, own_ref, edge_ref, field_ref, sent, sems = refs
        raw = planes_ref.at[s - 1]
        count = planes_ref.shape[0] + 1
        others = []
        for k, t in enumerate((0, 1) if s == 1 else (s,)):
            group = scalar_ref[count + t].astype(jnp.int32)
            others.append(pltpu.make_async_copy(back_ref.at[group], field_ref.at[k], sems.at[k]))
            others[-1].start()
        group = scalar_ref[count + s].astype(jnp.int32)
        angular = angular_of(scalar_ref[2 * count + group].astype(jnp.int32))
        cell_at = scalar_ref[s].astype(jnp.int32)
        weights_at = scalar_ref.shape[0] - 6 * count + 6 * s

        def weight(part, comp):
            return scalar_ref[weights_at + part * 3 + comp]

    depth, height, breadth = held_ref.shape
    steps = Steps(height, breadth)
    half = sent.dtype
    index = lax.axis_index("space")
    first = index * depth
    down = index & 1
    up = 1 - down
    last = depth - 1
    scales = RELAX * angular, -RELAX * angular
    point = Point(cell_at, first, steps)
    if s == 0:
        sent[up, 2 * SENT] = held_ref[last].astype(half)
        sent[down, 2 * SENT] = held_ref[0].astype(half)

    before = []
    for part in range(2):
        ey, ez = raw[part, 1, 0], raw[part, 2, 0]
        for k, f in enumerate((ey, ez)):
            sent[down, part * SENT + k] = f.astype(half)
            edge_ref[part, k] = f
        before.append((-ez, ey))
    for p in range(depth):
        for part in range(2):
            e = [raw[part, comp, p] for comp in range(3)]
            e_next = [None if comp == 0 else raw[part, comp, p + 1] for comp in range(3)] if p < last else None
            hy, hz = steps.magnetic_yz(e, e_next)
            if p == last:
                for k, f in enumerate((hy, hz)):
                    sent[up, part * SENT + k] = f.astype(half)
                    edge_ref[part, 2 + k] = f
            hx = steps.magnetic_x(e)
            coef = scales[part] * held_ref[p]
            for comp in range(3):
                curl = steps.curl_back(comp, hx, hy, hz, before[part])
                own_ref[part, comp, p] = e[comp] - RELAX * curl + coef * raw[1 - part, comp, p]
            before[part] = hy, hz
    point.add_to(own_ref, 0, depth, 0, weight)

    row = lax.broadcasted_iota(jnp.int32, (height, breadth), 0)
    at_last = jnp.where(point.plane == last, F32(1.0), F32(0.0))
    here = jnp.where((row == point.row) & (steps.lane == point.lane), RELAX * at_last, 0.0)
    for part in range(2):
        ex, ey, ez = [own_ref[part, comp, 0] for comp in range(3)]
        hy, hz = steps.up_z(ex) - own_ref[part, 2, 1], own_ref[part, 1, 1] - steps.up_y(ex)
        for k, f in enumerate((ey, ez, hy, hz)):
            sent[down, part * SENT + 2 + k] = f.astype(half)
        e = [own_ref[part, comp, last] for comp in range(3)]
        behind = steps.magnetic_yz([own_ref[part, comp, last - 1] for comp in range(3)], e)
        hy, hz = steps.magnetic_yz(e, None)
        hx = steps.magnetic_x(e)
        coef = scales[part] * held_ref[last]
        after = []
        for comp in range(3):
            curl = steps.curl_back(comp, hx, hy, hz, behind)
            value = e[comp] - RELAX * curl + coef * own_ref[1 - part, comp, last]
            after.append(value + here * weight(part, comp))
        for k, f in enumerate((hy, hz) + steps.magnetic_yz(after, None)):
            sent[up, part * SENT + 2 + k] = f.astype(half)
    far_ref[...] = sent[0]
    near_ref[...] = sent[1]
    for copy in others:
        copy.wait()


def sweep_kernel(s, count, field_at, planes, scalar_ref, own_ref, edge_ref, held_ref, field_ref, far_in, near_in, far_cond, near_cond, *refs):
    depth, height, breadth = held_ref.shape
    final = s == count - 1
    if final:
        earlier = refs[:s]
        rows_ref, far_ref, near_ref, one_, two_, got, conds, sent = refs[s:]
    else:
        rows_ref, one_, two_, got, conds = refs
    steps = Steps(height, breadth)
    index = lax.axis_index("space")
    first = index * depth
    relax_low = jnp.where(first > 0, F32(RELAX), F32(0.0))
    relax_high = jnp.where(first + depth < planes, F32(RELAX), F32(0.0))
    low = index & 1
    high = 1 - low
    receive(got, far_in, near_in, (first == 0) | (first + depth == planes))
    conds[0] = far_cond[2 * SENT]
    conds[1] = near_cond[2 * SENT]
    group = scalar_ref[count + s].astype(jnp.int32)
    angular = angular_of(scalar_ref[2 * count + group].astype(jnp.int32))
    scales = RELAX * angular, -RELAX * angular
    point = Point(scalar_ref[s].astype(jnp.int32), first, steps)
    weights_at = scalar_ref.shape[0] - 6 * count + 6 * s

    def conductivity(p):
        if p < 0:
            return conds[low].astype(F32)
        if p >= depth:
            return conds[high].astype(F32)
        return held_ref[p]

    def received(side, part, k):
        return got[side, part * SENT + k].astype(F32)

    def weight(part, comp):
        return scalar_ref[weights_at + part * 3 + comp]

    for part in range(2):
        ey, ez, ly, lz = [edge_ref[part, k] for k in range(4)]
        one_[part, 0, 0] = -relax_low * (steps.down_y(ey) + steps.down_z(ez))
        one_[part, 1, 0] = relax_low * ey
        one_[part, 2, 0] = relax_low * ez
        e = [own_ref[part, comp, 0] for comp in range(3)]
        one_[part, 0, 1] = e[0]
        one_[part, 1, 1] = e[1] - RELAX * received(low, part, 1)
        one_[part, 2, 1] = e[2] + RELAX * received(low, part, 0)
        for p in range(1, depth - 1):
            for comp in range(3):
                one_[part, comp, p + 1] = own_ref[part, comp, p]
        e = [own_ref[part, comp, depth - 1] for comp in range(3)]
        high_y, high_z = received(high, part, 0), received(high, part, 1)
        one_[part, 0, depth] = e[0] - RELAX * (steps.down_y(high_y) + steps.down_z(high_z))
        one_[part, 1, depth] = e[1] + RELAX * high_y
        one_[part, 2, depth] = e[2] + RELAX * high_z
        one_[part, 1, depth + 1] = received(high, part, 2) - relax_high * lz
        one_[part, 2, depth + 1] = received(high, part, 3) + relax_high * ly

    before = [(-one_[part, 2, 0], one_[part, 1, 0]) for part in range(2)]
    for p in range(-1, depth + 1):
        relax = relax_low if p < 0 else relax_high if p == depth else F32(RELAX)
        for part in range(2):
            e = [one_[part, comp, p + 1] if comp or p < depth else None for comp in range(3)]
            if p < depth:
                hy, hz = steps.magnetic_yz(e, [None, one_[part, 1, p + 2], one_[part, 2, p + 2]])
            else:
                hy, hz = received(high, part, 4) + e[2], received(high, part, 5) - e[1]
            hx = steps.magnetic_x(e)
            coef = scales[part] * conductivity(p)
            for comp in range(1 if p == depth else 0, 3):
                curl = steps.curl_back(comp, hx, hy, hz, before[part])
                two_[part, comp, p + 1] = e[comp] - relax * curl + coef * one_[1 - part, comp, p + 1]
            if p < 0:
                hy, hz = hy + received(low, part, 2), hz + received(low, part, 3)
            before[part] = hy, hz
    for part in range(2):
        two_[part, 0, depth + 1] = jnp.zeros((height, breadth), F32)
    point.add_to(two_, 0, depth + 1, 1, weight)

    row = lax.broadcasted_iota(jnp.int32, (height, breadth), 0)
    here = (row == point.row) & (steps.lane == point.lane)
    before = []
    for part in range(2):
        e = [two_[part, comp, 0] for comp in range(3)]
        hy, hz = steps.magnetic_yz(e, [None, two_[part, 1, 1], two_[part, 2, 1]])
        before.append((hy + received(low, part, 4), hz + received(low, part, 5)))
    for p in range(depth):
        spot = jnp.where(here, jnp.where(point.plane == p, F32(RELAX), F32(0.0)), 0.0)
        after = []
        for part in range(2):
            e = [two_[part, comp, p + 1] for comp in range(3)]
            hy, hz = steps.magnetic_yz(e, [None, two_[part, 1, p + 2], two_[part, 2, p + 2]])
            hx = steps.magnetic_x(e)
            coef = scales[part] * held_ref[p]
            for comp in range(3):
                curl = steps.curl_back(comp, hx, hy, hz, before[part])
                value = e[comp] - RELAX * curl + coef * two_[1 - part, comp, p + 1]
                after.append(value + spot * weight(part, comp))
            before[part] = hy, hz
        row_re = row_im = None
        for comp in range(3):
            re, im = after[comp], after[3 + comp]
            field_re, field_im = field_ref[field_at, 0, comp, p], field_ref[field_at, 1, comp, p]
            add_re, add_im = field_re * re - field_im * im, field_re * im + field_im * re
            row_re, row_im = (add_re, add_im) if comp == 0 else (row_re + add_re, row_im + add_im)
        coef = angular * held_ref[p]
        for part, value in enumerate((row_re, row_im)):
            value = (coef * value).astype(rows_ref.dtype)
            if not final:
                rows_ref[part, p] = value
                continue
            rows_ref[s, part, p] = value
            if p >= depth - REACH:
                sent[high, s, part, p - depth + REACH] = value
            if p < REACH:
                sent[low, s, part, p] = value
    if final:
        for t, ref in enumerate(earlier):
            rows_ref[t] = ref[...]
            sent[high, t] = ref[:, depth - REACH :]
            sent[low, t] = ref[:, :REACH]
        far_ref[...] = sent[0]
        near_ref[...] = sent[1]


def in_plane(steps, f):
    total = (steps.after_y(f) + steps.before_y(f)) + (steps.after_z(f) + steps.before_z(f))
    return (1.0 - 6.0 * KAPPA) * f + KAPPA * total


def smooth_kernel(planes, rows_ref, alone_ref):
    count, _, depth, height, breadth = rows_ref.shape
    steps = Steps(height, breadth)
    first = lax.axis_index("space") * depth
    below = jnp.where(first > 0, F32(KAPPA), F32(0.0))
    above = jnp.where(first + depth < planes, F32(KAPPA), F32(0.0))

    def one_row(s, part):
        value = [rows_ref[s, part, p].astype(F32) for p in range(depth)]
        once = []
        for p in range(depth):
            beside = [value[q] for q in (p - 1, p + 1) if 0 <= q < depth]
            once.append(in_plane(steps, value[p]) + KAPPA * functools.reduce(jnp.add, beside))
        once = [below * value[0]] + once + [above * value[-1]]
        for p in range(depth):
            alone_ref[s, part, p] = in_plane(steps, once[p + 1]) + KAPPA * (once[p] + once[p + 2])

    def one_source(s, _):
        for part in range(2):
            one_row(s, part)
        return 0

    lax.fori_loop(0, count, one_source, 0)


def block_kernel(cells, rows_ref, alone_ref, far_in, near_in, all_ref, smooth_ref, block_ref, got, rounded, sums, sem):
    count, _, depth, height, breadth = rows_ref.shape
    ranks = all_ref.shape[0]
    steps = Steps(height, breadth)
    many = ranks * count * 2
    index = lax.axis_index("space")
    receive(got, far_in, near_in, (index == 0) | (index == lax.axis_size("space") - 1))
    odd = index & 1
    low, high = odd, 1 - odd

    def one_row(s, part):
        value = [alone_ref[s, part, p] for p in range(depth)]
        for side, nearest, order in ((low, REACH - 1, 1), (high, 0, -1)):
            close = got[side, s, part, nearest].astype(F32)
            beyond = got[side, s, part, REACH - 1 - nearest].astype(F32)
            end = 0 if order > 0 else depth - 1
            value[end] = value[end] + (2.0 * KAPPA * in_plane(steps, close) + KAPPA * KAPPA * beyond)
            value[end + order] = value[end + order] + KAPPA * KAPPA * close
        for p in range(depth):
            rounded[s, part, p] = value[p].astype(rounded.dtype)

    def one_source(s, _):
        for part in range(2):
            one_row(s, part)
        return 0

    lax.fori_loop(0, count, one_source, 0)
    out = pltpu.make_async_copy(rounded, smooth_ref, sem)
    out.start()

    sums[...] = jnp.zeros_like(sums)

    def one_plane(p, _):
        mine = [rounded[a // 2, a % 2, p].astype(F32) for a in range(2 * count)]
        for b in range(many):
            r, t = divmod(b // 2, count)
            other = all_ref[r, t, b % 2, p].astype(F32)
            for a in range(2 * count):
                prod = mine[a] * other
                total = prod[:8]
                for k in range(8, height, 8):
                    total = total + prod[k : k + 8]
                sums[a * many + b] = sums[a * many + b] + total
        return 0

    lax.fori_loop(0, depth, one_plane, 0)
    half = jnp.bfloat16
    ones = jnp.ones((breadth, breadth), half)
    for a in range(2 * count):
        table = sums[a * many : (a + 1) * many].reshape(many * 8, breadth)
        coarse = table.astype(half)
        fine = (table - coarse.astype(F32)).astype(half)
        table = jnp.dot(coarse, ones, preferred_element_type=F32) + jnp.dot(fine, ones, preferred_element_type=F32)
        line = None
        for b in range(many):
            add = jnp.where(steps.lane[:8] == b, table[b * 8 : b * 8 + 8], 0.0)
            line = add if line is None else line + add
        line = jnp.sum(line, axis=0, keepdims=True) * (1.0 / cells)
        for peer in range(block_ref.shape[0]):
            block_ref[peer, a : a + 1, :] = line[:, :many]
    out.wait()


def in_hbm(x):
    return pltpu.with_memory_space_constraint(x, pltpu.HBM)


def shards(conductivity, background, warm_start, data_weight, recv_cell, src_group, group_freq):
    count = warm_start.shape[0]
    depth, height, breadth = conductivity.shape
    plane = (height, breadth)
    peers = lax.axis_size("space")
    ranks = lax.axis_size("rx")
    cells = depth * height * breadth * peers
    half = jnp.bfloat16
    integers = jnp.concatenate([recv_cell, src_group, group_freq]).astype(F32)
    scalars = jnp.concatenate([integers, data_weight.reshape(-1)])
    assert peers % 2 == 0 and ranks % 2 == 0
    both = ("rx", "space")
    far = [(r * peers + i, r * peers + i + 1) for r in range(ranks) for i in range(1, peers - 1, 2)]
    far += [(r * peers + i, (r + 1) * peers + i) for r in range(0, ranks, 2) for i in (0, peers - 1)]
    near = [(i, i + 1) for i in range(0, peers, 2)]
    far, near = [pairs + [(j, i) for i, j in pairs] for pairs in (far, near)]
    shape = jax.ShapeDtypeStruct
    assert count > 1

    own, edges, fars, nears, fields = [], [], [], [], []
    for s in range(count):
        message = shape((2 * SENT + (s == 0),) + plane, half)
        outs = [message, message, shape(warm_start.shape[1:], F32), shape((2, 4) + plane, F32)]
        scratch = [pltpu.VMEM((2,) + message.shape, half)]
        if s == 0:
            operands = [warm_start, conductivity, data_weight, recv_cell, src_group, group_freq]
            operands = [in_hbm(x) for x in operands]
            specs = [HBM] * 6
            outs += [
                shape(conductivity.shape, F32),
                shape((count - 1,) + warm_start.shape[1:], F32),
            ]
            scratch = [
                pltpu.VMEM(warm_start.shape[1:], F32),
                pltpu.SMEM(data_weight.shape, F32),
                pltpu.SMEM(recv_cell.shape, jnp.int32),
                pltpu.SMEM(src_group.shape, jnp.int32),
                pltpu.SMEM(group_freq.shape, jnp.int32),
            ] + scratch + [pltpu.SemaphoreType.DMA((7,))]
        else:
            operands = [later, scalars, held, in_hbm(background)]
            specs = [FULL, SCALARS, FULL, HBM]
            outs.append(shape((1 + (s == 1),) + background.shape[1:], F32))
            scratch.append(pltpu.SemaphoreType.DMA((2,)))
        result = pl.pallas_call(
            functools.partial(first_kernel, s),
            out_shape=tuple(outs),
            in_specs=specs,
            out_specs=(FULL,) * len(outs),
            scratch_shapes=scratch,
            compiler_params=KERNEL,
            name="first_sweep",
        )(*operands)
        if s == 0:
            held, later = result[4:]
        else:
            fields += [(result[4], k) for k in range(result[4].shape[0])]
        own.append(result[2])
        edges.append(result[3])
        fars.append(lax.ppermute(result[0], both, far))
        nears.append(lax.ppermute(result[1], "space", near))

    rows_of = shape((count, 2, depth) + plane, half)
    ends_of = shape((count, 2, REACH) + plane, half)
    earlier = []
    for s in range(count):
        operands = [scalars, own[s], edges[s], held, fields[s][0], fars[s], nears[s], fars[0], nears[0]]
        scratch = [
            pltpu.VMEM((2, 3, depth + 2) + plane, F32),
            pltpu.VMEM((2, 3, depth + 2) + plane, F32),
            pltpu.VMEM((2, 2 * SENT) + plane, half),
            pltpu.VMEM((2,) + plane, half),
        ]
        results = (shape((2, depth) + plane, half),)
        if s == count - 1:
            operands += earlier
            results = (rows_of, ends_of, ends_of)
            scratch.append(pltpu.VMEM((2,) + ends_of.shape, half))
        results = pl.pallas_call(
            functools.partial(sweep_kernel, s, count, fields[s][1], peers * depth),
            out_shape=results,
            in_specs=[SCALARS] + [FULL] * (len(operands) - 1),
            out_specs=(FULL,) * len(results),
            scratch_shapes=scratch,
            compiler_params=KERNEL,
            name="sweeps",
        )(*operands)
        earlier.append(results[0])
    rows, to_far, to_near = results
    from_far = lax.ppermute(to_far, both, far)
    from_near = lax.ppermute(to_near, "space", near)
    every = lax.all_gather(rows, "rx", axis=0)

    many = 2 * count * ranks
    alone = pl.pallas_call(
        functools.partial(smooth_kernel, peers * depth),
        out_shape=shape(rows_of.shape, F32),
        in_specs=[FULL],
        out_specs=FULL,
        compiler_params=KERNEL,
        name="smooth",
    )(rows)
    smoothed, partial_block = pl.pallas_call(
        functools.partial(block_kernel, cells),
        out_shape=(rows_of, shape((peers, 2 * count, many), F32)),
        in_specs=[FULL] * 5,
        out_specs=(HBM, FULL),
        scratch_shapes=[
            pltpu.VMEM((2,) + ends_of.shape, half),
            pltpu.VMEM(rows_of.shape, half),
            pltpu.VMEM((2 * count * many, 8, breadth), F32),
            pltpu.SemaphoreType.DMA,
        ],
        compiler_params=KERNEL,
        name="block",
    )(rows, alone, from_far, from_near, every)
    backwards = [list(range(peers - 1, -1, -1))]
    pieces = lax.all_to_all(partial_block, "space", 0, 0, axis_index_groups=backwards)
    return (jnp.sum(pieces, axis=0), smoothed)


def solution(mesh):
    in_specs = (
        P("space", None, None),
        P(None, None, None, "space", None, None),
        P("rx", None, None, "space", None, None),
        P("rx", None, None),
        P("rx"),
        P("rx"),
        P(),
    )
    out_specs = (P("rx", None), P("rx", None, "space", None, None))
    return jax.shard_map(shards, mesh=mesh, in_specs=in_specs, out_specs=out_specs, check_vma=False)
```

```python
import functools

import jax
import jax.numpy as jnp
from jax import lax
from jax.experimental import pallas as pl
from jax.experimental.pallas import tpu as pltpu
from jax.sharding import PartitionSpec as P

SENT = 6
RELAX = 0.2
KAPPA = 0.1
REACH = 2
FULL = pl.BlockSpec(memory_space=pltpu.VMEM)
HBM = pl.BlockSpec(memory_space=pltpu.HBM)
SCALARS = pl.BlockSpec(memory_space=pltpu.SMEM)
KERNEL = pltpu.CompilerParams(vmem_limit_bytes=8 * 2**20)
F32 = jnp.float32


class Steps:
    def __init__(self, height, breadth):
        self.height, self.breadth = height, breadth
        self.sub = lax.broadcasted_iota(jnp.int32, (8, breadth), 0)
        self.lane = lax.broadcasted_iota(jnp.int32, (height, breadth), 1)

    def after_y(self, f):
        f = pltpu.roll(f, self.height - 1, 0)
        return jnp.concatenate([f[:-8], jnp.where(self.sub < 7, f[-8:], 0.0)], axis=0)

    def before_y(self, f):
        f = pltpu.roll(f, 1, 0)
        return jnp.concatenate([jnp.where(self.sub > 0, f[:8], 0.0), f[8:]], axis=0)

    def after_z(self, f):
        return jnp.where(self.lane < self.breadth - 1, pltpu.roll(f, self.breadth - 1, 1), 0.0)

    def before_z(self, f):
        return jnp.where(self.lane > 0, pltpu.roll(f, 1, 1), 0.0)

    def up_y(self, f):
        return self.after_y(f) - f

    def up_z(self, f):
        return self.after_z(f) - f

    def down_y(self, f):
        return f - self.before_y(f)

    def down_z(self, f):
        return f - self.before_z(f)

    def magnetic_yz(self, e, e_next):
        ex, ey, ez = e
        if e_next is None:
            return self.up_z(ex) + ez, -ey - self.up_y(ex)
        return self.up_z(ex) - (e_next[2] - ez), (e_next[1] - ey) - self.up_y(ex)

    def magnetic_x(self, e):
        return self.up_y(e[2]) - self.up_z(e[1])

    def curl_back(self, comp, hx, hy, hz, before):
        if comp == 0:
            return self.down_y(hz) - self.down_z(hy)
        if comp == 1:
            return self.down_z(hx) - (hz - before[1])
        return (hy - before[0]) - self.down_y(hx)


def angular_of(freq):
    angular = F32(0.25)
    for bit, factor in ((1, 1.25), (2, 1.25**2), (4, 1.25**4)):
        angular = angular * jnp.where((freq & bit) != 0, F32(factor), F32(1.0))
    return angular


def split(number, size):
    if size & (size - 1):
        return number // size, number % size
    return number >> (size.bit_length() - 1), number & (size - 1)


class Point:
    def __init__(self, cell, first, steps):
        plane, inner = split(cell, steps.height * steps.breadth)
        row, lane = split(inner, steps.breadth)
        block, sub = split(row, 8)
        self.plane = plane - first
        self.rows = pl.ds(pl.multiple_of(block * 8, 8), 8)
        self.row, self.sub, self.lane, self.steps = row, sub, lane, steps

    def add_to(self, ref, low, high, shift, weight):
        reached = (self.plane >= low) & (self.plane < high)
        here = (self.steps.sub == self.sub) & (self.steps.lane[:8] == self.lane)
        amount = jnp.where(here, jnp.where(reached, F32(RELAX), F32(0.0)), 0.0)
        plane = jnp.clip(self.plane, low, high - 1) + shift
        for part in range(2):
            for comp in range(3):
                at = (part, comp, plane, self.rows)
                ref[at] = ref[at] + amount * weight(part, comp)


def receive(got, far_in, near_in, at_end):
    got[1] = near_in[: got.shape[1]]

    @pl.when(at_end)
    def _():
        got[0] = jnp.zeros(got.shape[1:], got.dtype)

    @pl.when(jnp.logical_not(at_end))
    def _():
        got[0] = far_in[: got.shape[1]]


def first_kernel(s, planes_ref, *refs):
    if s == 0:
        cond_ref, back_ref, weight_ref, cell_ref, group_ref, freq_ref = refs[:6]
        far_ref, near_ref, own_ref, edge_ref, held_ref, later_ref, field_ref = refs[6:13]
        raw, weight_of, cell, group, freq, sent, sems = refs[13:]
        count = planes_ref.shape[0]
        small = ((group_ref, group), (freq_ref, freq), (cell_ref, cell), (weight_ref, weight_of), (cond_ref, held_ref))
        copies = [pltpu.make_async_copy(planes_ref.at[0], raw, sems.at[0])]
        copies += [pltpu.make_async_copy(a, b, sems.at[k + 1]) for k, (a, b) in enumerate(small)]
        others = [pltpu.make_async_copy(planes_ref.at[pl.ds(1, count - 1)], later_ref, sems.at[len(copies)])]
        others.append(pltpu.make_async_copy(back_ref, field_ref, sems.at[len(copies) + 1]))
        for copy in copies + others:
            copy.start()
        for copy in copies:
            copy.wait()
        angular = angular_of(freq[group[s]])
        cell_at = cell[s]

        def weight(part, comp):
            return weight_of[s, part, comp]
    else:
        scalar_ref, held_ref, far_ref, near_ref, own_ref, edge_ref, sent = refs
        raw = planes_ref.at[s - 1]
        count = planes_ref.shape[0] + 1
        others = []
        group = scalar_ref[count + s].astype(jnp.int32)
        angular = angular_of(scalar_ref[2 * count + group].astype(jnp.int32))
        cell_at = scalar_ref[s].astype(jnp.int32)
        weights_at = scalar_ref.shape[0] - 6 * count + 6 * s

        def weight(part, comp):
            return scalar_ref[weights_at + part * 3 + comp]

    depth, height, breadth = held_ref.shape
    steps = Steps(height, breadth)
    half = sent.dtype
    index = lax.axis_index("space")
    first = index * depth
    down = index & 1
    up = 1 - down
    last = depth - 1
    scales = RELAX * angular, -RELAX * angular
    point = Point(cell_at, first, steps)
    if s == 0:
        sent[up, 2 * SENT] = held_ref[last].astype(half)
        sent[down, 2 * SENT] = held_ref[0].astype(half)

    before = []
    for part in range(2):
        ey, ez = raw[part, 1, 0], raw[part, 2, 0]
        for k, f in enumerate((ey, ez)):
            sent[down, part * SENT + k] = f.astype(half)
            edge_ref[part, k] = f
        before.append((-ez, ey))
    for p in range(depth):
        for part in range(2):
            e = [raw[part, comp, p] for comp in range(3)]
            e_next = [None if comp == 0 else raw[part, comp, p + 1] for comp in range(3)] if p < last else None
            hy, hz = steps.magnetic_yz(e, e_next)
            if p == last:
                for k, f in enumerate((hy, hz)):
                    sent[up, part * SENT + k] = f.astype(half)
                    edge_ref[part, 2 + k] = f
            hx = steps.magnetic_x(e)
            coef = scales[part] * held_ref[p]
            for comp in range(3):
                curl = steps.curl_back(comp, hx, hy, hz, before[part])
                own_ref[part, comp, p] = e[comp] - RELAX * curl + coef * raw[1 - part, comp, p]
            before[part] = hy, hz
    point.add_to(own_ref, 0, depth, 0, weight)

    row = lax.broadcasted_iota(jnp.int32, (height, breadth), 0)
    at_last = jnp.where(point.plane == last, F32(1.0), F32(0.0))
    here = jnp.where((row == point.row) & (steps.lane == point.lane), RELAX * at_last, 0.0)
    for part in range(2):
        ex, ey, ez = [own_ref[part, comp, 0] for comp in range(3)]
        hy, hz = steps.up_z(ex) - own_ref[part, 2, 1], own_ref[part, 1, 1] - steps.up_y(ex)
        for k, f in enumerate((ey, ez, hy, hz)):
            sent[down, part * SENT + 2 + k] = f.astype(half)
        e = [own_ref[part, comp, last] for comp in range(3)]
        behind = steps.magnetic_yz([own_ref[part, comp, last - 1] for comp in range(3)], e)
        hy, hz = steps.magnetic_yz(e, None)
        hx = steps.magnetic_x(e)
        coef = scales[part] * held_ref[last]
        after = []
        for comp in range(3):
            curl = steps.curl_back(comp, hx, hy, hz, behind)
            value = e[comp] - RELAX * curl + coef * own_ref[1 - part, comp, last]
            after.append(value + here * weight(part, comp))
        for k, f in enumerate((hy, hz) + steps.magnetic_yz(after, None)):
            sent[up, part * SENT + 2 + k] = f.astype(half)
    far_ref[...] = sent[0]
    near_ref[...] = sent[1]
    for copy in others:
        copy.wait()


def sweep_kernel(s, count, planes, scalar_ref, own_ref, edge_ref, held_ref, field_ref, far_in, near_in, far_cond, near_cond, *refs):
    depth, height, breadth = held_ref.shape
    final = s == count - 1
    if final:
        earlier = refs[:s]
        rows_ref, far_ref, near_ref, one_, two_, got, conds, sent = refs[s:]
    else:
        rows_ref, one_, two_, got, conds = refs
    steps = Steps(height, breadth)
    index = lax.axis_index("space")
    first = index * depth
    relax_low = jnp.where(first > 0, F32(RELAX), F32(0.0))
    relax_high = jnp.where(first + depth < planes, F32(RELAX), F32(0.0))
    low = index & 1
    high = 1 - low
    receive(got, far_in, near_in, (first == 0) | (first + depth == planes))
    conds[0] = far_cond[2 * SENT]
    conds[1] = near_cond[2 * SENT]
    group = scalar_ref[count + s].astype(jnp.int32)
    angular = angular_of(scalar_ref[2 * count + group].astype(jnp.int32))
    scales = RELAX * angular, -RELAX * angular
    point = Point(scalar_ref[s].astype(jnp.int32), first, steps)
    weights_at = scalar_ref.shape[0] - 6 * count + 6 * s

    def conductivity(p):
        if p < 0:
            return conds[low].astype(F32)
        if p >= depth:
            return conds[high].astype(F32)
        return held_ref[p]

    def received(side, part, k):
        return got[side, part * SENT + k].astype(F32)

    def weight(part, comp):
        return scalar_ref[weights_at + part * 3 + comp]

    for part in range(2):
        ey, ez, ly, lz = [edge_ref[part, k] for k in range(4)]
        one_[part, 0, 0] = -relax_low * (steps.down_y(ey) + steps.down_z(ez))
        one_[part, 1, 0] = relax_low * ey
        one_[part, 2, 0] = relax_low * ez
        e = [own_ref[part, comp, 0] for comp in range(3)]
        one_[part, 0, 1] = e[0]
        one_[part, 1, 1] = e[1] - RELAX * received(low, part, 1)
        one_[part, 2, 1] = e[2] + RELAX * received(low, part, 0)
        for p in range(1, depth - 1):
            for comp in range(3):
                one_[part, comp, p + 1] = own_ref[part, comp, p]
        e = [own_ref[part, comp, depth - 1] for comp in range(3)]
        high_y, high_z = received(high, part, 0), received(high, part, 1)
        one_[part, 0, depth] = e[0] - RELAX * (steps.down_y(high_y) + steps.down_z(high_z))
        one_[part, 1, depth] = e[1] + RELAX * high_y
        one_[part, 2, depth] = e[2] + RELAX * high_z
        one_[part, 1, depth + 1] = received(high, part, 2) - relax_high * lz
        one_[part, 2, depth + 1] = received(high, part, 3) + relax_high * ly

    before = [(-one_[part, 2, 0], one_[part, 1, 0]) for part in range(2)]
    for p in range(-1, depth + 1):
        relax = relax_low if p < 0 else relax_high if p == depth else F32(RELAX)
        for part in range(2):
            e = [one_[part, comp, p + 1] if comp or p < depth else None for comp in range(3)]
            if p < depth:
                hy, hz = steps.magnetic_yz(e, [None, one_[part, 1, p + 2], one_[part, 2, p + 2]])
            else:
                hy, hz = received(high, part, 4) + e[2], received(high, part, 5) - e[1]
            hx = steps.magnetic_x(e)
            coef = scales[part] * conductivity(p)
            for comp in range(1 if p == depth else 0, 3):
                curl = steps.curl_back(comp, hx, hy, hz, before[part])
                two_[part, comp, p + 1] = e[comp] - relax * curl + coef * one_[1 - part, comp, p + 1]
            if p < 0:
                hy, hz = hy + received(low, part, 2), hz + received(low, part, 3)
            before[part] = hy, hz
    for part in range(2):
        two_[part, 0, depth + 1] = jnp.zeros((height, breadth), F32)
    point.add_to(two_, 0, depth + 1, 1, weight)

    row = lax.broadcasted_iota(jnp.int32, (height, breadth), 0)
    here = (row == point.row) & (steps.lane == point.lane)
    before = []
    for part in range(2):
        e = [two_[part, comp, 0] for comp in range(3)]
        hy, hz = steps.magnetic_yz(e, [None, two_[part, 1, 1], two_[part, 2, 1]])
        before.append((hy + received(low, part, 4), hz + received(low, part, 5)))
    for p in range(depth):
        spot = jnp.where(here, jnp.where(point.plane == p, F32(RELAX), F32(0.0)), 0.0)
        after = []
        for part in range(2):
            e = [two_[part, comp, p + 1] for comp in range(3)]
            hy, hz = steps.magnetic_yz(e, [None, two_[part, 1, p + 2], two_[part, 2, p + 2]])
            hx = steps.magnetic_x(e)
            coef = scales[part] * held_ref[p]
            for comp in range(3):
                curl = steps.curl_back(comp, hx, hy, hz, before[part])
                value = e[comp] - RELAX * curl + coef * two_[1 - part, comp, p + 1]
                after.append(value + spot * weight(part, comp))
            before[part] = hy, hz
        row_re = row_im = None
        for comp in range(3):
            re, im = after[comp], after[3 + comp]
            field_re, field_im = field_ref[group, 0, comp, p], field_ref[group, 1, comp, p]
            add_re, add_im = field_re * re - field_im * im, field_re * im + field_im * re
            row_re, row_im = (add_re, add_im) if comp == 0 else (row_re + add_re, row_im + add_im)
        coef = angular * held_ref[p]
        for part, value in enumerate((row_re, row_im)):
            value = (coef * value).astype(rows_ref.dtype)
            if not final:
                rows_ref[part, p] = value
                continue
            rows_ref[s, part, p] = value
            if p >= depth - REACH:
                sent[high, s, part, p - depth + REACH] = value
            if p < REACH:
                sent[low, s, part, p] = value
    if final:
        for t, ref in enumerate(earlier):
            rows_ref[t] = ref[...]
            sent[high, t] = ref[:, depth - REACH :]
            sent[low, t] = ref[:, :REACH]
        far_ref[...] = sent[0]
        near_ref[...] = sent[1]


def in_plane(steps, f):
    total = (steps.after_y(f) + steps.before_y(f)) + (steps.after_z(f) + steps.before_z(f))
    return (1.0 - 6.0 * KAPPA) * f + KAPPA * total


def smooth_kernel(planes, rows_ref, alone_ref):
    count, _, depth, height, breadth = rows_ref.shape
    steps = Steps(height, breadth)
    first = lax.axis_index("space") * depth
    below = jnp.where(first > 0, F32(KAPPA), F32(0.0))
    above = jnp.where(first + depth < planes, F32(KAPPA), F32(0.0))

    def one_row(s, part):
        value = [rows_ref[s, part, p].astype(F32) for p in range(depth)]
        once = []
        for p in range(depth):
            beside = [value[q] for q in (p - 1, p + 1) if 0 <= q < depth]
            once.append(in_plane(steps, value[p]) + KAPPA * functools.reduce(jnp.add, beside))
        once = [below * value[0]] + once + [above * value[-1]]
        for p in range(depth):
            alone_ref[s, part, p] = in_plane(steps, once[p + 1]) + KAPPA * (once[p] + once[p + 2])

    def one_source(s, _):
        for part in range(2):
            one_row(s, part)
        return 0

    lax.fori_loop(0, count, one_source, 0)


def block_kernel(cells, rows_ref, alone_ref, far_in, near_in, all_ref, smooth_ref, block_ref, got, rounded, sums, sem):
    count, _, depth, height, breadth = rows_ref.shape
    ranks = all_ref.shape[0]
    steps = Steps(height, breadth)
    many = ranks * count * 2
    index = lax.axis_index("space")
    receive(got, far_in, near_in, (index == 0) | (index == lax.axis_size("space") - 1))
    odd = index & 1
    low, high = odd, 1 - odd

    def one_row(s, part):
        value = [alone_ref[s, part, p] for p in range(depth)]
        for side, nearest, order in ((low, REACH - 1, 1), (high, 0, -1)):
            close = got[side, s, part, nearest].astype(F32)
            beyond = got[side, s, part, REACH - 1 - nearest].astype(F32)
            end = 0 if order > 0 else depth - 1
            value[end] = value[end] + (2.0 * KAPPA * in_plane(steps, close) + KAPPA * KAPPA * beyond)
            value[end + order] = value[end + order] + KAPPA * KAPPA * close
        for p in range(depth):
            rounded[s, part, p] = value[p].astype(rounded.dtype)

    def one_source(s, _):
        for part in range(2):
            one_row(s, part)
        return 0

    lax.fori_loop(0, count, one_source, 0)
    out = pltpu.make_async_copy(rounded, smooth_ref, sem)
    out.start()

    sums[...] = jnp.zeros_like(sums)

    def one_plane(p, _):
        mine = [rounded[a // 2, a % 2, p].astype(F32) for a in range(2 * count)]
        for b in range(many):
            r, t = divmod(b // 2, count)
            other = all_ref[r, t, b % 2, p].astype(F32)
            for a in range(2 * count):
                prod = mine[a] * other
                total = prod[:8]
                for k in range(8, height, 8):
                    total = total + prod[k : k + 8]
                sums[a * many + b] = sums[a * many + b] + total
        return 0

    lax.fori_loop(0, depth, one_plane, 0)
    half = jnp.bfloat16
    ones = jnp.ones((breadth, breadth), half)
    for a in range(2 * count):
        table = sums[a * many : (a + 1) * many].reshape(many * 8, breadth)
        coarse = table.astype(half)
        fine = (table - coarse.astype(F32)).astype(half)
        table = jnp.dot(coarse, ones, preferred_element_type=F32) + jnp.dot(fine, ones, preferred_element_type=F32)
        line = None
        for b in range(many):
            add = jnp.where(steps.lane[:8] == b, table[b * 8 : b * 8 + 8], 0.0)
            line = add if line is None else line + add
        line = jnp.sum(line, axis=0, keepdims=True) * (1.0 / cells)
        for peer in range(block_ref.shape[0]):
            block_ref[peer, a : a + 1, :] = line[:, :many]
    out.wait()


def in_hbm(x):
    return pltpu.with_memory_space_constraint(x, pltpu.HBM)


def shards(conductivity, background, warm_start, data_weight, recv_cell, src_group, group_freq):
    count = warm_start.shape[0]
    depth, height, breadth = conductivity.shape
    plane = (height, breadth)
    peers = lax.axis_size("space")
    ranks = lax.axis_size("rx")
    cells = depth * height * breadth * peers
    half = jnp.bfloat16
    integers = jnp.concatenate([recv_cell, src_group, group_freq]).astype(F32)
    scalars = jnp.concatenate([integers, data_weight.reshape(-1)])
    assert peers % 2 == 0 and ranks % 2 == 0
    both = ("rx", "space")
    far = [(r * peers + i, r * peers + i + 1) for r in range(ranks) for i in range(1, peers - 1, 2)]
    far += [(r * peers + i, (r + 1) * peers + i) for r in range(0, ranks, 2) for i in (0, peers - 1)]
    near = [(i, i + 1) for i in range(0, peers, 2)]
    far, near = [pairs + [(j, i) for i, j in pairs] for pairs in (far, near)]
    shape = jax.ShapeDtypeStruct

    own, edges, fars, nears = [], [], [], []
    for s in range(count):
        message = shape((2 * SENT + (s == 0),) + plane, half)
        outs = [message, message, shape(warm_start.shape[1:], F32), shape((2, 4) + plane, F32)]
        scratch = [pltpu.VMEM((2,) + message.shape, half)]
        if s == 0:
            operands = [warm_start, conductivity, background, data_weight, recv_cell, src_group, group_freq]
            operands = [in_hbm(x) for x in operands]
            specs = [HBM] * 7
            outs += [
                shape(conductivity.shape, F32),
                shape((count - 1,) + warm_start.shape[1:], F32),
                shape(background.shape, F32),
            ]
            scratch = [
                pltpu.VMEM(warm_start.shape[1:], F32),
                pltpu.SMEM(data_weight.shape, F32),
                pltpu.SMEM(recv_cell.shape, jnp.int32),
                pltpu.SMEM(src_group.shape, jnp.int32),
                pltpu.SMEM(group_freq.shape, jnp.int32),
            ] + scratch + [pltpu.SemaphoreType.DMA((8,))]
        else:
            operands = [later, scalars, held]
            specs = [FULL, SCALARS, FULL]
        result = pl.pallas_call(
            functools.partial(first_kernel, s),
            out_shape=tuple(outs),
            in_specs=specs,
            out_specs=(FULL,) * len(outs),
            scratch_shapes=scratch,
            compiler_params=KERNEL,
            name="first_sweep",
        )(*operands)
        if s == 0:
            held, later, field = result[4:]
        own.append(result[2])
        edges.append(result[3])
        fars.append(lax.ppermute(result[0], both, far))
        nears.append(lax.ppermute(result[1], "space", near))

    rows_of = shape((count, 2, depth) + plane, half)
    ends_of = shape((count, 2, REACH) + plane, half)
    earlier = []
    for s in range(count):
        operands = [scalars, own[s], edges[s], held, field, fars[s], nears[s], fars[0], nears[0]]
        scratch = [
            pltpu.VMEM((2, 3, depth + 2) + plane, F32),
            pltpu.VMEM((2, 3, depth + 2) + plane, F32),
            pltpu.VMEM((2, 2 * SENT) + plane, half),
            pltpu.VMEM((2,) + plane, half),
        ]
        results = (shape((2, depth) + plane, half),)
        if s == count - 1:
            operands += earlier
            results = (rows_of, ends_of, ends_of)
            scratch.append(pltpu.VMEM((2,) + ends_of.shape, half))
        results = pl.pallas_call(
            functools.partial(sweep_kernel, s, count, peers * depth),
            out_shape=results,
            in_specs=[SCALARS] + [FULL] * (len(operands) - 1),
            out_specs=(FULL,) * len(results),
            scratch_shapes=scratch,
            compiler_params=KERNEL,
            name="sweeps",
        )(*operands)
        earlier.append(results[0])
    rows, to_far, to_near = results
    from_far = lax.ppermute(to_far, both, far)
    from_near = lax.ppermute(to_near, "space", near)
    every = lax.all_gather(rows, "rx", axis=0)

    many = 2 * count * ranks
    alone = pl.pallas_call(
        functools.partial(smooth_kernel, peers * depth),
        out_shape=shape(rows_of.shape, F32),
        in_specs=[FULL],
        out_specs=FULL,
        compiler_params=KERNEL,
        name="smooth",
    )(rows)
    smoothed, partial_block = pl.pallas_call(
        functools.partial(block_kernel, cells),
        out_shape=(rows_of, shape((peers, 2 * count, many), F32)),
        in_specs=[FULL] * 5,
        out_specs=(HBM, FULL),
        scratch_shapes=[
            pltpu.VMEM((2,) + ends_of.shape, half),
            pltpu.VMEM(rows_of.shape, half),
            pltpu.VMEM((2 * count * many, 8, breadth), F32),
            pltpu.SemaphoreType.DMA,
        ],
        compiler_params=KERNEL,
        name="block",
    )(rows, alone, from_far, from_near, every)
    backwards = [list(range(peers - 1, -1, -1))]
    pieces = lax.all_to_all(partial_block, "space", 0, 0, axis_index_groups=backwards)
    return (jnp.sum(pieces, axis=0), smoothed)


def solution(mesh):
    in_specs = (
        P("space", None, None),
        P(None, None, None, "space", None, None),
        P("rx", None, None, "space", None, None),
        P("rx", None, None),
        P("rx"),
        P("rx"),
        P(),
    )
    out_specs = (P("rx", None), P("rx", None, "space", None, None))
    return jax.shard_map(shards, mesh=mesh, in_specs=in_specs, out_specs=out_specs, check_vma=False)
```

```python
import functools

import jax
import jax.numpy as jnp
from jax import lax
from jax.experimental import pallas as pl
from jax.experimental.pallas import tpu as pltpu
from jax.sharding import PartitionSpec as P

SENT = 6
RELAX = 0.2
KAPPA = 0.1
REACH = 2
FULL = pl.BlockSpec(memory_space=pltpu.VMEM)
HBM = pl.BlockSpec(memory_space=pltpu.HBM)
SCALARS = pl.BlockSpec(memory_space=pltpu.SMEM)
KERNEL = pltpu.CompilerParams(vmem_limit_bytes=8 * 2**20)
F32 = jnp.float32


class Steps:
    def __init__(self, height, breadth):
        self.height, self.breadth = height, breadth
        self.sub = lax.broadcasted_iota(jnp.int32, (8, breadth), 0)
        self.lane = lax.broadcasted_iota(jnp.int32, (height, breadth), 1)

    def after_y(self, f):
        f = pltpu.roll(f, self.height - 1, 0)
        return jnp.concatenate([f[:-8], jnp.where(self.sub < 7, f[-8:], 0.0)], axis=0)

    def before_y(self, f):
        f = pltpu.roll(f, 1, 0)
        return jnp.concatenate([jnp.where(self.sub > 0, f[:8], 0.0), f[8:]], axis=0)

    def after_z(self, f):
        return jnp.where(self.lane < self.breadth - 1, pltpu.roll(f, self.breadth - 1, 1), 0.0)

    def before_z(self, f):
        return jnp.where(self.lane > 0, pltpu.roll(f, 1, 1), 0.0)

    def up_y(self, f):
        return self.after_y(f) - f

    def up_z(self, f):
        return self.after_z(f) - f

    def down_y(self, f):
        return f - self.before_y(f)

    def down_z(self, f):
        return f - self.before_z(f)

    def magnetic_yz(self, e, e_next):
        ex, ey, ez = e
        if e_next is None:
            return self.up_z(ex) + ez, -ey - self.up_y(ex)
        return self.up_z(ex) - (e_next[2] - ez), (e_next[1] - ey) - self.up_y(ex)

    def magnetic_x(self, e):
        return self.up_y(e[2]) - self.up_z(e[1])

    def curl_back(self, comp, hx, hy, hz, before):
        if comp == 0:
            return self.down_y(hz) - self.down_z(hy)
        if comp == 1:
            return self.down_z(hx) - (hz - before[1])
        return (hy - before[0]) - self.down_y(hx)


def angular_of(freq):
    angular = F32(0.25)
    for bit, factor in ((1, 1.25), (2, 1.25**2), (4, 1.25**4)):
        angular = angular * jnp.where((freq & bit) != 0, F32(factor), F32(1.0))
    return angular


def split(number, size):
    if size & (size - 1):
        return number // size, number % size
    return number >> (size.bit_length() - 1), number & (size - 1)


class Point:
    def __init__(self, cell, first, steps):
        plane, inner = split(cell, steps.height * steps.breadth)
        row, lane = split(inner, steps.breadth)
        block, sub = split(row, 8)
        self.plane = plane - first
        self.rows = pl.ds(pl.multiple_of(block * 8, 8), 8)
        self.row, self.sub, self.lane, self.steps = row, sub, lane, steps

    def add_to(self, ref, low, high, shift, weight):
        reached = (self.plane >= low) & (self.plane < high)
        here = (self.steps.sub == self.sub) & (self.steps.lane[:8] == self.lane)
        amount = jnp.where(here, jnp.where(reached, F32(RELAX), F32(0.0)), 0.0)
        plane = jnp.clip(self.plane, low, high - 1) + shift
        for part in range(2):
            for comp in range(3):
                at = (part, comp, plane, self.rows)
                ref[at] = ref[at] + amount * weight(part, comp)


def receive(got, far_in, near_in, at_end):
    got[1] = near_in[: got.shape[1]]

    @pl.when(at_end)
    def _():
        got[0] = jnp.zeros(got.shape[1:], got.dtype)

    @pl.when(jnp.logical_not(at_end))
    def _():
        got[0] = far_in[: got.shape[1]]


def first_kernel(s, planes_ref, *refs):
    if s == 0:
        cond_ref, back_ref, weight_ref, cell_ref, group_ref, freq_ref = refs[:6]
        far_ref, near_ref, own_ref, edge_ref, held_ref, later_ref, field_ref = refs[6:13]
        raw, weight_of, cell, group, freq, sent, sems = refs[13:]
        count = planes_ref.shape[0]
        small = ((group_ref, group), (freq_ref, freq), (cell_ref, cell), (weight_ref, weight_of), (cond_ref, held_ref))
        copies = [pltpu.make_async_copy(planes_ref.at[0], raw, sems.at[0])]
        copies += [pltpu.make_async_copy(a, b, sems.at[k + 1]) for k, (a, b) in enumerate(small)]
        others = [pltpu.make_async_copy(planes_ref.at[pl.ds(1, count - 1)], later_ref, sems.at[len(copies)])]
        others.append(pltpu.make_async_copy(back_ref, field_ref, sems.at[len(copies) + 1]))
        for copy in copies + others:
            copy.start()
        for copy in copies:
            copy.wait()
        angular = angular_of(freq[group[s]])
        cell_at = cell[s]

        def weight(part, comp):
            return weight_of[s, part, comp]
    else:
        scalar_ref, held_ref, far_ref, near_ref, own_ref, edge_ref, sent = refs
        raw = planes_ref.at[s - 1]
        count = planes_ref.shape[0] + 1
        others = []
        group = scalar_ref[count + s].astype(jnp.int32)
        angular = angular_of(scalar_ref[2 * count + group].astype(jnp.int32))
        cell_at = scalar_ref[s].astype(jnp.int32)
        weights_at = scalar_ref.shape[0] - 6 * count + 6 * s

        def weight(part, comp):
            return scalar_ref[weights_at + part * 3 + comp]

    depth, height, breadth = held_ref.shape
    steps = Steps(height, breadth)
    half = sent.dtype
    index = lax.axis_index("space")
    first = index * depth
    down = index & 1
    up = 1 - down
    last = depth - 1
    scales = RELAX * angular, -RELAX * angular
    point = Point(cell_at, first, steps)
    if s == 0:
        sent[up, 2 * SENT] = held_ref[last].astype(half)
        sent[down, 2 * SENT] = held_ref[0].astype(half)

    before = []
    for part in range(2):
        ey, ez = raw[part, 1, 0], raw[part, 2, 0]
        for k, f in enumerate((ey, ez)):
            sent[down, part * SENT + k] = f.astype(half)
            edge_ref[part, k] = f
        before.append((-ez, ey))
    for p in range(depth):
        for part in range(2):
            e = [raw[part, comp, p] for comp in range(3)]
            e_next = [None if comp == 0 else raw[part, comp, p + 1] for comp in range(3)] if p < last else None
            hy, hz = steps.magnetic_yz(e, e_next)
            if p == last:
                for k, f in enumerate((hy, hz)):
                    sent[up, part * SENT + k] = f.astype(half)
                    edge_ref[part, 2 + k] = f
            hx = steps.magnetic_x(e)
            coef = scales[part] * held_ref[p]
            for comp in range(3):
                curl = steps.curl_back(comp, hx, hy, hz, before[part])
                own_ref[part, comp, p] = e[comp] - RELAX * curl + coef * raw[1 - part, comp, p]
            before[part] = hy, hz
    point.add_to(own_ref, 0, depth, 0, weight)

    row = lax.broadcasted_iota(jnp.int32, (height, breadth), 0)
    at_last = jnp.where(point.plane == last, F32(1.0), F32(0.0))
    here = jnp.where((row == point.row) & (steps.lane == point.lane), RELAX * at_last, 0.0)
    for part in range(2):
        ex, ey, ez = [own_ref[part, comp, 0] for comp in range(3)]
        hy, hz = steps.up_z(ex) - own_ref[part, 2, 1], own_ref[part, 1, 1] - steps.up_y(ex)
        for k, f in enumerate((ey, ez, hy, hz)):
            sent[down, part * SENT + 2 + k] = f.astype(half)
        e = [own_ref[part, comp, last] for comp in range(3)]
        behind = steps.magnetic_yz([own_ref[part, comp, last - 1] for comp in range(3)], e)
        hy, hz = steps.magnetic_yz(e, None)
        hx = steps.magnetic_x(e)
        coef = scales[part] * held_ref[last]
        after = []
        for comp in range(3):
            curl = steps.curl_back(comp, hx, hy, hz, behind)
            value = e[comp] - RELAX * curl + coef * own_ref[1 - part, comp, last]
            after.append(value + here * weight(part, comp))
        for k, f in enumerate((hy, hz) + steps.magnetic_yz(after, None)):
            sent[up, part * SENT + 2 + k] = f.astype(half)
    far_ref[...] = sent[0]
    near_ref[...] = sent[1]
    for copy in others:
        copy.wait()


def sweep_kernel(s, count, planes, scalar_ref, own_ref, edge_ref, held_ref, field_ref, far_in, near_in, far_cond, near_cond, *refs):
    depth, height, breadth = held_ref.shape
    final = s == count - 1
    earlier = refs[:s] if final else ()
    rows_ref, far_ref, near_ref, one_, two_, got, conds, sent = refs[len(earlier) :]
    steps = Steps(height, breadth)
    index = lax.axis_index("space")
    first = index * depth
    relax_low = jnp.where(first > 0, F32(RELAX), F32(0.0))
    relax_high = jnp.where(first + depth < planes, F32(RELAX), F32(0.0))
    low = index & 1
    high = 1 - low
    receive(got, far_in, near_in, (first == 0) | (first + depth == planes))
    conds[0] = far_cond[2 * SENT]
    conds[1] = near_cond[2 * SENT]
    group = scalar_ref[count + s].astype(jnp.int32)
    angular = angular_of(scalar_ref[2 * count + group].astype(jnp.int32))
    scales = RELAX * angular, -RELAX * angular
    point = Point(scalar_ref[s].astype(jnp.int32), first, steps)
    weights_at = scalar_ref.shape[0] - 6 * count + 6 * s

    def conductivity(p):
        if p < 0:
            return conds[low].astype(F32)
        if p >= depth:
            return conds[high].astype(F32)
        return held_ref[p]

    def received(side, part, k):
        return got[side, part * SENT + k].astype(F32)

    def weight(part, comp):
        return scalar_ref[weights_at + part * 3 + comp]

    for part in range(2):
        ey, ez, ly, lz = [edge_ref[part, k] for k in range(4)]
        one_[part, 0, 0] = -relax_low * (steps.down_y(ey) + steps.down_z(ez))
        one_[part, 1, 0] = relax_low * ey
        one_[part, 2, 0] = relax_low * ez
        e = [own_ref[part, comp, 0] for comp in range(3)]
        one_[part, 0, 1] = e[0]
        one_[part, 1, 1] = e[1] - RELAX * received(low, part, 1)
        one_[part, 2, 1] = e[2] + RELAX * received(low, part, 0)
        for p in range(1, depth - 1):
            for comp in range(3):
                one_[part, comp, p + 1] = own_ref[part, comp, p]
        e = [own_ref[part, comp, depth - 1] for comp in range(3)]
        high_y, high_z = received(high, part, 0), received(high, part, 1)
        one_[part, 0, depth] = e[0] - RELAX * (steps.down_y(high_y) + steps.down_z(high_z))
        one_[part, 1, depth] = e[1] + RELAX * high_y
        one_[part, 2, depth] = e[2] + RELAX * high_z
        one_[part, 1, depth + 1] = received(high, part, 2) - relax_high * lz
        one_[part, 2, depth + 1] = received(high, part, 3) + relax_high * ly

    before = [(-one_[part, 2, 0], one_[part, 1, 0]) for part in range(2)]
    for p in range(-1, depth + 1):
        relax = relax_low if p < 0 else relax_high if p == depth else F32(RELAX)
        for part in range(2):
            e = [one_[part, comp, p + 1] if comp or p < depth else None for comp in range(3)]
            if p < depth:
                hy, hz = steps.magnetic_yz(e, [None, one_[part, 1, p + 2], one_[part, 2, p + 2]])
            else:
                hy, hz = received(high, part, 4) + e[2], received(high, part, 5) - e[1]
            hx = steps.magnetic_x(e)
            coef = scales[part] * conductivity(p)
            for comp in range(1 if p == depth else 0, 3):
                curl = steps.curl_back(comp, hx, hy, hz, before[part])
                two_[part, comp, p + 1] = e[comp] - relax * curl + coef * one_[1 - part, comp, p + 1]
            if p < 0:
                hy, hz = hy + received(low, part, 2), hz + received(low, part, 3)
            before[part] = hy, hz
    for part in range(2):
        two_[part, 0, depth + 1] = jnp.zeros((height, breadth), F32)
    point.add_to(two_, 0, depth + 1, 1, weight)

    row = lax.broadcasted_iota(jnp.int32, (height, breadth), 0)
    here = (row == point.row) & (steps.lane == point.lane)
    before = []
    for part in range(2):
        e = [two_[part, comp, 0] for comp in range(3)]
        hy, hz = steps.magnetic_yz(e, [None, two_[part, 1, 1], two_[part, 2, 1]])
        before.append((hy + received(low, part, 4), hz + received(low, part, 5)))
    for p in range(depth):
        spot = jnp.where(here, jnp.where(point.plane == p, F32(RELAX), F32(0.0)), 0.0)
        after = []
        for part in range(2):
            e = [two_[part, comp, p + 1] for comp in range(3)]
            hy, hz = steps.magnetic_yz(e, [None, two_[part, 1, p + 2], two_[part, 2, p + 2]])
            hx = steps.magnetic_x(e)
            coef = scales[part] * held_ref[p]
            for comp in range(3):
                curl = steps.curl_back(comp, hx, hy, hz, before[part])
                value = e[comp] - RELAX * curl + coef * two_[1 - part, comp, p + 1]
                after.append(value + spot * weight(part, comp))
            before[part] = hy, hz
        row_re = row_im = None
        for comp in range(3):
            re, im = after[comp], after[3 + comp]
            field_re, field_im = field_ref[group, 0, comp, p], field_ref[group, 1, comp, p]
            add_re, add_im = field_re * re - field_im * im, field_re * im + field_im * re
            row_re, row_im = (add_re, add_im) if comp == 0 else (row_re + add_re, row_im + add_im)
        coef = angular * held_ref[p]
        for part, value in enumerate((row_re, row_im)):
            value = (coef * value).astype(rows_ref.dtype)
            if final:
                rows_ref[s, part, p] = value
            else:
                rows_ref[part, p] = value
            if p >= depth - REACH:
                sent[high, part, p - depth + REACH] = value
            if p < REACH:
                sent[low, part, p] = value
    for t, ref in enumerate(earlier):
        rows_ref[t] = ref[...]
    far_ref[...] = sent[0]
    near_ref[...] = sent[1]


def in_plane(steps, f):
    total = (steps.after_y(f) + steps.before_y(f)) + (steps.after_z(f) + steps.before_z(f))
    return (1.0 - 6.0 * KAPPA) * f + KAPPA * total


def smooth_kernel(planes, rows_ref, alone_ref):
    count, _, depth, height, breadth = rows_ref.shape
    steps = Steps(height, breadth)
    first = lax.axis_index("space") * depth
    below = jnp.where(first > 0, F32(KAPPA), F32(0.0))
    above = jnp.where(first + depth < planes, F32(KAPPA), F32(0.0))

    def one_row(s, part):
        value = [rows_ref[s, part, p].astype(F32) for p in range(depth)]
        once = []
        for p in range(depth):
            beside = [value[q] for q in (p - 1, p + 1) if 0 <= q < depth]
            once.append(in_plane(steps, value[p]) + KAPPA * functools.reduce(jnp.add, beside))
        once = [below * value[0]] + once + [above * value[-1]]
        for p in range(depth):
            alone_ref[s, part, p] = in_plane(steps, once[p + 1]) + KAPPA * (once[p] + once[p + 2])

    def one_source(s, _):
        for part in range(2):
            one_row(s, part)
        return 0

    lax.fori_loop(0, count, one_source, 0)


def block_kernel(cells, rows_ref, alone_ref, all_ref, *refs):
    count, _, depth, height, breadth = rows_ref.shape
    ranks = all_ref.shape[0]
    steps = Steps(height, breadth)
    many = ranks * count * 2
    fars, nears = refs[:count], refs[count : 2 * count]
    smooth_ref, block_ref, got, rounded, sums, sem = refs[2 * count :]
    index = lax.axis_index("space")
    at_end = (index == 0) | (index == lax.axis_size("space") - 1)
    for s in range(count):
        receive(got.at[s], fars[s], nears[s], at_end)
    odd = index & 1
    low, high = odd, 1 - odd

    def one_row(s, part):
        value = [alone_ref[s, part, p] for p in range(depth)]
        for side, nearest, order in ((low, REACH - 1, 1), (high, 0, -1)):
            close = got[s, side, part, nearest].astype(F32)
            beyond = got[s, side, part, REACH - 1 - nearest].astype(F32)
            end = 0 if order > 0 else depth - 1
            value[end] = value[end] + (2.0 * KAPPA * in_plane(steps, close) + KAPPA * KAPPA * beyond)
            value[end + order] = value[end + order] + KAPPA * KAPPA * close
        for p in range(depth):
            rounded[s, part, p] = value[p].astype(rounded.dtype)

    def one_source(s, _):
        for part in range(2):
            one_row(s, part)
        return 0

    lax.fori_loop(0, count, one_source, 0)
    out = pltpu.make_async_copy(rounded, smooth_ref, sem)
    out.start()

    sums[...] = jnp.zeros_like(sums)

    def one_plane(p, _):
        mine = [rounded[a // 2, a % 2, p].astype(F32) for a in range(2 * count)]
        for b in range(many):
            r, t = divmod(b // 2, count)
            other = all_ref[r, t, b % 2, p].astype(F32)
            for a in range(2 * count):
                prod = mine[a] * other
                total = prod[:8]
                for k in range(8, height, 8):
                    total = total + prod[k : k + 8]
                sums[a * many + b] = sums[a * many + b] + total
        return 0

    lax.fori_loop(0, depth, one_plane, 0)
    half = jnp.bfloat16
    ones = jnp.ones((breadth, breadth), half)
    for a in range(2 * count):
        table = sums[a * many : (a + 1) * many].reshape(many * 8, breadth)
        coarse = table.astype(half)
        fine = (table - coarse.astype(F32)).astype(half)
        table = jnp.dot(coarse, ones, preferred_element_type=F32) + jnp.dot(fine, ones, preferred_element_type=F32)
        line = None
        for b in range(many):
            add = jnp.where(steps.lane[:8] == b, table[b * 8 : b * 8 + 8], 0.0)
            line = add if line is None else line + add
        line = jnp.sum(line, axis=0, keepdims=True) * (1.0 / cells)
        for peer in range(block_ref.shape[0]):
            block_ref[peer, a : a + 1, :] = line[:, :many]
    out.wait()


def in_hbm(x):
    return pltpu.with_memory_space_constraint(x, pltpu.HBM)


def shards(conductivity, background, warm_start, data_weight, recv_cell, src_group, group_freq):
    count = warm_start.shape[0]
    depth, height, breadth = conductivity.shape
    plane = (height, breadth)
    peers = lax.axis_size("space")
    ranks = lax.axis_size("rx")
    cells = depth * height * breadth * peers
    half = jnp.bfloat16
    integers = jnp.concatenate([recv_cell, src_group, group_freq]).astype(F32)
    scalars = jnp.concatenate([integers, data_weight.reshape(-1)])
    assert peers % 2 == 0 and ranks % 2 == 0
    both = ("rx", "space")
    far = [(r * peers + i, r * peers + i + 1) for r in range(ranks) for i in range(1, peers - 1, 2)]
    far += [(r * peers + i, (r + 1) * peers + i) for r in range(0, ranks, 2) for i in (0, peers - 1)]
    near = [(i, i + 1) for i in range(0, peers, 2)]
    far, near = [pairs + [(j, i) for i, j in pairs] for pairs in (far, near)]
    shape = jax.ShapeDtypeStruct

    own, edges, fars, nears = [], [], [], []
    for s in range(count):
        message = shape((2 * SENT + (s == 0),) + plane, half)
        outs = [message, message, shape(warm_start.shape[1:], F32), shape((2, 4) + plane, F32)]
        scratch = [pltpu.VMEM((2,) + message.shape, half)]
        if s == 0:
            operands = [warm_start, conductivity, background, data_weight, recv_cell, src_group, group_freq]
            operands = [in_hbm(x) for x in operands]
            specs = [HBM] * 7
            outs += [
                shape(conductivity.shape, F32),
                shape((count - 1,) + warm_start.shape[1:], F32),
                shape(background.shape, F32),
            ]
            scratch = [
                pltpu.VMEM(warm_start.shape[1:], F32),
                pltpu.SMEM(data_weight.shape, F32),
                pltpu.SMEM(recv_cell.shape, jnp.int32),
                pltpu.SMEM(src_group.shape, jnp.int32),
                pltpu.SMEM(group_freq.shape, jnp.int32),
            ] + scratch + [pltpu.SemaphoreType.DMA((8,))]
        else:
            operands = [later, scalars, held]
            specs = [FULL, SCALARS, FULL]
        result = pl.pallas_call(
            functools.partial(first_kernel, s),
            out_shape=tuple(outs),
            in_specs=specs,
            out_specs=(FULL,) * len(outs),
            scratch_shapes=scratch,
            compiler_params=KERNEL,
            name="first_sweep",
        )(*operands)
        if s == 0:
            held, later, field = result[4:]
        own.append(result[2])
        edges.append(result[3])
        fars.append(lax.ppermute(result[0], both, far))
        nears.append(lax.ppermute(result[1], "space", near))

    rows_of = shape((count, 2, depth) + plane, half)
    ends_of = shape((2, REACH) + plane, half)
    earlier, far_ends, near_ends = [], [], []
    for s in range(count):
        operands = [scalars, own[s], edges[s], held, field, fars[s], nears[s], fars[0], nears[0]]
        if s == count - 1:
            operands += earlier
        results = pl.pallas_call(
            functools.partial(sweep_kernel, s, count, peers * depth),
            out_shape=(rows_of if s == count - 1 else shape(rows_of.shape[1:], half), ends_of, ends_of),
            in_specs=[SCALARS] + [FULL] * (len(operands) - 1),
            out_specs=(FULL,) * 3,
            scratch_shapes=[
                pltpu.VMEM((2, 3, depth + 2) + plane, F32),
                pltpu.VMEM((2, 3, depth + 2) + plane, F32),
                pltpu.VMEM((2, 2 * SENT) + plane, half),
                pltpu.VMEM((2,) + plane, half),
                pltpu.VMEM((2,) + ends_of.shape, half),
            ],
            compiler_params=KERNEL,
            name="sweeps",
        )(*operands)
        earlier.append(results[0])
        far_ends.append(lax.ppermute(results[1], both, far))
        near_ends.append(lax.ppermute(results[2], "space", near))
    rows = earlier[-1]
    every = lax.all_gather(rows, "rx", axis=0)

    many = 2 * count * ranks
    alone = pl.pallas_call(
        functools.partial(smooth_kernel, peers * depth),
        out_shape=shape(rows_of.shape, F32),
        in_specs=[FULL],
        out_specs=FULL,
        compiler_params=KERNEL,
        name="smooth",
    )(rows)
    smoothed, partial_block = pl.pallas_call(
        functools.partial(block_kernel, cells),
        out_shape=(rows_of, shape((peers, 2 * count, many), F32)),
        in_specs=[FULL] * (3 + 2 * count),
        out_specs=(HBM, FULL),
        scratch_shapes=[
            pltpu.VMEM((count, 2) + ends_of.shape, half),
            pltpu.VMEM(rows_of.shape, half),
            pltpu.VMEM((2 * count * many, 8, breadth), F32),
            pltpu.SemaphoreType.DMA,
        ],
        compiler_params=KERNEL,
        name="block",
    )(rows, alone, every, *far_ends, *near_ends)
    backwards = [list(range(peers - 1, -1, -1))]
    pieces = lax.all_to_all(partial_block, "space", 0, 0, axis_index_groups=backwards)
    return (jnp.sum(pieces, axis=0), smoothed)


def solution(mesh):
    in_specs = (
        P("space", None, None),
        P(None, None, None, "space", None, None),
        P("rx", None, None, "space", None, None),
        P("rx", None, None),
        P("rx"),
        P("rx"),
        P(),
    )
    out_specs = (P("rx", None), P("rx", None, "space", None, None))
    return jax.shard_map(shards, mesh=mesh, in_specs=in_specs, out_specs=out_specs, check_vma=False)
```

```python
import functools

import jax
import jax.numpy as jnp
from jax import lax
from jax.experimental import pallas as pl
from jax.experimental.pallas import tpu as pltpu
from jax.sharding import PartitionSpec as P

SENT = 6
RELAX = 0.2
KAPPA = 0.1
REACH = 2
FULL = pl.BlockSpec(memory_space=pltpu.VMEM)
HBM = pl.BlockSpec(memory_space=pltpu.HBM)
SCALARS = pl.BlockSpec(memory_space=pltpu.SMEM)
KERNEL = pltpu.CompilerParams(vmem_limit_bytes=8 * 2**20)
F32 = jnp.float32


class Steps:
    def __init__(self, height, breadth):
        self.height, self.breadth = height, breadth
        self.sub = lax.broadcasted_iota(jnp.int32, (8, breadth), 0)
        self.lane = lax.broadcasted_iota(jnp.int32, (height, breadth), 1)

    def after_y(self, f):
        f = pltpu.roll(f, self.height - 1, 0)
        return jnp.concatenate([f[:-8], jnp.where(self.sub < 7, f[-8:], 0.0)], axis=0)

    def before_y(self, f):
        f = pltpu.roll(f, 1, 0)
        return jnp.concatenate([jnp.where(self.sub > 0, f[:8], 0.0), f[8:]], axis=0)

    def after_z(self, f):
        return jnp.where(self.lane < self.breadth - 1, pltpu.roll(f, self.breadth - 1, 1), 0.0)

    def before_z(self, f):
        return jnp.where(self.lane > 0, pltpu.roll(f, 1, 1), 0.0)

    def up_y(self, f):
        return self.after_y(f) - f

    def up_z(self, f):
        return self.after_z(f) - f

    def down_y(self, f):
        return f - self.before_y(f)

    def down_z(self, f):
        return f - self.before_z(f)

    def magnetic_yz(self, e, e_next):
        ex, ey, ez = e
        if e_next is None:
            return self.up_z(ex) + ez, -ey - self.up_y(ex)
        return self.up_z(ex) - (e_next[2] - ez), (e_next[1] - ey) - self.up_y(ex)

    def magnetic_x(self, e):
        return self.up_y(e[2]) - self.up_z(e[1])

    def curl_back(self, comp, hx, hy, hz, before):
        if comp == 0:
            return self.down_y(hz) - self.down_z(hy)
        if comp == 1:
            return self.down_z(hx) - (hz - before[1])
        return (hy - before[0]) - self.down_y(hx)


def angular_of(freq):
    angular = F32(0.25)
    for bit, factor in ((1, 1.25), (2, 1.25**2), (4, 1.25**4)):
        angular = angular * jnp.where((freq & bit) != 0, F32(factor), F32(1.0))
    return angular


def split(number, size):
    if size & (size - 1):
        return number // size, number % size
    return number >> (size.bit_length() - 1), number & (size - 1)


class Point:
    def __init__(self, cell, first, steps):
        plane, inner = split(cell, steps.height * steps.breadth)
        row, lane = split(inner, steps.breadth)
        block, sub = split(row, 8)
        self.plane = plane - first
        self.rows = pl.ds(pl.multiple_of(block * 8, 8), 8)
        self.row, self.sub, self.lane, self.steps = row, sub, lane, steps

    def add_to(self, ref, low, high, shift, weight):
        reached = (self.plane >= low) & (self.plane < high)
        here = (self.steps.sub == self.sub) & (self.steps.lane[:8] == self.lane)
        amount = jnp.where(here, jnp.where(reached, F32(RELAX), F32(0.0)), 0.0)
        plane = jnp.clip(self.plane, low, high - 1) + shift
        for part in range(2):
            for comp in range(3):
                at = (part, comp, plane, self.rows)
                ref[at] = ref[at] + amount * weight(part, comp)


def by_parity(far_ref, near_ref, body):
    odd = lax.axis_index("space") & 1

    @pl.when(odd == 0)
    def _():
        body(far_ref, near_ref)

    @pl.when(odd == 1)
    def _():
        body(near_ref, far_ref)


def first_kernel(s, planes_ref, *refs):
    if s == 0:
        cond_ref, back_ref, weight_ref, cell_ref, group_ref, freq_ref = refs[:6]
        far_ref, near_ref, own_ref, edge_ref, held_ref, later_ref, field_ref = refs[6:13]
        raw, weight_of, cell, group, freq, sems = refs[13:]
        count = planes_ref.shape[0]
        small = ((group_ref, group), (freq_ref, freq), (cell_ref, cell), (weight_ref, weight_of), (cond_ref, held_ref))
        copies = [pltpu.make_async_copy(planes_ref.at[0], raw, sems.at[0])]
        copies += [pltpu.make_async_copy(a, b, sems.at[k + 1]) for k, (a, b) in enumerate(small)]
        others = [pltpu.make_async_copy(planes_ref.at[pl.ds(1, count - 1)], later_ref, sems.at[len(copies)])]
        others.append(pltpu.make_async_copy(back_ref, field_ref, sems.at[len(copies) + 1]))
        for copy in copies + others:
            copy.start()
        for copy in copies:
            copy.wait()
        angular = angular_of(freq[group[s]])
        cell_at = cell[s]

        def weight(part, comp):
            return weight_of[s, part, comp]
    else:
        scalar_ref, held_ref, far_ref, near_ref, own_ref, edge_ref = refs
        raw = planes_ref.at[s - 1]
        count = planes_ref.shape[0] + 1
        others = []
        group = scalar_ref[count + s].astype(jnp.int32)
        angular = angular_of(scalar_ref[2 * count + group].astype(jnp.int32))
        cell_at = scalar_ref[s].astype(jnp.int32)
        weights_at = scalar_ref.shape[0] - 6 * count + 6 * s

        def weight(part, comp):
            return scalar_ref[weights_at + part * 3 + comp]

    depth, height, breadth = held_ref.shape
    steps = Steps(height, breadth)
    half = far_ref.dtype
    index = lax.axis_index("space")
    first = index * depth
    last = depth - 1
    scales = RELAX * angular, -RELAX * angular
    point = Point(cell_at, first, steps)
    def sweep_and_send(down_ref, up_ref):
        if s == 0:
            up_ref[2 * SENT] = held_ref[last].astype(half)
            down_ref[2 * SENT] = held_ref[0].astype(half)

        before = []
        for part in range(2):
            ey, ez = raw[part, 1, 0], raw[part, 2, 0]
            for k, f in enumerate((ey, ez)):
                down_ref[part * SENT + k] = f.astype(half)
                edge_ref[part, k] = f
            before.append((-ez, ey))
        for p in range(depth):
            for part in range(2):
                e = [raw[part, comp, p] for comp in range(3)]
                e_next = [None if comp == 0 else raw[part, comp, p + 1] for comp in range(3)] if p < last else None
                hy, hz = steps.magnetic_yz(e, e_next)
                if p == last:
                    for k, f in enumerate((hy, hz)):
                        up_ref[part * SENT + k] = f.astype(half)
                        edge_ref[part, 2 + k] = f
                hx = steps.magnetic_x(e)
                coef = scales[part] * held_ref[p]
                for comp in range(3):
                    curl = steps.curl_back(comp, hx, hy, hz, before[part])
                    own_ref[part, comp, p] = e[comp] - RELAX * curl + coef * raw[1 - part, comp, p]
                before[part] = hy, hz
        point.add_to(own_ref, 0, depth, 0, weight)

        row = lax.broadcasted_iota(jnp.int32, (height, breadth), 0)
        at_last = jnp.where(point.plane == last, F32(1.0), F32(0.0))
        here = jnp.where((row == point.row) & (steps.lane == point.lane), RELAX * at_last, 0.0)
        for part in range(2):
            ex, ey, ez = [own_ref[part, comp, 0] for comp in range(3)]
            hy, hz = steps.up_z(ex) - own_ref[part, 2, 1], own_ref[part, 1, 1] - steps.up_y(ex)
            for k, f in enumerate((ey, ez, hy, hz)):
                down_ref[part * SENT + 2 + k] = f.astype(half)
            e = [own_ref[part, comp, last] for comp in range(3)]
            behind = steps.magnetic_yz([own_ref[part, comp, last - 1] for comp in range(3)], e)
            hy, hz = steps.magnetic_yz(e, None)
            hx = steps.magnetic_x(e)
            coef = scales[part] * held_ref[last]
            after = []
            for comp in range(3):
                curl = steps.curl_back(comp, hx, hy, hz, behind)
                value = e[comp] - RELAX * curl + coef * own_ref[1 - part, comp, last]
                after.append(value + here * weight(part, comp))
            for k, f in enumerate((hy, hz) + steps.magnetic_yz(after, None)):
                up_ref[part * SENT + 2 + k] = f.astype(half)

    by_parity(far_ref, near_ref, sweep_and_send)
    for copy in others:
        copy.wait()


def sweep_kernel(s, count, planes, scalar_ref, own_ref, edge_ref, held_ref, field_ref, far_in, near_in, far_cond, near_cond, *refs):
    depth, height, breadth = held_ref.shape
    final = s == count - 1
    if final:
        earlier = refs[:s]
        rows_ref, far_ref, near_ref, one_, two_ = refs[s:]
    else:
        rows_ref, one_, two_ = refs
    steps = Steps(height, breadth)
    index = lax.axis_index("space")
    first = index * depth
    relax_low = jnp.where(first > 0, F32(RELAX), F32(0.0))
    relax_high = jnp.where(first + depth < planes, F32(RELAX), F32(0.0))
    inside_low = jnp.where(first > 0, F32(1.0), F32(0.0))
    inside_high = jnp.where(first + depth < planes, F32(1.0), F32(0.0))
    group = scalar_ref[count + s].astype(jnp.int32)
    angular = angular_of(scalar_ref[2 * count + group].astype(jnp.int32))
    scales = RELAX * angular, -RELAX * angular
    point = Point(scalar_ref[s].astype(jnp.int32), first, steps)
    weights_at = scalar_ref.shape[0] - 6 * count + 6 * s

    def sweeps(low_in, high_in, low_cond, high_cond, to_low, to_high):
        def conductivity(p):
            if p < 0:
                return low_cond[2 * SENT].astype(F32)
            if p >= depth:
                return high_cond[2 * SENT].astype(F32)
            return held_ref[p]

        def received(side, part, k):
            return side[part * SENT + k].astype(F32)

        def weight(part, comp):
            return scalar_ref[weights_at + part * 3 + comp]

        for part in range(2):
            ey, ez, ly, lz = [edge_ref[part, k] for k in range(4)]
            one_[part, 0, 0] = -relax_low * (steps.down_y(ey) + steps.down_z(ez))
            one_[part, 1, 0] = relax_low * ey
            one_[part, 2, 0] = relax_low * ez
            e = [own_ref[part, comp, 0] for comp in range(3)]
            one_[part, 0, 1] = e[0]
            one_[part, 1, 1] = e[1] - relax_low * received(low_in, part, 1)
            one_[part, 2, 1] = e[2] + relax_low * received(low_in, part, 0)
            for p in range(1, depth - 1):
                for comp in range(3):
                    one_[part, comp, p + 1] = own_ref[part, comp, p]
            e = [own_ref[part, comp, depth - 1] for comp in range(3)]
            high_y, high_z = received(high_in, part, 0), received(high_in, part, 1)
            one_[part, 0, depth] = e[0] - relax_high * (steps.down_y(high_y) + steps.down_z(high_z))
            one_[part, 1, depth] = e[1] + relax_high * high_y
            one_[part, 2, depth] = e[2] + relax_high * high_z
            one_[part, 1, depth + 1] = inside_high * received(high_in, part, 2) - relax_high * lz
            one_[part, 2, depth + 1] = inside_high * received(high_in, part, 3) + relax_high * ly

        before = [(-one_[part, 2, 0], one_[part, 1, 0]) for part in range(2)]
        for p in range(-1, depth + 1):
            relax = relax_low if p < 0 else relax_high if p == depth else F32(RELAX)
            for part in range(2):
                e = [one_[part, comp, p + 1] if comp or p < depth else None for comp in range(3)]
                if p < depth:
                    hy, hz = steps.magnetic_yz(e, [None, one_[part, 1, p + 2], one_[part, 2, p + 2]])
                else:
                    hy, hz = received(high_in, part, 4) + e[2], received(high_in, part, 5) - e[1]
                hx = steps.magnetic_x(e)
                coef = scales[part] * conductivity(p)
                for comp in range(1 if p == depth else 0, 3):
                    curl = steps.curl_back(comp, hx, hy, hz, before[part])
                    two_[part, comp, p + 1] = e[comp] - relax * curl + coef * one_[1 - part, comp, p + 1]
                if p < 0:
                    hy, hz = hy + inside_low * received(low_in, part, 2), hz + inside_low * received(low_in, part, 3)
                before[part] = hy, hz
        for part in range(2):
            two_[part, 0, depth + 1] = jnp.zeros((height, breadth), F32)
        point.add_to(two_, 0, depth + 1, 1, weight)

        row = lax.broadcasted_iota(jnp.int32, (height, breadth), 0)
        here = (row == point.row) & (steps.lane == point.lane)
        before = []
        for part in range(2):
            e = [two_[part, comp, 0] for comp in range(3)]
            hy, hz = steps.magnetic_yz(e, [None, two_[part, 1, 1], two_[part, 2, 1]])
            before.append((hy + inside_low * received(low_in, part, 4), hz + inside_low * received(low_in, part, 5)))
        for p in range(depth):
            spot = jnp.where(here, jnp.where(point.plane == p, F32(RELAX), F32(0.0)), 0.0)
            after = []
            for part in range(2):
                e = [two_[part, comp, p + 1] for comp in range(3)]
                hy, hz = steps.magnetic_yz(e, [None, two_[part, 1, p + 2], two_[part, 2, p + 2]])
                hx = steps.magnetic_x(e)
                coef = scales[part] * held_ref[p]
                for comp in range(3):
                    curl = steps.curl_back(comp, hx, hy, hz, before[part])
                    value = e[comp] - RELAX * curl + coef * two_[1 - part, comp, p + 1]
                    after.append(value + spot * weight(part, comp))
                before[part] = hy, hz
            row_re = row_im = None
            for comp in range(3):
                re, im = after[comp], after[3 + comp]
                field_re, field_im = field_ref[group, 0, comp, p], field_ref[group, 1, comp, p]
                add_re, add_im = field_re * re - field_im * im, field_re * im + field_im * re
                row_re, row_im = (add_re, add_im) if comp == 0 else (row_re + add_re, row_im + add_im)
            coef = angular * held_ref[p]
            for part, value in enumerate((row_re, row_im)):
                value = (coef * value).astype(rows_ref.dtype)
                if not final:
                    rows_ref[part, p] = value
                    continue
                rows_ref[s, part, p] = value
                if p >= depth - REACH:
                    to_high[s, part, p - depth + REACH] = value
                if p < REACH:
                    to_low[s, part, p] = value
        if final:
            for t, ref in enumerate(earlier):
                rows_ref[t] = ref[...]
                to_high[t] = ref[:, depth - REACH :]
                to_low[t] = ref[:, :REACH]

    far = far_in, far_cond, far_ref if final else None
    near = near_in, near_cond, near_ref if final else None
    by_parity(far, near, lambda low, high: sweeps(low[0], high[0], low[1], high[1], low[2], high[2]))


def in_plane(steps, f):
    total = (steps.after_y(f) + steps.before_y(f)) + (steps.after_z(f) + steps.before_z(f))
    return (1.0 - 6.0 * KAPPA) * f + KAPPA * total


def smooth_kernel(planes, rows_ref, alone_ref):
    count, _, depth, height, breadth = rows_ref.shape
    steps = Steps(height, breadth)
    first = lax.axis_index("space") * depth
    below = jnp.where(first > 0, F32(KAPPA), F32(0.0))
    above = jnp.where(first + depth < planes, F32(KAPPA), F32(0.0))

    def one_row(s, part):
        value = [rows_ref[s, part, p].astype(F32) for p in range(depth)]
        once = []
        for p in range(depth):
            beside = [value[q] for q in (p - 1, p + 1) if 0 <= q < depth]
            once.append(in_plane(steps, value[p]) + KAPPA * functools.reduce(jnp.add, beside))
        once = [below * value[0]] + once + [above * value[-1]]
        for p in range(depth):
            alone_ref[s, part, p] = in_plane(steps, once[p + 1]) + KAPPA * (once[p] + once[p + 2])

    def one_source(s, _):
        for part in range(2):
            one_row(s, part)
        return 0

    lax.fori_loop(0, count, one_source, 0)


def block_kernel(cells, rows_ref, alone_ref, far_in, near_in, all_ref, smooth_ref, block_ref, rounded, sums, sem):
    count, _, depth, height, breadth = rows_ref.shape
    ranks = all_ref.shape[0]
    steps = Steps(height, breadth)
    many = ranks * count * 2
    index = lax.axis_index("space")
    inside_low = jnp.where(index > 0, F32(KAPPA), F32(0.0))
    inside_high = jnp.where(index < lax.axis_size("space") - 1, F32(KAPPA), F32(0.0))

    def one_row(low_in, high_in, s, part):
        value = [alone_ref[s, part, p] for p in range(depth)]
        ends = (low_in, REACH - 1, 1, inside_low), (high_in, 0, -1, inside_high)
        for side, nearest, order, kappa in ends:
            close = side[s, part, nearest].astype(F32)
            beyond = side[s, part, REACH - 1 - nearest].astype(F32)
            end = 0 if order > 0 else depth - 1
            value[end] = value[end] + kappa * (2.0 * in_plane(steps, close) + KAPPA * beyond)
            value[end + order] = value[end + order] + kappa * (KAPPA * close)
        for p in range(depth):
            rounded[s, part, p] = value[p].astype(rounded.dtype)

    def join_rows(low_in, high_in):
        def one_source(s, _):
            for part in range(2):
                one_row(low_in, high_in, s, part)
            return 0

        lax.fori_loop(0, count, one_source, 0)

    by_parity(far_in, near_in, join_rows)
    out = pltpu.make_async_copy(rounded, smooth_ref, sem)
    out.start()

    sums[...] = jnp.zeros_like(sums)

    def one_plane(p, _):
        mine = [rounded[a // 2, a % 2, p].astype(F32) for a in range(2 * count)]
        for b in range(many):
            r, t = divmod(b // 2, count)
            other = all_ref[r, t, b % 2, p].astype(F32)
            for a in range(2 * count):
                prod = mine[a] * other
                total = prod[:8]
                for k in range(8, height, 8):
                    total = total + prod[k : k + 8]
                sums[a * many + b] = sums[a * many + b] + total
        return 0

    lax.fori_loop(0, depth, one_plane, 0)
    half = jnp.bfloat16
    ones = jnp.ones((breadth, breadth), half)
    for a in range(2 * count):
        table = sums[a * many : (a + 1) * many].reshape(many * 8, breadth)
        coarse = table.astype(half)
        fine = (table - coarse.astype(F32)).astype(half)
        table = jnp.dot(coarse, ones, preferred_element_type=F32) + jnp.dot(fine, ones, preferred_element_type=F32)
        line = None
        for b in range(many):
            add = jnp.where(steps.lane[:8] == b, table[b * 8 : b * 8 + 8], 0.0)
            line = add if line is None else line + add
        line = jnp.sum(line, axis=0, keepdims=True) * (1.0 / cells)
        for peer in range(block_ref.shape[0]):
            block_ref[peer, a : a + 1, :] = line[:, :many]
    out.wait()


def in_hbm(x):
    return pltpu.with_memory_space_constraint(x, pltpu.HBM)


def shards(conductivity, background, warm_start, data_weight, recv_cell, src_group, group_freq):
    count = warm_start.shape[0]
    depth, height, breadth = conductivity.shape
    plane = (height, breadth)
    peers = lax.axis_size("space")
    ranks = lax.axis_size("rx")
    cells = depth * height * breadth * peers
    half = jnp.bfloat16
    integers = jnp.concatenate([recv_cell, src_group, group_freq]).astype(F32)
    scalars = jnp.concatenate([integers, data_weight.reshape(-1)])
    assert peers % 2 == 0 and ranks % 2 == 0
    both = ("rx", "space")
    far = [(r * peers + i, r * peers + i + 1) for r in range(ranks) for i in range(1, peers - 1, 2)]
    far += [(r * peers + i, (r + 1) * peers + i) for r in range(0, ranks, 2) for i in (0, peers - 1)]
    near = [(i, i + 1) for i in range(0, peers, 2)]
    far, near = [pairs + [(j, i) for i, j in pairs] for pairs in (far, near)]
    shape = jax.ShapeDtypeStruct

    own, edges, fars, nears = [], [], [], []
    for s in range(count):
        message = shape((2 * SENT + (s == 0),) + plane, half)
        outs = [message, message, shape(warm_start.shape[1:], F32), shape((2, 4) + plane, F32)]
        scratch = []
        if s == 0:
            operands = [warm_start, conductivity, background, data_weight, recv_cell, src_group, group_freq]
            operands = [in_hbm(x) for x in operands]
            specs = [HBM] * 7
            outs += [
                shape(conductivity.shape, F32),
                shape((count - 1,) + warm_start.shape[1:], F32),
                shape(background.shape, F32),
            ]
            scratch = [
                pltpu.VMEM(warm_start.shape[1:], F32),
                pltpu.SMEM(data_weight.shape, F32),
                pltpu.SMEM(recv_cell.shape, jnp.int32),
                pltpu.SMEM(src_group.shape, jnp.int32),
                pltpu.SMEM(group_freq.shape, jnp.int32),
            ] + scratch + [pltpu.SemaphoreType.DMA((8,))]
        else:
            operands = [later, scalars, held]
            specs = [FULL, SCALARS, FULL]
        result = pl.pallas_call(
            functools.partial(first_kernel, s),
            out_shape=tuple(outs),
            in_specs=specs,
            out_specs=(FULL,) * len(outs),
            scratch_shapes=scratch,
            compiler_params=KERNEL,
            name="first_sweep",
        )(*operands)
        if s == 0:
            held, later, field = result[4:]
        own.append(result[2])
        edges.append(result[3])
        fars.append(lax.ppermute(result[0], both, far))
        nears.append(lax.ppermute(result[1], "space", near))

    rows_of = shape((count, 2, depth) + plane, half)
    ends_of = shape((count, 2, REACH) + plane, half)
    earlier = []
    for s in range(count):
        operands = [scalars, own[s], edges[s], held, field, fars[s], nears[s], fars[0], nears[0]]
        scratch = [
            pltpu.VMEM((2, 3, depth + 2) + plane, F32),
            pltpu.VMEM((2, 3, depth + 2) + plane, F32),
        ]
        results = (shape((2, depth) + plane, half),)
        if s == count - 1:
            operands += earlier
            results = (rows_of, ends_of, ends_of)
        results = pl.pallas_call(
            functools.partial(sweep_kernel, s, count, peers * depth),
            out_shape=results,
            in_specs=[SCALARS] + [FULL] * (len(operands) - 1),
            out_specs=(FULL,) * len(results),
            scratch_shapes=scratch,
            compiler_params=KERNEL,
            name="sweeps",
        )(*operands)
        earlier.append(results[0])
    rows, to_far, to_near = results
    from_far = lax.ppermute(to_far, both, far)
    from_near = lax.ppermute(to_near, "space", near)
    every = lax.all_gather(rows, "rx", axis=0)

    many = 2 * count * ranks
    alone = pl.pallas_call(
        functools.partial(smooth_kernel, peers * depth),
        out_shape=shape(rows_of.shape, F32),
        in_specs=[FULL],
        out_specs=FULL,
        compiler_params=KERNEL,
        name="smooth",
    )(rows)
    smoothed, partial_block = pl.pallas_call(
        functools.partial(block_kernel, cells),
        out_shape=(rows_of, shape((peers, 2 * count, many), F32)),
        in_specs=[FULL] * 5,
        out_specs=(HBM, FULL),
        scratch_shapes=[
            pltpu.VMEM(rows_of.shape, half),
            pltpu.VMEM((2 * count * many, 8, breadth), F32),
            pltpu.SemaphoreType.DMA,
        ],
        compiler_params=KERNEL,
        name="block",
    )(rows, alone, from_far, from_near, every)
    backwards = [list(range(peers - 1, -1, -1))]
    pieces = lax.all_to_all(partial_block, "space", 0, 0, axis_index_groups=backwards)
    return (jnp.sum(pieces, axis=0), smoothed)


def solution(mesh):
    in_specs = (
        P("space", None, None),
        P(None, None, None, "space", None, None),
        P("rx", None, None, "space", None, None),
        P("rx", None, None),
        P("rx"),
        P("rx"),
        P(),
    )
    out_specs = (P("rx", None), P("rx", None, "space", None, None))
    return jax.shard_map(shards, mesh=mesh, in_specs=in_specs, out_specs=out_specs, check_vma=False)
```

```python
import functools

import jax
import jax.numpy as jnp
from jax import lax
from jax.experimental import pallas as pl
from jax.experimental.pallas import tpu as pltpu
from jax.sharding import PartitionSpec as P

SENT = 6
RELAX = 0.2
KAPPA = 0.1
REACH = 2
FULL = pl.BlockSpec(memory_space=pltpu.VMEM)
HBM = pl.BlockSpec(memory_space=pltpu.HBM)
SCALARS = pl.BlockSpec(memory_space=pltpu.SMEM)
KERNEL = pltpu.CompilerParams(vmem_limit_bytes=8 * 2**20)
F32 = jnp.float32


class Steps:
    def __init__(self, height, breadth):
        self.height, self.breadth = height, breadth
        self.sub = lax.broadcasted_iota(jnp.int32, (8, breadth), 0)
        self.lane = lax.broadcasted_iota(jnp.int32, (height, breadth), 1)

    def after_y(self, f):
        f = pltpu.roll(f, self.height - 1, 0)
        return jnp.concatenate([f[:-8], jnp.where(self.sub < 7, f[-8:], 0.0)], axis=0)

    def before_y(self, f):
        f = pltpu.roll(f, 1, 0)
        return jnp.concatenate([jnp.where(self.sub > 0, f[:8], 0.0), f[8:]], axis=0)

    def after_z(self, f):
        return jnp.where(self.lane < self.breadth - 1, pltpu.roll(f, self.breadth - 1, 1), 0.0)

    def before_z(self, f):
        return jnp.where(self.lane > 0, pltpu.roll(f, 1, 1), 0.0)

    def up_y(self, f):
        return self.after_y(f) - f

    def up_z(self, f):
        return self.after_z(f) - f

    def down_y(self, f):
        return f - self.before_y(f)

    def down_z(self, f):
        return f - self.before_z(f)

    def magnetic_yz(self, e, e_next):
        ex, ey, ez = e
        if e_next is None:
            return self.up_z(ex) + ez, -ey - self.up_y(ex)
        return self.up_z(ex) - (e_next[2] - ez), (e_next[1] - ey) - self.up_y(ex)

    def magnetic_x(self, e):
        return self.up_y(e[2]) - self.up_z(e[1])

    def curl_back(self, comp, hx, hy, hz, before):
        if comp == 0:
            return self.down_y(hz) - self.down_z(hy)
        if comp == 1:
            return self.down_z(hx) - (hz - before[1])
        return (hy - before[0]) - self.down_y(hx)


def angular_of(freq):
    angular = F32(0.25)
    for bit, factor in ((1, 1.25), (2, 1.25**2), (4, 1.25**4)):
        angular = angular * jnp.where((freq & bit) != 0, F32(factor), F32(1.0))
    return angular


def split(number, size):
    if size & (size - 1):
        return number // size, number % size
    return number >> (size.bit_length() - 1), number & (size - 1)


class Point:
    def __init__(self, cell, first, steps):
        plane, inner = split(cell, steps.height * steps.breadth)
        row, lane = split(inner, steps.breadth)
        block, sub = split(row, 8)
        self.plane = plane - first
        self.rows = pl.ds(pl.multiple_of(block * 8, 8), 8)
        self.row, self.sub, self.lane, self.steps = row, sub, lane, steps

    def add_to(self, ref, low, high, shift, weight):
        reached = (self.plane >= low) & (self.plane < high)
        here = (self.steps.sub == self.sub) & (self.steps.lane[:8] == self.lane)
        amount = jnp.where(here, jnp.where(reached, F32(RELAX), F32(0.0)), 0.0)
        plane = jnp.clip(self.plane, low, high - 1) + shift
        for part in range(2):
            for comp in range(3):
                at = (part, comp, plane, self.rows)
                ref[at] = ref[at] + amount * weight(part, comp)


def receive(got, far_in, near_in, at_end):
    got[1] = near_in[: got.shape[1]]

    @pl.when(at_end)
    def _():
        got[0] = jnp.zeros(got.shape[1:], got.dtype)

    @pl.when(jnp.logical_not(at_end))
    def _():
        got[0] = far_in[: got.shape[1]]


def first_kernel(s, planes_ref, *refs):
    if s == 0:
        cond_ref, back_ref, weight_ref, cell_ref, group_ref, freq_ref = refs[:6]
        far_ref, near_ref, own_ref, edge_ref, held_ref, later_ref, field_ref = refs[6:13]
        raw, weight_of, cell, group, freq, sent, sems = refs[13:]
        count = planes_ref.shape[0]
        small = ((group_ref, group), (freq_ref, freq), (cell_ref, cell), (weight_ref, weight_of), (cond_ref, held_ref))
        copies = [pltpu.make_async_copy(planes_ref.at[0], raw, sems.at[0])]
        copies += [pltpu.make_async_copy(a, b, sems.at[k + 1]) for k, (a, b) in enumerate(small)]
        others = [pltpu.make_async_copy(planes_ref.at[pl.ds(1, count - 1)], later_ref, sems.at[len(copies)])]
        others.append(pltpu.make_async_copy(back_ref, field_ref, sems.at[len(copies) + 1]))
        for copy in copies + others:
            copy.start()
        for copy in copies:
            copy.wait()
        angular = angular_of(freq[group[s]])
        cell_at = cell[s]

        def weight(part, comp):
            return weight_of[s, part, comp]
    else:
        scalar_ref, held_ref, far_ref, near_ref, own_ref, edge_ref, sent = refs
        raw = planes_ref.at[s - 1]
        count = planes_ref.shape[0] + 1
        others = []
        group = scalar_ref[count + s].astype(jnp.int32)
        angular = angular_of(scalar_ref[2 * count + group].astype(jnp.int32))
        cell_at = scalar_ref[s].astype(jnp.int32)
        weights_at = scalar_ref.shape[0] - 6 * count + 6 * s

        def weight(part, comp):
            return scalar_ref[weights_at + part * 3 + comp]

    depth, height, breadth = held_ref.shape
    steps = Steps(height, breadth)
    half = sent.dtype
    index = lax.axis_index("space")
    first = index * depth
    down = index & 1
    up = 1 - down
    last = depth - 1
    scales = RELAX * angular, -RELAX * angular
    point = Point(cell_at, first, steps)
    if s == 0:
        sent[up, 2 * SENT] = held_ref[last].astype(half)
        sent[down, 2 * SENT] = held_ref[0].astype(half)

    before = []
    for part in range(2):
        ey, ez = raw[part, 1, 0], raw[part, 2, 0]
        for k, f in enumerate((ey, ez)):
            sent[down, part * SENT + k] = f.astype(half)
            edge_ref[part, k] = f
        before.append((-ez, ey))
    for p in range(depth):
        for part in range(2):
            e = [raw[part, comp, p] for comp in range(3)]
            e_next = [None if comp == 0 else raw[part, comp, p + 1] for comp in range(3)] if p < last else None
            hy, hz = steps.magnetic_yz(e, e_next)
            if p == last:
                for k, f in enumerate((hy, hz)):
                    sent[up, part * SENT + k] = f.astype(half)
                    edge_ref[part, 2 + k] = f
            hx = steps.magnetic_x(e)
            coef = scales[part] * held_ref[p]
            for comp in range(3):
                curl = steps.curl_back(comp, hx, hy, hz, before[part])
                own_ref[part, comp, p] = e[comp] - RELAX * curl + coef * raw[1 - part, comp, p]
            before[part] = hy, hz
    point.add_to(own_ref, 0, depth, 0, weight)

    row = lax.broadcasted_iota(jnp.int32, (height, breadth), 0)
    at_last = jnp.where(point.plane == last, F32(1.0), F32(0.0))
    here = jnp.where((row == point.row) & (steps.lane == point.lane), RELAX * at_last, 0.0)
    for part in range(2):
        ex, ey, ez = [own_ref[part, comp, 0] for comp in range(3)]
        hy, hz = steps.up_z(ex) - own_ref[part, 2, 1], own_ref[part, 1, 1] - steps.up_y(ex)
        for k, f in enumerate((ey, ez, hy, hz)):
            sent[down, part * SENT + 2 + k] = f.astype(half)
        e = [own_ref[part, comp, last] for comp in range(3)]
        behind = steps.magnetic_yz([own_ref[part, comp, last - 1] for comp in range(3)], e)
        hy, hz = steps.magnetic_yz(e, None)
        hx = steps.magnetic_x(e)
        coef = scales[part] * held_ref[last]
        after = []
        for comp in range(3):
            curl = steps.curl_back(comp, hx, hy, hz, behind)
            value = e[comp] - RELAX * curl + coef * own_ref[1 - part, comp, last]
            after.append(value + here * weight(part, comp))
        for k, f in enumerate((hy, hz) + steps.magnetic_yz(after, None)):
            sent[up, part * SENT + 2 + k] = f.astype(half)
    far_ref[...] = sent[0]
    near_ref[...] = sent[1]
    for copy in others:
        copy.wait()


def sweep_kernel(s, count, planes, scalar_ref, own_ref, edge_ref, held_ref, field_ref, near_in, far_in, near_cond, far_cond, *refs):
    depth, height, breadth = held_ref.shape
    final = s == count - 1
    if final:
        earlier = refs[:s]
        rows_ref, far_ref, near_ref, one_, two_, got, conds, sent = refs[s:]
    else:
        rows_ref, one_, two_, got, conds = refs
    steps = Steps(height, breadth)
    index = lax.axis_index("space")
    first = index * depth
    relax_low = jnp.where(first > 0, F32(RELAX), F32(0.0))
    relax_high = jnp.where(first + depth < planes, F32(RELAX), F32(0.0))
    low = index & 1
    high = 1 - low
    receive(got, far_in, near_in, (first == 0) | (first + depth == planes))
    conds[0] = far_cond[2 * SENT]
    conds[1] = near_cond[2 * SENT]
    group = scalar_ref[count + s].astype(jnp.int32)
    angular = angular_of(scalar_ref[2 * count + group].astype(jnp.int32))
    scales = RELAX * angular, -RELAX * angular
    point = Point(scalar_ref[s].astype(jnp.int32), first, steps)
    weights_at = scalar_ref.shape[0] - 6 * count + 6 * s

    def conductivity(p):
        if p < 0:
            return conds[low].astype(F32)
        if p >= depth:
            return conds[high].astype(F32)
        return held_ref[p]

    def received(side, part, k):
        return got[side, part * SENT + k].astype(F32)

    def weight(part, comp):
        return scalar_ref[weights_at + part * 3 + comp]

    for part in range(2):
        ey, ez, ly, lz = [edge_ref[part, k] for k in range(4)]
        one_[part, 0, 0] = -relax_low * (steps.down_y(ey) + steps.down_z(ez))
        one_[part, 1, 0] = relax_low * ey
        one_[part, 2, 0] = relax_low * ez
        e = [own_ref[part, comp, 0] for comp in range(3)]
        one_[part, 0, 1] = e[0]
        one_[part, 1, 1] = e[1] - RELAX * received(low, part, 1)
        one_[part, 2, 1] = e[2] + RELAX * received(low, part, 0)
        for p in range(1, depth - 1):
            for comp in range(3):
                one_[part, comp, p + 1] = own_ref[part, comp, p]
        e = [own_ref[part, comp, depth - 1] for comp in range(3)]
        high_y, high_z = received(high, part, 0), received(high, part, 1)
        one_[part, 0, depth] = e[0] - RELAX * (steps.down_y(high_y) + steps.down_z(high_z))
        one_[part, 1, depth] = e[1] + RELAX * high_y
        one_[part, 2, depth] = e[2] + RELAX * high_z
        one_[part, 1, depth + 1] = received(high, part, 2) - relax_high * lz
        one_[part, 2, depth + 1] = received(high, part, 3) + relax_high * ly

    before = [(-one_[part, 2, 0], one_[part, 1, 0]) for part in range(2)]
    for p in range(-1, depth + 1):
        relax = relax_low if p < 0 else relax_high if p == depth else F32(RELAX)
        for part in range(2):
            e = [one_[part, comp, p + 1] if comp or p < depth else None for comp in range(3)]
            if p < depth:
                hy, hz = steps.magnetic_yz(e, [None, one_[part, 1, p + 2], one_[part, 2, p + 2]])
            else:
                hy, hz = received(high, part, 4) + e[2], received(high, part, 5) - e[1]
            hx = steps.magnetic_x(e)
            coef = scales[part] * conductivity(p)
            for comp in range(1 if p == depth else 0, 3):
                curl = steps.curl_back(comp, hx, hy, hz, before[part])
                two_[part, comp, p + 1] = e[comp] - relax * curl + coef * one_[1 - part, comp, p + 1]
            if p < 0:
                hy, hz = hy + received(low, part, 2), hz + received(low, part, 3)
            before[part] = hy, hz
    for part in range(2):
        two_[part, 0, depth + 1] = jnp.zeros((height, breadth), F32)
    point.add_to(two_, 0, depth + 1, 1, weight)

    row = lax.broadcasted_iota(jnp.int32, (height, breadth), 0)
    here = (row == point.row) & (steps.lane == point.lane)
    before = []
    for part in range(2):
        e = [two_[part, comp, 0] for comp in range(3)]
        hy, hz = steps.magnetic_yz(e, [None, two_[part, 1, 1], two_[part, 2, 1]])
        before.append((hy + received(low, part, 4), hz + received(low, part, 5)))
    for p in range(depth):
        spot = jnp.where(here, jnp.where(point.plane == p, F32(RELAX), F32(0.0)), 0.0)
        after = []
        for part in range(2):
            e = [two_[part, comp, p + 1] for comp in range(3)]
            hy, hz = steps.magnetic_yz(e, [None, two_[part, 1, p + 2], two_[part, 2, p + 2]])
            hx = steps.magnetic_x(e)
            coef = scales[part] * held_ref[p]
            for comp in range(3):
                curl = steps.curl_back(comp, hx, hy, hz, before[part])
                value = e[comp] - RELAX * curl + coef * two_[1 - part, comp, p + 1]
                after.append(value + spot * weight(part, comp))
            before[part] = hy, hz
        row_re = row_im = None
        for comp in range(3):
            re, im = after[comp], after[3 + comp]
            field_re, field_im = field_ref[group, 0, comp, p], field_ref[group, 1, comp, p]
            add_re, add_im = field_re * re - field_im * im, field_re * im + field_im * re
            row_re, row_im = (add_re, add_im) if comp == 0 else (row_re + add_re, row_im + add_im)
        coef = angular * held_ref[p]
        for part, value in enumerate((row_re, row_im)):
            value = (coef * value).astype(rows_ref.dtype)
            if not final:
                rows_ref[part, p] = value
                continue
            rows_ref[s, part, p] = value
            if p >= depth - REACH:
                sent[high, s, part, p - depth + REACH] = value
            if p < REACH:
                sent[low, s, part, p] = value
    if final:
        for t, ref in enumerate(earlier):
            rows_ref[t] = ref[...]
            sent[high, t] = ref[:, depth - REACH :]
            sent[low, t] = ref[:, :REACH]
        far_ref[...] = sent[0]
        near_ref[...] = sent[1]


def in_plane(steps, f):
    total = (steps.after_y(f) + steps.before_y(f)) + (steps.after_z(f) + steps.before_z(f))
    return (1.0 - 6.0 * KAPPA) * f + KAPPA * total


def smooth_kernel(planes, rows_ref, alone_ref):
    count, _, depth, height, breadth = rows_ref.shape
    steps = Steps(height, breadth)
    first = lax.axis_index("space") * depth
    below = jnp.where(first > 0, F32(KAPPA), F32(0.0))
    above = jnp.where(first + depth < planes, F32(KAPPA), F32(0.0))

    def one_row(s, part):
        value = [rows_ref[s, part, p].astype(F32) for p in range(depth)]
        once = []
        for p in range(depth):
            beside = [value[q] for q in (p - 1, p + 1) if 0 <= q < depth]
            once.append(in_plane(steps, value[p]) + KAPPA * functools.reduce(jnp.add, beside))
        once = [below * value[0]] + once + [above * value[-1]]
        for p in range(depth):
            alone_ref[s, part, p] = in_plane(steps, once[p + 1]) + KAPPA * (once[p] + once[p + 2])

    def one_source(s, _):
        for part in range(2):
            one_row(s, part)
        return 0

    lax.fori_loop(0, count, one_source, 0)


def block_kernel(cells, rows_ref, alone_ref, far_in, near_in, all_ref, smooth_ref, block_ref, got, rounded, sums, sem):
    count, _, depth, height, breadth = rows_ref.shape
    ranks = all_ref.shape[0]
    steps = Steps(height, breadth)
    many = ranks * count * 2
    index = lax.axis_index("space")
    receive(got, far_in, near_in, (index == 0) | (index == lax.axis_size("space") - 1))
    odd = index & 1
    low, high = odd, 1 - odd

    def one_row(s, part):
        value = [alone_ref[s, part, p] for p in range(depth)]
        for side, nearest, order in ((low, REACH - 1, 1), (high, 0, -1)):
            close = got[side, s, part, nearest].astype(F32)
            beyond = got[side, s, part, REACH - 1 - nearest].astype(F32)
            end = 0 if order > 0 else depth - 1
            value[end] = value[end] + (2.0 * KAPPA * in_plane(steps, close) + KAPPA * KAPPA * beyond)
            value[end + order] = value[end + order] + KAPPA * KAPPA * close
        for p in range(depth):
            rounded[s, part, p] = value[p].astype(rounded.dtype)

    def one_source(s, _):
        for part in range(2):
            one_row(s, part)
        return 0

    lax.fori_loop(0, count, one_source, 0)
    out = pltpu.make_async_copy(rounded, smooth_ref, sem)
    out.start()

    sums[...] = jnp.zeros_like(sums)

    def one_plane(p, _):
        mine = [rounded[a // 2, a % 2, p].astype(F32) for a in range(2 * count)]
        for b in range(many):
            r, t = divmod(b // 2, count)
            other = all_ref[r, t, b % 2, p].astype(F32)
            for a in range(2 * count):
                prod = mine[a] * other
                total = prod[:8]
                for k in range(8, height, 8):
                    total = total + prod[k : k + 8]
                sums[a * many + b] = sums[a * many + b] + total
        return 0

    lax.fori_loop(0, depth, one_plane, 0)
    half = jnp.bfloat16
    ones = jnp.ones((breadth, breadth), half)
    for a in range(2 * count):
        table = sums[a * many : (a + 1) * many].reshape(many * 8, breadth)
        coarse = table.astype(half)
        fine = (table - coarse.astype(F32)).astype(half)
        table = jnp.dot(coarse, ones, preferred_element_type=F32) + jnp.dot(fine, ones, preferred_element_type=F32)
        line = None
        for b in range(many):
            add = jnp.where(steps.lane[:8] == b, table[b * 8 : b * 8 + 8], 0.0)
            line = add if line is None else line + add
        line = jnp.sum(line, axis=0, keepdims=True) * (1.0 / cells)
        for peer in range(block_ref.shape[0]):
            block_ref[peer, a : a + 1, :] = line[:, :many]
    out.wait()


def in_hbm(x):
    return pltpu.with_memory_space_constraint(x, pltpu.HBM)


def shards(conductivity, background, warm_start, data_weight, recv_cell, src_group, group_freq):
    count = warm_start.shape[0]
    depth, height, breadth = conductivity.shape
    plane = (height, breadth)
    peers = lax.axis_size("space")
    ranks = lax.axis_size("rx")
    cells = depth * height * breadth * peers
    half = jnp.bfloat16
    integers = jnp.concatenate([recv_cell, src_group, group_freq]).astype(F32)
    scalars = jnp.concatenate([integers, data_weight.reshape(-1)])
    assert peers % 2 == 0 and ranks % 2 == 0
    both = ("rx", "space")
    far = [(r * peers + i, r * peers + i + 1) for r in range(ranks) for i in range(1, peers - 1, 2)]
    far += [(r * peers + i, (r + 1) * peers + i) for r in range(0, ranks, 2) for i in (0, peers - 1)]
    near = [(i, i + 1) for i in range(0, peers, 2)]
    far, near = [pairs + [(j, i) for i, j in pairs] for pairs in (far, near)]
    shape = jax.ShapeDtypeStruct

    own, edges, fars, nears = [], [], [], []
    for s in range(count):
        message = shape((2 * SENT + (s == 0),) + plane, half)
        outs = [message, message, shape(warm_start.shape[1:], F32), shape((2, 4) + plane, F32)]
        scratch = [pltpu.VMEM((2,) + message.shape, half)]
        if s == 0:
            operands = [warm_start, conductivity, background, data_weight, recv_cell, src_group, group_freq]
            operands = [in_hbm(x) for x in operands]
            specs = [HBM] * 7
            outs += [
                shape(conductivity.shape, F32),
                shape((count - 1,) + warm_start.shape[1:], F32),
                shape(background.shape, F32),
            ]
            scratch = [
                pltpu.VMEM(warm_start.shape[1:], F32),
                pltpu.SMEM(data_weight.shape, F32),
                pltpu.SMEM(recv_cell.shape, jnp.int32),
                pltpu.SMEM(src_group.shape, jnp.int32),
                pltpu.SMEM(group_freq.shape, jnp.int32),
            ] + scratch + [pltpu.SemaphoreType.DMA((8,))]
        else:
            operands = [later, scalars, held]
            specs = [FULL, SCALARS, FULL]
        result = pl.pallas_call(
            functools.partial(first_kernel, s),
            out_shape=tuple(outs),
            in_specs=specs,
            out_specs=(FULL,) * len(outs),
            scratch_shapes=scratch,
            compiler_params=KERNEL,
            name="first_sweep",
        )(*operands)
        if s == 0:
            held, later, field = result[4:]
        own.append(result[2])
        edges.append(result[3])
        nears.append(lax.ppermute(result[1], "space", near))
        fars.append(lax.ppermute(result[0], both, far))

    rows_of = shape((count, 2, depth) + plane, half)
    ends_of = shape((count, 2, REACH) + plane, half)
    earlier = []
    for s in range(count):
        operands = [scalars, own[s], edges[s], held, field, nears[s], fars[s], nears[0], fars[0]]
        scratch = [
            pltpu.VMEM((2, 3, depth + 2) + plane, F32),
            pltpu.VMEM((2, 3, depth + 2) + plane, F32),
            pltpu.VMEM((2, 2 * SENT) + plane, half),
            pltpu.VMEM((2,) + plane, half),
        ]
        results = (shape((2, depth) + plane, half),)
        if s == count - 1:
            operands += earlier
            results = (rows_of, ends_of, ends_of)
            scratch.append(pltpu.VMEM((2,) + ends_of.shape, half))
        results = pl.pallas_call(
            functools.partial(sweep_kernel, s, count, peers * depth),
            out_shape=results,
            in_specs=[SCALARS] + [FULL] * (len(operands) - 1),
            out_specs=(FULL,) * len(results),
            scratch_shapes=scratch,
            compiler_params=KERNEL,
            name="sweeps",
        )(*operands)
        earlier.append(results[0])
    rows, to_far, to_near = results
    from_far = lax.ppermute(to_far, both, far)
    from_near = lax.ppermute(to_near, "space", near)
    every = lax.all_gather(rows, "rx", axis=0)

    many = 2 * count * ranks
    alone = pl.pallas_call(
        functools.partial(smooth_kernel, peers * depth),
        out_shape=shape(rows_of.shape, F32),
        in_specs=[FULL],
        out_specs=FULL,
        compiler_params=KERNEL,
        name="smooth",
    )(rows)
    smoothed, partial_block = pl.pallas_call(
        functools.partial(block_kernel, cells),
        out_shape=(rows_of, shape((peers, 2 * count, many), F32)),
        in_specs=[FULL] * 5,
        out_specs=(HBM, FULL),
        scratch_shapes=[
            pltpu.VMEM((2,) + ends_of.shape, half),
            pltpu.VMEM(rows_of.shape, half),
            pltpu.VMEM((2 * count * many, 8, breadth), F32),
            pltpu.SemaphoreType.DMA,
        ],
        compiler_params=KERNEL,
        name="block",
    )(rows, alone, from_far, from_near, every)
    backwards = [list(range(peers - 1, -1, -1))]
    pieces = lax.all_to_all(partial_block, "space", 0, 0, axis_index_groups=backwards)
    return (jnp.sum(pieces, axis=0), smoothed)


def solution(mesh):
    in_specs = (
        P("space", None, None),
        P(None, None, None, "space", None, None),
        P("rx", None, None, "space", None, None),
        P("rx", None, None),
        P("rx"),
        P("rx"),
        P(),
    )
    out_specs = (P("rx", None), P("rx", None, "space", None, None))
    return jax.shard_map(shards, mesh=mesh, in_specs=in_specs, out_specs=out_specs, check_vma=False)
```

```python
import functools

import jax
import jax.numpy as jnp
from jax import lax
from jax.experimental import pallas as pl
from jax.experimental.pallas import tpu as pltpu
from jax.sharding import PartitionSpec as P

SENT = 6
RELAX = 0.2
KAPPA = 0.1
REACH = 2
FULL = pl.BlockSpec(memory_space=pltpu.VMEM)
HBM = pl.BlockSpec(memory_space=pltpu.HBM)
SCALARS = pl.BlockSpec(memory_space=pltpu.SMEM)
KERNEL = pltpu.CompilerParams(vmem_limit_bytes=8 * 2**20)
F32 = jnp.float32


class Steps:
    def __init__(self, height, breadth):
        self.height, self.breadth = height, breadth
        self.sub = lax.broadcasted_iota(jnp.int32, (8, breadth), 0)
        self.lane = lax.broadcasted_iota(jnp.int32, (height, breadth), 1)

    def after_y(self, f):
        f = pltpu.roll(f, self.height - 1, 0)
        return jnp.concatenate([f[:-8], jnp.where(self.sub < 7, f[-8:], 0.0)], axis=0)

    def before_y(self, f):
        f = pltpu.roll(f, 1, 0)
        return jnp.concatenate([jnp.where(self.sub > 0, f[:8], 0.0), f[8:]], axis=0)

    def after_z(self, f):
        return jnp.where(self.lane < self.breadth - 1, pltpu.roll(f, self.breadth - 1, 1), 0.0)

    def before_z(self, f):
        return jnp.where(self.lane > 0, pltpu.roll(f, 1, 1), 0.0)

    def up_y(self, f):
        return self.after_y(f) - f

    def up_z(self, f):
        return self.after_z(f) - f

    def down_y(self, f):
        return f - self.before_y(f)

    def down_z(self, f):
        return f - self.before_z(f)

    def magnetic_yz(self, e, e_next):
        ex, ey, ez = e
        if e_next is None:
            return self.up_z(ex) + ez, -ey - self.up_y(ex)
        return self.up_z(ex) - (e_next[2] - ez), (e_next[1] - ey) - self.up_y(ex)

    def magnetic_x(self, e):
        return self.up_y(e[2]) - self.up_z(e[1])

    def curl_back(self, comp, hx, hy, hz, before):
        if comp == 0:
            return self.down_y(hz) - self.down_z(hy)
        if comp == 1:
            return self.down_z(hx) - (hz - before[1])
        return (hy - before[0]) - self.down_y(hx)


def angular_of(freq):
    angular = F32(0.25)
    for bit, factor in ((1, 1.25), (2, 1.25**2), (4, 1.25**4)):
        angular = angular * jnp.where((freq & bit) != 0, F32(factor), F32(1.0))
    return angular


def split(number, size):
    if size & (size - 1):
        return number // size, number % size
    return number >> (size.bit_length() - 1), number & (size - 1)


class Point:
    def __init__(self, cell, first, steps):
        plane, inner = split(cell, steps.height * steps.breadth)
        row, lane = split(inner, steps.breadth)
        block, sub = split(row, 8)
        self.plane = plane - first
        self.rows = pl.ds(pl.multiple_of(block * 8, 8), 8)
        self.row, self.sub, self.lane, self.steps = row, sub, lane, steps

    def add_to(self, ref, low, high, shift, weight):
        reached = (self.plane >= low) & (self.plane < high)
        here = (self.steps.sub == self.sub) & (self.steps.lane[:8] == self.lane)
        amount = jnp.where(here, jnp.where(reached, F32(RELAX), F32(0.0)), 0.0)
        plane = jnp.clip(self.plane, low, high - 1) + shift
        for part in range(2):
            for comp in range(3):
                at = (part, comp, plane, self.rows)
                ref[at] = ref[at] + amount * weight(part, comp)


def receive(got, far_in, near_in, at_end):
    got[1] = near_in[: got.shape[1]]

    @pl.when(at_end)
    def _():
        got[0] = jnp.zeros(got.shape[1:], got.dtype)

    @pl.when(jnp.logical_not(at_end))
    def _():
        got[0] = far_in[: got.shape[1]]


def first_kernel(s, planes_ref, *refs):
    if s == 0:
        cond_ref, back_ref, weight_ref, cell_ref, group_ref, freq_ref = refs[:6]
        far_ref, near_ref, own_ref, edge_ref, held_ref, later_ref, field_ref = refs[6:13]
        raw, weight_of, cell, group, freq, sent, sems = refs[13:]
        count = planes_ref.shape[0]
        small = ((group_ref, group), (freq_ref, freq), (cell_ref, cell), (weight_ref, weight_of), (cond_ref, held_ref))
        copies = [pltpu.make_async_copy(planes_ref.at[0], raw, sems.at[0])]
        copies += [pltpu.make_async_copy(a, b, sems.at[k + 1]) for k, (a, b) in enumerate(small)]
        others = [pltpu.make_async_copy(planes_ref.at[pl.ds(1, count - 1)], later_ref, sems.at[len(copies)])]
        others.append(pltpu.make_async_copy(back_ref, field_ref, sems.at[len(copies) + 1]))
        for copy in copies + others:
            copy.start()
        for copy in copies:
            copy.wait()
        angular = angular_of(freq[group[s]])
        cell_at = cell[s]

        def weight(part, comp):
            return weight_of[s, part, comp]
    else:
        scalar_ref, held_ref, far_ref, near_ref, own_ref, edge_ref, sent = refs
        raw = planes_ref.at[s - 1]
        count = planes_ref.shape[0] + 1
        others = []
        group = scalar_ref[count + s].astype(jnp.int32)
        angular = angular_of(scalar_ref[2 * count + group].astype(jnp.int32))
        cell_at = scalar_ref[s].astype(jnp.int32)
        weights_at = scalar_ref.shape[0] - 6 * count + 6 * s

        def weight(part, comp):
            return scalar_ref[weights_at + part * 3 + comp]

    depth, height, breadth = held_ref.shape
    steps = Steps(height, breadth)
    half = sent.dtype
    index = lax.axis_index("space")
    first = index * depth
    down = index & 1
    up = 1 - down
    last = depth - 1
    scales = RELAX * angular, -RELAX * angular
    point = Point(cell_at, first, steps)
    if s == 0:
        sent[up, 2 * SENT] = held_ref[last].astype(half)
        sent[down, 2 * SENT] = held_ref[0].astype(half)

    before = []
    for part in range(2):
        ey, ez = raw[part, 1, 0], raw[part, 2, 0]
        for k, f in enumerate((ey, ez)):
            sent[down, part * SENT + k] = f.astype(half)
            edge_ref[part, k] = f
        before.append((-ez, ey))
    for p in range(depth):
        for part in range(2):
            e = [raw[part, comp, p] for comp in range(3)]
            e_next = [None if comp == 0 else raw[part, comp, p + 1] for comp in range(3)] if p < last else None
            hy, hz = steps.magnetic_yz(e, e_next)
            if p == last:
                for k, f in enumerate((hy, hz)):
                    sent[up, part * SENT + k] = f.astype(half)
                    edge_ref[part, 2 + k] = f
            hx = steps.magnetic_x(e)
            coef = scales[part] * held_ref[p]
            for comp in range(3):
                curl = steps.curl_back(comp, hx, hy, hz, before[part])
                own_ref[part, comp, p] = e[comp] - RELAX * curl + coef * raw[1 - part, comp, p]
            before[part] = hy, hz
    point.add_to(own_ref, 0, depth, 0, weight)

    row = lax.broadcasted_iota(jnp.int32, (height, breadth), 0)
    at_last = jnp.where(point.plane == last, F32(1.0), F32(0.0))
    here = jnp.where((row == point.row) & (steps.lane == point.lane), RELAX * at_last, 0.0)
    for part in range(2):
        ex, ey, ez = [own_ref[part, comp, 0] for comp in range(3)]
        hy, hz = steps.up_z(ex) - own_ref[part, 2, 1], own_ref[part, 1, 1] - steps.up_y(ex)
        for k, f in enumerate((ey, ez, hy, hz)):
            sent[down, part * SENT + 2 + k] = f.astype(half)
        e = [own_ref[part, comp, last] for comp in range(3)]
        behind = steps.magnetic_yz([own_ref[part, comp, last - 1] for comp in range(3)], e)
        hy, hz = steps.magnetic_yz(e, None)
        hx = steps.magnetic_x(e)
        coef = scales[part] * held_ref[last]
        after = []
        for comp in range(3):
            curl = steps.curl_back(comp, hx, hy, hz, behind)
            value = e[comp] - RELAX * curl + coef * own_ref[1 - part, comp, last]
            after.append(value + here * weight(part, comp))
        for k, f in enumerate((hy, hz) + steps.magnetic_yz(after, None)):
            sent[up, part * SENT + 2 + k] = f.astype(half)
    far_ref[...] = sent[0]
    near_ref[...] = sent[1]
    for copy in others:
        copy.wait()


def sweep_kernel(s, count, planes, scalar_ref, own_ref, edge_ref, held_ref, field_ref, one_in, other_in, near_cond, far_cond, *refs):
    depth, height, breadth = held_ref.shape
    final = s == count - 1
    near_in, far_in = (one_in, other_in) if s == 0 else (other_in, one_in)
    if final:
        earlier = refs[:s]
        rows_ref, far_ref, near_ref, one_, two_, got, conds, sent = refs[s:]
    else:
        rows_ref, one_, two_, got, conds = refs
    steps = Steps(height, breadth)
    index = lax.axis_index("space")
    first = index * depth
    relax_low = jnp.where(first > 0, F32(RELAX), F32(0.0))
    relax_high = jnp.where(first + depth < planes, F32(RELAX), F32(0.0))
    low = index & 1
    high = 1 - low
    receive(got, far_in, near_in, (first == 0) | (first + depth == planes))
    conds[0] = far_cond[2 * SENT]
    conds[1] = near_cond[2 * SENT]
    group = scalar_ref[count + s].astype(jnp.int32)
    angular = angular_of(scalar_ref[2 * count + group].astype(jnp.int32))
    scales = RELAX * angular, -RELAX * angular
    point = Point(scalar_ref[s].astype(jnp.int32), first, steps)
    weights_at = scalar_ref.shape[0] - 6 * count + 6 * s

    def conductivity(p):
        if p < 0:
            return conds[low].astype(F32)
        if p >= depth:
            return conds[high].astype(F32)
        return held_ref[p]

    def received(side, part, k):
        return got[side, part * SENT + k].astype(F32)

    def weight(part, comp):
        return scalar_ref[weights_at + part * 3 + comp]

    for part in range(2):
        ey, ez, ly, lz = [edge_ref[part, k] for k in range(4)]
        one_[part, 0, 0] = -relax_low * (steps.down_y(ey) + steps.down_z(ez))
        one_[part, 1, 0] = relax_low * ey
        one_[part, 2, 0] = relax_low * ez
        e = [own_ref[part, comp, 0] for comp in range(3)]
        one_[part, 0, 1] = e[0]
        one_[part, 1, 1] = e[1] - RELAX * received(low, part, 1)
        one_[part, 2, 1] = e[2] + RELAX * received(low, part, 0)
        for p in range(1, depth - 1):
            for comp in range(3):
                one_[part, comp, p + 1] = own_ref[part, comp, p]
        e = [own_ref[part, comp, depth - 1] for comp in range(3)]
        high_y, high_z = received(high, part, 0), received(high, part, 1)
        one_[part, 0, depth] = e[0] - RELAX * (steps.down_y(high_y) + steps.down_z(high_z))
        one_[part, 1, depth] = e[1] + RELAX * high_y
        one_[part, 2, depth] = e[2] + RELAX * high_z
        one_[part, 1, depth + 1] = received(high, part, 2) - relax_high * lz
        one_[part, 2, depth + 1] = received(high, part, 3) + relax_high * ly

    before = [(-one_[part, 2, 0], one_[part, 1, 0]) for part in range(2)]
    for p in range(-1, depth + 1):
        relax = relax_low if p < 0 else relax_high if p == depth else F32(RELAX)
        for part in range(2):
            e = [one_[part, comp, p + 1] if comp or p < depth else None for comp in range(3)]
            if p < depth:
                hy, hz = steps.magnetic_yz(e, [None, one_[part, 1, p + 2], one_[part, 2, p + 2]])
            else:
                hy, hz = received(high, part, 4) + e[2], received(high, part, 5) - e[1]
            hx = steps.magnetic_x(e)
            coef = scales[part] * conductivity(p)
            for comp in range(1 if p == depth else 0, 3):
                curl = steps.curl_back(comp, hx, hy, hz, before[part])
                two_[part, comp, p + 1] = e[comp] - relax * curl + coef * one_[1 - part, comp, p + 1]
            if p < 0:
                hy, hz = hy + received(low, part, 2), hz + received(low, part, 3)
            before[part] = hy, hz
    for part in range(2):
        two_[part, 0, depth + 1] = jnp.zeros((height, breadth), F32)
    point.add_to(two_, 0, depth + 1, 1, weight)

    row = lax.broadcasted_iota(jnp.int32, (height, breadth), 0)
    here = (row == point.row) & (steps.lane == point.lane)
    before = []
    for part in range(2):
        e = [two_[part, comp, 0] for comp in range(3)]
        hy, hz = steps.magnetic_yz(e, [None, two_[part, 1, 1], two_[part, 2, 1]])
        before.append((hy + received(low, part, 4), hz + received(low, part, 5)))
    for p in range(depth):
        spot = jnp.where(here, jnp.where(point.plane == p, F32(RELAX), F32(0.0)), 0.0)
        after = []
        for part in range(2):
            e = [two_[part, comp, p + 1] for comp in range(3)]
            hy, hz = steps.magnetic_yz(e, [None, two_[part, 1, p + 2], two_[part, 2, p + 2]])
            hx = steps.magnetic_x(e)
            coef = scales[part] * held_ref[p]
            for comp in range(3):
                curl = steps.curl_back(comp, hx, hy, hz, before[part])
                value = e[comp] - RELAX * curl + coef * two_[1 - part, comp, p + 1]
                after.append(value + spot * weight(part, comp))
            before[part] = hy, hz
        row_re = row_im = None
        for comp in range(3):
            re, im = after[comp], after[3 + comp]
            field_re, field_im = field_ref[group, 0, comp, p], field_ref[group, 1, comp, p]
            add_re, add_im = field_re * re - field_im * im, field_re * im + field_im * re
            row_re, row_im = (add_re, add_im) if comp == 0 else (row_re + add_re, row_im + add_im)
        coef = angular * held_ref[p]
        for part, value in enumerate((row_re, row_im)):
            value = (coef * value).astype(rows_ref.dtype)
            if not final:
                rows_ref[part, p] = value
                continue
            rows_ref[s, part, p] = value
            if p >= depth - REACH:
                sent[high, s, part, p - depth + REACH] = value
            if p < REACH:
                sent[low, s, part, p] = value
    if final:
        for t, ref in enumerate(earlier):
            rows_ref[t] = ref[...]
            sent[high, t] = ref[:, depth - REACH :]
            sent[low, t] = ref[:, :REACH]
        far_ref[...] = sent[0]
        near_ref[...] = sent[1]


def in_plane(steps, f):
    total = (steps.after_y(f) + steps.before_y(f)) + (steps.after_z(f) + steps.before_z(f))
    return (1.0 - 6.0 * KAPPA) * f + KAPPA * total


def smooth_kernel(planes, rows_ref, alone_ref):
    count, _, depth, height, breadth = rows_ref.shape
    steps = Steps(height, breadth)
    first = lax.axis_index("space") * depth
    below = jnp.where(first > 0, F32(KAPPA), F32(0.0))
    above = jnp.where(first + depth < planes, F32(KAPPA), F32(0.0))

    def one_row(s, part):
        value = [rows_ref[s, part, p].astype(F32) for p in range(depth)]
        once = []
        for p in range(depth):
            beside = [value[q] for q in (p - 1, p + 1) if 0 <= q < depth]
            once.append(in_plane(steps, value[p]) + KAPPA * functools.reduce(jnp.add, beside))
        once = [below * value[0]] + once + [above * value[-1]]
        for p in range(depth):
            alone_ref[s, part, p] = in_plane(steps, once[p + 1]) + KAPPA * (once[p] + once[p + 2])

    def one_source(s, _):
        for part in range(2):
            one_row(s, part)
        return 0

    lax.fori_loop(0, count, one_source, 0)


def block_kernel(cells, rows_ref, alone_ref, far_in, near_in, all_ref, smooth_ref, block_ref, got, rounded, sums, sem):
    count, _, depth, height, breadth = rows_ref.shape
    ranks = all_ref.shape[0]
    steps = Steps(height, breadth)
    many = ranks * count * 2
    index = lax.axis_index("space")
    receive(got, far_in, near_in, (index == 0) | (index == lax.axis_size("space") - 1))
    odd = index & 1
    low, high = odd, 1 - odd

    def one_row(s, part):
        value = [alone_ref[s, part, p] for p in range(depth)]
        for side, nearest, order in ((low, REACH - 1, 1), (high, 0, -1)):
            close = got[side, s, part, nearest].astype(F32)
            beyond = got[side, s, part, REACH - 1 - nearest].astype(F32)
            end = 0 if order > 0 else depth - 1
            value[end] = value[end] + (2.0 * KAPPA * in_plane(steps, close) + KAPPA * KAPPA * beyond)
            value[end + order] = value[end + order] + KAPPA * KAPPA * close
        for p in range(depth):
            rounded[s, part, p] = value[p].astype(rounded.dtype)

    def one_source(s, _):
        for part in range(2):
            one_row(s, part)
        return 0

    lax.fori_loop(0, count, one_source, 0)
    out = pltpu.make_async_copy(rounded, smooth_ref, sem)
    out.start()

    sums[...] = jnp.zeros_like(sums)

    def one_plane(p, _):
        mine = [rounded[a // 2, a % 2, p].astype(F32) for a in range(2 * count)]
        for b in range(many):
            r, t = divmod(b // 2, count)
            other = all_ref[r, t, b % 2, p].astype(F32)
            for a in range(2 * count):
                prod = mine[a] * other
                total = prod[:8]
                for k in range(8, height, 8):
                    total = total + prod[k : k + 8]
                sums[a * many + b] = sums[a * many + b] + total
        return 0

    lax.fori_loop(0, depth, one_plane, 0)
    half = jnp.bfloat16
    ones = jnp.ones((breadth, breadth), half)
    for a in range(2 * count):
        table = sums[a * many : (a + 1) * many].reshape(many * 8, breadth)
        coarse = table.astype(half)
        fine = (table - coarse.astype(F32)).astype(half)
        table = jnp.dot(coarse, ones, preferred_element_type=F32) + jnp.dot(fine, ones, preferred_element_type=F32)
        line = None
        for b in range(many):
            add = jnp.where(steps.lane[:8] == b, table[b * 8 : b * 8 + 8], 0.0)
            line = add if line is None else line + add
        line = jnp.sum(line, axis=0, keepdims=True) * (1.0 / cells)
        for peer in range(block_ref.shape[0]):
            block_ref[peer, a : a + 1, :] = line[:, :many]
    out.wait()


def in_hbm(x):
    return pltpu.with_memory_space_constraint(x, pltpu.HBM)


def shards(conductivity, background, warm_start, data_weight, recv_cell, src_group, group_freq):
    count = warm_start.shape[0]
    depth, height, breadth = conductivity.shape
    plane = (height, breadth)
    peers = lax.axis_size("space")
    ranks = lax.axis_size("rx")
    cells = depth * height * breadth * peers
    half = jnp.bfloat16
    integers = jnp.concatenate([recv_cell, src_group, group_freq]).astype(F32)
    scalars = jnp.concatenate([integers, data_weight.reshape(-1)])
    assert peers % 2 == 0 and ranks % 2 == 0
    both = ("rx", "space")
    far = [(r * peers + i, r * peers + i + 1) for r in range(ranks) for i in range(1, peers - 1, 2)]
    far += [(r * peers + i, (r + 1) * peers + i) for r in range(0, ranks, 2) for i in (0, peers - 1)]
    near = [(i, i + 1) for i in range(0, peers, 2)]
    far, near = [pairs + [(j, i) for i, j in pairs] for pairs in (far, near)]
    shape = jax.ShapeDtypeStruct

    own, edges, fars, nears = [], [], [], []
    for s in range(count):
        message = shape((2 * SENT + (s == 0),) + plane, half)
        outs = [message, message, shape(warm_start.shape[1:], F32), shape((2, 4) + plane, F32)]
        scratch = [pltpu.VMEM((2,) + message.shape, half)]
        if s == 0:
            operands = [warm_start, conductivity, background, data_weight, recv_cell, src_group, group_freq]
            operands = [in_hbm(x) for x in operands]
            specs = [HBM] * 7
            outs += [
                shape(conductivity.shape, F32),
                shape((count - 1,) + warm_start.shape[1:], F32),
                shape(background.shape, F32),
            ]
            scratch = [
                pltpu.VMEM(warm_start.shape[1:], F32),
                pltpu.SMEM(data_weight.shape, F32),
                pltpu.SMEM(recv_cell.shape, jnp.int32),
                pltpu.SMEM(src_group.shape, jnp.int32),
                pltpu.SMEM(group_freq.shape, jnp.int32),
            ] + scratch + [pltpu.SemaphoreType.DMA((8,))]
        else:
            operands = [later, scalars, held]
            specs = [FULL, SCALARS, FULL]
        result = pl.pallas_call(
            functools.partial(first_kernel, s),
            out_shape=tuple(outs),
            in_specs=specs,
            out_specs=(FULL,) * len(outs),
            scratch_shapes=scratch,
            compiler_params=KERNEL,
            name="first_sweep",
        )(*operands)
        if s == 0:
            held, later, field = result[4:]
        own.append(result[2])
        edges.append(result[3])
        nears.append(lax.ppermute(result[1], "space", near))
        fars.append(lax.ppermute(result[0], both, far))

    rows_of = shape((count, 2, depth) + plane, half)
    ends_of = shape((count, 2, REACH) + plane, half)
    earlier = []
    for s in range(count):
        swaps = (nears[s], fars[s]) if s == 0 else (fars[s], nears[s])
        operands = [scalars, own[s], edges[s], held, field, *swaps, nears[0], fars[0]]
        scratch = [
            pltpu.VMEM((2, 3, depth + 2) + plane, F32),
            pltpu.VMEM((2, 3, depth + 2) + plane, F32),
            pltpu.VMEM((2, 2 * SENT) + plane, half),
            pltpu.VMEM((2,) + plane, half),
        ]
        results = (shape((2, depth) + plane, half),)
        if s == count - 1:
            operands += earlier
            results = (rows_of, ends_of, ends_of)
            scratch.append(pltpu.VMEM((2,) + ends_of.shape, half))
        results = pl.pallas_call(
            functools.partial(sweep_kernel, s, count, peers * depth),
            out_shape=results,
            in_specs=[SCALARS] + [FULL] * (len(operands) - 1),
            out_specs=(FULL,) * len(results),
            scratch_shapes=scratch,
            compiler_params=KERNEL,
            name="sweeps",
        )(*operands)
        earlier.append(results[0])
    rows, to_far, to_near = results
    from_far = lax.ppermute(to_far, both, far)
    from_near = lax.ppermute(to_near, "space", near)
    every = lax.all_gather(rows, "rx", axis=0)

    many = 2 * count * ranks
    alone = pl.pallas_call(
        functools.partial(smooth_kernel, peers * depth),
        out_shape=shape(rows_of.shape, F32),
        in_specs=[FULL],
        out_specs=FULL,
        compiler_params=KERNEL,
        name="smooth",
    )(rows)
    smoothed, partial_block = pl.pallas_call(
        functools.partial(block_kernel, cells),
        out_shape=(rows_of, shape((peers, 2 * count, many), F32)),
        in_specs=[FULL] * 5,
        out_specs=(HBM, FULL),
        scratch_shapes=[
            pltpu.VMEM((2,) + ends_of.shape, half),
            pltpu.VMEM(rows_of.shape, half),
            pltpu.VMEM((2 * count * many, 8, breadth), F32),
            pltpu.SemaphoreType.DMA,
        ],
        compiler_params=KERNEL,
        name="block",
    )(rows, alone, from_far, from_near, every)
    backwards = [list(range(peers - 1, -1, -1))]
    pieces = lax.all_to_all(partial_block, "space", 0, 0, axis_index_groups=backwards)
    return (jnp.sum(pieces, axis=0), smoothed)


def solution(mesh):
    in_specs = (
        P("space", None, None),
        P(None, None, None, "space", None, None),
        P("rx", None, None, "space", None, None),
        P("rx", None, None),
        P("rx"),
        P("rx"),
        P(),
    )
    out_specs = (P("rx", None), P("rx", None, "space", None, None))
    return jax.shard_map(shards, mesh=mesh, in_specs=in_specs, out_specs=out_specs, check_vma=False)
```

```python
import functools

import jax
import jax.numpy as jnp
from jax import lax
from jax.experimental import pallas as pl
from jax.experimental.pallas import tpu as pltpu
from jax.sharding import PartitionSpec as P

SENT = 6
RELAX = 0.2
KAPPA = 0.1
REACH = 2
FULL = pl.BlockSpec(memory_space=pltpu.VMEM)
HBM = pl.BlockSpec(memory_space=pltpu.HBM)
SCALARS = pl.BlockSpec(memory_space=pltpu.SMEM)
KERNEL = pltpu.CompilerParams(vmem_limit_bytes=8 * 2**20)
F32 = jnp.float32


class Steps:
    def __init__(self, height, breadth):
        self.height, self.breadth = height, breadth
        self.sub = lax.broadcasted_iota(jnp.int32, (8, breadth), 0)
        self.lane = lax.broadcasted_iota(jnp.int32, (height, breadth), 1)

    def after_y(self, f):
        f = pltpu.roll(f, self.height - 1, 0)
        return jnp.concatenate([f[:-8], jnp.where(self.sub < 7, f[-8:], 0.0)], axis=0)

    def before_y(self, f):
        f = pltpu.roll(f, 1, 0)
        return jnp.concatenate([jnp.where(self.sub > 0, f[:8], 0.0), f[8:]], axis=0)

    def after_z(self, f):
        return jnp.where(self.lane < self.breadth - 1, pltpu.roll(f, self.breadth - 1, 1), 0.0)

    def before_z(self, f):
        return jnp.where(self.lane > 0, pltpu.roll(f, 1, 1), 0.0)

    def up_y(self, f):
        return self.after_y(f) - f

    def up_z(self, f):
        return self.after_z(f) - f

    def down_y(self, f):
        return f - self.before_y(f)

    def down_z(self, f):
        return f - self.before_z(f)

    def magnetic_yz(self, e, e_next):
        ex, ey, ez = e
        if e_next is None:
            return self.up_z(ex) + ez, -ey - self.up_y(ex)
        return self.up_z(ex) - (e_next[2] - ez), (e_next[1] - ey) - self.up_y(ex)

    def magnetic_x(self, e):
        return self.up_y(e[2]) - self.up_z(e[1])

    def curl_back(self, comp, hx, hy, hz, before):
        if comp == 0:
            return self.down_y(hz) - self.down_z(hy)
        if comp == 1:
            return self.down_z(hx) - (hz - before[1])
        return (hy - before[0]) - self.down_y(hx)


def angular_of(freq):
    angular = F32(0.25)
    for bit, factor in ((1, 1.25), (2, 1.25**2), (4, 1.25**4)):
        angular = angular * jnp.where((freq & bit) != 0, F32(factor), F32(1.0))
    return angular


def split(number, size):
    if size & (size - 1):
        return number // size, number % size
    return number >> (size.bit_length() - 1), number & (size - 1)


class Point:
    def __init__(self, cell, first, steps):
        plane, inner = split(cell, steps.height * steps.breadth)
        row, lane = split(inner, steps.breadth)
        block, sub = split(row, 8)
        self.plane = plane - first
        self.rows = pl.ds(pl.multiple_of(block * 8, 8), 8)
        self.row, self.sub, self.lane, self.steps = row, sub, lane, steps

    def add_to(self, ref, low, high, shift, weight):
        reached = (self.plane >= low) & (self.plane < high)
        here = (self.steps.sub == self.sub) & (self.steps.lane[:8] == self.lane)
        amount = jnp.where(here, jnp.where(reached, F32(RELAX), F32(0.0)), 0.0)
        plane = jnp.clip(self.plane, low, high - 1) + shift
        for part in range(2):
            for comp in range(3):
                at = (part, comp, plane, self.rows)
                ref[at] = ref[at] + amount * weight(part, comp)


def receive(got, far_in, near_in, at_end):
    got[1] = near_in[: got.shape[1]]

    @pl.when(at_end)
    def _():
        got[0] = jnp.zeros(got.shape[1:], got.dtype)

    @pl.when(jnp.logical_not(at_end))
    def _():
        got[0] = far_in[: got.shape[1]]


def first_kernel(s, planes_ref, *refs):
    if s == 0:
        cond_ref, back_ref, weight_ref, cell_ref, group_ref, freq_ref = refs[:6]
        far_ref, near_ref, own_ref, edge_ref, held_ref, later_ref, field_ref = refs[6:13]
        raw, weight_of, cell, group, freq, sent, sems = refs[13:]
        count = planes_ref.shape[0]
        small = ((group_ref, group), (freq_ref, freq), (cell_ref, cell), (weight_ref, weight_of), (cond_ref, held_ref))
        copies = [pltpu.make_async_copy(planes_ref.at[0], raw, sems.at[0])]
        copies += [pltpu.make_async_copy(a, b, sems.at[k + 1]) for k, (a, b) in enumerate(small)]
        others = [pltpu.make_async_copy(planes_ref.at[pl.ds(1, count - 1)], later_ref, sems.at[len(copies)])]
        others.append(pltpu.make_async_copy(back_ref, field_ref, sems.at[len(copies) + 1]))
        for copy in copies + others:
            copy.start()
        for copy in copies:
            copy.wait()
        angular = angular_of(freq[group[s]])
        cell_at = cell[s]

        def weight(part, comp):
            return weight_of[s, part, comp]
    else:
        scalar_ref, held_ref, far_ref, near_ref, own_ref, edge_ref, sent = refs
        raw = planes_ref.at[s - 1]
        count = planes_ref.shape[0] + 1
        others = []
        group = scalar_ref[count + s].astype(jnp.int32)
        angular = angular_of(scalar_ref[2 * count + group].astype(jnp.int32))
        cell_at = scalar_ref[s].astype(jnp.int32)
        weights_at = scalar_ref.shape[0] - 6 * count + 6 * s

        def weight(part, comp):
            return scalar_ref[weights_at + part * 3 + comp]

    depth, height, breadth = held_ref.shape
    steps = Steps(height, breadth)
    half = sent.dtype
    index = lax.axis_index("space")
    first = index * depth
    down = index & 1
    up = 1 - down
    last = depth - 1
    scales = RELAX * angular, -RELAX * angular
    point = Point(cell_at, first, steps)
    if s == 0:
        sent[up, 2 * SENT] = held_ref[last].astype(half)
        sent[down, 2 * SENT] = held_ref[0].astype(half)

    before = []
    for part in range(2):
        ey, ez = raw[part, 1, 0], raw[part, 2, 0]
        for k, f in enumerate((ey, ez)):
            sent[down, part * SENT + k] = f.astype(half)
            edge_ref[part, k] = f
        before.append((-ez, ey))
    for p in range(depth):
        for part in range(2):
            e = [raw[part, comp, p] for comp in range(3)]
            e_next = [None if comp == 0 else raw[part, comp, p + 1] for comp in range(3)] if p < last else None
            hy, hz = steps.magnetic_yz(e, e_next)
            if p == last:
                for k, f in enumerate((hy, hz)):
                    sent[up, part * SENT + k] = f.astype(half)
                    edge_ref[part, 2 + k] = f
            hx = steps.magnetic_x(e)
            coef = scales[part] * held_ref[p]
            for comp in range(3):
                curl = steps.curl_back(comp, hx, hy, hz, before[part])
                own_ref[part, comp, p] = e[comp] - RELAX * curl + coef * raw[1 - part, comp, p]
            before[part] = hy, hz
    point.add_to(own_ref, 0, depth, 0, weight)

    row = lax.broadcasted_iota(jnp.int32, (height, breadth), 0)
    at_last = jnp.where(point.plane == last, F32(1.0), F32(0.0))
    here = jnp.where((row == point.row) & (steps.lane == point.lane), RELAX * at_last, 0.0)
    for part in range(2):
        ex, ey, ez = [own_ref[part, comp, 0] for comp in range(3)]
        hy, hz = steps.up_z(ex) - own_ref[part, 2, 1], own_ref[part, 1, 1] - steps.up_y(ex)
        for k, f in enumerate((ey, ez, hy, hz)):
            sent[down, part * SENT + 2 + k] = f.astype(half)
        e = [own_ref[part, comp, last] for comp in range(3)]
        behind = steps.magnetic_yz([own_ref[part, comp, last - 1] for comp in range(3)], e)
        hy, hz = steps.magnetic_yz(e, None)
        hx = steps.magnetic_x(e)
        coef = scales[part] * held_ref[last]
        after = []
        for comp in range(3):
            curl = steps.curl_back(comp, hx, hy, hz, behind)
            value = e[comp] - RELAX * curl + coef * own_ref[1 - part, comp, last]
            after.append(value + here * weight(part, comp))
        for k, f in enumerate((hy, hz) + steps.magnetic_yz(after, None)):
            sent[up, part * SENT + 2 + k] = f.astype(half)
    far_ref[...] = sent[0]
    near_ref[...] = sent[1]
    for copy in others:
        copy.wait()


def sweep_kernel(s, count, planes, scalar_ref, own_ref, edge_ref, held_ref, field_ref, one_in, other_in, near_cond, far_cond, *refs):
    depth, height, breadth = held_ref.shape
    final = s == count - 1
    near_in, far_in = (one_in, other_in) if s == 0 else (other_in, one_in)
    if final:
        earlier = refs[:s]
        rows_ref, far_ref, near_ref, one_, two_, got, conds, sent = refs[s:]
    else:
        rows_ref, one_, two_, got, conds = refs
    steps = Steps(height, breadth)
    index = lax.axis_index("space")
    first = index * depth
    relax_low = jnp.where(first > 0, F32(RELAX), F32(0.0))
    relax_high = jnp.where(first + depth < planes, F32(RELAX), F32(0.0))
    low = index & 1
    high = 1 - low
    receive(got, far_in, near_in, (first == 0) | (first + depth == planes))
    conds[0] = far_cond[2 * SENT]
    conds[1] = near_cond[2 * SENT]
    group = scalar_ref[count + s].astype(jnp.int32)
    angular = angular_of(scalar_ref[2 * count + group].astype(jnp.int32))
    scales = RELAX * angular, -RELAX * angular
    point = Point(scalar_ref[s].astype(jnp.int32), first, steps)
    weights_at = scalar_ref.shape[0] - 6 * count + 6 * s

    def conductivity(p):
        if p < 0:
            return conds[low].astype(F32)
        if p >= depth:
            return conds[high].astype(F32)
        return held_ref[p]

    def received(side, part, k):
        return got[side, part * SENT + k].astype(F32)

    def weight(part, comp):
        return scalar_ref[weights_at + part * 3 + comp]

    for part in range(2):
        ey, ez, ly, lz = [edge_ref[part, k] for k in range(4)]
        one_[part, 0, 0] = -relax_low * (steps.down_y(ey) + steps.down_z(ez))
        one_[part, 1, 0] = relax_low * ey
        one_[part, 2, 0] = relax_low * ez
        e = [own_ref[part, comp, 0] for comp in range(3)]
        one_[part, 0, 1] = e[0]
        one_[part, 1, 1] = e[1] - RELAX * received(low, part, 1)
        one_[part, 2, 1] = e[2] + RELAX * received(low, part, 0)
        for p in range(1, depth - 1):
            for comp in range(3):
                one_[part, comp, p + 1] = own_ref[part, comp, p]
        e = [own_ref[part, comp, depth - 1] for comp in range(3)]
        high_y, high_z = received(high, part, 0), received(high, part, 1)
        one_[part, 0, depth] = e[0] - RELAX * (steps.down_y(high_y) + steps.down_z(high_z))
        one_[part, 1, depth] = e[1] + RELAX * high_y
        one_[part, 2, depth] = e[2] + RELAX * high_z
        one_[part, 1, depth + 1] = received(high, part, 2) - relax_high * lz
        one_[part, 2, depth + 1] = received(high, part, 3) + relax_high * ly

    before = [(-one_[part, 2, 0], one_[part, 1, 0]) for part in range(2)]
    for p in range(-1, depth + 1):
        relax = relax_low if p < 0 else relax_high if p == depth else F32(RELAX)
        for part in range(2):
            e = [one_[part, comp, p + 1] if comp or p < depth else None for comp in range(3)]
            if p < depth:
                hy, hz = steps.magnetic_yz(e, [None, one_[part, 1, p + 2], one_[part, 2, p + 2]])
            else:
                hy, hz = received(high, part, 4) + e[2], received(high, part, 5) - e[1]
            hx = steps.magnetic_x(e)
            coef = scales[part] * conductivity(p)
            for comp in range(1 if p == depth else 0, 3):
                curl = steps.curl_back(comp, hx, hy, hz, before[part])
                two_[part, comp, p + 1] = e[comp] - relax * curl + coef * one_[1 - part, comp, p + 1]
            if p < 0:
                hy, hz = hy + received(low, part, 2), hz + received(low, part, 3)
            before[part] = hy, hz
    for part in range(2):
        two_[part, 0, depth + 1] = jnp.zeros((height, breadth), F32)
    point.add_to(two_, 0, depth + 1, 1, weight)

    row = lax.broadcasted_iota(jnp.int32, (height, breadth), 0)
    here = (row == point.row) & (steps.lane == point.lane)
    before = []
    for part in range(2):
        e = [two_[part, comp, 0] for comp in range(3)]
        hy, hz = steps.magnetic_yz(e, [None, two_[part, 1, 1], two_[part, 2, 1]])
        before.append((hy + received(low, part, 4), hz + received(low, part, 5)))
    for p in range(depth):
        spot = jnp.where(here, jnp.where(point.plane == p, F32(RELAX), F32(0.0)), 0.0)
        after = []
        for part in range(2):
            e = [two_[part, comp, p + 1] for comp in range(3)]
            hy, hz = steps.magnetic_yz(e, [None, two_[part, 1, p + 2], two_[part, 2, p + 2]])
            hx = steps.magnetic_x(e)
            coef = scales[part] * held_ref[p]
            for comp in range(3):
                curl = steps.curl_back(comp, hx, hy, hz, before[part])
                value = e[comp] - RELAX * curl + coef * two_[1 - part, comp, p + 1]
                after.append(value + spot * weight(part, comp))
            before[part] = hy, hz
        row_re = row_im = None
        for comp in range(3):
            re, im = after[comp], after[3 + comp]
            field_re, field_im = field_ref[group, 0, comp, p], field_ref[group, 1, comp, p]
            add_re, add_im = field_re * re - field_im * im, field_re * im + field_im * re
            row_re, row_im = (add_re, add_im) if comp == 0 else (row_re + add_re, row_im + add_im)
        coef = angular * held_ref[p]
        for part, value in enumerate((row_re, row_im)):
            value = (coef * value).astype(rows_ref.dtype)
            if not final:
                rows_ref[part, p] = value
                continue
            rows_ref[s, part, p] = value
            if p >= depth - REACH:
                sent[high, s, part, p - depth + REACH] = value
            if p < REACH:
                sent[low, s, part, p] = value
    if final:
        for t, ref in enumerate(earlier):
            rows_ref[t] = ref[...]
            sent[high, t] = ref[:, depth - REACH :]
            sent[low, t] = ref[:, :REACH]
        far_ref[...] = sent[0]
        near_ref[...] = sent[1]


def in_plane(steps, f):
    total = (steps.after_y(f) + steps.before_y(f)) + (steps.after_z(f) + steps.before_z(f))
    return (1.0 - 6.0 * KAPPA) * f + KAPPA * total


def smooth_kernel(planes, rows_ref, alone_ref):
    count, _, depth, height, breadth = rows_ref.shape
    steps = Steps(height, breadth)
    first = lax.axis_index("space") * depth
    below = jnp.where(first > 0, F32(KAPPA), F32(0.0))
    above = jnp.where(first + depth < planes, F32(KAPPA), F32(0.0))

    def one_row(s, part):
        value = [rows_ref[s, part, p].astype(F32) for p in range(depth)]
        once = []
        for p in range(depth):
            beside = [value[q] for q in (p - 1, p + 1) if 0 <= q < depth]
            once.append(in_plane(steps, value[p]) + KAPPA * functools.reduce(jnp.add, beside))
        once = [below * value[0]] + once + [above * value[-1]]
        for p in range(depth):
            alone_ref[s, part, p] = in_plane(steps, once[p + 1]) + KAPPA * (once[p] + once[p + 2])

    def one_source(s, _):
        for part in range(2):
            one_row(s, part)
        return 0

    lax.fori_loop(0, count, one_source, 0)


def block_kernel(cells, rows_ref, alone_ref, far_in, near_in, *refs):
    count, _, depth, height, breadth = rows_ref.shape
    ranks = len(refs) - 5
    all_refs = (rows_ref,) + refs[: ranks - 1]
    smooth_ref, block_ref, got, rounded, sums, sem = refs[ranks - 1 :]
    rank = lax.axis_index("rx")
    steps = Steps(height, breadth)
    many = ranks * count * 2
    index = lax.axis_index("space")
    receive(got, far_in, near_in, (index == 0) | (index == lax.axis_size("space") - 1))
    odd = index & 1
    low, high = odd, 1 - odd

    def one_row(s, part):
        value = [alone_ref[s, part, p] for p in range(depth)]
        for side, nearest, order in ((low, REACH - 1, 1), (high, 0, -1)):
            close = got[side, s, part, nearest].astype(F32)
            beyond = got[side, s, part, REACH - 1 - nearest].astype(F32)
            end = 0 if order > 0 else depth - 1
            value[end] = value[end] + (2.0 * KAPPA * in_plane(steps, close) + KAPPA * KAPPA * beyond)
            value[end + order] = value[end + order] + KAPPA * KAPPA * close
        for p in range(depth):
            rounded[s, part, p] = value[p].astype(rounded.dtype)

    def one_source(s, _):
        for part in range(2):
            one_row(s, part)
        return 0

    lax.fori_loop(0, count, one_source, 0)
    out = pltpu.make_async_copy(rounded, smooth_ref, sem)
    out.start()

    sums[...] = jnp.zeros_like(sums)

    def one_plane(p, _):
        mine = [rounded[a // 2, a % 2, p].astype(F32) for a in range(2 * count)]
        for b in range(many):
            r, t = divmod(b // 2, count)
            other = all_refs[r][t, b % 2, p].astype(F32)
            for a in range(2 * count):
                prod = mine[a] * other
                total = prod[:8]
                for k in range(8, height, 8):
                    total = total + prod[k : k + 8]
                sums[a * many + b] = sums[a * many + b] + total
        return 0

    lax.fori_loop(0, depth, one_plane, 0)
    half = jnp.bfloat16
    ones = jnp.ones((breadth, breadth), half)
    for a in range(2 * count):
        table = sums[a * many : (a + 1) * many].reshape(many * 8, breadth)
        coarse = table.astype(half)
        fine = (table - coarse.astype(F32)).astype(half)
        table = jnp.dot(coarse, ones, preferred_element_type=F32) + jnp.dot(fine, ones, preferred_element_type=F32)
        line = None
        for b in range(many):
            place = (rank ^ (b // (2 * count))) * (2 * count) + b % (2 * count)
            add = jnp.where(steps.lane[:8] == place, table[b * 8 : b * 8 + 8], 0.0)
            line = add if line is None else line + add
        line = jnp.sum(line, axis=0, keepdims=True) * (1.0 / cells)
        for peer in range(block_ref.shape[0]):
            block_ref[peer, a : a + 1, :] = line[:, :many]
    out.wait()


def in_hbm(x):
    return pltpu.with_memory_space_constraint(x, pltpu.HBM)


def shards(conductivity, background, warm_start, data_weight, recv_cell, src_group, group_freq):
    count = warm_start.shape[0]
    depth, height, breadth = conductivity.shape
    plane = (height, breadth)
    peers = lax.axis_size("space")
    ranks = lax.axis_size("rx")
    cells = depth * height * breadth * peers
    half = jnp.bfloat16
    integers = jnp.concatenate([recv_cell, src_group, group_freq]).astype(F32)
    scalars = jnp.concatenate([integers, data_weight.reshape(-1)])
    assert peers % 2 == 0 and ranks % 2 == 0
    both = ("rx", "space")
    far = [(r * peers + i, r * peers + i + 1) for r in range(ranks) for i in range(1, peers - 1, 2)]
    far += [(r * peers + i, (r + 1) * peers + i) for r in range(0, ranks, 2) for i in (0, peers - 1)]
    near = [(i, i + 1) for i in range(0, peers, 2)]
    far, near = [pairs + [(j, i) for i, j in pairs] for pairs in (far, near)]
    shape = jax.ShapeDtypeStruct

    own, edges, fars, nears = [], [], [], []
    for s in range(count):
        message = shape((2 * SENT + (s == 0),) + plane, half)
        outs = [message, message, shape(warm_start.shape[1:], F32), shape((2, 4) + plane, F32)]
        scratch = [pltpu.VMEM((2,) + message.shape, half)]
        if s == 0:
            operands = [warm_start, conductivity, background, data_weight, recv_cell, src_group, group_freq]
            operands = [in_hbm(x) for x in operands]
            specs = [HBM] * 7
            outs += [
                shape(conductivity.shape, F32),
                shape((count - 1,) + warm_start.shape[1:], F32),
                shape(background.shape, F32),
            ]
            scratch = [
                pltpu.VMEM(warm_start.shape[1:], F32),
                pltpu.SMEM(data_weight.shape, F32),
                pltpu.SMEM(recv_cell.shape, jnp.int32),
                pltpu.SMEM(src_group.shape, jnp.int32),
                pltpu.SMEM(group_freq.shape, jnp.int32),
            ] + scratch + [pltpu.SemaphoreType.DMA((8,))]
        else:
            operands = [later, scalars, held]
            specs = [FULL, SCALARS, FULL]
        result = pl.pallas_call(
            functools.partial(first_kernel, s),
            out_shape=tuple(outs),
            in_specs=specs,
            out_specs=(FULL,) * len(outs),
            scratch_shapes=scratch,
            compiler_params=KERNEL,
            name="first_sweep",
        )(*operands)
        if s == 0:
            held, later, field = result[4:]
        own.append(result[2])
        edges.append(result[3])
        nears.append(lax.ppermute(result[1], "space", near))
        fars.append(lax.ppermute(result[0], both, far))

    rows_of = shape((count, 2, depth) + plane, half)
    ends_of = shape((count, 2, REACH) + plane, half)
    earlier = []
    for s in range(count):
        swaps = (nears[s], fars[s]) if s == 0 else (fars[s], nears[s])
        operands = [scalars, own[s], edges[s], held, field, *swaps, nears[0], fars[0]]
        scratch = [
            pltpu.VMEM((2, 3, depth + 2) + plane, F32),
            pltpu.VMEM((2, 3, depth + 2) + plane, F32),
            pltpu.VMEM((2, 2 * SENT) + plane, half),
            pltpu.VMEM((2,) + plane, half),
        ]
        results = (shape((2, depth) + plane, half),)
        if s == count - 1:
            operands += earlier
            results = (rows_of, ends_of, ends_of)
            scratch.append(pltpu.VMEM((2,) + ends_of.shape, half))
        results = pl.pallas_call(
            functools.partial(sweep_kernel, s, count, peers * depth),
            out_shape=results,
            in_specs=[SCALARS] + [FULL] * (len(operands) - 1),
            out_specs=(FULL,) * len(results),
            scratch_shapes=scratch,
            compiler_params=KERNEL,
            name="sweeps",
        )(*operands)
        earlier.append(results[0])
    rows, to_far, to_near = results
    from_far = lax.ppermute(to_far, both, far)
    from_near = lax.ppermute(to_near, "space", near)
    assert ranks & (ranks - 1) == 0
    others = [lax.ppermute(rows, "rx", [(r, r ^ k) for r in range(ranks)]) for k in range(1, ranks)]

    many = 2 * count * ranks
    alone = pl.pallas_call(
        functools.partial(smooth_kernel, peers * depth),
        out_shape=shape(rows_of.shape, F32),
        in_specs=[FULL],
        out_specs=FULL,
        compiler_params=KERNEL,
        name="smooth",
    )(rows)
    smoothed, partial_block = pl.pallas_call(
        functools.partial(block_kernel, cells),
        out_shape=(rows_of, shape((peers, 2 * count, many), F32)),
        in_specs=[FULL] * (4 + len(others)),
        out_specs=(HBM, FULL),
        scratch_shapes=[
            pltpu.VMEM((2,) + ends_of.shape, half),
            pltpu.VMEM(rows_of.shape, half),
            pltpu.VMEM((2 * count * many, 8, breadth), F32),
            pltpu.SemaphoreType.DMA,
        ],
        compiler_params=KERNEL,
        name="block",
    )(rows, alone, from_far, from_near, *others)
    backwards = [list(range(peers - 1, -1, -1))]
    pieces = lax.all_to_all(partial_block, "space", 0, 0, axis_index_groups=backwards)
    return (jnp.sum(pieces, axis=0), smoothed)


def solution(mesh):
    in_specs = (
        P("space", None, None),
        P(None, None, None, "space", None, None),
        P("rx", None, None, "space", None, None),
        P("rx", None, None),
        P("rx"),
        P("rx"),
        P(),
    )
    out_specs = (P("rx", None), P("rx", None, "space", None, None))
    return jax.shard_map(shards, mesh=mesh, in_specs=in_specs, out_specs=out_specs, check_vma=False)
```

```python
import functools

import jax
import jax.numpy as jnp
from jax import lax
from jax.experimental import pallas as pl
from jax.experimental.pallas import tpu as pltpu
from jax.sharding import PartitionSpec as P

SENT = 6
RELAX = 0.2
KAPPA = 0.1
REACH = 2
FULL = pl.BlockSpec(memory_space=pltpu.VMEM)
HBM = pl.BlockSpec(memory_space=pltpu.HBM)
SCALARS = pl.BlockSpec(memory_space=pltpu.SMEM)
KERNEL = pltpu.CompilerParams(vmem_limit_bytes=8 * 2**20)
F32 = jnp.float32


class Steps:
    def __init__(self, height, breadth):
        self.height, self.breadth = height, breadth
        self.sub = lax.broadcasted_iota(jnp.int32, (8, breadth), 0)
        self.lane = lax.broadcasted_iota(jnp.int32, (height, breadth), 1)

    def after_y(self, f):
        f = pltpu.roll(f, self.height - 1, 0)
        return jnp.concatenate([f[:-8], jnp.where(self.sub < 7, f[-8:], 0.0)], axis=0)

    def before_y(self, f):
        f = pltpu.roll(f, 1, 0)
        return jnp.concatenate([jnp.where(self.sub > 0, f[:8], 0.0), f[8:]], axis=0)

    def after_z(self, f):
        return jnp.where(self.lane < self.breadth - 1, pltpu.roll(f, self.breadth - 1, 1), 0.0)

    def before_z(self, f):
        return jnp.where(self.lane > 0, pltpu.roll(f, 1, 1), 0.0)

    def up_y(self, f):
        return self.after_y(f) - f

    def up_z(self, f):
        return self.after_z(f) - f

    def down_y(self, f):
        return f - self.before_y(f)

    def down_z(self, f):
        return f - self.before_z(f)

    def magnetic_yz(self, e, e_next):
        ex, ey, ez = e
        if e_next is None:
            return self.up_z(ex) + ez, -ey - self.up_y(ex)
        return self.up_z(ex) - (e_next[2] - ez), (e_next[1] - ey) - self.up_y(ex)

    def magnetic_x(self, e):
        return self.up_y(e[2]) - self.up_z(e[1])

    def curl_back(self, comp, hx, hy, hz, before):
        if comp == 0:
            return self.down_y(hz) - self.down_z(hy)
        if comp == 1:
            return self.down_z(hx) - (hz - before[1])
        return (hy - before[0]) - self.down_y(hx)


def angular_of(freq):
    angular = F32(0.25)
    for bit, factor in ((1, 1.25), (2, 1.25**2), (4, 1.25**4)):
        angular = angular * jnp.where((freq & bit) != 0, F32(factor), F32(1.0))
    return angular


def split(number, size):
    if size & (size - 1):
        return number // size, number % size
    return number >> (size.bit_length() - 1), number & (size - 1)


class Point:
    def __init__(self, cell, first, steps):
        plane, inner = split(cell, steps.height * steps.breadth)
        row, lane = split(inner, steps.breadth)
        block, sub = split(row, 8)
        self.plane = plane - first
        self.rows = pl.ds(pl.multiple_of(block * 8, 8), 8)
        self.row, self.sub, self.lane, self.steps = row, sub, lane, steps

    def add_to(self, ref, low, high, shift, weight):
        reached = (self.plane >= low) & (self.plane < high)
        here = (self.steps.sub == self.sub) & (self.steps.lane[:8] == self.lane)
        amount = jnp.where(here, jnp.where(reached, F32(RELAX), F32(0.0)), 0.0)
        plane = jnp.clip(self.plane, low, high - 1) + shift
        for part in range(2):
            for comp in range(3):
                at = (part, comp, plane, self.rows)
                ref[at] = ref[at] + amount * weight(part, comp)


def receive(got, far_in, near_in, at_end):
    got[1] = near_in[: got.shape[1]]

    @pl.when(at_end)
    def _():
        got[0] = jnp.zeros(got.shape[1:], got.dtype)

    @pl.when(jnp.logical_not(at_end))
    def _():
        got[0] = far_in[: got.shape[1]]


def first_kernel(s, planes_ref, *refs):
    if s == 0:
        cond_ref, back_ref, weight_ref, cell_ref, group_ref, freq_ref = refs[:6]
        far_ref, near_ref, own_ref, edge_ref, held_ref, later_ref, field_ref = refs[6:13]
        raw, weight_of, cell, group, freq, sent, sems = refs[13:]
        count = planes_ref.shape[0]
        small = ((group_ref, group), (freq_ref, freq), (cell_ref, cell), (weight_ref, weight_of), (cond_ref, held_ref))
        copies = [pltpu.make_async_copy(planes_ref.at[0], raw, sems.at[0])]
        copies += [pltpu.make_async_copy(a, b, sems.at[k + 1]) for k, (a, b) in enumerate(small)]
        others = [pltpu.make_async_copy(planes_ref.at[pl.ds(1, count - 1)], later_ref, sems.at[len(copies)])]
        others.append(pltpu.make_async_copy(back_ref, field_ref, sems.at[len(copies) + 1]))
        for copy in copies[1:] + copies[:1] + others:
            copy.start()
        for copy in copies:
            copy.wait()
        angular = angular_of(freq[group[s]])
        cell_at = cell[s]

        def weight(part, comp):
            return weight_of[s, part, comp]
    else:
        scalar_ref, held_ref, far_ref, near_ref, own_ref, edge_ref, sent = refs
        raw = planes_ref.at[s - 1]
        count = planes_ref.shape[0] + 1
        others = []
        group = scalar_ref[count + s].astype(jnp.int32)
        angular = angular_of(scalar_ref[2 * count + group].astype(jnp.int32))
        cell_at = scalar_ref[s].astype(jnp.int32)
        weights_at = scalar_ref.shape[0] - 6 * count + 6 * s

        def weight(part, comp):
            return scalar_ref[weights_at + part * 3 + comp]

    depth, height, breadth = held_ref.shape
    steps = Steps(height, breadth)
    half = sent.dtype
    index = lax.axis_index("space")
    first = index * depth
    down = index & 1
    up = 1 - down
    last = depth - 1
    scales = RELAX * angular, -RELAX * angular
    point = Point(cell_at, first, steps)
    if s == 0:
        sent[up, 2 * SENT] = held_ref[last].astype(half)
        sent[down, 2 * SENT] = held_ref[0].astype(half)

    before = []
    for part in range(2):
        ey, ez = raw[part, 1, 0], raw[part, 2, 0]
        for k, f in enumerate((ey, ez)):
            sent[down, part * SENT + k] = f.astype(half)
            edge_ref[part, k] = f
        before.append((-ez, ey))
    for p in range(depth):
        for part in range(2):
            e = [raw[part, comp, p] for comp in range(3)]
            e_next = [None if comp == 0 else raw[part, comp, p + 1] for comp in range(3)] if p < last else None
            hy, hz = steps.magnetic_yz(e, e_next)
            if p == last:
                for k, f in enumerate((hy, hz)):
                    sent[up, part * SENT + k] = f.astype(half)
                    edge_ref[part, 2 + k] = f
            hx = steps.magnetic_x(e)
            coef = scales[part] * held_ref[p]
            for comp in range(3):
                curl = steps.curl_back(comp, hx, hy, hz, before[part])
                own_ref[part, comp, p] = e[comp] - RELAX * curl + coef * raw[1 - part, comp, p]
            before[part] = hy, hz
    point.add_to(own_ref, 0, depth, 0, weight)

    row = lax.broadcasted_iota(jnp.int32, (height, breadth), 0)
    at_last = jnp.where(point.plane == last, F32(1.0), F32(0.0))
    here = jnp.where((row == point.row) & (steps.lane == point.lane), RELAX * at_last, 0.0)
    for part in range(2):
        ex, ey, ez = [own_ref[part, comp, 0] for comp in range(3)]
        hy, hz = steps.up_z(ex) - own_ref[part, 2, 1], own_ref[part, 1, 1] - steps.up_y(ex)
        for k, f in enumerate((ey, ez, hy, hz)):
            sent[down, part * SENT + 2 + k] = f.astype(half)
        e = [own_ref[part, comp, last] for comp in range(3)]
        behind = steps.magnetic_yz([own_ref[part, comp, last - 1] for comp in range(3)], e)
        hy, hz = steps.magnetic_yz(e, None)
        hx = steps.magnetic_x(e)
        coef = scales[part] * held_ref[last]
        after = []
        for comp in range(3):
            curl = steps.curl_back(comp, hx, hy, hz, behind)
            value = e[comp] - RELAX * curl + coef * own_ref[1 - part, comp, last]
            after.append(value + here * weight(part, comp))
        for k, f in enumerate((hy, hz) + steps.magnetic_yz(after, None)):
            sent[up, part * SENT + 2 + k] = f.astype(half)
    far_ref[...] = sent[0]
    near_ref[...] = sent[1]
    for copy in others:
        copy.wait()


def sweep_kernel(s, count, planes, scalar_ref, own_ref, edge_ref, held_ref, field_ref, one_in, other_in, near_cond, far_cond, *refs):
    depth, height, breadth = held_ref.shape
    final = s == count - 1
    near_in, far_in = (one_in, other_in) if s == 0 else (other_in, one_in)
    if final:
        earlier = refs[:s]
        rows_ref, far_ref, near_ref, one_, two_, got, conds, sent = refs[s:]
    else:
        rows_ref, one_, two_, got, conds = refs
    steps = Steps(height, breadth)
    index = lax.axis_index("space")
    first = index * depth
    relax_low = jnp.where(first > 0, F32(RELAX), F32(0.0))
    relax_high = jnp.where(first + depth < planes, F32(RELAX), F32(0.0))
    low = index & 1
    high = 1 - low
    receive(got, far_in, near_in, (first == 0) | (first + depth == planes))
    conds[0] = far_cond[2 * SENT]
    conds[1] = near_cond[2 * SENT]
    group = scalar_ref[count + s].astype(jnp.int32)
    angular = angular_of(scalar_ref[2 * count + group].astype(jnp.int32))
    scales = RELAX * angular, -RELAX * angular
    point = Point(scalar_ref[s].astype(jnp.int32), first, steps)
    weights_at = scalar_ref.shape[0] - 6 * count + 6 * s

    def conductivity(p):
        if p < 0:
            return conds[low].astype(F32)
        if p >= depth:
            return conds[high].astype(F32)
        return held_ref[p]

    def received(side, part, k):
        return got[side, part * SENT + k].astype(F32)

    def weight(part, comp):
        return scalar_ref[weights_at + part * 3 + comp]

    for part in range(2):
        ey, ez, ly, lz = [edge_ref[part, k] for k in range(4)]
        one_[part, 0, 0] = -relax_low * (steps.down_y(ey) + steps.down_z(ez))
        one_[part, 1, 0] = relax_low * ey
        one_[part, 2, 0] = relax_low * ez
        e = [own_ref[part, comp, 0] for comp in range(3)]
        one_[part, 0, 1] = e[0]
        one_[part, 1, 1] = e[1] - RELAX * received(low, part, 1)
        one_[part, 2, 1] = e[2] + RELAX * received(low, part, 0)
        for p in range(1, depth - 1):
            for comp in range(3):
                one_[part, comp, p + 1] = own_ref[part, comp, p]
        e = [own_ref[part, comp, depth - 1] for comp in range(3)]
        high_y, high_z = received(high, part, 0), received(high, part, 1)
        one_[part, 0, depth] = e[0] - RELAX * (steps.down_y(high_y) + steps.down_z(high_z))
        one_[part, 1, depth] = e[1] + RELAX * high_y
        one_[part, 2, depth] = e[2] + RELAX * high_z
        one_[part, 1, depth + 1] = received(high, part, 2) - relax_high * lz
        one_[part, 2, depth + 1] = received(high, part, 3) + relax_high * ly

    before = [(-one_[part, 2, 0], one_[part, 1, 0]) for part in range(2)]
    for p in range(-1, depth + 1):
        relax = relax_low if p < 0 else relax_high if p == depth else F32(RELAX)
        for part in range(2):
            e = [one_[part, comp, p + 1] if comp or p < depth else None for comp in range(3)]
            if p < depth:
                hy, hz = steps.magnetic_yz(e, [None, one_[part, 1, p + 2], one_[part, 2, p + 2]])
            else:
                hy, hz = received(high, part, 4) + e[2], received(high, part, 5) - e[1]
            hx = steps.magnetic_x(e)
            coef = scales[part] * conductivity(p)
            for comp in range(1 if p == depth else 0, 3):
                curl = steps.curl_back(comp, hx, hy, hz, before[part])
                two_[part, comp, p + 1] = e[comp] - relax * curl + coef * one_[1 - part, comp, p + 1]
            if p < 0:
                hy, hz = hy + received(low, part, 2), hz + received(low, part, 3)
            before[part] = hy, hz
    for part in range(2):
        two_[part, 0, depth + 1] = jnp.zeros((height, breadth), F32)
    point.add_to(two_, 0, depth + 1, 1, weight)

    row = lax.broadcasted_iota(jnp.int32, (height, breadth), 0)
    here = (row == point.row) & (steps.lane == point.lane)
    before = []
    for part in range(2):
        e = [two_[part, comp, 0] for comp in range(3)]
        hy, hz = steps.magnetic_yz(e, [None, two_[part, 1, 1], two_[part, 2, 1]])
        before.append((hy + received(low, part, 4), hz + received(low, part, 5)))
    for p in range(depth):
        spot = jnp.where(here, jnp.where(point.plane == p, F32(RELAX), F32(0.0)), 0.0)
        after = []
        for part in range(2):
            e = [two_[part, comp, p + 1] for comp in range(3)]
            hy, hz = steps.magnetic_yz(e, [None, two_[part, 1, p + 2], two_[part, 2, p + 2]])
            hx = steps.magnetic_x(e)
            coef = scales[part] * held_ref[p]
            for comp in range(3):
                curl = steps.curl_back(comp, hx, hy, hz, before[part])
                value = e[comp] - RELAX * curl + coef * two_[1 - part, comp, p + 1]
                after.append(value + spot * weight(part, comp))
            before[part] = hy, hz
        row_re = row_im = None
        for comp in range(3):
            re, im = after[comp], after[3 + comp]
            field_re, field_im = field_ref[group, 0, comp, p], field_ref[group, 1, comp, p]
            add_re, add_im = field_re * re - field_im * im, field_re * im + field_im * re
            row_re, row_im = (add_re, add_im) if comp == 0 else (row_re + add_re, row_im + add_im)
        coef = angular * held_ref[p]
        for part, value in enumerate((row_re, row_im)):
            value = (coef * value).astype(rows_ref.dtype)
            if not final:
                rows_ref[part, p] = value
                continue
            rows_ref[s, part, p] = value
            if p >= depth - REACH:
                sent[high, s, part, p - depth + REACH] = value
            if p < REACH:
                sent[low, s, part, p] = value
    if final:
        for t, ref in enumerate(earlier):
            rows_ref[t] = ref[...]
            sent[high, t] = ref[:, depth - REACH :]
            sent[low, t] = ref[:, :REACH]
        far_ref[...] = sent[0]
        near_ref[...] = sent[1]


def in_plane(steps, f):
    total = (steps.after_y(f) + steps.before_y(f)) + (steps.after_z(f) + steps.before_z(f))
    return (1.0 - 6.0 * KAPPA) * f + KAPPA * total


def smooth_kernel(planes, rows_ref, alone_ref):
    count, _, depth, height, breadth = rows_ref.shape
    steps = Steps(height, breadth)
    first = lax.axis_index("space") * depth
    below = jnp.where(first > 0, F32(KAPPA), F32(0.0))
    above = jnp.where(first + depth < planes, F32(KAPPA), F32(0.0))

    def one_row(s, part):
        value = [rows_ref[s, part, p].astype(F32) for p in range(depth)]
        once = []
        for p in range(depth):
            beside = [value[q] for q in (p - 1, p + 1) if 0 <= q < depth]
            once.append(in_plane(steps, value[p]) + KAPPA * functools.reduce(jnp.add, beside))
        once = [below * value[0]] + once + [above * value[-1]]
        for p in range(depth):
            alone_ref[s, part, p] = in_plane(steps, once[p + 1]) + KAPPA * (once[p] + once[p + 2])

    def one_source(s, _):
        for part in range(2):
            one_row(s, part)
        return 0

    lax.fori_loop(0, count, one_source, 0)


def block_kernel(cells, rows_ref, alone_ref, far_in, near_in, all_ref, smooth_ref, block_ref, got, rounded, sums, sem):
    count, _, depth, height, breadth = rows_ref.shape
    ranks = all_ref.shape[0]
    steps = Steps(height, breadth)
    many = ranks * count * 2
    index = lax.axis_index("space")
    receive(got, far_in, near_in, (index == 0) | (index == lax.axis_size("space") - 1))
    odd = index & 1
    low, high = odd, 1 - odd

    def one_row(s, part):
        value = [alone_ref[s, part, p] for p in range(depth)]
        for side, nearest, order in ((low, REACH - 1, 1), (high, 0, -1)):
            close = got[side, s, part, nearest].astype(F32)
            beyond = got[side, s, part, REACH - 1 - nearest].astype(F32)
            end = 0 if order > 0 else depth - 1
            value[end] = value[end] + (2.0 * KAPPA * in_plane(steps, close) + KAPPA * KAPPA * beyond)
            value[end + order] = value[end + order] + KAPPA * KAPPA * close
        for p in range(depth):
            rounded[s, part, p] = value[p].astype(rounded.dtype)

    def one_source(s, _):
        for part in range(2):
            one_row(s, part)
        return 0

    lax.fori_loop(0, count, one_source, 0)
    out = pltpu.make_async_copy(rounded, smooth_ref, sem)
    out.start()

    sums[...] = jnp.zeros_like(sums)

    def one_plane(p, _):
        mine = [rounded[a // 2, a % 2, p].astype(F32) for a in range(2 * count)]
        for b in range(many):
            r, t = divmod(b // 2, count)
            other = all_ref[r, t, b % 2, p].astype(F32)
            for a in range(2 * count):
                prod = mine[a] * other
                total = prod[:8]
                for k in range(8, height, 8):
                    total = total + prod[k : k + 8]
                sums[a * many + b] = sums[a * many + b] + total
        return 0

    lax.fori_loop(0, depth, one_plane, 0)
    half = jnp.bfloat16
    ones = jnp.ones((breadth, breadth), half)
    for a in range(2 * count):
        table = sums[a * many : (a + 1) * many].reshape(many * 8, breadth)
        coarse = table.astype(half)
        fine = (table - coarse.astype(F32)).astype(half)
        table = jnp.dot(coarse, ones, preferred_element_type=F32) + jnp.dot(fine, ones, preferred_element_type=F32)
        line = None
        for b in range(many):
            add = jnp.where(steps.lane[:8] == b, table[b * 8 : b * 8 + 8], 0.0)
            line = add if line is None else line + add
        line = jnp.sum(line, axis=0, keepdims=True) * (1.0 / cells)
        for peer in range(block_ref.shape[0]):
            block_ref[peer, a : a + 1, :] = line[:, :many]
    out.wait()


def in_hbm(x):
    return pltpu.with_memory_space_constraint(x, pltpu.HBM)


def shards(conductivity, background, warm_start, data_weight, recv_cell, src_group, group_freq):
    count = warm_start.shape[0]
    depth, height, breadth = conductivity.shape
    plane = (height, breadth)
    peers = lax.axis_size("space")
    ranks = lax.axis_size("rx")
    cells = depth * height * breadth * peers
    half = jnp.bfloat16
    integers = jnp.concatenate([recv_cell, src_group, group_freq]).astype(F32)
    scalars = jnp.concatenate([integers, data_weight.reshape(-1)])
    assert peers % 2 == 0 and ranks % 2 == 0
    both = ("rx", "space")
    far = [(r * peers + i, r * peers + i + 1) for r in range(ranks) for i in range(1, peers - 1, 2)]
    far += [(r * peers + i, (r + 1) * peers + i) for r in range(0, ranks, 2) for i in (0, peers - 1)]
    near = [(i, i + 1) for i in range(0, peers, 2)]
    far, near = [pairs + [(j, i) for i, j in pairs] for pairs in (far, near)]
    shape = jax.ShapeDtypeStruct

    own, edges, fars, nears = [], [], [], []
    for s in range(count):
        message = shape((2 * SENT + (s == 0),) + plane, half)
        outs = [message, message, shape(warm_start.shape[1:], F32), shape((2, 4) + plane, F32)]
        scratch = [pltpu.VMEM((2,) + message.shape, half)]
        if s == 0:
            operands = [warm_start, conductivity, background, data_weight, recv_cell, src_group, group_freq]
            operands = [in_hbm(x) for x in operands]
            specs = [HBM] * 7
            outs += [
                shape(conductivity.shape, F32),
                shape((count - 1,) + warm_start.shape[1:], F32),
                shape(background.shape, F32),
            ]
            scratch = [
                pltpu.VMEM(warm_start.shape[1:], F32),
                pltpu.SMEM(data_weight.shape, F32),
                pltpu.SMEM(recv_cell.shape, jnp.int32),
                pltpu.SMEM(src_group.shape, jnp.int32),
                pltpu.SMEM(group_freq.shape, jnp.int32),
            ] + scratch + [pltpu.SemaphoreType.DMA((8,))]
        else:
            operands = [later, scalars, held]
            specs = [FULL, SCALARS, FULL]
        result = pl.pallas_call(
            functools.partial(first_kernel, s),
            out_shape=tuple(outs),
            in_specs=specs,
            out_specs=(FULL,) * len(outs),
            scratch_shapes=scratch,
            compiler_params=KERNEL,
            name="first_sweep",
        )(*operands)
        if s == 0:
            held, later, field = result[4:]
        own.append(result[2])
        edges.append(result[3])
        nears.append(lax.ppermute(result[1], "space", near))
        fars.append(lax.ppermute(result[0], both, far))

    rows_of = shape((count, 2, depth) + plane, half)
    ends_of = shape((count, 2, REACH) + plane, half)
    earlier = []
    for s in range(count):
        swaps = (nears[s], fars[s]) if s == 0 else (fars[s], nears[s])
        operands = [scalars, own[s], edges[s], held, field, *swaps, nears[0], fars[0]]
        scratch = [
            pltpu.VMEM((2, 3, depth + 2) + plane, F32),
            pltpu.VMEM((2, 3, depth + 2) + plane, F32),
            pltpu.VMEM((2, 2 * SENT) + plane, half),
            pltpu.VMEM((2,) + plane, half),
        ]
        results = (shape((2, depth) + plane, half),)
        if s == count - 1:
            operands += earlier
            results = (rows_of, ends_of, ends_of)
            scratch.append(pltpu.VMEM((2,) + ends_of.shape, half))
        results = pl.pallas_call(
            functools.partial(sweep_kernel, s, count, peers * depth),
            out_shape=results,
            in_specs=[SCALARS] + [FULL] * (len(operands) - 1),
            out_specs=(FULL,) * len(results),
            scratch_shapes=scratch,
            compiler_params=KERNEL,
            name="sweeps",
        )(*operands)
        earlier.append(results[0])
    rows, to_far, to_near = results
    from_far = lax.ppermute(to_far, both, far)
    from_near = lax.ppermute(to_near, "space", near)
    every = lax.all_gather(rows, "rx", axis=0)

    many = 2 * count * ranks
    alone = pl.pallas_call(
        functools.partial(smooth_kernel, peers * depth),
        out_shape=shape(rows_of.shape, F32),
        in_specs=[FULL],
        out_specs=FULL,
        compiler_params=KERNEL,
        name="smooth",
    )(rows)
    smoothed, partial_block = pl.pallas_call(
        functools.partial(block_kernel, cells),
        out_shape=(rows_of, shape((peers, 2 * count, many), F32)),
        in_specs=[FULL] * 5,
        out_specs=(HBM, FULL),
        scratch_shapes=[
            pltpu.VMEM((2,) + ends_of.shape, half),
            pltpu.VMEM(rows_of.shape, half),
            pltpu.VMEM((2 * count * many, 8, breadth), F32),
            pltpu.SemaphoreType.DMA,
        ],
        compiler_params=KERNEL,
        name="block",
    )(rows, alone, from_far, from_near, every)
    backwards = [list(range(peers - 1, -1, -1))]
    pieces = lax.all_to_all(partial_block, "space", 0, 0, axis_index_groups=backwards)
    return (jnp.sum(pieces, axis=0), smoothed)


def solution(mesh):
    in_specs = (
        P("space", None, None),
        P(None, None, None, "space", None, None),
        P("rx", None, None, "space", None, None),
        P("rx", None, None),
        P("rx"),
        P("rx"),
        P(),
    )
    out_specs = (P("rx", None), P("rx", None, "space", None, None))
    return jax.shard_map(shards, mesh=mesh, in_specs=in_specs, out_specs=out_specs, check_vma=False)
```
